32 devices in a mesh: expert: 8 (over y, x, core), shard: 4 (over z).
Axes of the slice: x: 2, y: 2, z: 4, core: 2. Of those that a mesh axis runs over, the one named last changes fastest.
Arguments:
- hidden_in: bfloat16 [4, 1024, 1, 768], P('shard', 'expert'), may hold values from -6 to 6
- attn_gain: bfloat16 [2, 768], P(None, 'shard'), may hold values from 0.5 to 1.5
- qkv_weight: bfloat16 [2, 768, 2304], P(None, 'shard'), may hold values from -0.36084392 to 0.36084392
- out_weight: bfloat16 [2, 768, 768], P(None, 'shard'), may hold values from -1.25 to 1.25
- rel_bias: bfloat16 [2, 32, 12], P(None, 'shard'), may hold values from -4 to 4
- bucket_table: int32 [1024], replicated, may hold values from 0 to 31, as said below
- mlp_gain: bfloat16 [2, 768], P(None, 'shard'), may hold values from 0.5 to 1.5
- mlp_up: bfloat16 [768, 3072], P('shard'), may hold values from -0.21875 to 0.21875
- mlp_down: bfloat16 [3072, 768], P('shard'), may hold values from -0.109375 to 0.109375
- router_weight: bfloat16 [768, 16], P('shard'), may hold values from -0.375 to 0.375
- expert_up: bfloat16 [16, 768, 3072], P('expert', 'shard'), may hold values from -0.21875 to 0.21875
- expert_down: bfloat16 [16, 3072, 768], P('expert', 'shard'), may hold values from -0.109375 to 0.109375
- routes: int32 [4, 1024, 1, 2], P('shard', 'expert'), may hold values from 0 to 15, all different within a row; in each aligned block of 128 rows (0 to 127, 128 to 255, ..., all dimensions but the last counted through in order) at most 32 rows name the same one
- out_grad: bfloat16 [4, 1024, 1, 768], P('shard', 'expert'), may hold values from -6 to 6
Outputs:
- hidden_out: bfloat16 [4, 1024, 1, 768], P('shard', 'expert')
- hidden_grad: float32 [4, 1024, 1, 768], P('shard', 'expert')
- attn_gain_grad: float32 [2, 768], P(None, 'shard')
- qkv_grad: float32 [2, 768, 2304], P(None, 'shard')
- out_weight_grad: float32 [2, 768, 768], P(None, 'shard')
- rel_bias_grad: float32 [2, 32, 12], P(None, 'shard')
- mlp_gain_grad: float32 [2, 768], P(None, 'shard')
- mlp_up_grad: float32 [768, 3072], P('shard')
- mlp_down_grad: float32 [3072, 768], P('shard')
- router_grad: float32 [768, 16], P('shard')
- expert_up_grad: float32 [16, 768, 3072], P('expert', 'shard')
- expert_down_grad: float32 [16, 3072, 768], P('expert', 'shard')
- clip_scales: float32 [2, 12], replicated
The draws below stay inside these ranges and needn't reach their ends.
Inputs may be any that keep to these rules, and one draw needn't show every extreme that they name: `routes`: each row names two different experts; among the 128 tokens that one device holds (an aligned block of the flattened rows), no expert is named more than 32 times, a bound that some block reaches. `bucket_table`: Non-decreasing in the distance; 0 at distance 0 and 31 at distance 1024 - 1.
All inputs are finite; a program needn't handle non-finite values.
Results may differ from the reference program's by a relative error of at most 0.03.
Values may be sent and summed in bfloat16 or wider, within the bound.
A program may use at most 320 MiB of HBM per device.

```python
import math
import jax
import jax.numpy as jnp
import numpy as np
from jax import lax

D = 768
H = 12
HD = 64
FF = 3072
NB = 32
SEQS = 1
LENGTH = 1024
TOK_DEV = 128
GROUPS = 4
EXPERTS = 16
CAP = 32
N_EXPERT = 8
N_SHARD = 4


def draw_bucket_table(key, part):
    key = jax.random.fold_in(key, 11)
    buckets = jax.random.randint(key, (LENGTH,), 0, NB)
    buckets = jnp.sort(buckets)
    buckets = buckets.at[0].set(0).at[LENGTH - 1].set(NB - 1)
    return buckets.astype(jnp.int32)


def draw_qkv_weight(key, part):
    key = jax.random.fold_in(key, 5)
    weight_key, order_key = jax.random.split(key)
    base = jax.random.truncated_normal(weight_key, -4.0, 4.0, (2, D, 3 * D), jnp.float32) * D ** (-0.5)
    orders = jnp.stack([jax.random.permutation(jax.random.fold_in(order_key, 0), H), jax.random.permutation(jax.random.fold_in(order_key, 1), H)])
    levels = 0.6 * (2.5 / 0.6) ** (orders.astype(jnp.float32) / (H - 1))
    column = jnp.arange(3 * D, dtype=jnp.int32)
    head_of = jnp.minimum(column // HD, H - 1)
    factor = jnp.where(column[None, :] < D, jnp.take(levels, head_of, axis=1), 1.0)
    return (base * factor[:, None, :]).astype(jnp.bfloat16)


def block_levels(rng, shape, cuts, smallest, high):
    factor_of, own = 1.0, jax.random.fold_in(rng, 6)
    for axis_at, parts in cuts:
        heights = jnp.exp(jax.random.uniform(jax.random.fold_in(own, axis_at), (parts,), jnp.float32, smallest / len(cuts), high / len(cuts)))
        factor_of = factor_of * jnp.repeat(heights, shape[axis_at] // parts).reshape([-1 if axis == axis_at else 1 for axis in range(len(shape))])
    return factor_of


def assign_block(rng, own, number, rows, number_of, top, most, slope):
    order = jax.random.permutation(rng, number_of)
    packed, common = load_shares(number_of, rows * top, most, slope, True), load_shares(number_of, rows * top, most, slope, False)
    places = jnp.arange(number_of)

    def named(sizes, rotation):
        used = int((sizes > 0).sum())
        fixed = max(1, used // 4)
        moved = fixed + (places - fixed + rotation * (used - fixed)) % max(1, number_of - fixed)
        return jnp.zeros((number_of,), jnp.int32).at[order[jnp.where(places < fixed, places, moved)]].set(jnp.asarray(sizes, jnp.int32))

    sizes = jnp.where(number % 4 == 0, named(packed, number // 4), named(common, number - number // 4 - 1))
    mixed = jax.random.permutation(jax.random.fold_in(own, 3), number_of)
    giver, receiver = mixed[0:number_of // 2 * 2:2], mixed[1:number_of // 2 * 2:2]
    slack = jnp.minimum(sizes[giver] - 1, most - sizes[receiver]) // 2
    slack = jnp.where((giver == order[0]) | (receiver == order[0]) | (sizes[receiver] == 0), 0, jnp.maximum(slack, 0))
    moved = jax.random.randint(jax.random.fold_in(own, 4), (number_of // 2,), 0, 1 << 20) % (slack + 1)
    sizes = sizes.at[giver].add(-moved).at[receiver].add(moved)
    members = jnp.searchsorted(jnp.cumsum(sizes), jnp.arange(rows * top), side="right").astype(jnp.int32)
    grid = members.reshape(top, rows).T
    grid = grid[jax.random.permutation(jax.random.fold_in(own, 1), rows)]
    rotation = jax.random.randint(jax.random.fold_in(own, 2), (rows, 1), 0, top)
    return jnp.take_along_axis(grid, (jnp.arange(top)[None, :] + rotation) % top, axis=1)


def load_shares(number_of, total, reach, lean, full):
    loads = [(1 << 20) // math.isqrt(rank ** lean) + 1 for rank in range(1, number_of + 1)]
    largest = reach if full else min(reach, max(-(-total // number_of), total * loads[0] // sum(loads)))
    least = 1 if total - largest >= number_of - 1 else 0
    given, rest = [largest] + [least] * (number_of - 1), total - largest - least * (number_of - 1)
    while rest > 0:
        movable = [i for i in range(1, number_of) if given[i] < largest] or [i for i in range(1, number_of) if given[i] < reach]
        mass, left = sum([loads[i] for i in movable]), rest
        for i in movable:
            addition = min(reach - given[i], max(1, left * loads[i] // mass), rest)
            given[i] = given[i] + addition
            rest = rest - addition
    return np.array(given)


def gaussian(rng, dims, scale, reach, pieces=(), held_as=jnp.bfloat16):
    drawn = scale * jax.random.normal(rng, dims, jnp.float32)
    if pieces:
        drawn = drawn * block_levels(rng, dims, pieces, -0.22, 0.18)
    return jnp.clip(drawn, -reach, reach).astype(held_as)


def setup_inputs(seed: int = 0) -> dict:
    splits = jax.random.split(jax.random.key(seed), 15)
    hidden_in = gaussian(splits[0], (GROUPS, LENGTH, SEQS, D), 1.0, 6.0, ((0, 4), (1, 8)))
    attn_gain = jnp.clip(1.0 + 0.1 * jax.random.normal(splits[1], (2, D), jnp.float32), 0.5, 1.5).astype(jnp.bfloat16)
    qkv_weight = draw_qkv_weight(jax.random.fold_in(splits[14], 71), 0)
    out_weight = gaussian(splits[3], (2, D, D), (D // 32) ** -0.5, 1.25, ((1, 4),))
    rel_bias = gaussian(splits[4], (2, NB, H), 1.0, 4.0, ((1, 4),))
    bucket_table = draw_bucket_table(jax.random.fold_in(splits[14], 71), 0)
    mlp_gain = jnp.clip(1.0 + 0.1 * jax.random.normal(splits[6], (2, D), jnp.float32), 0.5, 1.5).astype(jnp.bfloat16)
    mlp_up = gaussian(splits[7], (D, FF), D ** -0.5, 0.21875, ((0, 4),))
    mlp_down = gaussian(splits[8], (FF, D), FF ** -0.5, 0.109375, ((0, 4),))
    router_weight = gaussian(splits[9], (D, EXPERTS), (0.7 * D ** -0.5), 0.375, ((0, 4),))
    expert_up = gaussian(splits[10], (EXPERTS, D, FF), D ** -0.5, 0.21875, ((0, 8), (1, 4)))
    expert_down = gaussian(splits[11], (EXPERTS, FF, D), FF ** -0.5, 0.109375, ((0, 8), (1, 4)))
    routes_keys = jax.random.split(jax.random.fold_in(splits[12], 1), GROUPS * LENGTH * SEQS // TOK_DEV)
    routes_turns = jax.random.permutation(jax.random.fold_in(splits[12], 3), GROUPS * LENGTH * SEQS // TOK_DEV)
    routes = jax.vmap(lambda own, number: assign_block(jax.random.fold_in(splits[12], 2), own, number, TOK_DEV, EXPERTS, 2, CAP, 1))(routes_keys, routes_turns).reshape((GROUPS, LENGTH, SEQS, 2))
    out_grad = gaussian(splits[13], (GROUPS, LENGTH, SEQS, D), 1.0, 6.0, ((0, 4), (1, 8)))
    return dict(hidden_in=hidden_in, attn_gain=attn_gain, qkv_weight=qkv_weight, out_weight=out_weight, rel_bias=rel_bias, bucket_table=bucket_table, mlp_gain=mlp_gain, mlp_up=mlp_up, mlp_down=mlp_down, router_weight=router_weight, expert_up=expert_up, expert_down=expert_down, routes=routes, out_grad=out_grad)


@jax.custom_vjp
def reduced_precision(v):
    return lax.optimization_barrier(v.astype(jnp.bfloat16)).astype(jnp.float32)

@jax.custom_vjp
def reduced_backward(v):
    return v

def low_keep(v):
    return (reduced_precision(v), None)

def low_pass(kept, grad):
    return (grad,)

def back_keep(v):
    return (v, None)

def back_low(kept, grad):
    return (reduced_precision(grad),)
reduced_precision.defvjp(low_keep, low_pass)
reduced_backward.defvjp(back_keep, back_low)
epsilon = 1e-06
clip_limit = 6.0
highest_precision = lax.Precision.HIGHEST

def rms_norm(inputs, norm_gain):
    return inputs * lax.rsqrt(lax.optimization_barrier(jnp.mean(inputs * inputs, axis=-1, keepdims=True)) + epsilon) * norm_gain

def matmul(left, right):
    return jnp.dot(left, right, precision=highest_precision)

def sequence_attention(stacked_projection, score_table):
    length = stacked_projection.shape[0]
    queries = stacked_projection[:, :D].reshape(length, H, HD)
    keys = stacked_projection[:, D:2 * D].reshape(length, H, HD)
    values = stacked_projection[:, 2 * D:].reshape(length, H, HD)
    block = min(512, length)
    scale = HD ** (-0.5)

    def one_block(start):
        rows = lax.dynamic_slice_in_dim(queries, start, block, 0)
        raw_scores = jnp.einsum('ihd,jhd->hij', rows, keys, precision=highest_precision) * scale
        position = start + jnp.arange(block, dtype=jnp.int32)
        distance = position[:, None] - jnp.arange(length, dtype=jnp.int32)[None, :]
        causal = distance >= 0
        shifted = jnp.take(score_table, jnp.maximum(distance, 0), axis=1)
        scores = reduced_backward(raw_scores + shifted)
        scores = jnp.where(causal[None], scores, -jnp.inf)
        softmax_probs = jax.nn.softmax(scores, axis=-1)
        output = jnp.einsum('hij,jhd->ihd', reduced_precision(softmax_probs), values, precision=highest_precision)
        head_peak = lax.optimization_barrier(jnp.max(jnp.where(causal[None], raw_scores, -jnp.inf), axis=(1, 2)))
        return (output, head_peak)
    starts = jnp.arange(length // block, dtype=jnp.int32) * block
    output, head_peak = lax.map(jax.checkpoint(one_block), starts)
    return (output.reshape(length, D), lax.optimization_barrier(jnp.max(head_peak, axis=0)))

def attention_layer(hidden, layer_number, gains, stacked_weights, output_projection, bias_weights, bucket_table):
    groups, length, sequences, width = hidden.shape
    seq_major = hidden.transpose(0, 2, 1, 3).reshape(groups * sequences, length, width)
    normalized_rows = reduced_precision(rms_norm(seq_major, gains[layer_number]))
    stacked_projection = reduced_backward(reduced_precision(jnp.einsum('kym,mr->kyr', normalized_rows, stacked_weights[layer_number], precision=highest_precision)))
    score_table = jnp.take(bias_weights[layer_number], bucket_table, axis=0).T

    def per_sequence(item):
        return sequence_attention(item, score_table)
    attention_result, head_peak = lax.map(jax.checkpoint(per_sequence), stacked_projection)
    attention_result = reduced_backward(reduced_precision(attention_result))
    branch_output = reduced_backward(jnp.einsum('kym,mr->kyr', attention_result, output_projection[layer_number], precision=highest_precision))
    branch_output = branch_output.reshape(groups, sequences, length, width).transpose(0, 2, 1, 3)
    return (hidden + branch_output, lax.optimization_barrier(jnp.max(head_peak, axis=0)))

def expert_block(items):
    rows, up_matrix, down_matrix = items
    expert_pre = reduced_backward(matmul(rows, up_matrix))
    expert_act = reduced_precision(jax.nn.gelu(expert_pre))
    return reduced_backward(reduced_precision(matmul(expert_act, down_matrix)))

def reference(hidden_in, attn_gain, qkv_weight, out_weight, rel_bias, bucket_table, mlp_gain, mlp_up, mlp_down, router_weight, expert_up, expert_down, routes, out_grad):
    shape = hidden_in.shape
    route_rows = routes.reshape(-1, 2).astype(jnp.int32)
    flat_routes = route_rows.reshape(-1)
    marks = (flat_routes[:, None] == jnp.arange(EXPERTS, dtype=jnp.int32)[None, :]).astype(jnp.int32)
    before = jnp.cumsum(marks, axis=0) - marks
    rank = lax.optimization_barrier(jnp.sum(before * marks, axis=1)).astype(jnp.int32)
    capacity_all = N_EXPERT * N_SHARD * CAP
    slot_of_route = (flat_routes * capacity_all + rank).astype(jnp.int32)
    token_of_route = (jnp.arange(flat_routes.shape[0], dtype=jnp.int32) // 2).astype(jnp.int32)

    def forward(hidden, gain_attn, stacked_weights, output_projection, bias_weights, gain_mlp, dense_up, dense_down, router_full, experts_up, experts_down):
        hidden, peak_first = attention_layer(hidden, 0, gain_attn, stacked_weights, output_projection, bias_weights, bucket_table)
        tokens = hidden.reshape(-1, D)
        normalized_rows = reduced_precision(rms_norm(tokens, gain_mlp[0]))
        pre_act = reduced_backward(matmul(normalized_rows, dense_up))
        activation = reduced_precision(jax.nn.gelu(pre_act))
        tokens = tokens + reduced_backward(matmul(activation, dense_down))
        hidden = tokens.reshape(shape)
        hidden, peak_second = attention_layer(hidden, 1, gain_attn, stacked_weights, output_projection, bias_weights, bucket_table)
        tokens = hidden.reshape(-1, D)
        normalized_rows = reduced_precision(rms_norm(tokens, gain_mlp[1]))
        router_logits = reduced_backward(matmul(normalized_rows, router_full))
        chosen = jnp.take_along_axis(router_logits, route_rows, axis=1)
        gates = jax.nn.softmax(chosen, axis=-1)
        rows = jnp.take(normalized_rows, token_of_route, axis=0)
        buffer = jnp.zeros((EXPERTS * capacity_all, D), jnp.float32).at[slot_of_route].set(rows)
        buffer = reduced_backward(buffer).reshape(EXPERTS, capacity_all, D)
        outputs = lax.map(jax.checkpoint(expert_block), (buffer, experts_up, experts_down)).reshape(-1, D)
        picked = jnp.take(outputs, slot_of_route, axis=0).reshape(-1, 2, D)
        tokens = tokens + lax.optimization_barrier(jnp.sum(gates[:, :, None] * picked, axis=1))
        return (tokens.reshape(shape), jnp.stack([peak_first, peak_second]))
    primals = (hidden_in, attn_gain, qkv_weight, out_weight, rel_bias, mlp_gain, mlp_up, mlp_down, router_weight, expert_up, expert_down)
    primals = tuple((item.astype(jnp.float32) for item in primals))
    result, pullback, peaks = jax.vjp(forward, *primals, has_aux=True)
    grads = pullback(out_grad.astype(jnp.float32))
    clip_scales = jnp.sqrt(clip_limit / jnp.maximum(peaks, clip_limit))
    return (result.astype(jnp.bfloat16), grads[0], grads[1], grads[2], grads[3], grads[4], grads[5], grads[6], grads[7], grads[8], grads[9], grads[10], clip_scales)
```

```python
import math

import jax
import jax.numpy as jnp
from jax import lax
from jax.sharding import PartitionSpec as P

D = 768
H = 12
HD = 64
NB = 32
EXP_DEV = 2

epsilon = 1e-06
clip_limit = 6.0
bfloat = jnp.bfloat16
single = jnp.float32


def rms_norm(inputs, norm_gain):
    return (
        inputs * lax.rsqrt(jnp.mean(inputs * inputs, axis=-1, keepdims=True) + epsilon) * norm_gain
    )


def norm_back(inputs, norm_gain, upstream):
    _, pullback = jax.vjp(rms_norm, inputs, norm_gain)
    return pullback(upstream)


def gelu_back(pre_values, upstream):
    _, pullback = jax.vjp(jax.nn.gelu, pre_values)
    return pullback(upstream)[0]


def matmul(left, right):
    return jnp.dot(left, right, preferred_element_type=single)


def shard_shift(block, amount):
    count = lax.axis_size("shard")
    return lax.ppermute(block, "shard", [(i, (i + amount) % count) for i in range(count)])


def gather_shard(block):
    count = lax.axis_size("shard")
    here = lax.axis_index("shard")
    result = jnp.zeros((count,) + block.shape, block.dtype)
    for step in range(count):
        piece = block if step == 0 else shard_shift(block, step)
        result = lax.dynamic_update_slice_in_dim(result, piece[None], (here - step) % count, 0)
    return result


def scatter_shard(blocks, sent=bfloat):
    count = lax.axis_size("shard")
    here = lax.axis_index("shard")
    total = lax.dynamic_index_in_dim(blocks, here, 0, keepdims=False).astype(single)
    for step in range(1, count):
        part = lax.dynamic_index_in_dim(blocks, (here + step) % count, 0, keepdims=False)
        total = total + shard_shift(part.astype(sent), step).astype(single)
    return total


def spread(columns):
    experts, shard_count = lax.axis_size("expert"), lax.axis_size("shard")
    rows, width = columns.shape
    cut = columns.reshape(rows, shard_count, experts, width // (shard_count * experts))
    return cut.transpose(0, 2, 1, 3).reshape(rows, width)


def unspread(columns):
    experts, shard_count = lax.axis_size("expert"), lax.axis_size("shard")
    rows, width = columns.shape
    cut = columns.reshape(rows, experts, shard_count, width // (shard_count * experts))
    return cut.transpose(0, 2, 1, 3).reshape(rows, width)


def gather_weight(block):
    part = block.shape[0] // lax.axis_size("expert")
    own = lax.dynamic_slice_in_dim(block, lax.axis_index("expert") * part, part, 0)
    column = gather_shard(own).reshape(-1, block.shape[1])
    return lax.all_gather(column, "expert", axis=0, tiled=True)


def reduce_weight(grad):
    part = lax.psum_scatter(grad.astype(bfloat), "expert", scatter_dimension=0, tiled=True)
    blocks = part.reshape((lax.axis_size("shard"), -1) + part.shape[1:])
    own = scatter_shard(blocks).astype(bfloat)
    return lax.all_gather(own, "expert", axis=0, tiled=True).astype(single)


def bucket_marks(distance, lower, upper):
    inside = (distance[None] >= lower[:, None, None]) & (distance[None] < upper[:, None, None])
    return inside.astype(bfloat)


def position_bias(marks, bias_pair):
    return jnp.einsum("bij,bh->hij", marks, bias_pair, preferred_element_type=single)


def attention_forward(hidden, norm_gain, qkv, projection, bias_pair, geometry):
    distance, marks, scale = geometry
    rows = hidden.shape[0]
    normalized = spread(rms_norm(hidden, norm_gain).astype(bfloat))
    packed = matmul(normalized, qkv).astype(bfloat)
    key_value = lax.all_gather(packed[:, D:], "expert", axis=0, tiled=True)
    shifted = position_bias(marks, bias_pair)
    causal = distance >= 0
    queries = packed[:, :D].reshape(rows, H, HD)
    keys = key_value[:, :D].reshape(-1, H, HD)
    values = key_value[:, D:].reshape(-1, H, HD)
    raw_scores = jnp.einsum("ihd,jhd->hij", queries, keys, preferred_element_type=single) * scale
    head_peak = jnp.max(jnp.where(causal[None], raw_scores, -jnp.inf), axis=(1, 2))
    masked = jnp.where(causal[None], raw_scores + shifted, -jnp.inf)
    softmax_top = jnp.max(masked, axis=-1, keepdims=True)
    exponent = jnp.exp(masked - softmax_top)
    softmax_sum = jnp.sum(exponent, axis=-1, keepdims=True)
    probs = (exponent / softmax_sum).astype(bfloat)
    log_total = softmax_top[..., 0] + jnp.log(softmax_sum[..., 0])
    attended = jnp.einsum("hij,jhd->ihd", probs, values, preferred_element_type=single)
    attended = spread(attended.astype(bfloat).reshape(rows, D))
    saved = (normalized, packed, key_value, log_total, attended)
    return hidden + matmul(attended, projection), head_peak, saved


def attention_backward(
    upstream, hidden, norm_gain, qkv, projection, bias_pair, geometry, saved
):
    distance, marks, scale = geometry
    normalized, packed, key_value, log_total, attended = saved
    rows = hidden.shape[0]
    branch_grad = upstream.astype(bfloat)
    projection_grad = matmul(attended.T, branch_grad)
    attended_grad = unspread(matmul(branch_grad, projection.T).astype(bfloat))
    shifted = position_bias(marks, bias_pair)
    causal = distance >= 0
    queries = packed[:, :D].reshape(rows, H, HD)
    keys = key_value[:, :D].reshape(-1, H, HD)
    values = key_value[:, D:].reshape(-1, H, HD)
    grad_heads = attended_grad.reshape(rows, H, HD)
    raw_scores = jnp.einsum("ihd,jhd->hij", queries, keys, preferred_element_type=single) * scale
    probs = jnp.where(causal[None], jnp.exp(raw_scores + shifted - log_total[..., None]), 0.0)
    prob_grad = jnp.einsum("ihd,jhd->hij", grad_heads, values, preferred_element_type=single)
    row_dot = jnp.sum(prob_grad * probs, axis=-1)
    score_grad = (probs * (prob_grad - row_dot[..., None])).astype(bfloat)
    query_grad = jnp.einsum("hij,jhd->ihd", score_grad, keys, preferred_element_type=single) * scale
    query_grad = query_grad.astype(bfloat).reshape(rows, D)
    bias_grad = jnp.einsum("hij,bij->bh", score_grad, marks, preferred_element_type=single)
    key_grad = (
        jnp.einsum("hij,ihd->jhd", score_grad, queries, preferred_element_type=single) * scale
    )
    value_grad = jnp.einsum(
        "hij,ihd->jhd", probs.astype(bfloat), grad_heads, preferred_element_type=single
    )
    pair = jnp.concatenate([key_grad.reshape(-1, D), value_grad.reshape(-1, D)], axis=-1)
    pair_grad = lax.psum_scatter(pair.astype(bfloat), "expert", scatter_dimension=0, tiled=True)
    packed_grad = jnp.concatenate([query_grad, pair_grad], axis=-1)
    qkv_grad = matmul(normalized.T, packed_grad)
    normed_grad = unspread(matmul(packed_grad, qkv.T))
    input_grad, gain_grad = norm_back(hidden, norm_gain, normed_grad)
    return upstream + input_grad, gain_grad, qkv_grad, projection_grad, bias_grad


def exchange(blocks):
    return lax.all_to_all(blocks, "expert", split_axis=0, concat_axis=0, tiled=True)


def shards(
    hidden_in,
    attn_gain,
    qkv_weight,
    out_weight,
    rel_bias,
    bucket_table,
    mlp_gain,
    mlp_up,
    mlp_down,
    router_weight,
    expert_up,
    expert_down,
    routes,
    out_grad,
):
    block_rows = hidden_in.shape[1]
    length = bucket_table.shape[0]
    experts = lax.axis_size("expert")
    groups = lax.axis_size("shard")
    here = lax.axis_index("shard")
    expert_total = EXP_DEV * experts
    capacity = 4 * block_rows // expert_total
    width = expert_down.shape[1]
    scale = 1.0 / math.sqrt(HD)

    small = jnp.concatenate(
        [attn_gain.reshape(-1), mlp_gain.reshape(-1), rel_bias.reshape(-1), router_weight.reshape(-1)]
    )
    small = gather_shard(small)
    part = D // groups
    cuts = [0, 2 * part, 4 * part, 4 * part + 2 * (NB // groups) * H, small.shape[1]]
    gain_attn, gain_mlp, bias_weights, router_full = (
        small[:, cuts[i] : cuts[i + 1]] for i in range(4)
    )
    gain_attn = gain_attn.reshape(groups, 2, part).transpose(1, 0, 2).reshape(2, D).astype(single)
    gain_mlp = gain_mlp.reshape(groups, 2, part).transpose(1, 0, 2).reshape(2, D).astype(single)
    bias_weights = (
        bias_weights.reshape(groups, 2, NB // groups, H).transpose(1, 0, 2, 3).reshape(2, NB, H)
    )
    router_full = router_full.reshape(D, expert_total)

    first = gather_weight(jnp.concatenate([qkv_weight[0], out_weight[0]], axis=1))
    dense_up = gather_weight(mlp_up)
    dense_down = gather_weight(mlp_down)
    second = gather_weight(jnp.concatenate([qkv_weight[1], out_weight[1]], axis=1))
    qkv = (first[:, : 3 * D], second[:, : 3 * D])
    projection = (first[:, 3 * D :], second[:, 3 * D :])

    up_own = jnp.zeros((EXP_DEV, groups, part, width), bfloat)
    for step in range(groups):
        target = (here + step) % groups
        piece = lax.dynamic_slice_in_dim(expert_up, target * width, width, 2)
        if step:
            piece = shard_shift(piece, step)
        up_own = lax.dynamic_update_slice_in_dim(up_own, piece[:, None], (here - step) % groups, 1)
    up_own = up_own.reshape(EXP_DEV, D, width)

    route_rows = gather_shard(routes.reshape(block_rows, 2))
    upstream_all = gather_shard(out_grad.reshape(block_rows, D))
    expert_ids = jnp.arange(expert_total, dtype=jnp.int32)
    flat_routes = route_rows.reshape(groups, -1)
    marks = (flat_routes[:, :, None] == expert_ids).astype(jnp.int32)
    rank = jnp.sum((jnp.cumsum(marks, axis=1) - marks) * marks, axis=2)
    slot_of_route = flat_routes * capacity + rank
    slot_ids = jnp.arange(expert_total * capacity, dtype=jnp.int32)
    slot_marks = (slot_of_route[:, :, None] == slot_ids).astype(bfloat)
    token_marks = jnp.sum(
        slot_marks.reshape(groups, block_rows, 2, -1).astype(single), axis=2
    ).astype(bfloat)

    def dispatch(rows):
        slots = jnp.einsum("gts,gtd->gsd", token_marks, rows, preferred_element_type=single)
        slots = slots.astype(bfloat).reshape(groups, experts, EXP_DEV, capacity, D)
        return exchange(slots.transpose(1, 2, 0, 3, 4)).reshape(
            experts, EXP_DEV, groups * capacity, D
        )

    def collect(blocks):
        back = exchange(blocks.astype(bfloat)).reshape(experts, EXP_DEV, groups, capacity, D)
        return back.transpose(2, 0, 1, 3, 4).reshape(groups, expert_total * capacity, D)

    owner_rows = dispatch(upstream_all)

    own_positions = lax.axis_index("expert") * block_rows + jnp.arange(block_rows, dtype=jnp.int32)
    distance = own_positions[:, None] - jnp.arange(length, dtype=jnp.int32)[None, :]
    bounds = jnp.sum(
        (bucket_table[:, None] < jnp.arange(NB + 1, dtype=jnp.int32)[None, :]).astype(jnp.int32),
        axis=0,
    )
    geometry = (distance, bucket_marks(distance, bounds[:NB], bounds[1:]), scale)

    hidden_zero = hidden_in.reshape(block_rows, D).astype(single)
    mid_first, peak_first, saved_first = attention_forward(
        hidden_zero, gain_attn[0], qkv[0], projection[0], bias_weights[0], geometry
    )
    dense_normed = spread(rms_norm(mid_first, gain_mlp[0]).astype(bfloat))
    pre_act = matmul(dense_normed, dense_up)
    activation = spread(jax.nn.gelu(pre_act).astype(bfloat))
    layer_one = mid_first + matmul(activation, dense_down)
    mid_second, peak_second, saved_second = attention_forward(
        layer_one, gain_attn[1], qkv[1], projection[1], bias_weights[1], geometry
    )

    moe_normed = rms_norm(mid_second, gain_mlp[1]).astype(bfloat)
    normed_all = gather_shard(moe_normed)
    received = dispatch(normed_all)
    router_logits = jnp.einsum("gtd,de->gte", normed_all, router_full, preferred_element_type=single)
    selected = (route_rows[..., None] == expert_ids).astype(single)
    gates_all = jax.nn.softmax(jnp.sum(selected * router_logits[:, :, None, :], axis=-1), axis=-1)
    slot_gates = jnp.sum(
        gates_all.reshape(groups, -1)[:, :, None] * (slot_of_route[:, :, None] == slot_ids), axis=1
    )
    owner_gates = exchange(
        slot_gates.reshape(groups, experts, EXP_DEV, capacity).transpose(1, 2, 0, 3)
    ).reshape(experts, EXP_DEV, groups * capacity)

    expert_pre = jnp.einsum("sjcd,jdf->sjcf", received, up_own, preferred_element_type=single)
    expert_act = jax.nn.gelu(expert_pre).astype(bfloat)
    expert_out = jnp.einsum(
        "sjcf,jfd->sjcd", expert_act, expert_down, preferred_element_type=single
    )
    owner_grad = (owner_gates[..., None] * owner_rows.astype(single)).astype(bfloat)
    act_grad = jnp.einsum("sjcd,jfd->sjcf", owner_grad, expert_down, preferred_element_type=single)
    pre_grad = gelu_back(expert_pre, act_grad).astype(bfloat)
    row_grad = jnp.einsum("sjcf,jdf->sjcd", pre_grad, up_own, preferred_element_type=single)

    returned = collect(expert_out)
    back_rows = collect(row_grad)
    expert_down_grad = jnp.einsum(
        "sjcf,sjcd->jfd", expert_act, owner_grad, preferred_element_type=single
    )
    up_grad = jnp.einsum(
        "sjcd,sjcf->jdf", received, pre_grad, preferred_element_type=single
    ).astype(bfloat)

    route_out = jnp.einsum("grs,gsd->grd", slot_marks, returned, preferred_element_type=single)
    route_out = route_out.reshape(groups, block_rows, 2, D)
    gate_grad = scatter_shard(
        jnp.sum(route_out * upstream_all[:, :, None, :].astype(single), axis=-1), single
    )
    mixed = scatter_shard(jnp.sum(gates_all[..., None] * route_out, axis=2))
    hidden_out = (mid_second + mixed).astype(bfloat).reshape(hidden_in.shape)

    gates = lax.dynamic_index_in_dim(gates_all, here, 0, keepdims=False)
    own_selected = lax.dynamic_index_in_dim(selected, here, 0, keepdims=False)
    upstream = out_grad.reshape(block_rows, D).astype(single)
    chosen_grad = gates * (gate_grad - jnp.sum(gates * gate_grad, axis=-1, keepdims=True))
    logit_grad = jnp.sum(chosen_grad[:, :, None] * own_selected, axis=1).astype(bfloat)
    router_grad = matmul(moe_normed.T, logit_grad)
    row_terms = jnp.einsum("gts,gsd->gtd", token_marks, back_rows, preferred_element_type=single)
    normed_grad = matmul(logit_grad, router_full.T) + scatter_shard(row_terms)
    moe_input_grad, moe_gain_grad = norm_back(mid_second, gain_mlp[1], normed_grad)
    mid_grad = upstream + moe_input_grad

    up_grad = up_grad.reshape(EXP_DEV, groups, part, width)
    expert_up_grad = jnp.zeros((EXP_DEV, part, groups * width), single)
    for step in range(groups):
        piece = lax.dynamic_index_in_dim(up_grad, (here + step) % groups, 1, keepdims=False)
        if step:
            piece = shard_shift(piece, step)
        expert_up_grad = lax.dynamic_update_slice_in_dim(
            expert_up_grad, piece.astype(single), ((here - step) % groups) * width, 2
        )

    layer_grad, gain_second, qkv_second, projection_second, bias_second = attention_backward(
        mid_grad, layer_one, gain_attn[1], qkv[1], projection[1], bias_weights[1], geometry,
        saved_second,
    )
    second_grad = reduce_weight(jnp.concatenate([qkv_second, projection_second], axis=1))
    dense_branch = layer_grad.astype(bfloat)
    mlp_down_grad = reduce_weight(matmul(activation.T, dense_branch))
    hidden_act_grad = unspread(matmul(dense_branch, dense_down.T))
    pre_act_grad = gelu_back(pre_act, hidden_act_grad).astype(bfloat)
    mlp_up_grad = reduce_weight(matmul(dense_normed.T, pre_act_grad))
    dense_normed_grad = unspread(matmul(pre_act_grad, dense_up.T))
    dense_input_grad, dense_gain_grad = norm_back(mid_first, gain_mlp[0], dense_normed_grad)
    first_grad = layer_grad + dense_input_grad
    input_grad, gain_first, qkv_first, projection_first, bias_first = attention_backward(
        first_grad, hidden_zero, gain_attn[0], qkv[0], projection[0], bias_weights[0], geometry,
        saved_first,
    )
    first_weight_grad = reduce_weight(jnp.concatenate([qkv_first, projection_first], axis=1))

    gains = jnp.stack([gain_first, gain_second, dense_gain_grad, moe_gain_grad])
    biases = jnp.stack([bias_first, bias_second])
    small_grad = jnp.concatenate(
        [
            gains.reshape(4, groups, part).transpose(1, 0, 2).reshape(groups, -1),
            biases.reshape(2, groups, NB // groups, H).transpose(1, 0, 2, 3).reshape(groups, -1),
            router_grad.reshape(groups, -1),
        ],
        axis=1,
    )
    small_grad = lax.psum(scatter_shard(small_grad, single), "expert")
    gain_cut = 4 * part
    bias_cut = gain_cut + 2 * (NB // groups) * H
    own_gains = small_grad[:gain_cut].reshape(4, part)
    peaks = lax.pmax(jnp.stack([peak_first, peak_second]), ("expert", "shard"))
    clip_scales = jnp.sqrt(clip_limit / jnp.maximum(peaks, clip_limit))
    return (
        hidden_out,
        input_grad.reshape(hidden_in.shape),
        own_gains[:2],
        jnp.stack([first_weight_grad[:, : 3 * D], second_grad[:, : 3 * D]]),
        jnp.stack([first_weight_grad[:, 3 * D :], second_grad[:, 3 * D :]]),
        small_grad[gain_cut:bias_cut].reshape(2, NB // groups, H),
        own_gains[2:],
        mlp_up_grad,
        mlp_down_grad,
        small_grad[bias_cut:].reshape(part, expert_total),
        expert_up_grad,
        expert_down_grad,
        clip_scales,
    )


def solution(mesh):
    tokens = P("shard", "expert", None, None)
    columns = P(None, "shard")
    layers = P(None, "shard", None)
    rows = P("shard", None)
    owned = P("expert", "shard", None)
    in_specs = (
        tokens, columns, layers, layers, layers, P(), columns, rows, rows, rows, owned, owned,
        tokens, tokens,
    )
    out_specs = (
        tokens, tokens, columns, layers, layers, layers, columns, rows, rows, rows, owned, owned,
        P(),
    )
    return jax.shard_map(shards, mesh=mesh, in_specs=in_specs, out_specs=out_specs, check_vma=False)
```

```python
import functools
import math

import jax
import jax.numpy as jnp
from jax import lax
from jax.experimental import pallas as pl
from jax.experimental.pallas import tpu as pltpu
from jax.sharding import PartitionSpec as P

D = 768
H = 12
HD = 64
NB = 32
EXP_DEV = 2

epsilon = 1e-06
clip_limit = 6.0
bfloat = jnp.bfloat16
single = jnp.float32


def rms_norm(inputs, norm_gain):
    return (
        inputs * lax.rsqrt(jnp.mean(inputs * inputs, axis=-1, keepdims=True) + epsilon) * norm_gain
    )


def norm_back(inputs, norm_gain, upstream):
    _, pullback = jax.vjp(rms_norm, inputs, norm_gain)
    return pullback(upstream)


def gelu_back(pre_values, upstream):
    _, pullback = jax.vjp(jax.nn.gelu, pre_values)
    return pullback(upstream)[0]


def matmul(left, right):
    return jnp.dot(left, right, preferred_element_type=single)


def shard_shift(block, amount):
    count = lax.axis_size("shard")
    return lax.ppermute(block, "shard", [(i, (i + amount) % count) for i in range(count)])


def gather_shard(block):
    count = lax.axis_size("shard")
    here = lax.axis_index("shard")
    result = jnp.zeros((count,) + block.shape, block.dtype)
    for step in range(count):
        piece = block if step == 0 else shard_shift(block, step)
        result = lax.dynamic_update_slice_in_dim(result, piece[None], (here - step) % count, 0)
    return result


def scatter_shard(blocks, sent=bfloat):
    count = lax.axis_size("shard")
    here = lax.axis_index("shard")
    total = lax.dynamic_index_in_dim(blocks, here, 0, keepdims=False).astype(single)
    for step in range(1, count):
        part = lax.dynamic_index_in_dim(blocks, (here + step) % count, 0, keepdims=False)
        total = total + shard_shift(part.astype(sent), step).astype(single)
    return total


def spread(columns):
    experts, shard_count = lax.axis_size("expert"), lax.axis_size("shard")
    rows, width = columns.shape
    cut = columns.reshape(rows, shard_count, experts, width // (shard_count * experts))
    return cut.transpose(0, 2, 1, 3).reshape(rows, width)


def unspread(columns):
    experts, shard_count = lax.axis_size("expert"), lax.axis_size("shard")
    rows, width = columns.shape
    cut = columns.reshape(rows, experts, shard_count, width // (shard_count * experts))
    return cut.transpose(0, 2, 1, 3).reshape(rows, width)


def gather_weight(block):
    part = block.shape[0] // lax.axis_size("expert")
    own = lax.dynamic_slice_in_dim(block, lax.axis_index("expert") * part, part, 0)
    column = gather_shard(own).reshape(-1, block.shape[1])
    return lax.all_gather(column, "expert", axis=0, tiled=True)


def reduce_weight(grad):
    part = lax.psum_scatter(grad.astype(bfloat), "expert", scatter_dimension=0, tiled=True)
    blocks = part.reshape((lax.axis_size("shard"), -1) + part.shape[1:])
    own = scatter_shard(blocks).astype(bfloat)
    return lax.all_gather(own, "expert", axis=0, tiled=True).astype(single)


def bucket_marks(distance, lower, upper):
    inside = (distance[None] >= lower[:, None, None]) & (distance[None] < upper[:, None, None])
    return inside.astype(bfloat)


def position_bias(marks, bias_pair):
    return jnp.einsum("bij,bh->hij", marks, bias_pair, preferred_element_type=single)


def attention_forward(hidden, norm_gain, qkv, projection, bias_pair, geometry):
    distance, marks, scale = geometry
    rows = hidden.shape[0]
    normalized = spread(rms_norm(hidden, norm_gain).astype(bfloat))
    packed = matmul(normalized, qkv).astype(bfloat)
    key_value = lax.all_gather(packed[:, D:], "expert", axis=0, tiled=True)
    shifted = position_bias(marks, bias_pair)
    causal = distance >= 0
    queries = packed[:, :D].reshape(rows, H, HD)
    keys = key_value[:, :D].reshape(-1, H, HD)
    values = key_value[:, D:].reshape(-1, H, HD)
    raw_scores = jnp.einsum("ihd,jhd->hij", queries, keys, preferred_element_type=single) * scale
    head_peak = jnp.max(jnp.where(causal[None], raw_scores, -jnp.inf), axis=(1, 2))
    masked = jnp.where(causal[None], raw_scores + shifted, -jnp.inf)
    softmax_top = jnp.max(masked, axis=-1, keepdims=True)
    exponent = jnp.exp(masked - softmax_top)
    softmax_sum = jnp.sum(exponent, axis=-1, keepdims=True)
    probs = (exponent / softmax_sum).astype(bfloat)
    log_total = softmax_top[..., 0] + jnp.log(softmax_sum[..., 0])
    attended = jnp.einsum("hij,jhd->ihd", probs, values, preferred_element_type=single)
    attended = spread(attended.astype(bfloat).reshape(rows, D))
    saved = (normalized, packed, key_value, log_total, attended)
    return hidden + matmul(attended, projection), head_peak, saved


def attention_backward(
    upstream, hidden, norm_gain, qkv, projection, bias_pair, geometry, saved
):
    distance, marks, scale = geometry
    normalized, packed, key_value, log_total, attended = saved
    rows = hidden.shape[0]
    branch_grad = upstream.astype(bfloat)
    projection_grad = matmul(attended.T, branch_grad)
    attended_grad = unspread(matmul(branch_grad, projection.T).astype(bfloat))
    shifted = position_bias(marks, bias_pair)
    causal = distance >= 0
    queries = packed[:, :D].reshape(rows, H, HD)
    keys = key_value[:, :D].reshape(-1, H, HD)
    values = key_value[:, D:].reshape(-1, H, HD)
    grad_heads = attended_grad.reshape(rows, H, HD)
    raw_scores = jnp.einsum("ihd,jhd->hij", queries, keys, preferred_element_type=single) * scale
    probs = jnp.where(causal[None], jnp.exp(raw_scores + shifted - log_total[..., None]), 0.0)
    prob_grad = jnp.einsum("ihd,jhd->hij", grad_heads, values, preferred_element_type=single)
    row_dot = jnp.sum(prob_grad * probs, axis=-1)
    score_grad = (probs * (prob_grad - row_dot[..., None])).astype(bfloat)
    query_grad = jnp.einsum("hij,jhd->ihd", score_grad, keys, preferred_element_type=single) * scale
    query_grad = query_grad.astype(bfloat).reshape(rows, D)
    bias_grad = jnp.einsum("hij,bij->bh", score_grad, marks, preferred_element_type=single)
    key_grad = (
        jnp.einsum("hij,ihd->jhd", score_grad, queries, preferred_element_type=single) * scale
    )
    value_grad = jnp.einsum(
        "hij,ihd->jhd", probs.astype(bfloat), grad_heads, preferred_element_type=single
    )
    pair = jnp.concatenate([key_grad.reshape(-1, D), value_grad.reshape(-1, D)], axis=-1)
    pair_grad = lax.psum_scatter(pair.astype(bfloat), "expert", scatter_dimension=0, tiled=True)
    packed_grad = jnp.concatenate([query_grad, pair_grad], axis=-1)
    qkv_grad = matmul(normalized.T, packed_grad)
    normed_grad = unspread(matmul(packed_grad, qkv.T))
    input_grad, gain_grad = norm_back(hidden, norm_gain, normed_grad)
    return upstream + input_grad, gain_grad, qkv_grad, projection_grad, bias_grad


def exchange(blocks):
    return lax.all_to_all(blocks, "expert", split_axis=0, concat_axis=0, tiled=True)


def plain_shards(
    hidden_in,
    attn_gain,
    qkv_weight,
    out_weight,
    rel_bias,
    bucket_table,
    mlp_gain,
    mlp_up,
    mlp_down,
    router_weight,
    expert_up,
    expert_down,
    routes,
    out_grad,
):
    block_rows = hidden_in.shape[1]
    length = bucket_table.shape[0]
    experts = lax.axis_size("expert")
    groups = lax.axis_size("shard")
    here = lax.axis_index("shard")
    expert_total = EXP_DEV * experts
    capacity = 4 * block_rows // expert_total
    width = expert_down.shape[1]
    scale = 1.0 / math.sqrt(HD)

    small = jnp.concatenate(
        [attn_gain.reshape(-1), mlp_gain.reshape(-1), rel_bias.reshape(-1), router_weight.reshape(-1)]
    )
    small = gather_shard(small)
    part = D // groups
    cuts = [0, 2 * part, 4 * part, 4 * part + 2 * (NB // groups) * H, small.shape[1]]
    gain_attn, gain_mlp, bias_weights, router_full = (
        small[:, cuts[i] : cuts[i + 1]] for i in range(4)
    )
    gain_attn = gain_attn.reshape(groups, 2, part).transpose(1, 0, 2).reshape(2, D).astype(single)
    gain_mlp = gain_mlp.reshape(groups, 2, part).transpose(1, 0, 2).reshape(2, D).astype(single)
    bias_weights = (
        bias_weights.reshape(groups, 2, NB // groups, H).transpose(1, 0, 2, 3).reshape(2, NB, H)
    )
    router_full = router_full.reshape(D, expert_total)

    first = gather_weight(jnp.concatenate([qkv_weight[0], out_weight[0]], axis=1))
    dense_up = gather_weight(mlp_up)
    dense_down = gather_weight(mlp_down)
    second = gather_weight(jnp.concatenate([qkv_weight[1], out_weight[1]], axis=1))
    qkv = (first[:, : 3 * D], second[:, : 3 * D])
    projection = (first[:, 3 * D :], second[:, 3 * D :])

    up_own = jnp.zeros((EXP_DEV, groups, part, width), bfloat)
    for step in range(groups):
        target = (here + step) % groups
        piece = lax.dynamic_slice_in_dim(expert_up, target * width, width, 2)
        if step:
            piece = shard_shift(piece, step)
        up_own = lax.dynamic_update_slice_in_dim(up_own, piece[:, None], (here - step) % groups, 1)
    up_own = up_own.reshape(EXP_DEV, D, width)

    route_rows = gather_shard(routes.reshape(block_rows, 2))
    upstream_all = gather_shard(out_grad.reshape(block_rows, D))
    expert_ids = jnp.arange(expert_total, dtype=jnp.int32)
    flat_routes = route_rows.reshape(groups, -1)
    marks = (flat_routes[:, :, None] == expert_ids).astype(jnp.int32)
    rank = jnp.sum((jnp.cumsum(marks, axis=1) - marks) * marks, axis=2)
    slot_of_route = flat_routes * capacity + rank
    slot_ids = jnp.arange(expert_total * capacity, dtype=jnp.int32)
    slot_marks = (slot_of_route[:, :, None] == slot_ids).astype(bfloat)
    token_marks = jnp.sum(
        slot_marks.reshape(groups, block_rows, 2, -1).astype(single), axis=2
    ).astype(bfloat)

    def dispatch(rows):
        slots = jnp.einsum("gts,gtd->gsd", token_marks, rows, preferred_element_type=single)
        slots = slots.astype(bfloat).reshape(groups, experts, EXP_DEV, capacity, D)
        return exchange(slots.transpose(1, 2, 0, 3, 4)).reshape(
            experts, EXP_DEV, groups * capacity, D
        )

    def collect(blocks):
        back = exchange(blocks.astype(bfloat)).reshape(experts, EXP_DEV, groups, capacity, D)
        return back.transpose(2, 0, 1, 3, 4).reshape(groups, expert_total * capacity, D)

    owner_rows = dispatch(upstream_all)

    own_positions = lax.axis_index("expert") * block_rows + jnp.arange(block_rows, dtype=jnp.int32)
    distance = own_positions[:, None] - jnp.arange(length, dtype=jnp.int32)[None, :]
    bounds = jnp.sum(
        (bucket_table[:, None] < jnp.arange(NB + 1, dtype=jnp.int32)[None, :]).astype(jnp.int32),
        axis=0,
    )
    geometry = (distance, bucket_marks(distance, bounds[:NB], bounds[1:]), scale)

    hidden_zero = hidden_in.reshape(block_rows, D).astype(single)
    mid_first, peak_first, saved_first = attention_forward(
        hidden_zero, gain_attn[0], qkv[0], projection[0], bias_weights[0], geometry
    )
    dense_normed = spread(rms_norm(mid_first, gain_mlp[0]).astype(bfloat))
    pre_act = matmul(dense_normed, dense_up)
    activation = spread(jax.nn.gelu(pre_act).astype(bfloat))
    layer_one = mid_first + matmul(activation, dense_down)
    mid_second, peak_second, saved_second = attention_forward(
        layer_one, gain_attn[1], qkv[1], projection[1], bias_weights[1], geometry
    )

    moe_normed = rms_norm(mid_second, gain_mlp[1]).astype(bfloat)
    normed_all = gather_shard(moe_normed)
    received = dispatch(normed_all)
    router_logits = jnp.einsum("gtd,de->gte", normed_all, router_full, preferred_element_type=single)
    selected = (route_rows[..., None] == expert_ids).astype(single)
    gates_all = jax.nn.softmax(jnp.sum(selected * router_logits[:, :, None, :], axis=-1), axis=-1)
    slot_gates = jnp.sum(
        gates_all.reshape(groups, -1)[:, :, None] * (slot_of_route[:, :, None] == slot_ids), axis=1
    )
    owner_gates = exchange(
        slot_gates.reshape(groups, experts, EXP_DEV, capacity).transpose(1, 2, 0, 3)
    ).reshape(experts, EXP_DEV, groups * capacity)

    expert_pre = jnp.einsum("sjcd,jdf->sjcf", received, up_own, preferred_element_type=single)
    expert_act = jax.nn.gelu(expert_pre).astype(bfloat)
    expert_out = jnp.einsum(
        "sjcf,jfd->sjcd", expert_act, expert_down, preferred_element_type=single
    )
    owner_grad = (owner_gates[..., None] * owner_rows.astype(single)).astype(bfloat)
    act_grad = jnp.einsum("sjcd,jfd->sjcf", owner_grad, expert_down, preferred_element_type=single)
    pre_grad = gelu_back(expert_pre, act_grad).astype(bfloat)
    row_grad = jnp.einsum("sjcf,jdf->sjcd", pre_grad, up_own, preferred_element_type=single)

    returned = collect(expert_out)
    back_rows = collect(row_grad)
    expert_down_grad = jnp.einsum(
        "sjcf,sjcd->jfd", expert_act, owner_grad, preferred_element_type=single
    )
    up_grad = jnp.einsum(
        "sjcd,sjcf->jdf", received, pre_grad, preferred_element_type=single
    ).astype(bfloat)

    route_out = jnp.einsum("grs,gsd->grd", slot_marks, returned, preferred_element_type=single)
    route_out = route_out.reshape(groups, block_rows, 2, D)
    gate_grad = scatter_shard(
        jnp.sum(route_out * upstream_all[:, :, None, :].astype(single), axis=-1), single
    )
    mixed = scatter_shard(jnp.sum(gates_all[..., None] * route_out, axis=2))
    hidden_out = (mid_second + mixed).astype(bfloat).reshape(hidden_in.shape)

    gates = lax.dynamic_index_in_dim(gates_all, here, 0, keepdims=False)
    own_selected = lax.dynamic_index_in_dim(selected, here, 0, keepdims=False)
    upstream = out_grad.reshape(block_rows, D).astype(single)
    chosen_grad = gates * (gate_grad - jnp.sum(gates * gate_grad, axis=-1, keepdims=True))
    logit_grad = jnp.sum(chosen_grad[:, :, None] * own_selected, axis=1).astype(bfloat)
    router_grad = matmul(moe_normed.T, logit_grad)
    row_terms = jnp.einsum("gts,gsd->gtd", token_marks, back_rows, preferred_element_type=single)
    normed_grad = matmul(logit_grad, router_full.T) + scatter_shard(row_terms)
    moe_input_grad, moe_gain_grad = norm_back(mid_second, gain_mlp[1], normed_grad)
    mid_grad = upstream + moe_input_grad

    up_grad = up_grad.reshape(EXP_DEV, groups, part, width)
    expert_up_grad = jnp.zeros((EXP_DEV, part, groups * width), single)
    for step in range(groups):
        piece = lax.dynamic_index_in_dim(up_grad, (here + step) % groups, 1, keepdims=False)
        if step:
            piece = shard_shift(piece, step)
        expert_up_grad = lax.dynamic_update_slice_in_dim(
            expert_up_grad, piece.astype(single), ((here - step) % groups) * width, 2
        )

    layer_grad, gain_second, qkv_second, projection_second, bias_second = attention_backward(
        mid_grad, layer_one, gain_attn[1], qkv[1], projection[1], bias_weights[1], geometry,
        saved_second,
    )
    second_grad = reduce_weight(jnp.concatenate([qkv_second, projection_second], axis=1))
    dense_branch = layer_grad.astype(bfloat)
    mlp_down_grad = reduce_weight(matmul(activation.T, dense_branch))
    hidden_act_grad = unspread(matmul(dense_branch, dense_down.T))
    pre_act_grad = gelu_back(pre_act, hidden_act_grad).astype(bfloat)
    mlp_up_grad = reduce_weight(matmul(dense_normed.T, pre_act_grad))
    dense_normed_grad = unspread(matmul(pre_act_grad, dense_up.T))
    dense_input_grad, dense_gain_grad = norm_back(mid_first, gain_mlp[0], dense_normed_grad)
    first_grad = layer_grad + dense_input_grad
    input_grad, gain_first, qkv_first, projection_first, bias_first = attention_backward(
        first_grad, hidden_zero, gain_attn[0], qkv[0], projection[0], bias_weights[0], geometry,
        saved_first,
    )
    first_weight_grad = reduce_weight(jnp.concatenate([qkv_first, projection_first], axis=1))

    gains = jnp.stack([gain_first, gain_second, dense_gain_grad, moe_gain_grad])
    biases = jnp.stack([bias_first, bias_second])
    small_grad = jnp.concatenate(
        [
            gains.reshape(4, groups, part).transpose(1, 0, 2).reshape(groups, -1),
            biases.reshape(2, groups, NB // groups, H).transpose(1, 0, 2, 3).reshape(groups, -1),
            router_grad.reshape(groups, -1),
        ],
        axis=1,
    )
    small_grad = lax.psum(scatter_shard(small_grad, single), "expert")
    gain_cut = 4 * part
    bias_cut = gain_cut + 2 * (NB // groups) * H
    own_gains = small_grad[:gain_cut].reshape(4, part)
    peaks = lax.pmax(jnp.stack([peak_first, peak_second]), ("expert", "shard"))
    clip_scales = jnp.sqrt(clip_limit / jnp.maximum(peaks, clip_limit))
    return (
        hidden_out,
        input_grad.reshape(hidden_in.shape),
        own_gains[:2],
        jnp.stack([first_weight_grad[:, : 3 * D], second_grad[:, : 3 * D]]),
        jnp.stack([first_weight_grad[:, 3 * D :], second_grad[:, 3 * D :]]),
        small_grad[gain_cut:bias_cut].reshape(2, NB // groups, H),
        own_gains[2:],
        mlp_up_grad,
        mlp_down_grad,
        small_grad[bias_cut:].reshape(part, expert_total),
        expert_up_grad,
        expert_down_grad,
        clip_scales,
    )


MESH = pl.DeviceIdType.MESH
ANY = pl.ANY
VMEM = pltpu.VMEM


def place():
    return lax.axis_index("expert"), lax.axis_index("shard")


def greet(devices):
    barrier = pltpu.get_barrier_semaphore()
    for device in devices:
        pl.semaphore_signal(barrier, inc=1, device_id=device, device_id_type=MESH)
    pl.semaphore_wait(barrier, len(devices))


def push(sent, source, target, send_sem, recv_sem, device):
    copy = pltpu.make_async_remote_copy(
        src_ref=source,
        dst_ref=target,
        send_sem=send_sem,
        recv_sem=recv_sem,
        device_id=device,
        device_id_type=MESH,
    )
    copy.start()
    sent.append(copy)
    return copy


def small_kernel(groups, small_ref, routes_ref, small_out, routes_out, ssem, rsem, lsem):
    e, s = place()
    others = [(e, lax.rem(s + k, groups)) for k in range(1, groups)]
    local = [
        pltpu.make_async_copy(small_ref, small_out.at[s], lsem.at[0]),
        pltpu.make_async_copy(routes_ref, routes_out.at[s], lsem.at[1]),
    ]
    for copy in local:
        copy.start()
    greet(others)
    sent = []
    for k, device in enumerate(others):
        push(sent, small_ref, small_out.at[s], ssem.at[0, k], rsem.at[0, k], device)
        push(sent, routes_ref, routes_out.at[s], ssem.at[1, k], rsem.at[1, k], device)
    for copy in local:
        copy.wait()
    for copy in sent:
        copy.wait()


def gather_small(small, routes):
    groups = lax.axis_size("shard")
    vmem = pl.BlockSpec(memory_space=VMEM)
    return pl.pallas_call(
        functools.partial(small_kernel, groups),
        name="gather_small",
        out_shape=(
            jax.ShapeDtypeStruct((groups,) + small.shape, small.dtype),
            jax.ShapeDtypeStruct((groups,) + routes.shape, routes.dtype),
        ),
        in_specs=[vmem, vmem],
        out_specs=(vmem, vmem),
        scratch_shapes=[
            pltpu.SemaphoreType.DMA((2, groups - 1)),
            pltpu.SemaphoreType.DMA((2, groups - 1)),
            pltpu.SemaphoreType.DMA((2,)),
        ],
        compiler_params=pltpu.CompilerParams(collective_id=1, has_side_effects=True),
    )(small, routes)


def norm_rows(inputs, gain):
    return inputs * lax.rsqrt(jnp.mean(inputs * inputs, axis=-1, keepdims=True) + epsilon) * gain


def dot_rows(left, right):
    return lax.dot_general(left, right, (((1,), (1,)), ((), ())), preferred_element_type=single)


def loop(count, body):
    def step(i, carry):
        body(i)
        return carry

    lax.fori_loop(0, count, step, 0)


def lane_block(i, width):
    return pl.ds(pl.multiple_of(i * width, 128), width)


def row_block(i, height):
    return pl.ds(pl.multiple_of(i * height, height), height)


T = 128
PAIRS = H // 2
TOE = 1152


def forward_kernel(
    hidden_ref,
    gains_ref,
    table_ref,
    qkv_hbm,
    out_hbm,
    up_hbm,
    down_hbm,
    expert_up_hbm,
    cot_hbm,
    normed_out,
    query_out,
    attended_out,
    mid_out,
    dense_normed_out,
    pre_out,
    act_out,
    one_out,
    peak_out,
    normed_all,
    qkv0_out,
    qkv1_out,
    proj0_out,
    proj1_out,
    up_out,
    down_out,
    kv_out,
    probs_out,
    up_own,
    cot_all,
    w_qkv0,
    w_qkv1,
    w_out0,
    w_out1,
    w_up,
    w_down,
    kv,
    probs,
    scores,
    zs,
    zr,
    f1s,
    f1r,
    f2s,
    f2r,
    cs,
    cr,
    locals_sem,
    k1s,
    k1r,
    k2s,
    k2r,
    kcs,
    kcr,
    us,
    ur,
    gs,
    gr,
    ns,
    nr,
    outs_sem,
):
    e, s = place()
    core = lax.rem(e, 2)
    quarter = e // 2
    at_x = e + 2 - 4 * lax.rem(quarter, 2)
    at_y = lax.rem(e + 4, 8)
    at_core = e + 1 - 2 * core
    inward = jnp.where(core == 0, at_x, at_y)
    onward = jnp.where(core == 0, at_y, at_x)
    others = [lax.rem(s + k, 4) for k in range(1, 4)]
    sources = [lax.rem(s + 4 - k, 4) for k in range(1, 4)]
    sent = []
    kept = []

    def local(source, target, sem):
        copy = pltpu.make_async_copy(source, target, sem)
        copy.start()
        return copy

    chunks = [
        (qkv_hbm.at[0], w_qkv0, 48, 1152),
        (out_hbm.at[0], w_out0, 48, 384),
        (up_hbm, w_up, 48, 1536),
        (down_hbm, w_down, 192, 384),
        (qkv_hbm.at[1], w_qkv1, 48, 1152),
        (out_hbm.at[1], w_out1, 48, 384),
    ]

    def block(target, who, position, height, half, width):
        rows = pl.ds(pl.multiple_of(position * 4 * height + who * height, height), height)
        return target.at[rows, lane_block(half, width)]

    stage1, stage2, stage3, stage4, own = {}, {}, {}, {}, {}

    def z_send(c):
        source, target, height, width = chunks[c]
        piece = source.at[row_block(quarter, height), lane_block(core, width)]
        mine = block(target, quarter, s, height, core, width)
        stage1[c] = [
            push(sent, piece, mine, zs.at[c, k], zr.at[c, k], (e, others[k])) for k in range(3)
        ]
        own[c] = local(source, target.at[row_block(s, 4 * height), :], locals_sem.at[c])

    def plane_send(c):
        _, target, height, width = chunks[c]
        stage2[c] = []
        for k in range(3):
            stage1[c][k].wait_recv()
            mine = block(target, quarter, sources[k], height, core, width)
            stage2[c].append(
                [
                    push(sent, mine, mine, f1s.at[c, k, i], f1r.at[c, k, i], (partner, s))
                    for i, partner in enumerate((at_x, at_y))
                ]
            )

    def plane_forward(c):
        _, target, height, width = chunks[c]
        stage3[c] = []
        for k in range(3):
            pltpu.make_async_remote_copy(
                src_ref=block(target, quarter, sources[k], height, core, width),
                dst_ref=block(target, quarter, sources[k], height, core, width),
                send_sem=f1s.at[c, k, core],
                recv_sem=f1r.at[c, k, core],
                device_id=(inward, s),
                device_id_type=MESH,
            ).wait_recv()
            theirs = block(target, inward // 2, sources[k], height, core, width)
            stage3[c].append(
                push(sent, theirs, theirs, f2s.at[c, k], f2r.at[c, k], (onward, s))
            )

    def core_send(c):
        _, target, height, width = chunks[c]
        stage4[c] = []
        for k in range(3):
            pltpu.make_async_remote_copy(
                src_ref=block(target, quarter, sources[k], height, core, width),
                dst_ref=block(target, quarter, sources[k], height, core, width),
                send_sem=f1s.at[c, k, 1 - core],
                recv_sem=f1r.at[c, k, 1 - core],
                device_id=(onward, s),
                device_id_type=MESH,
            ).wait_recv()
            stage3[c][k].wait_recv()
            half = target.at[row_block(sources[k], 4 * height), lane_block(core, width)]
            stage4[c].append(push(sent, half, half, cs.at[c, k], cr.at[c, k], (at_core, s)))

    weight_outs = [qkv0_out, proj0_out, up_out, down_out, qkv1_out, proj1_out]

    def ready(c):
        for k in range(3):
            stage4[c][k].wait_recv()
        own[c].wait()
        kept.append(local(chunks[c][1], weight_outs[c], outs_sem.at[c]))

    greet(
        [(at_core, s), (at_x, s), (at_y, s)] + [(e, other) for other in others]
    )
    z_send(0)
    z_send(1)
    z_send(2)

    def attention(layer, inputs, w_qkv, w_out, work):
        normed = norm_rows(inputs, gains_ref[pl.ds(layer, 1), :]).astype(bfloat)
        normed_out[layer] = normed
        if layer == 0:
            plane_send(0)
            plane_forward(0)
            core_send(0)
            ready(0)
        else:
            ready(4)
        own_rows = row_block(e, T)
        first, second, third = [], [], []
        for part in range(3):
            x = normed_out[layer]
            for i, base in enumerate((D, 2 * D)):
                columns = w_qkv[:, base + 256 * part : base + 256 * (part + 1)]
                kv[layer, part, own_rows, 256 * i : 256 * (i + 1)] = jnp.dot(
                    x, columns, preferred_element_type=single
                ).astype(bfloat)
            mine = kv.at[layer, part, own_rows, :]
            first.append(
                [
                    push(sent, mine, mine, k1s.at[layer, part, i], k1r.at[layer, part, i], (p, s))
                    for i, p in enumerate((at_x, at_y))
                ]
            )
            third.append(
                [
                    push(
                        sent, mine, mine, kcs.at[layer, part, 0], kcr.at[layer, part, 0],
                        (at_core, s),
                    )
                ]
            )
        query_out[layer] = jnp.dot(
            normed_out[layer], w_qkv[:, :D], preferred_element_type=single
        ).astype(bfloat)
        if work:
            work[0]()
        at_diagonal = inward + onward - e
        for part in range(3):
            pltpu.make_async_remote_copy(
                src_ref=kv.at[layer, part, own_rows, :],
                dst_ref=kv.at[layer, part, own_rows, :],
                send_sem=k1s.at[layer, part, core],
                recv_sem=k1r.at[layer, part, core],
                device_id=(inward, s),
                device_id_type=MESH,
            ).wait_recv()
            theirs = kv.at[layer, part, row_block(inward, T), :]
            second.append(
                push(
                    sent, theirs, theirs, k2s.at[layer, part], k2r.at[layer, part], (onward, s)
                )
            )
            third[part].append(
                push(
                    sent, theirs, theirs, kcs.at[layer, part, 1], kcr.at[layer, part, 1],
                    (at_core, s),
                )
            )
        if work:
            work[1]()
        for part in range(3):
            pltpu.make_async_remote_copy(
                src_ref=kv.at[layer, part, own_rows, :],
                dst_ref=kv.at[layer, part, own_rows, :],
                send_sem=k1s.at[layer, part, 1 - core],
                recv_sem=k1r.at[layer, part, 1 - core],
                device_id=(onward, s),
                device_id_type=MESH,
            ).wait_recv()
            theirs = kv.at[layer, part, row_block(onward, T), :]
            third[part].append(
                push(
                    sent, theirs, theirs, kcs.at[layer, part, 2], kcr.at[layer, part, 2],
                    (at_core, s),
                )
            )
            second[part].wait_recv()
            theirs = kv.at[layer, part, row_block(at_diagonal, T), :]
            third[part].append(
                push(
                    sent, theirs, theirs, kcs.at[layer, part, 3], kcr.at[layer, part, 3],
                    (at_core, s),
                )
            )
        for part in range(3):
            for i in range(4):
                third[part][i].wait_recv()

            def one_pair(local_pair):
                pair = 2 * part + local_pair
                lanes = lane_block(pair, 128)
                queries = query_out[layer, :, lanes]
                lane = lax.broadcasted_iota(jnp.int32, (T, 128), 1)
                zero = jnp.zeros_like(queries)
                both = jnp.concatenate(
                    [jnp.where(lane < HD, queries, zero), jnp.where(lane >= HD, queries, zero)]
                )
                keys = kv[layer, part, :, lane_block(local_pair, 128)]
                scores[...] = dot_rows(both, keys) * (1.0 / math.sqrt(HD))
                for half in range(2):
                    head = 2 * pair + half
                    toeplitz = table_ref[pl.ds(layer * H + head, 1), :]
                    peak = jnp.full((1, 1), -jnp.inf, single)
                    for rows in range(0, T, 32):
                        raw = scores[half * T + rows : half * T + rows + 32, :]
                        row = e * T + rows + lax.broadcasted_iota(jnp.int32, raw.shape, 0)
                        causal = row >= lax.broadcasted_iota(jnp.int32, raw.shape, 1)
                        shifted = pltpu.roll(
                            jnp.broadcast_to(toeplitz, (32, TOE)),
                            TOE - (T - 1) + rows,
                            1,
                            stride=1,
                            stride_axis=0,
                        )[:, : raw.shape[1]]
                        peak = jnp.maximum(
                            peak, jnp.max(jnp.where(causal, raw, -jnp.inf), keepdims=True)
                        )
                        masked = jnp.where(causal, raw + shifted, -jnp.inf)
                        top = jnp.max(masked, axis=-1, keepdims=True)
                        exponent = jnp.exp(masked - top)
                        total = jnp.sum(exponent, axis=-1, keepdims=True)
                        probs[layer, pl.ds(pl.multiple_of(head * T + rows, 32), 32), :] = (
                            exponent / total
                        ).astype(bfloat)
                    peak_out[pl.ds(layer * H + head, 1), :] = jnp.broadcast_to(peak, (1, 128))
                values = kv[layer, part, :, pl.ds(pl.multiple_of(256 + local_pair * 128, 128), 128)]
                mixed = jnp.dot(
                    probs[layer, pl.ds(pl.multiple_of(pair * 2 * T, 2 * T), 2 * T), :],
                    values,
                    preferred_element_type=single,
                )
                attended_out[layer, :, lanes] = jnp.where(
                    lane < HD, mixed[:T], mixed[T:]
                ).astype(bfloat)

            loop(2, one_pair)
            if work:
                work[2 + part]()
        kept.append(local(kv.at[layer], kv_out.at[layer], outs_sem.at[6 + layer]))
        kept.append(local(probs.at[layer], probs_out.at[layer], outs_sem.at[8 + layer]))

    def nothing():
        pass

    def work0():
        plane_send(1)
        z_send(3)

    def work1():
        plane_forward(1)

    def work2():
        core_send(1)
        plane_send(2)

    def work3():
        plane_forward(2)
        z_send(4)
        z_send(5)

    def work4():
        core_send(2)
        plane_send(3)

    hidden = hidden_ref[...].astype(single)
    attention(0, hidden, w_qkv0, w_out0, [work0, work1, work2, work3, work4])
    ready(1)
    mid_out[0] = hidden + jnp.dot(
        attended_out[0], w_out0[...], preferred_element_type=single
    )
    dense_normed_out[...] = norm_rows(mid_out[0], gains_ref[pl.ds(2, 1), :]).astype(bfloat)
    reshard = []
    for k in range(3):
        reshard.append(
            push(
                sent,
                expert_up_hbm.at[:, :, lane_block(others[k], 768)],
                up_own.at[:, row_block(s, 192), :],
                us.at[k],
                ur.at[k],
                (e, others[k]),
            )
        )
        reshard.append(
            push(sent, cot_hbm, cot_all.at[s], gs.at[k], gr.at[k], (e, others[k]))
        )
    kept.append(
        local(
            expert_up_hbm.at[:, :, lane_block(s, 768)],
            up_own.at[:, row_block(s, 192), :],
            us.at[3],
        )
    )
    kept.append(local(cot_hbm, cot_all.at[s], gs.at[3]))
    ready(2)

    def up_part(i):
        lanes = lane_block(i, 512)
        before = jnp.dot(dense_normed_out[...], w_up[:, lanes], preferred_element_type=single)
        pre_out[:, lanes] = before
        act_out[:, lanes] = jax.nn.gelu(before).astype(bfloat)

    plane_forward(3)
    loop(3, up_part)
    core_send(3)
    plane_send(4)
    plane_send(5)

    def up_later(i):
        up_part(i + 3)

    loop(3, up_later)
    plane_forward(4)
    plane_forward(5)
    ready(3)
    one_out[...] = mid_out[0]

    def down_part(i):
        rows = row_block(i, 768)
        one_out[...] += jnp.dot(
            act_out[:, lane_block(i, 768)], w_down[rows, :], preferred_element_type=single
        )

    loop(4, down_part)
    core_send(4)
    core_send(5)
    attention(1, one_out[...], w_qkv1, w_out1, None)
    ready(5)
    mid_out[1] = one_out[...] + jnp.dot(
        attended_out[1], w_out1[...], preferred_element_type=single
    )
    normed_all[s] = norm_rows(mid_out[1], gains_ref[pl.ds(3, 1), :]).astype(bfloat)
    last = [
        push(sent, normed_all.at[s], normed_all.at[s], ns.at[k], nr.at[k], (e, others[k]))
        for k in range(3)
    ]
    for copy in last + reshard:
        copy.wait_recv()
    for copy in kept:
        copy.wait()
    for copy in sent:
        copy.wait_send()


def forward(hidden, gains, table, qkv, out, up, down, expert_up, cotangent):
    length = T * lax.axis_size("expert")
    vmem = pl.BlockSpec(memory_space=VMEM)
    anywhere = pl.BlockSpec(memory_space=ANY)
    shape = jax.ShapeDtypeStruct
    ff = up.shape[1]
    sem = pltpu.SemaphoreType.DMA
    return pl.pallas_call(
        forward_kernel,
        name="forward_layers",
        out_shape=(
            shape((2, T, D), bfloat),
            shape((2, T, D), bfloat),
            shape((2, T, D), bfloat),
            shape((2, T, D), single),
            shape((T, D), bfloat),
            shape((T, ff), single),
            shape((T, ff), bfloat),
            shape((T, D), single),
            shape((2 * H, 128), single),
            shape((4, T, D), bfloat),
            shape((D, 3 * D), bfloat),
            shape((D, 3 * D), bfloat),
            shape((D, D), bfloat),
            shape((D, D), bfloat),
            shape((D, ff), bfloat),
            shape((ff, D), bfloat),
            shape((2, 3, length, 512), bfloat),
            shape((2, H * T, length), bfloat),
            shape((EXP_DEV, D, 768), bfloat),
            shape((4, T, D), bfloat),
        ),
        in_specs=[vmem] * 3 + [anywhere] * 6,
        out_specs=(vmem,) * 10 + (anywhere,) * 10,
        scratch_shapes=[
            VMEM((D, 3 * D), bfloat),
            VMEM((D, 3 * D), bfloat),
            VMEM((D, D), bfloat),
            VMEM((D, D), bfloat),
            VMEM((D, ff), bfloat),
            VMEM((ff, D), bfloat),
            VMEM((2, 3, length, 512), bfloat),
            VMEM((2, H * T, length), bfloat),
            VMEM((2 * T, length), single),
            sem((6, 3)), sem((6, 3)),
            sem((6, 3, 2)), sem((6, 3, 2)),
            sem((6, 3)), sem((6, 3)),
            sem((6, 3)), sem((6, 3)),
            sem((6,)),
            sem((2, 3, 2)), sem((2, 3, 2)),
            sem((2, 3)), sem((2, 3)),
            sem((2, 3, 4)), sem((2, 3, 4)),
            sem((4,)), sem((3,)),
            sem((4,)), sem((3,)),
            sem((3,)), sem((3,)),
            sem((10,)),
        ],
        compiler_params=pltpu.CompilerParams(
            collective_id=2, has_side_effects=True, vmem_limit_bytes=56 * 2**20
        ),
    )(hidden, gains, table, qkv, out, up, down, expert_up, cotangent)


def kernel_backward(upstream, hidden, norm_gain, qkv, projection, marks, saved):
    normalized, queries, kv, probs, attended = saved
    rows = hidden.shape[0]
    scale = 1.0 / math.sqrt(HD)
    branch_grad = upstream.astype(bfloat)
    projection_grad = matmul(spread(attended).T, branch_grad)
    attended_grad = matmul(branch_grad, projection.T).astype(bfloat)
    queries = queries.reshape(rows, H, HD)
    keys = kv[:, :, :256].transpose(1, 0, 2).reshape(-1, H, HD)
    values = kv[:, :, 256:].transpose(1, 0, 2).reshape(-1, H, HD)
    grad_heads = attended_grad.reshape(rows, H, HD)
    probs_low = probs.reshape(H, rows, -1)
    probs = probs_low.astype(single)
    prob_grad = jnp.einsum("ihd,jhd->hij", grad_heads, values, preferred_element_type=single)
    row_dot = jnp.sum(prob_grad * probs, axis=-1)
    score_grad = (probs * (prob_grad - row_dot[..., None])).astype(bfloat)
    query_grad = jnp.einsum("hij,jhd->ihd", score_grad, keys, preferred_element_type=single) * scale
    query_grad = query_grad.astype(bfloat).reshape(rows, D)
    bias_grad = jnp.einsum("hij,bij->bh", score_grad, marks, preferred_element_type=single)
    key_grad = (
        jnp.einsum("hij,ihd->jhd", score_grad, queries, preferred_element_type=single) * scale
    )
    value_grad = jnp.einsum("hij,ihd->jhd", probs_low, grad_heads, preferred_element_type=single)
    pair = jnp.concatenate([key_grad.reshape(-1, D), value_grad.reshape(-1, D)], axis=-1)
    pair_grad = lax.psum_scatter(pair.astype(bfloat), "expert", scatter_dimension=0, tiled=True)
    packed_grad = jnp.concatenate([query_grad, pair_grad], axis=-1)
    qkv_grad = matmul(spread(normalized).T, packed_grad)
    normed_grad = matmul(packed_grad, qkv.T)
    input_grad, gain_grad = norm_back(hidden, norm_gain, normed_grad)
    return upstream + input_grad, gain_grad, qkv_grad, projection_grad, bias_grad


def shards(
    hidden_in,
    attn_gain,
    qkv_weight,
    out_weight,
    rel_bias,
    bucket_table,
    mlp_gain,
    mlp_up,
    mlp_down,
    router_weight,
    expert_up,
    expert_down,
    routes,
    out_grad,
):
    block_rows = hidden_in.shape[1]
    length = bucket_table.shape[0]
    experts = lax.axis_size("expert")
    groups = lax.axis_size("shard")
    here = lax.axis_index("shard")
    expert_total = EXP_DEV * experts
    capacity = 4 * block_rows // expert_total
    width = expert_down.shape[1]

    small = jnp.concatenate(
        [attn_gain.reshape(-1), mlp_gain.reshape(-1), rel_bias.reshape(-1), router_weight.reshape(-1)]
    ).astype(single)
    part = D // groups
    used = small.shape[0]
    small = jnp.pad(small, (0, -used % 1024)).reshape(-1, 128)
    small, route_rows = gather_small(small, routes.reshape(-1, 128))
    small = small.reshape(groups, -1)
    route_rows = route_rows.reshape(groups, block_rows, 2)
    cuts = [0, 4 * part, 4 * part + 2 * (NB // groups) * H, used]
    gains, bias_weights, router_full = (small[:, cuts[i] : cuts[i + 1]] for i in range(3))
    gains = gains.reshape(groups, 4, part).transpose(1, 0, 2).reshape(4, D)
    gain_attn, gain_mlp = gains[:2], gains[2:]
    bias_weights = (
        bias_weights.reshape(groups, 2, NB // groups, H).transpose(1, 0, 2, 3).reshape(2, NB, H)
    )
    router_full = router_full.reshape(D, expert_total).astype(bfloat)

    distances = lax.axis_index("expert") * block_rows + block_rows - 1 - jnp.arange(TOE)
    buckets = jnp.take(bucket_table, jnp.clip(distances, 0, length - 1))
    toeplitz_marks = (buckets[None] == jnp.arange(NB, dtype=jnp.int32)[:, None]).astype(bfloat)
    table = jnp.einsum(
        "lbh,bm->lhm", bias_weights.astype(bfloat), toeplitz_marks, preferred_element_type=single
    ).reshape(2 * H, TOE)

    (
        normed, queries, attended, mid, dense_normed, pre_act, activation, layer_one, peak_rows,
        normed_all, qkv0, qkv1, projection0, projection1, dense_up, dense_down, kv, probs, up_own,
        upstream_all,
    ) = forward(
        hidden_in.reshape(block_rows, D), gains, table, qkv_weight, out_weight, mlp_up, mlp_down,
        expert_up, out_grad.reshape(block_rows, D),
    )
    mid_first, mid_second = mid[0], mid[1]
    hidden_zero = hidden_in.reshape(block_rows, D).astype(single)
    moe_normed = lax.dynamic_index_in_dim(normed_all, here, 0, keepdims=False)
    own_positions = lax.axis_index("expert") * block_rows + jnp.arange(block_rows, dtype=jnp.int32)
    distance = own_positions[:, None] - jnp.arange(length, dtype=jnp.int32)[None, :]
    bounds = jnp.sum(
        (bucket_table[:, None] < jnp.arange(NB + 1, dtype=jnp.int32)[None, :]).astype(jnp.int32),
        axis=0,
    )
    attention_marks = bucket_marks(distance, bounds[:NB], bounds[1:])

    expert_ids = jnp.arange(expert_total, dtype=jnp.int32)
    flat_routes = route_rows.reshape(groups, -1)
    marks = (flat_routes[:, :, None] == expert_ids).astype(jnp.int32)
    rank = jnp.sum((jnp.cumsum(marks, axis=1) - marks) * marks, axis=2)
    slot_of_route = flat_routes * capacity + rank
    slot_ids = jnp.arange(expert_total * capacity, dtype=jnp.int32)
    slot_marks = (slot_of_route[:, :, None] == slot_ids).astype(bfloat)
    token_marks = jnp.sum(
        slot_marks.reshape(groups, block_rows, 2, -1).astype(single), axis=2
    ).astype(bfloat)

    def dispatch(rows):
        slots = jnp.einsum("gts,gtd->gsd", token_marks, rows, preferred_element_type=single)
        slots = slots.astype(bfloat).reshape(groups, experts, EXP_DEV, capacity, D)
        return exchange(slots.transpose(1, 2, 0, 3, 4)).reshape(
            experts, EXP_DEV, groups * capacity, D
        )

    def collect(blocks):
        back = exchange(blocks.astype(bfloat)).reshape(experts, EXP_DEV, groups, capacity, D)
        return back.transpose(2, 0, 1, 3, 4).reshape(groups, expert_total * capacity, D)

    owner_rows = dispatch(upstream_all)
    received = dispatch(normed_all)
    router_logits = jnp.einsum("gtd,de->gte", normed_all, router_full, preferred_element_type=single)
    selected = (route_rows[..., None] == expert_ids).astype(single)
    gates_all = jax.nn.softmax(jnp.sum(selected * router_logits[:, :, None, :], axis=-1), axis=-1)
    slot_gates = jnp.sum(
        gates_all.reshape(groups, -1)[:, :, None] * (slot_of_route[:, :, None] == slot_ids), axis=1
    )
    owner_gates = exchange(
        slot_gates.reshape(groups, experts, EXP_DEV, capacity).transpose(1, 2, 0, 3)
    ).reshape(experts, EXP_DEV, groups * capacity)

    expert_pre = jnp.einsum("sjcd,jdf->sjcf", received, up_own, preferred_element_type=single)
    expert_act = jax.nn.gelu(expert_pre).astype(bfloat)
    expert_out = jnp.einsum(
        "sjcf,jfd->sjcd", expert_act, expert_down, preferred_element_type=single
    )
    owner_grad = (owner_gates[..., None] * owner_rows.astype(single)).astype(bfloat)
    act_grad = jnp.einsum("sjcd,jfd->sjcf", owner_grad, expert_down, preferred_element_type=single)
    pre_grad = gelu_back(expert_pre, act_grad).astype(bfloat)
    row_grad = jnp.einsum("sjcf,jdf->sjcd", pre_grad, up_own, preferred_element_type=single)

    returned = collect(expert_out)
    back_rows = collect(row_grad)
    expert_down_grad = jnp.einsum(
        "sjcf,sjcd->jfd", expert_act, owner_grad, preferred_element_type=single
    )
    up_grad = jnp.einsum(
        "sjcd,sjcf->jdf", received, pre_grad, preferred_element_type=single
    ).astype(bfloat)

    route_out = jnp.einsum("grs,gsd->grd", slot_marks, returned, preferred_element_type=single)
    route_out = route_out.reshape(groups, block_rows, 2, D)
    gate_grad = scatter_shard(
        jnp.sum(route_out * upstream_all[:, :, None, :].astype(single), axis=-1), single
    )
    mixed = scatter_shard(jnp.sum(gates_all[..., None] * route_out, axis=2))
    hidden_out = (mid_second + mixed).astype(bfloat).reshape(hidden_in.shape)

    gates = lax.dynamic_index_in_dim(gates_all, here, 0, keepdims=False)
    own_selected = lax.dynamic_index_in_dim(selected, here, 0, keepdims=False)
    upstream = out_grad.reshape(block_rows, D).astype(single)
    chosen_grad = gates * (gate_grad - jnp.sum(gates * gate_grad, axis=-1, keepdims=True))
    logit_grad = jnp.sum(chosen_grad[:, :, None] * own_selected, axis=1).astype(bfloat)
    router_grad = matmul(moe_normed.T, logit_grad)
    row_terms = jnp.einsum("gts,gsd->gtd", token_marks, back_rows, preferred_element_type=single)
    normed_grad = matmul(logit_grad, router_full.T) + scatter_shard(row_terms)
    moe_input_grad, moe_gain_grad = norm_back(mid_second, gain_mlp[1], normed_grad)
    mid_grad = upstream + moe_input_grad

    up_grad = up_grad.reshape(EXP_DEV, groups, part, width)
    expert_up_grad = jnp.zeros((EXP_DEV, part, groups * width), single)
    for step in range(groups):
        piece = lax.dynamic_index_in_dim(up_grad, (here + step) % groups, 1, keepdims=False)
        if step:
            piece = shard_shift(piece, step)
        expert_up_grad = lax.dynamic_update_slice_in_dim(
            expert_up_grad, piece.astype(single), ((here - step) % groups) * width, 2
        )

    layer_grad, gain_second, qkv_second, projection_second, bias_second = kernel_backward(
        mid_grad, layer_one, gain_attn[1], qkv1, projection1, attention_marks,
        (normed[1], queries[1], kv[1], probs[1], attended[1]),
    )
    second_grad = reduce_weight(jnp.concatenate([qkv_second, projection_second], axis=1))
    dense_branch = layer_grad.astype(bfloat)
    mlp_down_grad = reduce_weight(matmul(spread(activation).T, dense_branch))
    hidden_act_grad = matmul(dense_branch, dense_down.T)
    pre_act_grad = gelu_back(pre_act, hidden_act_grad).astype(bfloat)
    mlp_up_grad = reduce_weight(matmul(spread(dense_normed).T, pre_act_grad))
    dense_normed_grad = matmul(pre_act_grad, dense_up.T)
    dense_input_grad, dense_gain_grad = norm_back(mid_first, gain_mlp[0], dense_normed_grad)
    first_grad = layer_grad + dense_input_grad
    input_grad, gain_first, qkv_first, projection_first, bias_first = kernel_backward(
        first_grad, hidden_zero, gain_attn[0], qkv0, projection0, attention_marks,
        (normed[0], queries[0], kv[0], probs[0], attended[0]),
    )
    first_weight_grad = reduce_weight(jnp.concatenate([qkv_first, projection_first], axis=1))

    gains = jnp.stack([gain_first, gain_second, dense_gain_grad, moe_gain_grad])
    biases = jnp.stack([bias_first, bias_second])
    small_grad = jnp.concatenate(
        [
            gains.reshape(4, groups, part).transpose(1, 0, 2).reshape(groups, -1),
            biases.reshape(2, groups, NB // groups, H).transpose(1, 0, 2, 3).reshape(groups, -1),
            router_grad.reshape(groups, -1),
        ],
        axis=1,
    )
    small_grad = lax.psum(scatter_shard(small_grad, single), "expert")
    gain_cut = 4 * part
    bias_cut = gain_cut + 2 * (NB // groups) * H
    own_gains = small_grad[:gain_cut].reshape(4, part)
    peaks = lax.pmax(peak_rows[:, 0].reshape(2, H), ("expert", "shard"))
    clip_scales = jnp.sqrt(clip_limit / jnp.maximum(peaks, clip_limit))
    return (
        hidden_out,
        input_grad.reshape(hidden_in.shape),
        own_gains[:2],
        jnp.stack([first_weight_grad[:, : 3 * D], second_grad[:, : 3 * D]]),
        jnp.stack([first_weight_grad[:, 3 * D :], second_grad[:, 3 * D :]]),
        small_grad[gain_cut:bias_cut].reshape(2, NB // groups, H),
        own_gains[2:],
        mlp_up_grad,
        mlp_down_grad,
        small_grad[bias_cut:].reshape(part, expert_total),
        expert_up_grad,
        expert_down_grad,
        clip_scales,
    )


def solution(mesh):
    tokens = P("shard", "expert", None, None)
    columns = P(None, "shard")
    layers = P(None, "shard", None)
    rows = P("shard", None)
    owned = P("expert", "shard", None)
    in_specs = (
        tokens, columns, layers, layers, layers, P(), columns, rows, rows, rows, owned, owned,
        tokens, tokens,
    )
    out_specs = (
        tokens, tokens, columns, layers, layers, layers, columns, rows, rows, rows, owned, owned,
        P(),
    )
    sized = mesh.shape["expert"] == 8 and mesh.shape["shard"] == 4
    part = shards if sized else plain_shards
    return jax.shard_map(part, mesh=mesh, in_specs=in_specs, out_specs=out_specs, check_vma=False)
```

```python
import functools
import math

import jax
import jax.numpy as jnp
from jax import lax
from jax.experimental import pallas as pl
from jax.experimental.pallas import tpu as pltpu
from jax.sharding import PartitionSpec as P

D = 768
H = 12
HD = 64
NB = 32
EXP_DEV = 2

epsilon = 1e-06
clip_limit = 6.0
bfloat = jnp.bfloat16
single = jnp.float32


def rms_norm(inputs, norm_gain):
    return (
        inputs * lax.rsqrt(jnp.mean(inputs * inputs, axis=-1, keepdims=True) + epsilon) * norm_gain
    )


def norm_back(inputs, norm_gain, upstream):
    _, pullback = jax.vjp(rms_norm, inputs, norm_gain)
    return pullback(upstream)


def gelu_back(pre_values, upstream):
    _, pullback = jax.vjp(jax.nn.gelu, pre_values)
    return pullback(upstream)[0]


def matmul(left, right):
    return jnp.dot(left, right, preferred_element_type=single)


def shard_shift(block, amount):
    count = lax.axis_size("shard")
    return lax.ppermute(block, "shard", [(i, (i + amount) % count) for i in range(count)])


def gather_shard(block):
    count = lax.axis_size("shard")
    here = lax.axis_index("shard")
    result = jnp.zeros((count,) + block.shape, block.dtype)
    for step in range(count):
        piece = block if step == 0 else shard_shift(block, step)
        result = lax.dynamic_update_slice_in_dim(result, piece[None], (here - step) % count, 0)
    return result


def scatter_shard(blocks, sent=bfloat):
    count = lax.axis_size("shard")
    here = lax.axis_index("shard")
    total = lax.dynamic_index_in_dim(blocks, here, 0, keepdims=False).astype(single)
    for step in range(1, count):
        part = lax.dynamic_index_in_dim(blocks, (here + step) % count, 0, keepdims=False)
        total = total + shard_shift(part.astype(sent), step).astype(single)
    return total


def spread(columns):
    experts, shard_count = lax.axis_size("expert"), lax.axis_size("shard")
    rows, width = columns.shape
    cut = columns.reshape(rows, shard_count, experts, width // (shard_count * experts))
    return cut.transpose(0, 2, 1, 3).reshape(rows, width)


def unspread(columns):
    experts, shard_count = lax.axis_size("expert"), lax.axis_size("shard")
    rows, width = columns.shape
    cut = columns.reshape(rows, experts, shard_count, width // (shard_count * experts))
    return cut.transpose(0, 2, 1, 3).reshape(rows, width)


def gather_weight(block):
    part = block.shape[0] // lax.axis_size("expert")
    own = lax.dynamic_slice_in_dim(block, lax.axis_index("expert") * part, part, 0)
    column = gather_shard(own).reshape(-1, block.shape[1])
    return lax.all_gather(column, "expert", axis=0, tiled=True)


def reduce_weight(grad):
    part = lax.psum_scatter(grad.astype(bfloat), "expert", scatter_dimension=0, tiled=True)
    blocks = part.reshape((lax.axis_size("shard"), -1) + part.shape[1:])
    own = scatter_shard(blocks).astype(bfloat)
    return lax.all_gather(own, "expert", axis=0, tiled=True).astype(single)


def bucket_marks(distance, lower, upper):
    inside = (distance[None] >= lower[:, None, None]) & (distance[None] < upper[:, None, None])
    return inside.astype(bfloat)


def position_bias(marks, bias_pair):
    return jnp.einsum("bij,bh->hij", marks, bias_pair, preferred_element_type=single)


def attention_forward(hidden, norm_gain, qkv, projection, bias_pair, geometry):
    distance, marks, scale = geometry
    rows = hidden.shape[0]
    normalized = spread(rms_norm(hidden, norm_gain).astype(bfloat))
    packed = matmul(normalized, qkv).astype(bfloat)
    key_value = lax.all_gather(packed[:, D:], "expert", axis=0, tiled=True)
    shifted = position_bias(marks, bias_pair)
    causal = distance >= 0
    queries = packed[:, :D].reshape(rows, H, HD)
    keys = key_value[:, :D].reshape(-1, H, HD)
    values = key_value[:, D:].reshape(-1, H, HD)
    raw_scores = jnp.einsum("ihd,jhd->hij", queries, keys, preferred_element_type=single) * scale
    head_peak = jnp.max(jnp.where(causal[None], raw_scores, -jnp.inf), axis=(1, 2))
    masked = jnp.where(causal[None], raw_scores + shifted, -jnp.inf)
    softmax_top = jnp.max(masked, axis=-1, keepdims=True)
    exponent = jnp.exp(masked - softmax_top)
    softmax_sum = jnp.sum(exponent, axis=-1, keepdims=True)
    probs = (exponent / softmax_sum).astype(bfloat)
    log_total = softmax_top[..., 0] + jnp.log(softmax_sum[..., 0])
    attended = jnp.einsum("hij,jhd->ihd", probs, values, preferred_element_type=single)
    attended = spread(attended.astype(bfloat).reshape(rows, D))
    saved = (normalized, packed, key_value, log_total, attended)
    return hidden + matmul(attended, projection), head_peak, saved


def attention_backward(
    upstream, hidden, norm_gain, qkv, projection, bias_pair, geometry, saved
):
    distance, marks, scale = geometry
    normalized, packed, key_value, log_total, attended = saved
    rows = hidden.shape[0]
    branch_grad = upstream.astype(bfloat)
    projection_grad = matmul(attended.T, branch_grad)
    attended_grad = unspread(matmul(branch_grad, projection.T).astype(bfloat))
    shifted = position_bias(marks, bias_pair)
    causal = distance >= 0
    queries = packed[:, :D].reshape(rows, H, HD)
    keys = key_value[:, :D].reshape(-1, H, HD)
    values = key_value[:, D:].reshape(-1, H, HD)
    grad_heads = attended_grad.reshape(rows, H, HD)
    raw_scores = jnp.einsum("ihd,jhd->hij", queries, keys, preferred_element_type=single) * scale
    probs = jnp.where(causal[None], jnp.exp(raw_scores + shifted - log_total[..., None]), 0.0)
    prob_grad = jnp.einsum("ihd,jhd->hij", grad_heads, values, preferred_element_type=single)
    row_dot = jnp.sum(prob_grad * probs, axis=-1)
    score_grad = (probs * (prob_grad - row_dot[..., None])).astype(bfloat)
    query_grad = jnp.einsum("hij,jhd->ihd", score_grad, keys, preferred_element_type=single) * scale
    query_grad = query_grad.astype(bfloat).reshape(rows, D)
    bias_grad = jnp.einsum("hij,bij->bh", score_grad, marks, preferred_element_type=single)
    key_grad = (
        jnp.einsum("hij,ihd->jhd", score_grad, queries, preferred_element_type=single) * scale
    )
    value_grad = jnp.einsum(
        "hij,ihd->jhd", probs.astype(bfloat), grad_heads, preferred_element_type=single
    )
    pair = jnp.concatenate([key_grad.reshape(-1, D), value_grad.reshape(-1, D)], axis=-1)
    pair_grad = lax.psum_scatter(pair.astype(bfloat), "expert", scatter_dimension=0, tiled=True)
    packed_grad = jnp.concatenate([query_grad, pair_grad], axis=-1)
    qkv_grad = matmul(normalized.T, packed_grad)
    normed_grad = unspread(matmul(packed_grad, qkv.T))
    input_grad, gain_grad = norm_back(hidden, norm_gain, normed_grad)
    return upstream + input_grad, gain_grad, qkv_grad, projection_grad, bias_grad


def exchange(blocks):
    return lax.all_to_all(blocks, "expert", split_axis=0, concat_axis=0, tiled=True)


def plain_shards(
    hidden_in,
    attn_gain,
    qkv_weight,
    out_weight,
    rel_bias,
    bucket_table,
    mlp_gain,
    mlp_up,
    mlp_down,
    router_weight,
    expert_up,
    expert_down,
    routes,
    out_grad,
):
    block_rows = hidden_in.shape[1]
    length = bucket_table.shape[0]
    experts = lax.axis_size("expert")
    groups = lax.axis_size("shard")
    here = lax.axis_index("shard")
    expert_total = EXP_DEV * experts
    capacity = 4 * block_rows // expert_total
    width = expert_down.shape[1]
    scale = 1.0 / math.sqrt(HD)

    small = jnp.concatenate(
        [attn_gain.reshape(-1), mlp_gain.reshape(-1), rel_bias.reshape(-1), router_weight.reshape(-1)]
    )
    small = gather_shard(small)
    part = D // groups
    cuts = [0, 2 * part, 4 * part, 4 * part + 2 * (NB // groups) * H, small.shape[1]]
    gain_attn, gain_mlp, bias_weights, router_full = (
        small[:, cuts[i] : cuts[i + 1]] for i in range(4)
    )
    gain_attn = gain_attn.reshape(groups, 2, part).transpose(1, 0, 2).reshape(2, D).astype(single)
    gain_mlp = gain_mlp.reshape(groups, 2, part).transpose(1, 0, 2).reshape(2, D).astype(single)
    bias_weights = (
        bias_weights.reshape(groups, 2, NB // groups, H).transpose(1, 0, 2, 3).reshape(2, NB, H)
    )
    router_full = router_full.reshape(D, expert_total)

    first = gather_weight(jnp.concatenate([qkv_weight[0], out_weight[0]], axis=1))
    dense_up = gather_weight(mlp_up)
    dense_down = gather_weight(mlp_down)
    second = gather_weight(jnp.concatenate([qkv_weight[1], out_weight[1]], axis=1))
    qkv = (first[:, : 3 * D], second[:, : 3 * D])
    projection = (first[:, 3 * D :], second[:, 3 * D :])

    up_own = jnp.zeros((EXP_DEV, groups, part, width), bfloat)
    for step in range(groups):
        target = (here + step) % groups
        piece = lax.dynamic_slice_in_dim(expert_up, target * width, width, 2)
        if step:
            piece = shard_shift(piece, step)
        up_own = lax.dynamic_update_slice_in_dim(up_own, piece[:, None], (here - step) % groups, 1)
    up_own = up_own.reshape(EXP_DEV, D, width)

    route_rows = gather_shard(routes.reshape(block_rows, 2))
    upstream_all = gather_shard(out_grad.reshape(block_rows, D))
    expert_ids = jnp.arange(expert_total, dtype=jnp.int32)
    flat_routes = route_rows.reshape(groups, -1)
    marks = (flat_routes[:, :, None] == expert_ids).astype(jnp.int32)
    rank = jnp.sum((jnp.cumsum(marks, axis=1) - marks) * marks, axis=2)
    slot_of_route = flat_routes * capacity + rank
    slot_ids = jnp.arange(expert_total * capacity, dtype=jnp.int32)
    slot_marks = (slot_of_route[:, :, None] == slot_ids).astype(bfloat)
    token_marks = jnp.sum(
        slot_marks.reshape(groups, block_rows, 2, -1).astype(single), axis=2
    ).astype(bfloat)

    def dispatch(rows):
        slots = jnp.einsum("gts,gtd->gsd", token_marks, rows, preferred_element_type=single)
        slots = slots.astype(bfloat).reshape(groups, experts, EXP_DEV, capacity, D)
        return exchange(slots.transpose(1, 2, 0, 3, 4)).reshape(
            experts, EXP_DEV, groups * capacity, D
        )

    def collect(blocks):
        back = exchange(blocks.astype(bfloat)).reshape(experts, EXP_DEV, groups, capacity, D)
        return back.transpose(2, 0, 1, 3, 4).reshape(groups, expert_total * capacity, D)

    owner_rows = dispatch(upstream_all)

    own_positions = lax.axis_index("expert") * block_rows + jnp.arange(block_rows, dtype=jnp.int32)
    distance = own_positions[:, None] - jnp.arange(length, dtype=jnp.int32)[None, :]
    bounds = jnp.sum(
        (bucket_table[:, None] < jnp.arange(NB + 1, dtype=jnp.int32)[None, :]).astype(jnp.int32),
        axis=0,
    )
    geometry = (distance, bucket_marks(distance, bounds[:NB], bounds[1:]), scale)

    hidden_zero = hidden_in.reshape(block_rows, D).astype(single)
    mid_first, peak_first, saved_first = attention_forward(
        hidden_zero, gain_attn[0], qkv[0], projection[0], bias_weights[0], geometry
    )
    dense_normed = spread(rms_norm(mid_first, gain_mlp[0]).astype(bfloat))
    pre_act = matmul(dense_normed, dense_up)
    activation = spread(jax.nn.gelu(pre_act).astype(bfloat))
    layer_one = mid_first + matmul(activation, dense_down)
    mid_second, peak_second, saved_second = attention_forward(
        layer_one, gain_attn[1], qkv[1], projection[1], bias_weights[1], geometry
    )

    moe_normed = rms_norm(mid_second, gain_mlp[1]).astype(bfloat)
    normed_all = gather_shard(moe_normed)
    received = dispatch(normed_all)
    router_logits = jnp.einsum("gtd,de->gte", normed_all, router_full, preferred_element_type=single)
    selected = (route_rows[..., None] == expert_ids).astype(single)
    gates_all = jax.nn.softmax(jnp.sum(selected * router_logits[:, :, None, :], axis=-1), axis=-1)
    slot_gates = jnp.sum(
        gates_all.reshape(groups, -1)[:, :, None] * (slot_of_route[:, :, None] == slot_ids), axis=1
    )
    owner_gates = exchange(
        slot_gates.reshape(groups, experts, EXP_DEV, capacity).transpose(1, 2, 0, 3)
    ).reshape(experts, EXP_DEV, groups * capacity)

    expert_pre = jnp.einsum("sjcd,jdf->sjcf", received, up_own, preferred_element_type=single)
    expert_act = jax.nn.gelu(expert_pre).astype(bfloat)
    expert_out = jnp.einsum(
        "sjcf,jfd->sjcd", expert_act, expert_down, preferred_element_type=single
    )
    owner_grad = (owner_gates[..., None] * owner_rows.astype(single)).astype(bfloat)
    act_grad = jnp.einsum("sjcd,jfd->sjcf", owner_grad, expert_down, preferred_element_type=single)
    pre_grad = gelu_back(expert_pre, act_grad).astype(bfloat)
    row_grad = jnp.einsum("sjcf,jdf->sjcd", pre_grad, up_own, preferred_element_type=single)

    returned = collect(expert_out)
    back_rows = collect(row_grad)
    expert_down_grad = jnp.einsum(
        "sjcf,sjcd->jfd", expert_act, owner_grad, preferred_element_type=single
    )
    up_grad = jnp.einsum(
        "sjcd,sjcf->jdf", received, pre_grad, preferred_element_type=single
    ).astype(bfloat)

    route_out = jnp.einsum("grs,gsd->grd", slot_marks, returned, preferred_element_type=single)
    route_out = route_out.reshape(groups, block_rows, 2, D)
    gate_grad = scatter_shard(
        jnp.sum(route_out * upstream_all[:, :, None, :].astype(single), axis=-1), single
    )
    mixed = scatter_shard(jnp.sum(gates_all[..., None] * route_out, axis=2))
    hidden_out = (mid_second + mixed).astype(bfloat).reshape(hidden_in.shape)

    gates = lax.dynamic_index_in_dim(gates_all, here, 0, keepdims=False)
    own_selected = lax.dynamic_index_in_dim(selected, here, 0, keepdims=False)
    upstream = out_grad.reshape(block_rows, D).astype(single)
    chosen_grad = gates * (gate_grad - jnp.sum(gates * gate_grad, axis=-1, keepdims=True))
    logit_grad = jnp.sum(chosen_grad[:, :, None] * own_selected, axis=1).astype(bfloat)
    router_grad = matmul(moe_normed.T, logit_grad)
    row_terms = jnp.einsum("gts,gsd->gtd", token_marks, back_rows, preferred_element_type=single)
    normed_grad = matmul(logit_grad, router_full.T) + scatter_shard(row_terms)
    moe_input_grad, moe_gain_grad = norm_back(mid_second, gain_mlp[1], normed_grad)
    mid_grad = upstream + moe_input_grad

    up_grad = up_grad.reshape(EXP_DEV, groups, part, width)
    expert_up_grad = jnp.zeros((EXP_DEV, part, groups * width), single)
    for step in range(groups):
        piece = lax.dynamic_index_in_dim(up_grad, (here + step) % groups, 1, keepdims=False)
        if step:
            piece = shard_shift(piece, step)
        expert_up_grad = lax.dynamic_update_slice_in_dim(
            expert_up_grad, piece.astype(single), ((here - step) % groups) * width, 2
        )

    layer_grad, gain_second, qkv_second, projection_second, bias_second = attention_backward(
        mid_grad, layer_one, gain_attn[1], qkv[1], projection[1], bias_weights[1], geometry,
        saved_second,
    )
    second_grad = reduce_weight(jnp.concatenate([qkv_second, projection_second], axis=1))
    dense_branch = layer_grad.astype(bfloat)
    mlp_down_grad = reduce_weight(matmul(activation.T, dense_branch))
    hidden_act_grad = unspread(matmul(dense_branch, dense_down.T))
    pre_act_grad = gelu_back(pre_act, hidden_act_grad).astype(bfloat)
    mlp_up_grad = reduce_weight(matmul(dense_normed.T, pre_act_grad))
    dense_normed_grad = unspread(matmul(pre_act_grad, dense_up.T))
    dense_input_grad, dense_gain_grad = norm_back(mid_first, gain_mlp[0], dense_normed_grad)
    first_grad = layer_grad + dense_input_grad
    input_grad, gain_first, qkv_first, projection_first, bias_first = attention_backward(
        first_grad, hidden_zero, gain_attn[0], qkv[0], projection[0], bias_weights[0], geometry,
        saved_first,
    )
    first_weight_grad = reduce_weight(jnp.concatenate([qkv_first, projection_first], axis=1))

    gains = jnp.stack([gain_first, gain_second, dense_gain_grad, moe_gain_grad])
    biases = jnp.stack([bias_first, bias_second])
    small_grad = jnp.concatenate(
        [
            gains.reshape(4, groups, part).transpose(1, 0, 2).reshape(groups, -1),
            biases.reshape(2, groups, NB // groups, H).transpose(1, 0, 2, 3).reshape(groups, -1),
            router_grad.reshape(groups, -1),
        ],
        axis=1,
    )
    small_grad = lax.psum(scatter_shard(small_grad, single), "expert")
    gain_cut = 4 * part
    bias_cut = gain_cut + 2 * (NB // groups) * H
    own_gains = small_grad[:gain_cut].reshape(4, part)
    peaks = lax.pmax(jnp.stack([peak_first, peak_second]), ("expert", "shard"))
    clip_scales = jnp.sqrt(clip_limit / jnp.maximum(peaks, clip_limit))
    return (
        hidden_out,
        input_grad.reshape(hidden_in.shape),
        own_gains[:2],
        jnp.stack([first_weight_grad[:, : 3 * D], second_grad[:, : 3 * D]]),
        jnp.stack([first_weight_grad[:, 3 * D :], second_grad[:, 3 * D :]]),
        small_grad[gain_cut:bias_cut].reshape(2, NB // groups, H),
        own_gains[2:],
        mlp_up_grad,
        mlp_down_grad,
        small_grad[bias_cut:].reshape(part, expert_total),
        expert_up_grad,
        expert_down_grad,
        clip_scales,
    )


MESH = pl.DeviceIdType.MESH
ANY = pl.ANY
VMEM = pltpu.VMEM


def place():
    return lax.axis_index("expert"), lax.axis_index("shard")


def greet(devices):
    barrier = pltpu.get_barrier_semaphore()
    for device in devices:
        pl.semaphore_signal(barrier, inc=1, device_id=device, device_id_type=MESH)
    pl.semaphore_wait(barrier, len(devices))


def push(sent, source, target, send_sem, recv_sem, device):
    copy = pltpu.make_async_remote_copy(
        src_ref=source,
        dst_ref=target,
        send_sem=send_sem,
        recv_sem=recv_sem,
        device_id=device,
        device_id_type=MESH,
    )
    copy.start()
    sent.append(copy)
    return copy


def small_kernel(groups, small_ref, routes_ref, small_out, routes_out, ssem, rsem, lsem):
    e, s = place()
    others = [(e, lax.rem(s + k, groups)) for k in range(1, groups)]
    local = [
        pltpu.make_async_copy(small_ref, small_out.at[s], lsem.at[0]),
        pltpu.make_async_copy(routes_ref, routes_out.at[s], lsem.at[1]),
    ]
    for copy in local:
        copy.start()
    greet(others)
    sent = []
    for k, device in enumerate(others):
        push(sent, small_ref, small_out.at[s], ssem.at[0, k], rsem.at[0, k], device)
        push(sent, routes_ref, routes_out.at[s], ssem.at[1, k], rsem.at[1, k], device)
    for copy in local:
        copy.wait()
    for copy in sent:
        copy.wait()


def gather_small(small, routes):
    groups = lax.axis_size("shard")
    vmem = pl.BlockSpec(memory_space=VMEM)
    return pl.pallas_call(
        functools.partial(small_kernel, groups),
        name="gather_small",
        out_shape=(
            jax.ShapeDtypeStruct((groups,) + small.shape, small.dtype),
            jax.ShapeDtypeStruct((groups,) + routes.shape, routes.dtype),
        ),
        in_specs=[vmem, vmem],
        out_specs=(vmem, vmem),
        scratch_shapes=[
            pltpu.SemaphoreType.DMA((2, groups - 1)),
            pltpu.SemaphoreType.DMA((2, groups - 1)),
            pltpu.SemaphoreType.DMA((2,)),
        ],
        compiler_params=pltpu.CompilerParams(collective_id=1, has_side_effects=True),
    )(small, routes)


def norm_rows(inputs, gain):
    return inputs * lax.rsqrt(jnp.mean(inputs * inputs, axis=-1, keepdims=True) + epsilon) * gain


def dot_rows(left, right):
    return lax.dot_general(left, right, (((1,), (1,)), ((), ())), preferred_element_type=single)


def loop(count, body):
    def step(i, carry):
        body(i)
        return carry

    lax.fori_loop(0, count, step, 0)


def lane_block(i, width):
    return pl.ds(pl.multiple_of(i * width, 128), width)


def row_block(i, height):
    return pl.ds(pl.multiple_of(i * height, height), height)


T = 128
PAIRS = H // 2
TOE = 1152


def forward_kernel(
    hidden_ref,
    gains_ref,
    table_ref,
    qkv_hbm,
    out_hbm,
    up_hbm,
    down_hbm,
    expert_up_hbm,
    cot_hbm,
    normed_out,
    query_out,
    attended_out,
    mid_out,
    dense_normed_out,
    pre_out,
    act_out,
    one_out,
    peak_out,
    normed_all,
    qkv0_out,
    qkv1_out,
    proj0_out,
    proj1_out,
    up_out,
    down_out,
    kv_out,
    probs_out,
    up_own,
    cot_all,
    w_qkv0,
    w_qkv1,
    w_out0,
    w_out1,
    w_up,
    w_down,
    kv,
    probs,
    scores,
    zs,
    zr,
    f1s,
    f1r,
    f2s,
    f2r,
    cs,
    cr,
    locals_sem,
    k1s,
    k1r,
    k2s,
    k2r,
    kcs,
    kcr,
    us,
    ur,
    gs,
    gr,
    ns,
    nr,
    outs_sem,
):
    e, s = place()
    core = lax.rem(e, 2)
    quarter = e // 2
    at_x = e + 2 - 4 * lax.rem(quarter, 2)
    at_y = lax.rem(e + 4, 8)
    at_core = e + 1 - 2 * core
    inward = jnp.where(core == 0, at_x, at_y)
    onward = jnp.where(core == 0, at_y, at_x)
    others = [lax.rem(s + k, 4) for k in range(1, 4)]
    sources = [lax.rem(s + 4 - k, 4) for k in range(1, 4)]
    sent = []
    kept = []

    def local(source, target, sem):
        copy = pltpu.make_async_copy(source, target, sem)
        copy.start()
        return copy

    chunks = [
        (qkv_hbm.at[0], w_qkv0, 48, 1152),
        (out_hbm.at[0], w_out0, 48, 384),
        (up_hbm, w_up, 48, 1536),
        (down_hbm, w_down, 192, 384),
        (qkv_hbm.at[1], w_qkv1, 48, 1152),
        (out_hbm.at[1], w_out1, 48, 384),
    ]

    def block(target, who, position, height, half, width):
        rows = pl.ds(pl.multiple_of(position * 4 * height + who * height, height), height)
        return target.at[rows, lane_block(half, width)]

    stage1, stage2, stage3, stage4, own = {}, {}, {}, {}, {}

    def z_send(c):
        source, target, height, width = chunks[c]
        piece = source.at[row_block(quarter, height), lane_block(core, width)]
        mine = block(target, quarter, s, height, core, width)
        stage1[c] = [
            push(sent, piece, mine, zs.at[c, k], zr.at[c, k], (e, others[k])) for k in range(3)
        ]
        own[c] = local(source, target.at[row_block(s, 4 * height), :], locals_sem.at[c])

    def plane_send(c):
        _, target, height, width = chunks[c]
        stage2[c] = []
        for k in range(3):
            stage1[c][k].wait_recv()
            mine = block(target, quarter, sources[k], height, core, width)
            stage2[c].append(
                [
                    push(sent, mine, mine, f1s.at[c, k, i], f1r.at[c, k, i], (partner, s))
                    for i, partner in enumerate((at_x, at_y))
                ]
            )

    def plane_forward(c):
        _, target, height, width = chunks[c]
        stage3[c] = []
        for k in range(3):
            pltpu.make_async_remote_copy(
                src_ref=block(target, quarter, sources[k], height, core, width),
                dst_ref=block(target, quarter, sources[k], height, core, width),
                send_sem=f1s.at[c, k, core],
                recv_sem=f1r.at[c, k, core],
                device_id=(inward, s),
                device_id_type=MESH,
            ).wait_recv()
            theirs = block(target, inward // 2, sources[k], height, core, width)
            stage3[c].append(
                push(sent, theirs, theirs, f2s.at[c, k], f2r.at[c, k], (onward, s))
            )

    def core_send(c):
        _, target, height, width = chunks[c]
        stage4[c] = []
        for k in range(3):
            pltpu.make_async_remote_copy(
                src_ref=block(target, quarter, sources[k], height, core, width),
                dst_ref=block(target, quarter, sources[k], height, core, width),
                send_sem=f1s.at[c, k, 1 - core],
                recv_sem=f1r.at[c, k, 1 - core],
                device_id=(onward, s),
                device_id_type=MESH,
            ).wait_recv()
            stage3[c][k].wait_recv()
            half = target.at[row_block(sources[k], 4 * height), lane_block(core, width)]
            stage4[c].append(push(sent, half, half, cs.at[c, k], cr.at[c, k], (at_core, s)))

    weight_outs = [qkv0_out, proj0_out, up_out, down_out, qkv1_out, proj1_out]

    def ready(c):
        for k in range(3):
            stage4[c][k].wait_recv()
        own[c].wait()
        kept.append(local(chunks[c][1], weight_outs[c], outs_sem.at[c]))

    greet(
        [(at_core, s), (at_x, s), (at_y, s)] + [(e, other) for other in others]
    )
    z_send(0)
    z_send(1)
    z_send(2)

    def attention(layer, inputs, w_qkv, w_out, work):
        normed = norm_rows(inputs, gains_ref[pl.ds(layer, 1), :]).astype(bfloat)
        normed_out[layer] = normed
        if layer == 0:
            plane_send(0)
            plane_forward(0)
            core_send(0)
            ready(0)
        else:
            ready(4)
        own_rows = row_block(e, T)
        first, second, third = [], [], []
        for part in range(3):
            x = normed_out[layer]
            for i, base in enumerate((D, 2 * D)):
                columns = w_qkv[:, base + 256 * part : base + 256 * (part + 1)]
                kv[layer, part, own_rows, 256 * i : 256 * (i + 1)] = jnp.dot(
                    x, columns, preferred_element_type=single
                ).astype(bfloat)
            mine = kv.at[layer, part, own_rows, :]
            first.append(
                [
                    push(sent, mine, mine, k1s.at[layer, part, i], k1r.at[layer, part, i], (p, s))
                    for i, p in enumerate((at_x, at_y))
                ]
            )
            third.append(
                [
                    push(
                        sent, mine, mine, kcs.at[layer, part, 0], kcr.at[layer, part, 0],
                        (at_core, s),
                    )
                ]
            )
        query_out[layer] = jnp.dot(
            normed_out[layer], w_qkv[:, :D], preferred_element_type=single
        ).astype(bfloat)
        if work:
            work[0]()
        at_diagonal = inward + onward - e
        for part in range(3):
            pltpu.make_async_remote_copy(
                src_ref=kv.at[layer, part, own_rows, :],
                dst_ref=kv.at[layer, part, own_rows, :],
                send_sem=k1s.at[layer, part, core],
                recv_sem=k1r.at[layer, part, core],
                device_id=(inward, s),
                device_id_type=MESH,
            ).wait_recv()
            theirs = kv.at[layer, part, row_block(inward, T), :]
            second.append(
                push(
                    sent, theirs, theirs, k2s.at[layer, part], k2r.at[layer, part], (onward, s)
                )
            )
            third[part].append(
                push(
                    sent, theirs, theirs, kcs.at[layer, part, 1], kcr.at[layer, part, 1],
                    (at_core, s),
                )
            )
        if work:
            work[1]()
        for part in range(3):
            pltpu.make_async_remote_copy(
                src_ref=kv.at[layer, part, own_rows, :],
                dst_ref=kv.at[layer, part, own_rows, :],
                send_sem=k1s.at[layer, part, 1 - core],
                recv_sem=k1r.at[layer, part, 1 - core],
                device_id=(onward, s),
                device_id_type=MESH,
            ).wait_recv()
            theirs = kv.at[layer, part, row_block(onward, T), :]
            third[part].append(
                push(
                    sent, theirs, theirs, kcs.at[layer, part, 2], kcr.at[layer, part, 2],
                    (at_core, s),
                )
            )
            second[part].wait_recv()
            theirs = kv.at[layer, part, row_block(at_diagonal, T), :]
            third[part].append(
                push(
                    sent, theirs, theirs, kcs.at[layer, part, 3], kcr.at[layer, part, 3],
                    (at_core, s),
                )
            )
        for part in range(3):
            for i in range(4):
                third[part][i].wait_recv()

            def one_pair(local_pair):
                pair = 2 * part + local_pair
                lanes = lane_block(pair, 128)
                queries = query_out[layer, :, lanes]
                lane = lax.broadcasted_iota(jnp.int32, (T, 128), 1)
                zero = jnp.zeros_like(queries)
                both = jnp.concatenate(
                    [jnp.where(lane < HD, queries, zero), jnp.where(lane >= HD, queries, zero)]
                )
                keys = kv[layer, part, :, lane_block(local_pair, 128)]
                scores[...] = dot_rows(both, keys) * (1.0 / math.sqrt(HD))
                for half in range(2):
                    head = 2 * pair + half
                    toeplitz = table_ref[pl.ds(layer * H + head, 1), :]
                    peak = jnp.full((1, 1), -jnp.inf, single)
                    for rows in range(0, T, 32):
                        raw = scores[half * T + rows : half * T + rows + 32, :]
                        row = e * T + rows + lax.broadcasted_iota(jnp.int32, raw.shape, 0)
                        causal = row >= lax.broadcasted_iota(jnp.int32, raw.shape, 1)
                        shifted = pltpu.roll(
                            jnp.broadcast_to(toeplitz, (32, TOE)),
                            TOE - (T - 1) + rows,
                            1,
                            stride=1,
                            stride_axis=0,
                        )[:, : raw.shape[1]]
                        peak = jnp.maximum(
                            peak, jnp.max(jnp.where(causal, raw, -jnp.inf), keepdims=True)
                        )
                        masked = jnp.where(causal, raw + shifted, -jnp.inf)
                        top = jnp.max(masked, axis=-1, keepdims=True)
                        exponent = jnp.exp(masked - top)
                        total = jnp.sum(exponent, axis=-1, keepdims=True)
                        probs[layer, pl.ds(pl.multiple_of(head * T + rows, 32), 32), :] = (
                            exponent / total
                        ).astype(bfloat)
                    peak_out[pl.ds(layer * H + head, 1), :] = jnp.broadcast_to(peak, (1, 128))
                values = kv[layer, part, :, pl.ds(pl.multiple_of(256 + local_pair * 128, 128), 128)]
                mixed = jnp.dot(
                    probs[layer, pl.ds(pl.multiple_of(pair * 2 * T, 2 * T), 2 * T), :],
                    values,
                    preferred_element_type=single,
                )
                attended_out[layer, :, lanes] = jnp.where(
                    lane < HD, mixed[:T], mixed[T:]
                ).astype(bfloat)

            loop(2, one_pair)
            if work:
                work[2 + part]()
        kept.append(local(kv.at[layer], kv_out.at[layer], outs_sem.at[6 + layer]))
        kept.append(local(probs.at[layer], probs_out.at[layer], outs_sem.at[8 + layer]))

    def nothing():
        pass

    def work0():
        plane_send(1)
        z_send(3)

    def work1():
        plane_forward(1)

    def work2():
        core_send(1)
        plane_send(2)

    def work3():
        plane_forward(2)
        z_send(4)
        z_send(5)

    def work4():
        core_send(2)
        plane_send(3)

    hidden = hidden_ref[...].astype(single)
    attention(0, hidden, w_qkv0, w_out0, [work0, work1, work2, work3, work4])
    ready(1)
    mid_out[0] = hidden + jnp.dot(
        attended_out[0], w_out0[...], preferred_element_type=single
    )
    dense_normed_out[...] = norm_rows(mid_out[0], gains_ref[pl.ds(2, 1), :]).astype(bfloat)
    reshard = []
    for k in range(3):
        reshard.append(
            push(
                sent,
                expert_up_hbm.at[:, :, lane_block(others[k], 768)],
                up_own.at[:, row_block(s, 192), :],
                us.at[k],
                ur.at[k],
                (e, others[k]),
            )
        )
        reshard.append(
            push(sent, cot_hbm, cot_all.at[s], gs.at[k], gr.at[k], (e, others[k]))
        )
    kept.append(
        local(
            expert_up_hbm.at[:, :, lane_block(s, 768)],
            up_own.at[:, row_block(s, 192), :],
            us.at[3],
        )
    )
    kept.append(local(cot_hbm, cot_all.at[s], gs.at[3]))
    ready(2)

    def up_part(i):
        lanes = lane_block(i, 512)
        before = jnp.dot(dense_normed_out[...], w_up[:, lanes], preferred_element_type=single)
        pre_out[:, lanes] = before
        act_out[:, lanes] = jax.nn.gelu(before).astype(bfloat)

    plane_forward(3)
    loop(3, up_part)
    core_send(3)
    plane_send(4)
    plane_send(5)

    def up_later(i):
        up_part(i + 3)

    loop(3, up_later)
    plane_forward(4)
    plane_forward(5)
    ready(3)
    one_out[...] = mid_out[0]

    def down_part(i):
        rows = row_block(i, 768)
        one_out[...] += jnp.dot(
            act_out[:, lane_block(i, 768)], w_down[rows, :], preferred_element_type=single
        )

    loop(4, down_part)
    core_send(4)
    core_send(5)
    attention(1, one_out[...], w_qkv1, w_out1, None)
    ready(5)
    mid_out[1] = one_out[...] + jnp.dot(
        attended_out[1], w_out1[...], preferred_element_type=single
    )
    normed_all[s] = norm_rows(mid_out[1], gains_ref[pl.ds(3, 1), :]).astype(bfloat)
    last = [
        push(sent, normed_all.at[s], normed_all.at[s], ns.at[k], nr.at[k], (e, others[k]))
        for k in range(3)
    ]
    for copy in last + reshard:
        copy.wait_recv()
    for copy in kept:
        copy.wait()
    for copy in sent:
        copy.wait_send()


def forward(hidden, gains, table, qkv, out, up, down, expert_up, cotangent):
    length = T * lax.axis_size("expert")
    vmem = pl.BlockSpec(memory_space=VMEM)
    anywhere = pl.BlockSpec(memory_space=ANY)
    shape = jax.ShapeDtypeStruct
    ff = up.shape[1]
    sem = pltpu.SemaphoreType.DMA
    return pl.pallas_call(
        forward_kernel,
        name="forward_layers",
        out_shape=(
            shape((2, T, D), bfloat),
            shape((2, T, D), bfloat),
            shape((2, T, D), bfloat),
            shape((2, T, D), single),
            shape((T, D), bfloat),
            shape((T, ff), single),
            shape((T, ff), bfloat),
            shape((T, D), single),
            shape((2 * H, 128), single),
            shape((4, T, D), bfloat),
            shape((D, 3 * D), bfloat),
            shape((D, 3 * D), bfloat),
            shape((D, D), bfloat),
            shape((D, D), bfloat),
            shape((D, ff), bfloat),
            shape((ff, D), bfloat),
            shape((2, 3, length, 512), bfloat),
            shape((2, H * T, length), bfloat),
            shape((EXP_DEV, D, 768), bfloat),
            shape((4, T, D), bfloat),
        ),
        in_specs=[vmem] * 3 + [anywhere] * 6,
        out_specs=(vmem,) * 10 + (anywhere,) * 10,
        scratch_shapes=[
            VMEM((D, 3 * D), bfloat),
            VMEM((D, 3 * D), bfloat),
            VMEM((D, D), bfloat),
            VMEM((D, D), bfloat),
            VMEM((D, ff), bfloat),
            VMEM((ff, D), bfloat),
            VMEM((2, 3, length, 512), bfloat),
            VMEM((2, H * T, length), bfloat),
            VMEM((2 * T, length), single),
            sem((6, 3)), sem((6, 3)),
            sem((6, 3, 2)), sem((6, 3, 2)),
            sem((6, 3)), sem((6, 3)),
            sem((6, 3)), sem((6, 3)),
            sem((6,)),
            sem((2, 3, 2)), sem((2, 3, 2)),
            sem((2, 3)), sem((2, 3)),
            sem((2, 3, 4)), sem((2, 3, 4)),
            sem((4,)), sem((3,)),
            sem((4,)), sem((3,)),
            sem((3,)), sem((3,)),
            sem((10,)),
        ],
        compiler_params=pltpu.CompilerParams(
            collective_id=2, has_side_effects=True, vmem_limit_bytes=56 * 2**20
        ),
    )(hidden, gains, table, qkv, out, up, down, expert_up, cotangent)


class Plane:
    def __init__(self):
        self.e, self.s = place()
        e = self.e
        self.core = lax.rem(e, 2)
        self.quarter = e // 2
        self.at_x = e + 2 - 4 * lax.rem(self.quarter, 2)
        self.at_y = lax.rem(e + 4, 8)
        self.at_core = e + 1 - 2 * self.core
        self.inward = jnp.where(self.core == 0, self.at_x, self.at_y)
        self.onward = jnp.where(self.core == 0, self.at_y, self.at_x)
        self.diagonal = self.inward + self.onward - e
        self.others = [lax.rem(self.s + k, 4) for k in range(1, 4)]
        self.around = [lax.rem(e + k, 8) for k in range(1, 8)]
        self.sent = []

    def push(self, source, target, send_sem, recv_sem, device):
        return push(self.sent, source, target, send_sem, recv_sem, device)

    def arrived(self, view, recv_sem):
        pltpu.make_async_remote_copy(
            src_ref=view,
            dst_ref=view,
            send_sem=recv_sem,
            recv_sem=recv_sem,
            device_id=(self.at_core, self.s),
            device_id_type=MESH,
        ).wait_recv()


class PlaneGather:
    def __init__(self, plane, view, send_sems, recv_sems):
        self.plane, self.view, self.ss, self.rs = plane, view, send_sems, recv_sems

    def _push(self, who, i, target):
        p = self.plane
        block = self.view(who)
        p.push(block, block, self.ss.at[i], self.rs.at[i], (target, p.s))

    def first(self):
        p = self.plane
        self._push(p.e, 0, p.at_x)
        self._push(p.e, 1, p.at_y)
        self._push(p.e, 3, p.at_core)

    def second(self):
        p = self.plane
        p.arrived(self.view(p.inward), self.rs.at[p.core])
        self._push(p.inward, 2, p.onward)
        self._push(p.inward, 4, p.at_core)

    def third(self):
        p = self.plane
        p.arrived(self.view(p.onward), self.rs.at[1 - p.core])
        self._push(p.onward, 5, p.at_core)
        p.arrived(self.view(p.diagonal), self.rs.at[2])
        self._push(p.diagonal, 6, p.at_core)

    def done(self):
        for i in range(3, 7):
            self.plane.arrived(self.view(self.plane.e), self.rs.at[i])


class SmallReduce:
    def __init__(self, plane, value, z_in, plane_in, op, sems):
        self.plane, self.value, self.z_in, self.plane_in = plane, value, z_in, plane_in
        self.op, self.sems = op, sems

    def start(self):
        p = self.plane
        zs, zr, _, _ = self.sems
        for k in range(3):
            p.push(self.value, self.z_in.at[k], zs.at[k], zr.at[k], (p.e, p.others[k]))

    def middle(self, middle):
        p = self.plane
        zs, zr, ps, pr = self.sems
        total = self.value[...]
        for k in range(3):
            p.arrived(self.z_in.at[k], zr.at[k])
            total = self.op(total, self.z_in[k])
        middle[...] = total
        for k in range(7):
            p.push(middle, self.plane_in.at[k], ps.at[k], pr.at[k], (p.around[k], p.s))

    def finish(self, middle, result):
        p = self.plane
        total = middle[...]
        for k in range(7):
            p.arrived(self.plane_in.at[k], self.sems[3].at[k])
            total = self.op(total, self.plane_in[k])
        result[...] = total


def norm_pull(inputs, gain, upstream):
    inverse = lax.rsqrt(jnp.mean(inputs * inputs, axis=-1, keepdims=True) + epsilon)
    scaled = upstream * gain
    inner = jnp.mean(scaled * inputs, axis=-1, keepdims=True)
    gain_grad = jnp.sum(upstream * inputs * inverse, axis=0, keepdims=True)
    return inverse * scaled - inputs * (inverse * inverse * inverse * inner), gain_grad


def gelu_slope(value):
    root = math.sqrt(2.0 / math.pi)
    squared = value * value
    bend = jnp.tanh(root * value * (1.0 + 0.044715 * squared))
    return 0.5 * (1.0 + bend) + 0.5 * value * (1.0 - bend * bend) * root * (
        1.0 + 3 * 0.044715 * squared
    )


def dot_columns(left, right):
    return lax.dot_general(left, right, (((0,), (0,)), ((), ())), preferred_element_type=single)


def backward_kernel(
    mid_grad_ref,
    one_ref,
    hidden_ref,
    mid_ref,
    gains_ref,
    query_ref,
    pre_ref,
    marks_ref,
    small_ref,
    peak_ref,
    normed_hbm,
    attended_hbm,
    dense_normed_hbm,
    act_hbm,
    qkv0_hbm,
    qkv1_hbm,
    proj0_hbm,
    proj1_hbm,
    up_hbm,
    down_hbm,
    kv_hbm,
    probs_hbm,
    up_grad_hbm,
    hidden_grad_out,
    att_out,
    up_out,
    down_out,
    small_out,
    late_out,
    peak_out,
    expert_up_out,
    w_wide,
    w_down,
    kv,
    probs,
    xg,
    gx,
    gsrc,
    zb,
    zin,
    zb_down,
    zin_down,
    slopes,
    score_low,
    dk,
    cin,
    rin,
    attended_grad,
    layer_grad,
    biases,
    early,
    early_z,
    early_p,
    early_m,
    late,
    late_z,
    late_p,
    late_m,
    peak_z,
    peak_p,
    peak_m,
    gs,
    gr,
    xs,
    xr,
    zs,
    zr,
    dcs,
    dcr,
    drs,
    drr,
    szs,
    szr,
    sps,
    spr,
    us,
    ur,
    loads,
):
    p = Plane()
    e, s, core = p.e, p.s, p.core
    own_rows = row_block(e, T)

    def load(source, target, i):
        copy = pltpu.make_async_copy(source, target, loads.at[i])
        copy.start()
        return copy

    own_parts = [
        load(source, xg.at[n, own_rows, :], 11 + n)
        for n, source in enumerate(
            (
                normed_hbm.at[1],
                attended_hbm.at[1],
                normed_hbm.at[0],
                attended_hbm.at[0],
                dense_normed_hbm,
            )
        )
    ]
    own_act = load(act_hbm.at[:, lane_block(e, 384)], gx.at[3, own_rows, :], 16)
    greet([(d, s) for d in p.around] + [(e, other) for other in p.others])

    w_qkv = w_wide.at[:, : 3 * D]
    w_out = w_wide.at[:, 3 * D :]
    got_out = load(proj1_hbm, w_out, 0)
    got_kv = load(kv_hbm.at[1], kv, 2)
    got_probs = load(probs_hbm.at[1], probs, 3)
    got_qkv = load(qkv1_hbm, w_qkv, 1)
    got_down = load(down_hbm, w_down, 5)

    peaks = SmallReduce(
        p, peak_ref, peak_z, peak_p, jnp.maximum, (szs.at[0], szr.at[0], sps.at[0], spr.at[0])
    )
    peaks.start()

    def rows_gather(n):
        return PlaneGather(
            p, lambda who: xg.at[n, row_block(who, T), :], gs.at[n], gr.at[n]
        )

    gathers = [rows_gather(n) for n in range(6)]
    for copy in own_parts:
        copy.wait()
    gathers[0].first()
    gathers[1].first()

    exchanges = {}

    def exchange_start(j, source):
        if j == 3:
            own_act.wait()
        else:
            gx[j, own_rows, :] = source[:, lane_block(e, 384)]
        for k, d in enumerate(p.around):
            p.push(
                source.at[:, lane_block(d, 384)],
                gx.at[j, own_rows, :],
                xs.at[j, k],
                xr.at[j, k],
                (d, s),
            )

    def exchange_wait(j):
        for k in range(7):
            p.arrived(gx.at[j, own_rows, :], xr.at[j, k])

    def out_gather(j, target, height):
        return PlaneGather(
            p, lambda who: target.at[pl.ds(who, 1)], gs.at[6 + j], gr.at[6 + j]
        )

    def z_start(j, tile, received, height):
        for k in range(3):
            p.push(
                tile.at[row_block(p.others[k], height), :],
                received.at[k],
                zs.at[j, k],
                zr.at[j, k],
                (e, p.others[k]),
            )

    def z_finish(j, tile, received, height, target):
        total = tile[row_block(s, height), :].astype(single)
        for k in range(3):
            p.arrived(received.at[k], zr.at[j, k])
            total = total + received[k].astype(single)
        target[pl.ds(e, 1)] = total.astype(bfloat)[None]

    def tile_attention(layer):
        j = 1 - layer
        exchange_wait(j)
        rows = xg[2 * j + e // 6]
        for part in range(3):
            lanes = slice(128 * part, 128 * (part + 1))
            zb[j, :, lanes] = dot_columns(rows, gx[j, :, lanes]).astype(bfloat)
        z_start(j, zb.at[j], zin.at[j], 192)

    def tile_up():
        exchange_wait(2)
        for part in range(3):
            lanes = slice(128 * part, 128 * (part + 1))
            zb[2, :, lanes] = dot_columns(xg[4], gx[2, :, lanes]).astype(bfloat)
        z_start(2, zb.at[2], zin.at[2], 192)

    def tile_down():
        exchange_wait(3)
        for part in range(3):
            lanes = slice(128 * part, 128 * (part + 1))
            zb_down[lanes, :] = dot_columns(gx[3, :, lanes], xg[5]).astype(bfloat)
        z_start(3, zb_down, zin_down, 96)

    gather_att1 = out_gather(0, att_out.at[1], 192)
    gather_att0 = out_gather(1, att_out.at[0], 192)
    gather_up = out_gather(2, up_out, 192)
    gather_down = out_gather(3, down_out, 96)

    scale = 1.0 / math.sqrt(HD)

    def attention(layer, upstream, work):
        j = 1 - layer
        grads = gsrc.at[j]
        branch = upstream.astype(bfloat)
        grads[:, 3 * D :] = branch
        got_out_now = got_out if layer == 1 else reloads["out"]
        got_out_now.wait()
        attended_grad[...] = dot_rows(branch, w_out[...]).astype(bfloat)
        if layer == 1:
            got_kv.wait()
            got_probs.wait()
        else:
            reloads["kv"].wait()
            reloads["probs"].wait()
            for copy in dk_sent:
                copy.wait_send()
            dk_sent.clear()

        def first_step(part):
            push(
                dk_sent,
                dk.at[part, 1 - core],
                cin.at[layer, part],
                dcs.at[layer, part],
                dcr.at[layer, part],
                (p.at_core, s),
            )

        def second_step(part):
            p.arrived(cin.at[layer, part], dcr.at[layer, part])
            for q in range(4):
                dk[part, core, q] = (
                    dk[part, core, q].astype(single) + cin[layer, part, q].astype(single)
                ).astype(bfloat)
            for k, d in enumerate((p.at_x, p.at_y, p.diagonal)):
                push(
                    dk_sent,
                    dk.at[part, core, d // 2],
                    rin.at[layer, part, k],
                    drs.at[layer, part, k],
                    drr.at[layer, part, k],
                    (d, s),
                )

        def third_step(part):
            total = dk[part, core, p.quarter].astype(single)
            for k in range(3):
                p.arrived(rin.at[layer, part, k], drr.at[layer, part, k])
                total = total + rin[layer, part, k].astype(single)
            turned = total.T.astype(bfloat)
            grads[:, D + 256 * part : D + 256 * (part + 1)] = turned[:, :256]
            grads[:, 2 * D + 256 * part : 2 * D + 256 * (part + 1)] = turned[:, 256:]

        for part in range(3):

            def one_pair(local_pair):
                pair = 2 * part + local_pair
                lanes = lane_block(pair, 128)
                lane = lax.broadcasted_iota(jnp.int32, (T, 128), 1)

                def split(value):
                    zero = jnp.zeros_like(value)
                    return jnp.concatenate(
                        [jnp.where(lane < HD, value, zero), jnp.where(lane >= HD, value, zero)]
                    )

                queries = split(query_ref[layer, :, lanes])
                outputs = split(attended_grad[:, lanes])
                keys = kv[part, :, lane_block(local_pair, 128)]
                values = kv[part, :, pl.ds(pl.multiple_of(256 + local_pair * 128, 128), 128)]
                slopes[...] = dot_rows(outputs, values)
                pair_rows = pl.ds(pl.multiple_of(pair * 2 * T, 2 * T), 2 * T)
                for half in range(2):
                    head = 2 * pair + half
                    gathered = jnp.zeros((8, TOE), single)
                    for rows in range(0, T, 32):
                        at = half * T + rows
                        prob = probs[
                            pl.ds(pl.multiple_of(head * T + rows, 32), 32), :
                        ].astype(single)
                        slope = slopes[at : at + 32, :]
                        inner = jnp.sum(prob * slope, axis=-1, keepdims=True)
                        low = (prob * (slope - inner)).astype(bfloat)
                        score_low[at : at + 32, :] = low
                        fold = jnp.concatenate(
                            [low.astype(single), jnp.zeros((32, TOE - low.shape[1]), single)],
                            axis=1,
                        )
                        fold = pltpu.roll(fold[:16], 16, 1) + fold[16:]
                        fold = pltpu.roll(fold[:8], 8, 1) + fold[8:]
                        if rows < T - 32:
                            fold = pltpu.roll(fold, T - 32 - rows, 1)
                        gathered = gathered + fold
                    fold = pltpu.roll(gathered[:4], 4, 1) + gathered[4:]
                    fold = pltpu.roll(fold[:2], 2, 1) + fold[2:]
                    fold = pltpu.roll(fold[:1], 1, 1) + fold[1:]
                    biases[pl.ds(layer * H + head, 1), :] = fold
                mixed = jnp.dot(score_low[...], keys, preferred_element_type=single) * scale
                grads[:, lanes] = jnp.where(lane < HD, mixed[:T], mixed[T:]).astype(bfloat)
                key_grad = dot_columns(queries, score_low[...]) * scale
                value_grad = dot_columns(outputs, probs[pair_rows, :])
                for d in range(8):
                    columns = slice(128 * d, 128 * (d + 1))
                    dk[
                        part, d % 2, d // 2, pl.ds(pl.multiple_of(local_pair * 128, 128), 128), :
                    ] = key_grad[:, columns].astype(bfloat)
                    dk[
                        part,
                        d % 2,
                        d // 2,
                        pl.ds(pl.multiple_of(256 + local_pair * 128, 128), 128),
                        :,
                    ] = value_grad[:, columns].astype(bfloat)

            loop(2, one_pair)
            first_step(part)
            if part > 0:
                second_step(part - 1)
            work[part]()
        second_step(2)
        third_step(0)
        work[3]()
        third_step(1)
        third_step(2)
        exchange_start(j, gsrc.at[j])
        if layer == 1:
            got_qkv.wait()
        else:
            reloads["qkv"].wait()
        return dot_rows(gsrc[j, :, : 3 * D], w_qkv[...])

    dk_sent = []
    reloads = {}

    def part0():
        gathers[0].second()
        gathers[1].second()
        exchange_start(3, act_hbm)
        gathers[4].first()
        for k in range(3):
            reshard.append(
                p.push(
                    up_grad_hbm.at[:, row_block(p.others[k], 192), :],
                    expert_up_out.at[:, :, lane_block(s, 768)],
                    us.at[k],
                    ur.at[k],
                    (e, p.others[k]),
                )
            )
        reshard_own.append(
            load(
                up_grad_hbm.at[:, row_block(s, 192), :],
                expert_up_out.at[:, :, lane_block(s, 768)],
                6,
            )
        )

    def part1():
        gathers[0].third()
        gathers[1].third()
        peaks.middle(peak_m)

    def part2():
        gathers[4].second()
        gathers[2].first()
        gathers[3].first()

    def part3():
        gathers[4].third()
        peaks.finish(peak_m, peak_out)

    reshard, reshard_own = [], []
    mid_grad = mid_grad_ref[...]
    normed_grad = attention(1, mid_grad, [part0, part1, part2, part3])
    reloads["kv"] = load(kv_hbm.at[0], kv, 7)
    reloads["probs"] = load(probs_hbm.at[0], probs, 8)
    got_up = load(up_hbm, w_wide, 4)
    input_grad, gain_grad = norm_pull(one_ref[...], gains_ref[1:2, :], normed_grad)
    early[...] = small_ref[...]
    early[17:18, :] = gain_grad
    layer_grad[...] = mid_grad + input_grad
    branch = layer_grad[...].astype(bfloat)
    xg[5, own_rows, :] = branch
    gathers[5].first()
    got_down.wait()

    def slope_part(i):
        lanes = lane_block(i, 512)
        act_grad = dot_rows(xg[5, own_rows, :], w_down[row_block(i, 512), :])
        gsrc[2, :, lanes] = (act_grad * gelu_slope(pre_ref[:, lanes])).astype(bfloat)

    loop(6, slope_part)
    exchange_start(2, gsrc.at[2])
    gathers[2].second()
    gathers[3].second()
    gathers[5].second()
    got_up.wait()
    dense_grad = dot_rows(gsrc[2], w_wide[...])
    reloads["out"] = load(proj0_hbm, w_out, 9)
    reloads["qkv"] = load(qkv0_hbm, w_qkv, 10)
    input_grad, gain_grad = norm_pull(mid_ref[...], gains_ref[2:3, :], dense_grad)
    early[18:19, :] = gain_grad
    layer_grad[...] = layer_grad[...] + input_grad
    small = SmallReduce(
        p, early, early_z, early_p, jnp.add, (szs.at[1], szr.at[1], sps.at[1], spr.at[1])
    )
    small.start()
    gathers[0].done()
    gathers[1].done()
    tile_attention(1)

    def part4():
        gathers[5].third()
        gathers[2].third()
        gathers[3].third()
        gathers[4].done()
        tile_up()

    def part5():
        gathers[5].done()
        tile_down()
        z_finish(0, zb.at[0], zin.at[0], 192, att_out.at[1])
        gather_att1.first()
        small.middle(early_m)

    def part6():
        z_finish(2, zb.at[2], zin.at[2], 192, up_out)
        gather_up.first()
        gather_att1.second()

    def part7():
        z_finish(3, zb_down, zin_down, 96, down_out)
        gather_down.first()
        gather_up.second()
        gather_att1.third()

    normed_grad = attention(0, layer_grad[...], [part4, part5, part6, part7])
    input_grad, gain_grad = norm_pull(
        hidden_ref[...].astype(single), gains_ref[0:1, :], normed_grad
    )
    hidden_grad_out[...] = layer_grad[...] + input_grad
    late[...] = jnp.zeros_like(late)
    for i in range(6):
        late[i : i + 1, :] = gain_grad[:, 128 * i : 128 * (i + 1)]
    late[8:32, :NB] = lax.dot_general(
        biases[...],
        marks_ref[...].astype(single),
        (((1,), (1,)), ((), ())),
        precision=lax.Precision.HIGHEST,
        preferred_element_type=single,
    )
    tail = SmallReduce(
        p, late, late_z, late_p, jnp.add, (szs.at[2], szr.at[2], sps.at[2], spr.at[2])
    )
    tail.start()
    gathers[2].done()
    gathers[3].done()
    tile_attention(0)
    gather_down.second()
    gather_up.third()
    small.finish(early_m, small_out)
    gather_down.third()
    tail.middle(late_m)
    z_finish(1, zb.at[1], zin.at[1], 192, att_out.at[0])
    gather_att0.first()
    gather_att1.done()
    gather_up.done()
    gather_down.done()
    gather_att0.second()
    gather_att0.third()
    tail.finish(late_m, late_out)
    for copy in reshard:
        copy.wait_recv()
    reshard_own[0].wait()
    gather_att0.done()
    for copy in p.sent + dk_sent:
        copy.wait_send()


def backward(
    mid_grad, layer_one, hidden, mid, gains, normed, queries, attended, dense_normed, act, pre_act,
    marks, small, peak_rows, weights, kv, probs, up_grad,
):
    length = T * lax.axis_size("expert")
    vmem = pl.BlockSpec(memory_space=VMEM)
    anywhere = pl.BlockSpec(memory_space=ANY)
    shape = jax.ShapeDtypeStruct
    ff = pre_act.shape[1]
    sem = pltpu.SemaphoreType.DMA
    peak_shape, early_shape, late_shape = (2 * H, 128), small.shape, (32, 128)
    return pl.pallas_call(
        backward_kernel,
        name="backward_layers",
        out_shape=(
            shape((T, D), single),
            shape((2, 8, 192, 384), bfloat),
            shape((8, 192, 384), bfloat),
            shape((8, 96, D), bfloat),
            shape(early_shape, single),
            shape(late_shape, single),
            shape(peak_shape, single),
            shape((EXP_DEV, 192, ff), bfloat),
        ),
        in_specs=[vmem] * 10 + [anywhere] * 13,
        out_specs=(vmem,) * 7 + (anywhere,),
        scratch_shapes=[
            VMEM((D, ff), bfloat),
            VMEM((ff, D), bfloat),
            VMEM((3, length, 512), bfloat),
            VMEM((H * T, length), bfloat),
            VMEM((6, length, D), bfloat),
            VMEM((4, length, 384), bfloat),
            VMEM((3, T, 4 * D), bfloat),
            VMEM((3, D, 384), bfloat),
            VMEM((3, 3, 192, 384), bfloat),
            VMEM((384, D), bfloat),
            VMEM((3, 96, D), bfloat),
            VMEM((2 * T, length), single),
            VMEM((2 * T, length), bfloat),
            VMEM((3, 2, 4, 512, 128), bfloat),
            VMEM((2, 3, 4, 512, 128), bfloat),
            VMEM((2, 3, 3, 512, 128), bfloat),
            VMEM((T, D), bfloat),
            VMEM((T, D), single),
            VMEM((2 * H, TOE), single),
            VMEM(early_shape, single),
            VMEM((3,) + early_shape, single),
            VMEM((7,) + early_shape, single),
            VMEM(early_shape, single),
            VMEM(late_shape, single),
            VMEM((3,) + late_shape, single),
            VMEM((7,) + late_shape, single),
            VMEM(late_shape, single),
            VMEM((3,) + peak_shape, single),
            VMEM((7,) + peak_shape, single),
            VMEM(peak_shape, single),
            sem((10, 7)), sem((10, 7)),
            sem((4, 7)), sem((4, 7)),
            sem((4, 3)), sem((4, 3)),
            sem((2, 3)), sem((2, 3)),
            sem((2, 3, 3)), sem((2, 3, 3)),
            sem((3, 3)), sem((3, 3)),
            sem((3, 7)), sem((3, 7)),
            sem((3,)), sem((3,)),
            sem((17,)),
        ],
        compiler_params=pltpu.CompilerParams(
            collective_id=3, has_side_effects=True, vmem_limit_bytes=60 * 2**20
        ),
    )(
        mid_grad, layer_one, hidden, mid, gains, queries, pre_act, marks, small, peak_rows, normed,
        attended, dense_normed, act, *weights, kv, probs, up_grad,
    )


def shards(
    hidden_in,
    attn_gain,
    qkv_weight,
    out_weight,
    rel_bias,
    bucket_table,
    mlp_gain,
    mlp_up,
    mlp_down,
    router_weight,
    expert_up,
    expert_down,
    routes,
    out_grad,
):
    block_rows = hidden_in.shape[1]
    length = bucket_table.shape[0]
    experts = lax.axis_size("expert")
    groups = lax.axis_size("shard")
    here = lax.axis_index("shard")
    expert_total = EXP_DEV * experts
    capacity = 4 * block_rows // expert_total
    width = expert_down.shape[1]

    small = jnp.concatenate(
        [attn_gain.reshape(-1), mlp_gain.reshape(-1), rel_bias.reshape(-1), router_weight.reshape(-1)]
    ).astype(single)
    part = D // groups
    used = small.shape[0]
    small = jnp.pad(small, (0, -used % 1024)).reshape(-1, 128)
    small, route_rows = gather_small(small, routes.reshape(-1, 128))
    small = small.reshape(groups, -1)
    route_rows = route_rows.reshape(groups, block_rows, 2)
    cuts = [0, 4 * part, 4 * part + 2 * (NB // groups) * H, used]
    gains, bias_weights, router_full = (small[:, cuts[i] : cuts[i + 1]] for i in range(3))
    gains = gains.reshape(groups, 4, part).transpose(1, 0, 2).reshape(4, D)
    gain_mlp = gains[2:]
    bias_weights = (
        bias_weights.reshape(groups, 2, NB // groups, H).transpose(1, 0, 2, 3).reshape(2, NB, H)
    )
    router_full = router_full.reshape(D, expert_total).astype(bfloat)

    distances = lax.axis_index("expert") * block_rows + block_rows - 1 - jnp.arange(TOE)
    buckets = jnp.take(bucket_table, jnp.clip(distances, 0, length - 1))
    toeplitz_marks = (buckets[None] == jnp.arange(NB, dtype=jnp.int32)[:, None]).astype(bfloat)
    table = jnp.einsum(
        "lbh,bm->lhm", bias_weights.astype(bfloat), toeplitz_marks, preferred_element_type=single
    ).reshape(2 * H, TOE)

    (
        normed, queries, attended, mid, dense_normed, pre_act, activation, layer_one, peak_rows,
        normed_all, qkv0, qkv1, projection0, projection1, dense_up, dense_down, kv, probs, up_own,
        upstream_all,
    ) = forward(
        hidden_in.reshape(block_rows, D), gains, table, qkv_weight, out_weight, mlp_up, mlp_down,
        expert_up, out_grad.reshape(block_rows, D),
    )
    mid_second = mid[1]
    moe_normed = lax.dynamic_index_in_dim(normed_all, here, 0, keepdims=False)
    expert_ids = jnp.arange(expert_total, dtype=jnp.int32)
    flat_routes = route_rows.reshape(groups, -1)
    marks = (flat_routes[:, :, None] == expert_ids).astype(jnp.int32)
    rank = jnp.sum((jnp.cumsum(marks, axis=1) - marks) * marks, axis=2)
    slot_of_route = flat_routes * capacity + rank
    slot_ids = jnp.arange(expert_total * capacity, dtype=jnp.int32)
    slot_marks = (slot_of_route[:, :, None] == slot_ids).astype(bfloat)
    token_marks = jnp.sum(
        slot_marks.reshape(groups, block_rows, 2, -1).astype(single), axis=2
    ).astype(bfloat)

    def dispatch(rows):
        slots = jnp.einsum("gts,gtd->gsd", token_marks, rows, preferred_element_type=single)
        slots = slots.astype(bfloat).reshape(groups, experts, EXP_DEV, capacity, D)
        return exchange(slots.transpose(1, 2, 0, 3, 4)).reshape(
            experts, EXP_DEV, groups * capacity, D
        )

    def collect(blocks):
        back = exchange(blocks.astype(bfloat)).reshape(experts, EXP_DEV, groups, capacity, D)
        return back.transpose(2, 0, 1, 3, 4).reshape(groups, expert_total * capacity, D)

    owner_rows = dispatch(upstream_all)
    received = dispatch(normed_all)
    router_logits = jnp.einsum("gtd,de->gte", normed_all, router_full, preferred_element_type=single)
    selected = (route_rows[..., None] == expert_ids).astype(single)
    gates_all = jax.nn.softmax(jnp.sum(selected * router_logits[:, :, None, :], axis=-1), axis=-1)
    slot_gates = jnp.sum(
        gates_all.reshape(groups, -1)[:, :, None] * (slot_of_route[:, :, None] == slot_ids), axis=1
    )
    owner_gates = exchange(
        slot_gates.reshape(groups, experts, EXP_DEV, capacity).transpose(1, 2, 0, 3)
    ).reshape(experts, EXP_DEV, groups * capacity)

    expert_pre = jnp.einsum("sjcd,jdf->sjcf", received, up_own, preferred_element_type=single)
    expert_act = jax.nn.gelu(expert_pre).astype(bfloat)
    expert_out = jnp.einsum(
        "sjcf,jfd->sjcd", expert_act, expert_down, preferred_element_type=single
    )
    owner_grad = (owner_gates[..., None] * owner_rows.astype(single)).astype(bfloat)
    act_grad = jnp.einsum("sjcd,jfd->sjcf", owner_grad, expert_down, preferred_element_type=single)
    pre_grad = gelu_back(expert_pre, act_grad).astype(bfloat)
    row_grad = jnp.einsum("sjcf,jdf->sjcd", pre_grad, up_own, preferred_element_type=single)

    returned = collect(expert_out)
    back_rows = collect(row_grad)
    expert_down_grad = jnp.einsum(
        "sjcf,sjcd->jfd", expert_act, owner_grad, preferred_element_type=single
    )
    up_grad = jnp.einsum(
        "sjcd,sjcf->jdf", received, pre_grad, preferred_element_type=single
    ).astype(bfloat)

    route_out = jnp.einsum("grs,gsd->grd", slot_marks, returned, preferred_element_type=single)
    route_out = route_out.reshape(groups, block_rows, 2, D)
    gate_grad = scatter_shard(
        jnp.sum(route_out * upstream_all[:, :, None, :].astype(single), axis=-1), single
    )
    mixed = scatter_shard(jnp.sum(gates_all[..., None] * route_out, axis=2))
    hidden_out = (mid_second + mixed).astype(bfloat).reshape(hidden_in.shape)

    gates = lax.dynamic_index_in_dim(gates_all, here, 0, keepdims=False)
    own_selected = lax.dynamic_index_in_dim(selected, here, 0, keepdims=False)
    upstream = out_grad.reshape(block_rows, D).astype(single)
    chosen_grad = gates * (gate_grad - jnp.sum(gates * gate_grad, axis=-1, keepdims=True))
    logit_grad = jnp.sum(chosen_grad[:, :, None] * own_selected, axis=1).astype(bfloat)
    router_grad = matmul(moe_normed.T, logit_grad)
    row_terms = jnp.einsum("gts,gsd->gtd", token_marks, back_rows, preferred_element_type=single)
    normed_grad = matmul(logit_grad, router_full.T) + scatter_shard(row_terms)
    moe_input_grad, moe_gain_grad = norm_back(mid_second, gain_mlp[1], normed_grad)
    mid_grad = upstream + moe_input_grad

    small_in = jnp.concatenate(
        [router_grad.T, moe_gain_grad[None], jnp.zeros((24 - expert_total - 1, D), single)]
    )
    hidden_grad, attention_sum, up_sum, down_sum, small_sum, late_sum, peaks, expert_up_low = (
        backward(
            mid_grad, layer_one, hidden_in.reshape(block_rows, D), mid[0], gains, normed, queries,
            attended, dense_normed, spread(activation), pre_act, toeplitz_marks, small_in,
            peak_rows, (qkv0, qkv1, projection0, projection1, dense_up, dense_down), kv, probs,
            up_grad,
        )
    )
    attention_sum = (
        attention_sum.transpose(0, 2, 1, 3).reshape(2, part, 4 * D).astype(single)
    )
    mlp_up_grad = up_sum.transpose(1, 0, 2).reshape(part, -1).astype(single)
    mlp_down_grad = down_sum.reshape(-1, D).astype(single)

    def columns(rows):
        return lax.dynamic_slice_in_dim(rows, here * part, part, rows.ndim - 1)

    first_gain = late_sum[:6].reshape(1, D)
    rows = columns(small_sum)
    gain_rows = columns(first_gain)
    biases = lax.dynamic_slice_in_dim(late_sum[8:32], here * (NB // groups), NB // groups, 1)
    clip_scales = jnp.sqrt(clip_limit / jnp.maximum(peaks[:, 0].reshape(2, H), clip_limit))
    return (
        hidden_out,
        hidden_grad.reshape(hidden_in.shape),
        jnp.concatenate([gain_rows, rows[expert_total + 1 : expert_total + 2]]),
        attention_sum[:, :, : 3 * D],
        attention_sum[:, :, 3 * D :],
        biases.reshape(2, H, NB // groups).transpose(0, 2, 1),
        jnp.stack([rows[expert_total + 2], rows[expert_total]]),
        mlp_up_grad,
        mlp_down_grad,
        rows[:expert_total].T,
        expert_up_low.astype(single),
        expert_down_grad,
        clip_scales,
    )


def solution(mesh):
    tokens = P("shard", "expert", None, None)
    columns = P(None, "shard")
    layers = P(None, "shard", None)
    rows = P("shard", None)
    owned = P("expert", "shard", None)
    in_specs = (
        tokens, columns, layers, layers, layers, P(), columns, rows, rows, rows, owned, owned,
        tokens, tokens,
    )
    out_specs = (
        tokens, tokens, columns, layers, layers, layers, columns, rows, rows, rows, owned, owned,
        P(),
    )
    sized = mesh.shape["expert"] == 8 and mesh.shape["shard"] == 4
    part = shards if sized else plain_shards
    return jax.shard_map(part, mesh=mesh, in_specs=in_specs, out_specs=out_specs, check_vma=False)
```

```python
import functools
import math

import jax
import jax.numpy as jnp
from jax import lax
from jax.experimental import pallas as pl
from jax.experimental.pallas import tpu as pltpu
from jax.sharding import PartitionSpec as P

D = 768
H = 12
HD = 64
NB = 32
EXP_DEV = 2

epsilon = 1e-06
clip_limit = 6.0
bfloat = jnp.bfloat16
single = jnp.float32


def rms_norm(inputs, norm_gain):
    return (
        inputs * lax.rsqrt(jnp.mean(inputs * inputs, axis=-1, keepdims=True) + epsilon) * norm_gain
    )


def norm_back(inputs, norm_gain, upstream):
    _, pullback = jax.vjp(rms_norm, inputs, norm_gain)
    return pullback(upstream)


def gelu_back(pre_values, upstream):
    _, pullback = jax.vjp(jax.nn.gelu, pre_values)
    return pullback(upstream)[0]


def matmul(left, right):
    return jnp.dot(left, right, preferred_element_type=single)


def shard_shift(block, amount):
    count = lax.axis_size("shard")
    return lax.ppermute(block, "shard", [(i, (i + amount) % count) for i in range(count)])


def gather_shard(block):
    count = lax.axis_size("shard")
    here = lax.axis_index("shard")
    result = jnp.zeros((count,) + block.shape, block.dtype)
    for step in range(count):
        piece = block if step == 0 else shard_shift(block, step)
        result = lax.dynamic_update_slice_in_dim(result, piece[None], (here - step) % count, 0)
    return result


def scatter_shard(blocks, sent=bfloat):
    count = lax.axis_size("shard")
    here = lax.axis_index("shard")
    total = lax.dynamic_index_in_dim(blocks, here, 0, keepdims=False).astype(single)
    for step in range(1, count):
        part = lax.dynamic_index_in_dim(blocks, (here + step) % count, 0, keepdims=False)
        total = total + shard_shift(part.astype(sent), step).astype(single)
    return total


def spread(columns):
    experts, shard_count = lax.axis_size("expert"), lax.axis_size("shard")
    rows, width = columns.shape
    cut = columns.reshape(rows, shard_count, experts, width // (shard_count * experts))
    return cut.transpose(0, 2, 1, 3).reshape(rows, width)


def unspread(columns):
    experts, shard_count = lax.axis_size("expert"), lax.axis_size("shard")
    rows, width = columns.shape
    cut = columns.reshape(rows, experts, shard_count, width // (shard_count * experts))
    return cut.transpose(0, 2, 1, 3).reshape(rows, width)


def gather_weight(block):
    part = block.shape[0] // lax.axis_size("expert")
    own = lax.dynamic_slice_in_dim(block, lax.axis_index("expert") * part, part, 0)
    column = gather_shard(own).reshape(-1, block.shape[1])
    return lax.all_gather(column, "expert", axis=0, tiled=True)


def reduce_weight(grad):
    part = lax.psum_scatter(grad.astype(bfloat), "expert", scatter_dimension=0, tiled=True)
    blocks = part.reshape((lax.axis_size("shard"), -1) + part.shape[1:])
    own = scatter_shard(blocks).astype(bfloat)
    return lax.all_gather(own, "expert", axis=0, tiled=True).astype(single)


def bucket_marks(distance, lower, upper):
    inside = (distance[None] >= lower[:, None, None]) & (distance[None] < upper[:, None, None])
    return inside.astype(bfloat)


def position_bias(marks, bias_pair):
    return jnp.einsum("bij,bh->hij", marks, bias_pair, preferred_element_type=single)


def attention_forward(hidden, norm_gain, qkv, projection, bias_pair, geometry):
    distance, marks, scale = geometry
    rows = hidden.shape[0]
    normalized = spread(rms_norm(hidden, norm_gain).astype(bfloat))
    packed = matmul(normalized, qkv).astype(bfloat)
    key_value = lax.all_gather(packed[:, D:], "expert", axis=0, tiled=True)
    shifted = position_bias(marks, bias_pair)
    causal = distance >= 0
    queries = packed[:, :D].reshape(rows, H, HD)
    keys = key_value[:, :D].reshape(-1, H, HD)
    values = key_value[:, D:].reshape(-1, H, HD)
    raw_scores = jnp.einsum("ihd,jhd->hij", queries, keys, preferred_element_type=single) * scale
    head_peak = jnp.max(jnp.where(causal[None], raw_scores, -jnp.inf), axis=(1, 2))
    masked = jnp.where(causal[None], raw_scores + shifted, -jnp.inf)
    softmax_top = jnp.max(masked, axis=-1, keepdims=True)
    exponent = jnp.exp(masked - softmax_top)
    softmax_sum = jnp.sum(exponent, axis=-1, keepdims=True)
    probs = (exponent / softmax_sum).astype(bfloat)
    log_total = softmax_top[..., 0] + jnp.log(softmax_sum[..., 0])
    attended = jnp.einsum("hij,jhd->ihd", probs, values, preferred_element_type=single)
    attended = spread(attended.astype(bfloat).reshape(rows, D))
    saved = (normalized, packed, key_value, log_total, attended)
    return hidden + matmul(attended, projection), head_peak, saved


def attention_backward(
    upstream, hidden, norm_gain, qkv, projection, bias_pair, geometry, saved
):
    distance, marks, scale = geometry
    normalized, packed, key_value, log_total, attended = saved
    rows = hidden.shape[0]
    branch_grad = upstream.astype(bfloat)
    projection_grad = matmul(attended.T, branch_grad)
    attended_grad = unspread(matmul(branch_grad, projection.T).astype(bfloat))
    shifted = position_bias(marks, bias_pair)
    causal = distance >= 0
    queries = packed[:, :D].reshape(rows, H, HD)
    keys = key_value[:, :D].reshape(-1, H, HD)
    values = key_value[:, D:].reshape(-1, H, HD)
    grad_heads = attended_grad.reshape(rows, H, HD)
    raw_scores = jnp.einsum("ihd,jhd->hij", queries, keys, preferred_element_type=single) * scale
    probs = jnp.where(causal[None], jnp.exp(raw_scores + shifted - log_total[..., None]), 0.0)
    prob_grad = jnp.einsum("ihd,jhd->hij", grad_heads, values, preferred_element_type=single)
    row_dot = jnp.sum(prob_grad * probs, axis=-1)
    score_grad = (probs * (prob_grad - row_dot[..., None])).astype(bfloat)
    query_grad = jnp.einsum("hij,jhd->ihd", score_grad, keys, preferred_element_type=single) * scale
    query_grad = query_grad.astype(bfloat).reshape(rows, D)
    bias_grad = jnp.einsum("hij,bij->bh", score_grad, marks, preferred_element_type=single)
    key_grad = (
        jnp.einsum("hij,ihd->jhd", score_grad, queries, preferred_element_type=single) * scale
    )
    value_grad = jnp.einsum(
        "hij,ihd->jhd", probs.astype(bfloat), grad_heads, preferred_element_type=single
    )
    pair = jnp.concatenate([key_grad.reshape(-1, D), value_grad.reshape(-1, D)], axis=-1)
    pair_grad = lax.psum_scatter(pair.astype(bfloat), "expert", scatter_dimension=0, tiled=True)
    packed_grad = jnp.concatenate([query_grad, pair_grad], axis=-1)
    qkv_grad = matmul(normalized.T, packed_grad)
    normed_grad = unspread(matmul(packed_grad, qkv.T))
    input_grad, gain_grad = norm_back(hidden, norm_gain, normed_grad)
    return upstream + input_grad, gain_grad, qkv_grad, projection_grad, bias_grad


def exchange(blocks):
    return lax.all_to_all(blocks, "expert", split_axis=0, concat_axis=0, tiled=True)


def plain_shards(
    hidden_in,
    attn_gain,
    qkv_weight,
    out_weight,
    rel_bias,
    bucket_table,
    mlp_gain,
    mlp_up,
    mlp_down,
    router_weight,
    expert_up,
    expert_down,
    routes,
    out_grad,
):
    block_rows = hidden_in.shape[1]
    length = bucket_table.shape[0]
    experts = lax.axis_size("expert")
    groups = lax.axis_size("shard")
    here = lax.axis_index("shard")
    expert_total = EXP_DEV * experts
    capacity = 4 * block_rows // expert_total
    width = expert_down.shape[1]
    scale = 1.0 / math.sqrt(HD)

    small = jnp.concatenate(
        [attn_gain.reshape(-1), mlp_gain.reshape(-1), rel_bias.reshape(-1), router_weight.reshape(-1)]
    )
    small = gather_shard(small)
    part = D // groups
    cuts = [0, 2 * part, 4 * part, 4 * part + 2 * (NB // groups) * H, small.shape[1]]
    gain_attn, gain_mlp, bias_weights, router_full = (
        small[:, cuts[i] : cuts[i + 1]] for i in range(4)
    )
    gain_attn = gain_attn.reshape(groups, 2, part).transpose(1, 0, 2).reshape(2, D).astype(single)
    gain_mlp = gain_mlp.reshape(groups, 2, part).transpose(1, 0, 2).reshape(2, D).astype(single)
    bias_weights = (
        bias_weights.reshape(groups, 2, NB // groups, H).transpose(1, 0, 2, 3).reshape(2, NB, H)
    )
    router_full = router_full.reshape(D, expert_total)

    first = gather_weight(jnp.concatenate([qkv_weight[0], out_weight[0]], axis=1))
    dense_up = gather_weight(mlp_up)
    dense_down = gather_weight(mlp_down)
    second = gather_weight(jnp.concatenate([qkv_weight[1], out_weight[1]], axis=1))
    qkv = (first[:, : 3 * D], second[:, : 3 * D])
    projection = (first[:, 3 * D :], second[:, 3 * D :])

    up_own = jnp.zeros((EXP_DEV, groups, part, width), bfloat)
    for step in range(groups):
        target = (here + step) % groups
        piece = lax.dynamic_slice_in_dim(expert_up, target * width, width, 2)
        if step:
            piece = shard_shift(piece, step)
        up_own = lax.dynamic_update_slice_in_dim(up_own, piece[:, None], (here - step) % groups, 1)
    up_own = up_own.reshape(EXP_DEV, D, width)

    route_rows = gather_shard(routes.reshape(block_rows, 2))
    upstream_all = gather_shard(out_grad.reshape(block_rows, D))
    expert_ids = jnp.arange(expert_total, dtype=jnp.int32)
    flat_routes = route_rows.reshape(groups, -1)
    marks = (flat_routes[:, :, None] == expert_ids).astype(jnp.int32)
    rank = jnp.sum((jnp.cumsum(marks, axis=1) - marks) * marks, axis=2)
    slot_of_route = flat_routes * capacity + rank
    slot_ids = jnp.arange(expert_total * capacity, dtype=jnp.int32)
    slot_marks = (slot_of_route[:, :, None] == slot_ids).astype(bfloat)
    token_marks = jnp.sum(
        slot_marks.reshape(groups, block_rows, 2, -1).astype(single), axis=2
    ).astype(bfloat)

    def dispatch(rows):
        slots = jnp.einsum("gts,gtd->gsd", token_marks, rows, preferred_element_type=single)
        slots = slots.astype(bfloat).reshape(groups, experts, EXP_DEV, capacity, D)
        return exchange(slots.transpose(1, 2, 0, 3, 4)).reshape(
            experts, EXP_DEV, groups * capacity, D
        )

    def collect(blocks):
        back = exchange(blocks.astype(bfloat)).reshape(experts, EXP_DEV, groups, capacity, D)
        return back.transpose(2, 0, 1, 3, 4).reshape(groups, expert_total * capacity, D)

    owner_rows = dispatch(upstream_all)

    own_positions = lax.axis_index("expert") * block_rows + jnp.arange(block_rows, dtype=jnp.int32)
    distance = own_positions[:, None] - jnp.arange(length, dtype=jnp.int32)[None, :]
    bounds = jnp.sum(
        (bucket_table[:, None] < jnp.arange(NB + 1, dtype=jnp.int32)[None, :]).astype(jnp.int32),
        axis=0,
    )
    geometry = (distance, bucket_marks(distance, bounds[:NB], bounds[1:]), scale)

    hidden_zero = hidden_in.reshape(block_rows, D).astype(single)
    mid_first, peak_first, saved_first = attention_forward(
        hidden_zero, gain_attn[0], qkv[0], projection[0], bias_weights[0], geometry
    )
    dense_normed = spread(rms_norm(mid_first, gain_mlp[0]).astype(bfloat))
    pre_act = matmul(dense_normed, dense_up)
    activation = spread(jax.nn.gelu(pre_act).astype(bfloat))
    layer_one = mid_first + matmul(activation, dense_down)
    mid_second, peak_second, saved_second = attention_forward(
        layer_one, gain_attn[1], qkv[1], projection[1], bias_weights[1], geometry
    )

    moe_normed = rms_norm(mid_second, gain_mlp[1]).astype(bfloat)
    normed_all = gather_shard(moe_normed)
    received = dispatch(normed_all)
    router_logits = jnp.einsum("gtd,de->gte", normed_all, router_full, preferred_element_type=single)
    selected = (route_rows[..., None] == expert_ids).astype(single)
    gates_all = jax.nn.softmax(jnp.sum(selected * router_logits[:, :, None, :], axis=-1), axis=-1)
    slot_gates = jnp.sum(
        gates_all.reshape(groups, -1)[:, :, None] * (slot_of_route[:, :, None] == slot_ids), axis=1
    )
    owner_gates = exchange(
        slot_gates.reshape(groups, experts, EXP_DEV, capacity).transpose(1, 2, 0, 3)
    ).reshape(experts, EXP_DEV, groups * capacity)

    expert_pre = jnp.einsum("sjcd,jdf->sjcf", received, up_own, preferred_element_type=single)
    expert_act = jax.nn.gelu(expert_pre).astype(bfloat)
    expert_out = jnp.einsum(
        "sjcf,jfd->sjcd", expert_act, expert_down, preferred_element_type=single
    )
    owner_grad = (owner_gates[..., None] * owner_rows.astype(single)).astype(bfloat)
    act_grad = jnp.einsum("sjcd,jfd->sjcf", owner_grad, expert_down, preferred_element_type=single)
    pre_grad = gelu_back(expert_pre, act_grad).astype(bfloat)
    row_grad = jnp.einsum("sjcf,jdf->sjcd", pre_grad, up_own, preferred_element_type=single)

    returned = collect(expert_out)
    back_rows = collect(row_grad)
    expert_down_grad = jnp.einsum(
        "sjcf,sjcd->jfd", expert_act, owner_grad, preferred_element_type=single
    )
    up_grad = jnp.einsum(
        "sjcd,sjcf->jdf", received, pre_grad, preferred_element_type=single
    ).astype(bfloat)

    route_out = jnp.einsum("grs,gsd->grd", slot_marks, returned, preferred_element_type=single)
    route_out = route_out.reshape(groups, block_rows, 2, D)
    gate_grad = scatter_shard(
        jnp.sum(route_out * upstream_all[:, :, None, :].astype(single), axis=-1), single
    )
    mixed = scatter_shard(jnp.sum(gates_all[..., None] * route_out, axis=2))
    hidden_out = (mid_second + mixed).astype(bfloat).reshape(hidden_in.shape)

    gates = lax.dynamic_index_in_dim(gates_all, here, 0, keepdims=False)
    own_selected = lax.dynamic_index_in_dim(selected, here, 0, keepdims=False)
    upstream = out_grad.reshape(block_rows, D).astype(single)
    chosen_grad = gates * (gate_grad - jnp.sum(gates * gate_grad, axis=-1, keepdims=True))
    logit_grad = jnp.sum(chosen_grad[:, :, None] * own_selected, axis=1).astype(bfloat)
    router_grad = matmul(moe_normed.T, logit_grad)
    row_terms = jnp.einsum("gts,gsd->gtd", token_marks, back_rows, preferred_element_type=single)
    normed_grad = matmul(logit_grad, router_full.T) + scatter_shard(row_terms)
    moe_input_grad, moe_gain_grad = norm_back(mid_second, gain_mlp[1], normed_grad)
    mid_grad = upstream + moe_input_grad

    up_grad = up_grad.reshape(EXP_DEV, groups, part, width)
    expert_up_grad = jnp.zeros((EXP_DEV, part, groups * width), single)
    for step in range(groups):
        piece = lax.dynamic_index_in_dim(up_grad, (here + step) % groups, 1, keepdims=False)
        if step:
            piece = shard_shift(piece, step)
        expert_up_grad = lax.dynamic_update_slice_in_dim(
            expert_up_grad, piece.astype(single), ((here - step) % groups) * width, 2
        )

    layer_grad, gain_second, qkv_second, projection_second, bias_second = attention_backward(
        mid_grad, layer_one, gain_attn[1], qkv[1], projection[1], bias_weights[1], geometry,
        saved_second,
    )
    second_grad = reduce_weight(jnp.concatenate([qkv_second, projection_second], axis=1))
    dense_branch = layer_grad.astype(bfloat)
    mlp_down_grad = reduce_weight(matmul(activation.T, dense_branch))
    hidden_act_grad = unspread(matmul(dense_branch, dense_down.T))
    pre_act_grad = gelu_back(pre_act, hidden_act_grad).astype(bfloat)
    mlp_up_grad = reduce_weight(matmul(dense_normed.T, pre_act_grad))
    dense_normed_grad = unspread(matmul(pre_act_grad, dense_up.T))
    dense_input_grad, dense_gain_grad = norm_back(mid_first, gain_mlp[0], dense_normed_grad)
    first_grad = layer_grad + dense_input_grad
    input_grad, gain_first, qkv_first, projection_first, bias_first = attention_backward(
        first_grad, hidden_zero, gain_attn[0], qkv[0], projection[0], bias_weights[0], geometry,
        saved_first,
    )
    first_weight_grad = reduce_weight(jnp.concatenate([qkv_first, projection_first], axis=1))

    gains = jnp.stack([gain_first, gain_second, dense_gain_grad, moe_gain_grad])
    biases = jnp.stack([bias_first, bias_second])
    small_grad = jnp.concatenate(
        [
            gains.reshape(4, groups, part).transpose(1, 0, 2).reshape(groups, -1),
            biases.reshape(2, groups, NB // groups, H).transpose(1, 0, 2, 3).reshape(groups, -1),
            router_grad.reshape(groups, -1),
        ],
        axis=1,
    )
    small_grad = lax.psum(scatter_shard(small_grad, single), "expert")
    gain_cut = 4 * part
    bias_cut = gain_cut + 2 * (NB // groups) * H
    own_gains = small_grad[:gain_cut].reshape(4, part)
    peaks = lax.pmax(jnp.stack([peak_first, peak_second]), ("expert", "shard"))
    clip_scales = jnp.sqrt(clip_limit / jnp.maximum(peaks, clip_limit))
    return (
        hidden_out,
        input_grad.reshape(hidden_in.shape),
        own_gains[:2],
        jnp.stack([first_weight_grad[:, : 3 * D], second_grad[:, : 3 * D]]),
        jnp.stack([first_weight_grad[:, 3 * D :], second_grad[:, 3 * D :]]),
        small_grad[gain_cut:bias_cut].reshape(2, NB // groups, H),
        own_gains[2:],
        mlp_up_grad,
        mlp_down_grad,
        small_grad[bias_cut:].reshape(part, expert_total),
        expert_up_grad,
        expert_down_grad,
        clip_scales,
    )


MESH = pl.DeviceIdType.MESH
ANY = pl.ANY
VMEM = pltpu.VMEM


def place():
    return lax.axis_index("expert"), lax.axis_index("shard")


def greet(devices):
    barrier = pltpu.get_barrier_semaphore()
    for device in devices:
        pl.semaphore_signal(barrier, inc=1, device_id=device, device_id_type=MESH)
    pl.semaphore_wait(barrier, len(devices))


def push(sent, source, target, send_sem, recv_sem, device):
    copy = pltpu.make_async_remote_copy(
        src_ref=source,
        dst_ref=target,
        send_sem=send_sem,
        recv_sem=recv_sem,
        device_id=device,
        device_id_type=MESH,
    )
    copy.start()
    sent.append(copy)
    return copy


def small_kernel(groups, small_ref, slots_ref, small_out, slots_out, zs, zr, ps, pr, lsem):
    e, s = place()
    others = [(e, lax.rem(s + k, groups)) for k in range(1, groups)]
    around = [(lax.rem(e + k, 8), s) for k in range(1, 8)]
    local = [
        pltpu.make_async_copy(small_ref, small_out.at[s], lsem.at[0]),
        pltpu.make_async_copy(slots_ref, slots_out.at[s, e], lsem.at[1]),
    ]
    for copy in local:
        copy.start()
    greet(others + around)
    sent, first = [], []
    for k, device in enumerate(others):
        push(sent, small_ref, small_out.at[s], zs.at[0, k], zr.at[0, k], device)
        first.append(
            push(sent, slots_ref, slots_out.at[s, e], zs.at[1, k], zr.at[1, k], device)
        )
    for copy in local:
        copy.wait()
    for copy in first:
        copy.wait_recv()
    column = slots_out.at[:, e]
    for k, device in enumerate(around):
        push(sent, column, column, ps.at[k], pr.at[k], device)
    for copy in sent:
        if all(copy is not other for other in first):
            copy.wait_recv()
    for copy in sent:
        copy.wait_send()


def gather_small(small, slots):
    groups = lax.axis_size("shard")
    vmem = pl.BlockSpec(memory_space=VMEM)
    sem = pltpu.SemaphoreType.DMA
    return pl.pallas_call(
        functools.partial(small_kernel, groups),
        name="gather_small",
        out_shape=(
            jax.ShapeDtypeStruct((groups,) + small.shape, small.dtype),
            jax.ShapeDtypeStruct((groups, 8) + slots.shape, slots.dtype),
        ),
        in_specs=[vmem, vmem],
        out_specs=(vmem, vmem),
        scratch_shapes=[sem((2, 3)), sem((2, 3)), sem((7,)), sem((7,)), sem((2,))],
        compiler_params=pltpu.CompilerParams(collective_id=1, has_side_effects=True),
    )(small, slots)


def norm_rows(inputs, gain):
    return inputs * lax.rsqrt(jnp.mean(inputs * inputs, axis=-1, keepdims=True) + epsilon) * gain


def dot_rows(left, right):
    return lax.dot_general(left, right, (((1,), (1,)), ((), ())), preferred_element_type=single)


def loop(count, body):
    def step(i, carry):
        body(i)
        return carry

    lax.fori_loop(0, count, step, 0)


def lane_block(i, width):
    return pl.ds(pl.multiple_of(i * width, 128), width)


def row_block(i, height):
    return pl.ds(pl.multiple_of(i * height, height), height)


T = 128
PAIRS = H // 2
TOE = 1152
CAP = 32


class Plane:
    def __init__(self):
        self.e, self.s = place()
        e = self.e
        self.core = lax.rem(e, 2)
        self.quarter = e // 2
        self.at_x = e + 2 - 4 * lax.rem(self.quarter, 2)
        self.at_y = lax.rem(e + 4, 8)
        self.at_core = e + 1 - 2 * self.core
        self.inward = jnp.where(self.core == 0, self.at_x, self.at_y)
        self.onward = jnp.where(self.core == 0, self.at_y, self.at_x)
        self.diagonal = self.inward + self.onward - e
        self.others = [lax.rem(self.s + k, 4) for k in range(1, 4)]
        self.around = [lax.rem(e + k, 8) for k in range(1, 8)]
        self.sent = []

    def push(self, source, target, send_sem, recv_sem, device):
        return push(self.sent, source, target, send_sem, recv_sem, device)

    def arrived(self, view, recv_sem):
        pltpu.make_async_remote_copy(
            src_ref=view,
            dst_ref=view,
            send_sem=recv_sem,
            recv_sem=recv_sem,
            device_id=(self.at_core, self.s),
            device_id_type=MESH,
        ).wait_recv()


class PlaneGather:
    def __init__(self, plane, view, send_sems, recv_sems):
        self.plane, self.view, self.ss, self.rs = plane, view, send_sems, recv_sems

    def _push(self, who, i, target):
        p = self.plane
        block = self.view(who)
        p.push(block, block, self.ss.at[i], self.rs.at[i], (target, p.s))

    def first(self):
        p = self.plane
        self._push(p.e, 0, p.at_x)
        self._push(p.e, 1, p.at_y)
        self._push(p.e, 3, p.at_core)

    def second(self):
        p = self.plane
        p.arrived(self.view(p.inward), self.rs.at[p.core])
        self._push(p.inward, 2, p.onward)
        self._push(p.inward, 4, p.at_core)

    def third(self):
        p = self.plane
        p.arrived(self.view(p.onward), self.rs.at[1 - p.core])
        self._push(p.onward, 5, p.at_core)
        p.arrived(self.view(p.diagonal), self.rs.at[2])
        self._push(p.diagonal, 6, p.at_core)

    def done(self):
        for i in range(3, 7):
            self.plane.arrived(self.view(self.plane.e), self.rs.at[i])


def forward_kernel(
    hidden_ref,
    gains_ref,
    table_ref,
    qkv_hbm,
    out_hbm,
    up_hbm,
    down_hbm,
    expert_up_hbm,
    cot_hbm,
    normed_out,
    query_out,
    attended_out,
    mid_out,
    dense_normed_out,
    pre_out,
    act_out,
    one_out,
    peak_out,
    moe_normed_out,
    qkv0_out,
    qkv1_out,
    proj0_out,
    proj1_out,
    up_out,
    down_out,
    kv_out,
    probs_out,
    up_own,
    cot_all,
    w_qkv0,
    w_qkv1,
    w_out0,
    w_out1,
    w_up,
    w_down,
    kv,
    probs,
    scores,
    zs,
    zr,
    f1s,
    f1r,
    f2s,
    f2r,
    cs,
    cr,
    locals_sem,
    k1s,
    k1r,
    k2s,
    k2r,
    kcs,
    kcr,
    us,
    ur,
    gs,
    gr,
    ns,
    nr,
    outs_sem,
):
    e, s = place()
    core = lax.rem(e, 2)
    quarter = e // 2
    at_x = e + 2 - 4 * lax.rem(quarter, 2)
    at_y = lax.rem(e + 4, 8)
    at_core = e + 1 - 2 * core
    inward = jnp.where(core == 0, at_x, at_y)
    onward = jnp.where(core == 0, at_y, at_x)
    others = [lax.rem(s + k, 4) for k in range(1, 4)]
    sources = [lax.rem(s + 4 - k, 4) for k in range(1, 4)]
    sent = []
    kept = []

    def local(source, target, sem):
        copy = pltpu.make_async_copy(source, target, sem)
        copy.start()
        return copy

    chunks = [
        (qkv_hbm.at[0], w_qkv0, 48, 1152),
        (out_hbm.at[0], w_out0, 48, 384),
        (up_hbm, w_up, 48, 1536),
        (down_hbm, w_down, 192, 384),
        (qkv_hbm.at[1], w_qkv1, 48, 1152),
        (out_hbm.at[1], w_out1, 48, 384),
    ]

    def block(target, who, position, height, half, width):
        rows = pl.ds(pl.multiple_of(position * 4 * height + who * height, height), height)
        return target.at[rows, lane_block(half, width)]

    def cot_block(g, who):
        return cot_all.at[g, who]

    stage1, stage2, stage3, stage4, own = {}, {}, {}, {}, {}

    def z_send(c):
        source, target, height, width = chunks[c]
        piece = source.at[row_block(quarter, height), lane_block(core, width)]
        mine = block(target, quarter, s, height, core, width)
        stage1[c] = [
            push(sent, piece, mine, zs.at[c, k], zr.at[c, k], (e, others[k])) for k in range(3)
        ]
        own[c] = local(source, target.at[row_block(s, 4 * height), :], locals_sem.at[c])

    def plane_send(c):
        _, target, height, width = chunks[c]
        stage2[c] = []
        for k in range(3):
            stage1[c][k].wait_recv()
            mine = block(target, quarter, sources[k], height, core, width)
            stage2[c].append(
                [
                    push(sent, mine, mine, f1s.at[c, k, i], f1r.at[c, k, i], (partner, s))
                    for i, partner in enumerate((at_x, at_y))
                ]
            )

    def plane_forward(c):
        _, target, height, width = chunks[c]
        stage3[c] = []
        for k in range(3):
            pltpu.make_async_remote_copy(
                src_ref=block(target, quarter, sources[k], height, core, width),
                dst_ref=block(target, quarter, sources[k], height, core, width),
                send_sem=f1s.at[c, k, core],
                recv_sem=f1r.at[c, k, core],
                device_id=(inward, s),
                device_id_type=MESH,
            ).wait_recv()
            theirs = block(target, inward // 2, sources[k], height, core, width)
            stage3[c].append(
                push(sent, theirs, theirs, f2s.at[c, k], f2r.at[c, k], (onward, s))
            )

    def core_send(c):
        _, target, height, width = chunks[c]
        stage4[c] = []
        for k in range(3):
            pltpu.make_async_remote_copy(
                src_ref=block(target, quarter, sources[k], height, core, width),
                dst_ref=block(target, quarter, sources[k], height, core, width),
                send_sem=f1s.at[c, k, 1 - core],
                recv_sem=f1r.at[c, k, 1 - core],
                device_id=(onward, s),
                device_id_type=MESH,
            ).wait_recv()
            stage3[c][k].wait_recv()
            half = target.at[row_block(sources[k], 4 * height), lane_block(core, width)]
            stage4[c].append(push(sent, half, half, cs.at[c, k], cr.at[c, k], (at_core, s)))

    weight_outs = [qkv0_out, proj0_out, up_out, down_out, qkv1_out, proj1_out]

    def ready(c):
        for k in range(3):
            stage4[c][k].wait_recv()
        own[c].wait()
        kept.append(local(chunks[c][1], weight_outs[c], outs_sem.at[c]))

    greet([(at_core, s), (at_x, s), (at_y, s)] + [(e, other) for other in others])
    z_send(0)
    z_send(1)
    z_send(2)

    def attention(layer, inputs, w_qkv, w_out, work):
        normed = norm_rows(inputs, gains_ref[pl.ds(layer, 1), :]).astype(bfloat)
        normed_out[layer] = normed
        if layer == 0:
            plane_send(0)
            plane_forward(0)
            core_send(0)
            ready(0)
        else:
            ready(4)
        own_rows = row_block(e, T)
        first, second, third = [], [], []
        for part in range(3):
            x = normed_out[layer]
            for i, base in enumerate((D, 2 * D)):
                columns = w_qkv[:, base + 256 * part : base + 256 * (part + 1)]
                kv[layer, part, own_rows, 256 * i : 256 * (i + 1)] = jnp.dot(
                    x, columns, preferred_element_type=single
                ).astype(bfloat)
            mine = kv.at[layer, part, own_rows, :]
            first.append(
                [
                    push(sent, mine, mine, k1s.at[layer, part, i], k1r.at[layer, part, i], (p, s))
                    for i, p in enumerate((at_x, at_y))
                ]
            )
            third.append(
                [
                    push(
                        sent, mine, mine, kcs.at[layer, part, 0], kcr.at[layer, part, 0],
                        (at_core, s),
                    )
                ]
            )
        query_out[layer] = jnp.dot(
            normed_out[layer], w_qkv[:, :D], preferred_element_type=single
        ).astype(bfloat)
        if work:
            work[0]()
        at_diagonal = inward + onward - e
        for part in range(3):
            pltpu.make_async_remote_copy(
                src_ref=kv.at[layer, part, own_rows, :],
                dst_ref=kv.at[layer, part, own_rows, :],
                send_sem=k1s.at[layer, part, core],
                recv_sem=k1r.at[layer, part, core],
                device_id=(inward, s),
                device_id_type=MESH,
            ).wait_recv()
            theirs = kv.at[layer, part, row_block(inward, T), :]
            second.append(
                push(
                    sent, theirs, theirs, k2s.at[layer, part], k2r.at[layer, part], (onward, s)
                )
            )
            third[part].append(
                push(
                    sent, theirs, theirs, kcs.at[layer, part, 1], kcr.at[layer, part, 1],
                    (at_core, s),
                )
            )
        if work:
            work[1]()
        for part in range(3):
            pltpu.make_async_remote_copy(
                src_ref=kv.at[layer, part, own_rows, :],
                dst_ref=kv.at[layer, part, own_rows, :],
                send_sem=k1s.at[layer, part, 1 - core],
                recv_sem=k1r.at[layer, part, 1 - core],
                device_id=(onward, s),
                device_id_type=MESH,
            ).wait_recv()
            theirs = kv.at[layer, part, row_block(onward, T), :]
            third[part].append(
                push(
                    sent, theirs, theirs, kcs.at[layer, part, 2], kcr.at[layer, part, 2],
                    (at_core, s),
                )
            )
            second[part].wait_recv()
            theirs = kv.at[layer, part, row_block(at_diagonal, T), :]
            third[part].append(
                push(
                    sent, theirs, theirs, kcs.at[layer, part, 3], kcr.at[layer, part, 3],
                    (at_core, s),
                )
            )
        for part in range(3):
            for i in range(4):
                third[part][i].wait_recv()

            def one_pair(local_pair):
                pair = 2 * part + local_pair
                lanes = lane_block(pair, 128)
                queries = query_out[layer, :, lanes]
                lane = lax.broadcasted_iota(jnp.int32, (T, 128), 1)
                zero = jnp.zeros_like(queries)
                both = jnp.concatenate(
                    [jnp.where(lane < HD, queries, zero), jnp.where(lane >= HD, queries, zero)]
                )
                keys = kv[layer, part, :, lane_block(local_pair, 128)]
                scores[...] = dot_rows(both, keys) * (1.0 / math.sqrt(HD))
                for half in range(2):
                    head = 2 * pair + half
                    toeplitz = table_ref[pl.ds(layer * H + head, 1), :]
                    peak = jnp.full((1, 1), -jnp.inf, single)
                    for rows in range(0, T, 32):
                        raw = scores[half * T + rows : half * T + rows + 32, :]
                        row = e * T + rows + lax.broadcasted_iota(jnp.int32, raw.shape, 0)
                        causal = row >= lax.broadcasted_iota(jnp.int32, raw.shape, 1)
                        shifted = pltpu.roll(
                            jnp.broadcast_to(toeplitz, (32, TOE)),
                            TOE - (T - 1) + rows,
                            1,
                            stride=1,
                            stride_axis=0,
                        )[:, : raw.shape[1]]
                        peak = jnp.maximum(
                            peak, jnp.max(jnp.where(causal, raw, -jnp.inf), keepdims=True)
                        )
                        masked = jnp.where(causal, raw + shifted, -jnp.inf)
                        top = jnp.max(masked, axis=-1, keepdims=True)
                        exponent = jnp.exp(masked - top)
                        total = jnp.sum(exponent, axis=-1, keepdims=True)
                        probs[layer, pl.ds(pl.multiple_of(head * T + rows, 32), 32), :] = (
                            exponent / total
                        ).astype(bfloat)
                    peak_out[pl.ds(layer * H + head, 1), :] = jnp.broadcast_to(peak, (1, 128))
                values = kv[layer, part, :, pl.ds(pl.multiple_of(256 + local_pair * 128, 128), 128)]
                mixed = jnp.dot(
                    probs[layer, pl.ds(pl.multiple_of(pair * 2 * T, 2 * T), 2 * T), :],
                    values,
                    preferred_element_type=single,
                )
                attended_out[layer, :, lanes] = jnp.where(
                    lane < HD, mixed[:T], mixed[T:]
                ).astype(bfloat)

            loop(2, one_pair)
            if work:
                work[2 + part]()
        kept.append(local(kv.at[layer], kv_out.at[layer], outs_sem.at[6 + layer]))
        kept.append(local(probs.at[layer], probs_out.at[layer], outs_sem.at[8 + layer]))

    def nothing():
        pass

    def work0():
        plane_send(1)
        z_send(3)

    def work1():
        plane_forward(1)

    def work2():
        core_send(1)
        plane_send(2)

    def work3():
        plane_forward(2)
        z_send(4)
        z_send(5)

    def work4():
        core_send(2)
        plane_send(3)

    plane = Plane()
    cot_groups = [s] + sources
    cot_gathers = []
    for k, g in enumerate(cot_groups):
        cot_gathers.append(
            PlaneGather(plane, functools.partial(cot_block, g), ns.at[k], nr.at[k])
        )

    def cot_send():
        for k in range(3):
            push(sent, cot_hbm, cot_block(s, e), gs.at[k], gr.at[k], (e, others[k]))
        copy = local(cot_hbm, cot_block(s, e), gs.at[3])
        copy.wait()
        cot_gathers[0].first()

    def cot_first(k):
        plane.arrived(cot_block(s, e), gr.at[k - 1])
        cot_gathers[k].first()

    hidden = hidden_ref[...].astype(single)
    attention(0, hidden, w_qkv0, w_out0, [work0, work1, work2, work3, work4])
    ready(1)
    mid_out[0] = hidden + jnp.dot(
        attended_out[0], w_out0[...], preferred_element_type=single
    )
    dense_normed_out[...] = norm_rows(mid_out[0], gains_ref[pl.ds(2, 1), :]).astype(bfloat)
    reshard = []
    for k in range(3):
        reshard.append(
            push(
                sent,
                expert_up_hbm.at[:, :, lane_block(others[k], 768)],
                up_own.at[:, row_block(s, 192), :],
                us.at[k],
                ur.at[k],
                (e, others[k]),
            )
        )
    kept.append(
        local(
            expert_up_hbm.at[:, :, lane_block(s, 768)],
            up_own.at[:, row_block(s, 192), :],
            us.at[3],
        )
    )
    cot_send()
    ready(2)

    def up_part(i):
        lanes = lane_block(i, 512)
        before = jnp.dot(dense_normed_out[...], w_up[:, lanes], preferred_element_type=single)
        pre_out[:, lanes] = before
        act_out[:, lanes] = jax.nn.gelu(before).astype(bfloat)

    plane_forward(3)
    loop(3, up_part)
    core_send(3)
    plane_send(4)
    plane_send(5)

    def up_later(i):
        up_part(i + 3)

    loop(3, up_later)
    plane_forward(4)
    plane_forward(5)
    ready(3)
    one_out[...] = mid_out[0]

    def down_part(i):
        rows = row_block(i, 768)
        one_out[...] += jnp.dot(
            act_out[:, lane_block(i, 768)], w_down[rows, :], preferred_element_type=single
        )

    loop(4, down_part)
    core_send(4)
    core_send(5)

    def work5():
        cot_first(1)
        cot_gathers[0].second()

    def work6():
        cot_first(2)

    def work7():
        cot_gathers[0].third()
        cot_gathers[1].second()

    def work8():
        cot_first(3)
        cot_gathers[1].third()
        cot_gathers[2].second()

    def work9():
        cot_gathers[2].third()
        cot_gathers[3].second()

    attention(1, one_out[...], w_qkv1, w_out1, [work5, work6, work7, work8, work9])
    cot_gathers[3].third()
    ready(5)
    mid_out[1] = one_out[...] + jnp.dot(
        attended_out[1], w_out1[...], preferred_element_type=single
    )
    moe_normed_out[...] = norm_rows(mid_out[1], gains_ref[pl.ds(3, 1), :]).astype(bfloat)
    for gather in cot_gathers:
        gather.done()
    for copy in reshard:
        copy.wait_recv()
    for copy in kept:
        copy.wait()
    for copy in sent + plane.sent:
        copy.wait_send()


def forward(hidden, gains, table, qkv, out, up, down, expert_up, cotangent):
    length = T * lax.axis_size("expert")
    vmem = pl.BlockSpec(memory_space=VMEM)
    anywhere = pl.BlockSpec(memory_space=ANY)
    shape = jax.ShapeDtypeStruct
    ff = up.shape[1]
    sem = pltpu.SemaphoreType.DMA
    return pl.pallas_call(
        forward_kernel,
        name="forward_layers",
        out_shape=(
            shape((2, T, D), bfloat),
            shape((2, T, D), bfloat),
            shape((2, T, D), bfloat),
            shape((2, T, D), single),
            shape((T, D), bfloat),
            shape((T, ff), single),
            shape((T, ff), bfloat),
            shape((T, D), single),
            shape((2 * H, 128), single),
            shape((T, D), bfloat),
            shape((D, 3 * D), bfloat),
            shape((D, 3 * D), bfloat),
            shape((D, D), bfloat),
            shape((D, D), bfloat),
            shape((D, ff), bfloat),
            shape((ff, D), bfloat),
            shape((2, 3, length, 512), bfloat),
            shape((2, H * T, length), bfloat),
            shape((EXP_DEV, D, 768), bfloat),
            shape((4, 8, T, D), bfloat),
        ),
        in_specs=[vmem] * 3 + [anywhere] * 6,
        out_specs=(vmem,) * 10 + (anywhere,) * 10,
        scratch_shapes=[
            VMEM((D, 3 * D), bfloat),
            VMEM((D, 3 * D), bfloat),
            VMEM((D, D), bfloat),
            VMEM((D, D), bfloat),
            VMEM((D, ff), bfloat),
            VMEM((ff, D), bfloat),
            VMEM((2, 3, length, 512), bfloat),
            VMEM((2, H * T, length), bfloat),
            VMEM((2 * T, length), single),
            sem((6, 3)), sem((6, 3)),
            sem((6, 3, 2)), sem((6, 3, 2)),
            sem((6, 3)), sem((6, 3)),
            sem((6, 3)), sem((6, 3)),
            sem((6,)),
            sem((2, 3, 2)), sem((2, 3, 2)),
            sem((2, 3)), sem((2, 3)),
            sem((2, 3, 4)), sem((2, 3, 4)),
            sem((4,)), sem((3,)),
            sem((4,)), sem((3,)),
            sem((4, 7)), sem((4, 7)),
            sem((10,)),
        ],
        compiler_params=pltpu.CompilerParams(
            collective_id=2, has_side_effects=True, vmem_limit_bytes=56 * 2**20
        ),
    )(hidden, gains, table, qkv, out, up, down, expert_up, cotangent)


class SmallReduce:
    def __init__(self, plane, value, z_in, plane_in, op, sems):
        self.plane, self.value, self.z_in, self.plane_in = plane, value, z_in, plane_in
        self.op, self.sems = op, sems

    def start(self):
        p = self.plane
        zs, zr, _, _ = self.sems
        for k in range(3):
            p.push(self.value, self.z_in.at[k], zs.at[k], zr.at[k], (p.e, p.others[k]))

    def middle(self, middle):
        p = self.plane
        zs, zr, ps, pr = self.sems
        total = self.value[...]
        for k in range(3):
            p.arrived(self.z_in.at[k], zr.at[k])
            total = self.op(total, self.z_in[k])
        middle[...] = total
        for k in range(7):
            p.push(middle, self.plane_in.at[k], ps.at[k], pr.at[k], (p.around[k], p.s))

    def finish(self, middle, result):
        p = self.plane
        total = middle[...]
        for k in range(7):
            p.arrived(self.plane_in.at[k], self.sems[3].at[k])
            total = self.op(total, self.plane_in[k])
        result[...] = total


def norm_pull(inputs, gain, upstream):
    inverse = lax.rsqrt(jnp.mean(inputs * inputs, axis=-1, keepdims=True) + epsilon)
    scaled = upstream * gain
    inner = jnp.mean(scaled * inputs, axis=-1, keepdims=True)
    gain_grad = jnp.sum(upstream * inputs * inverse, axis=0, keepdims=True)
    return inverse * scaled - inputs * (inverse * inverse * inverse * inner), gain_grad


def gelu_slope(value):
    root = math.sqrt(2.0 / math.pi)
    squared = value * value
    bend = jnp.tanh(root * value * (1.0 + 0.044715 * squared))
    return 0.5 * (1.0 + bend) + 0.5 * value * (1.0 - bend * bend) * root * (
        1.0 + 3 * 0.044715 * squared
    )


def dot_columns(left, right):
    return lax.dot_general(left, right, (((0,), (0,)), ((), ())), preferred_element_type=single)


def backward_kernel(
    mid_grad_ref,
    one_ref,
    hidden_ref,
    mid_ref,
    gains_ref,
    query_ref,
    pre_ref,
    marks_ref,
    small_ref,
    peak_ref,
    normed_hbm,
    attended_hbm,
    dense_normed_hbm,
    act_hbm,
    qkv0_hbm,
    qkv1_hbm,
    proj0_hbm,
    proj1_hbm,
    up_hbm,
    down_hbm,
    kv_hbm,
    probs_hbm,
    up_grad_hbm,
    hidden_grad_out,
    att_out,
    up_out,
    down_out,
    small_out,
    late_out,
    peak_out,
    expert_up_out,
    w_wide,
    w_down,
    kv,
    probs,
    xg,
    gx,
    gsrc,
    zb,
    zin,
    zb_down,
    zin_down,
    slopes,
    score_low,
    dk,
    cin,
    rin,
    attended_grad,
    layer_grad,
    biases,
    early,
    early_z,
    early_p,
    early_m,
    late,
    late_z,
    late_p,
    late_m,
    peak_z,
    peak_p,
    peak_m,
    gs,
    gr,
    xs,
    xr,
    zs,
    zr,
    dcs,
    dcr,
    drs,
    drr,
    szs,
    szr,
    sps,
    spr,
    us,
    ur,
    loads,
):
    p = Plane()
    e, s, core = p.e, p.s, p.core
    own_rows = row_block(e, T)

    def load(source, target, i):
        copy = pltpu.make_async_copy(source, target, loads.at[i])
        copy.start()
        return copy

    own_parts = [
        load(source, xg.at[n, own_rows, :], 11 + n)
        for n, source in enumerate(
            (
                normed_hbm.at[1],
                attended_hbm.at[1],
                normed_hbm.at[0],
                attended_hbm.at[0],
                dense_normed_hbm,
            )
        )
    ]
    own_act = load(act_hbm.at[:, lane_block(e, 384)], gx.at[3, own_rows, :], 16)
    greet([(d, s) for d in p.around] + [(e, other) for other in p.others])

    w_qkv = w_wide.at[:, : 3 * D]
    w_out = w_wide.at[:, 3 * D :]
    got_out = load(proj1_hbm, w_out, 0)
    got_kv = load(kv_hbm.at[1], kv, 2)
    got_probs = load(probs_hbm.at[1], probs, 3)
    got_qkv = load(qkv1_hbm, w_qkv, 1)
    got_down = load(down_hbm, w_down, 5)

    peaks = SmallReduce(
        p, peak_ref, peak_z, peak_p, jnp.maximum, (szs.at[0], szr.at[0], sps.at[0], spr.at[0])
    )
    peaks.start()

    def rows_gather(n):
        return PlaneGather(
            p, lambda who: xg.at[n, row_block(who, T), :], gs.at[n], gr.at[n]
        )

    gathers = [rows_gather(n) for n in range(6)]
    for copy in own_parts:
        copy.wait()
    gathers[0].first()
    gathers[1].first()

    exchanges = {}

    def exchange_start(j, source):
        if j == 3:
            own_act.wait()
        else:
            gx[j, own_rows, :] = source[:, lane_block(e, 384)]
        for k, d in enumerate(p.around):
            p.push(
                source.at[:, lane_block(d, 384)],
                gx.at[j, own_rows, :],
                xs.at[j, k],
                xr.at[j, k],
                (d, s),
            )

    def exchange_wait(j):
        for k in range(7):
            p.arrived(gx.at[j, own_rows, :], xr.at[j, k])

    def out_gather(j, target, height):
        return PlaneGather(
            p, lambda who: target.at[pl.ds(who, 1)], gs.at[6 + j], gr.at[6 + j]
        )

    def z_start(j, tile, received, height):
        for k in range(3):
            p.push(
                tile.at[row_block(p.others[k], height), :],
                received.at[k],
                zs.at[j, k],
                zr.at[j, k],
                (e, p.others[k]),
            )

    def z_finish(j, tile, received, height, target):
        total = tile[row_block(s, height), :].astype(single)
        for k in range(3):
            p.arrived(received.at[k], zr.at[j, k])
            total = total + received[k].astype(single)
        target[pl.ds(e, 1)] = total.astype(bfloat)[None]

    def tile_attention(layer):
        j = 1 - layer
        exchange_wait(j)
        rows = xg[2 * j + e // 6]
        for part in range(3):
            lanes = slice(128 * part, 128 * (part + 1))
            zb[j, :, lanes] = dot_columns(rows, gx[j, :, lanes]).astype(bfloat)
        z_start(j, zb.at[j], zin.at[j], 192)

    def tile_up():
        exchange_wait(2)
        for part in range(3):
            lanes = slice(128 * part, 128 * (part + 1))
            zb[2, :, lanes] = dot_columns(xg[4], gx[2, :, lanes]).astype(bfloat)
        z_start(2, zb.at[2], zin.at[2], 192)

    def tile_down():
        exchange_wait(3)
        for part in range(3):
            lanes = slice(128 * part, 128 * (part + 1))
            zb_down[lanes, :] = dot_columns(gx[3, :, lanes], xg[5]).astype(bfloat)
        z_start(3, zb_down, zin_down, 96)

    gather_att1 = out_gather(0, att_out.at[1], 192)
    gather_att0 = out_gather(1, att_out.at[0], 192)
    gather_up = out_gather(2, up_out, 192)
    gather_down = out_gather(3, down_out, 96)

    scale = 1.0 / math.sqrt(HD)

    def attention(layer, upstream, work):
        j = 1 - layer
        grads = gsrc.at[j]
        branch = upstream.astype(bfloat)
        grads[:, 3 * D :] = branch
        got_out_now = got_out if layer == 1 else reloads["out"]
        got_out_now.wait()
        attended_grad[...] = dot_rows(branch, w_out[...]).astype(bfloat)
        if layer == 1:
            got_kv.wait()
            got_probs.wait()
        else:
            reloads["kv"].wait()
            reloads["probs"].wait()
            for copy in dk_sent:
                copy.wait_send()
            dk_sent.clear()

        def first_step(part):
            push(
                dk_sent,
                dk.at[part, 1 - core],
                cin.at[layer, part],
                dcs.at[layer, part],
                dcr.at[layer, part],
                (p.at_core, s),
            )

        def second_step(part):
            p.arrived(cin.at[layer, part], dcr.at[layer, part])
            for q in range(4):
                dk[part, core, q] = (
                    dk[part, core, q].astype(single) + cin[layer, part, q].astype(single)
                ).astype(bfloat)
            for k, d in enumerate((p.at_x, p.at_y, p.diagonal)):
                push(
                    dk_sent,
                    dk.at[part, core, d // 2],
                    rin.at[layer, part, k],
                    drs.at[layer, part, k],
                    drr.at[layer, part, k],
                    (d, s),
                )

        def third_step(part):
            total = dk[part, core, p.quarter].astype(single)
            for k in range(3):
                p.arrived(rin.at[layer, part, k], drr.at[layer, part, k])
                total = total + rin[layer, part, k].astype(single)
            turned = total.T.astype(bfloat)
            grads[:, D + 256 * part : D + 256 * (part + 1)] = turned[:, :256]
            grads[:, 2 * D + 256 * part : 2 * D + 256 * (part + 1)] = turned[:, 256:]

        for part in range(3):

            def one_pair(local_pair):
                pair = 2 * part + local_pair
                lanes = lane_block(pair, 128)
                lane = lax.broadcasted_iota(jnp.int32, (T, 128), 1)

                def split(value):
                    zero = jnp.zeros_like(value)
                    return jnp.concatenate(
                        [jnp.where(lane < HD, value, zero), jnp.where(lane >= HD, value, zero)]
                    )

                queries = split(query_ref[layer, :, lanes])
                outputs = split(attended_grad[:, lanes])
                keys = kv[part, :, lane_block(local_pair, 128)]
                values = kv[part, :, pl.ds(pl.multiple_of(256 + local_pair * 128, 128), 128)]
                slopes[...] = dot_rows(outputs, values)
                pair_rows = pl.ds(pl.multiple_of(pair * 2 * T, 2 * T), 2 * T)
                for half in range(2):
                    head = 2 * pair + half
                    gathered = jnp.zeros((8, TOE), single)
                    for rows in range(0, T, 32):
                        at = half * T + rows
                        prob = probs[
                            pl.ds(pl.multiple_of(head * T + rows, 32), 32), :
                        ].astype(single)
                        slope = slopes[at : at + 32, :]
                        inner = jnp.sum(prob * slope, axis=-1, keepdims=True)
                        low = (prob * (slope - inner)).astype(bfloat)
                        score_low[at : at + 32, :] = low
                        fold = jnp.concatenate(
                            [low.astype(single), jnp.zeros((32, TOE - low.shape[1]), single)],
                            axis=1,
                        )
                        fold = pltpu.roll(fold[:16], 16, 1) + fold[16:]
                        fold = pltpu.roll(fold[:8], 8, 1) + fold[8:]
                        if rows < T - 32:
                            fold = pltpu.roll(fold, T - 32 - rows, 1)
                        gathered = gathered + fold
                    fold = pltpu.roll(gathered[:4], 4, 1) + gathered[4:]
                    fold = pltpu.roll(fold[:2], 2, 1) + fold[2:]
                    fold = pltpu.roll(fold[:1], 1, 1) + fold[1:]
                    biases[pl.ds(layer * H + head, 1), :] = fold
                mixed = jnp.dot(score_low[...], keys, preferred_element_type=single) * scale
                grads[:, lanes] = jnp.where(lane < HD, mixed[:T], mixed[T:]).astype(bfloat)
                key_grad = dot_columns(queries, score_low[...]) * scale
                value_grad = dot_columns(outputs, probs[pair_rows, :])
                for d in range(8):
                    columns = slice(128 * d, 128 * (d + 1))
                    dk[
                        part, d % 2, d // 2, pl.ds(pl.multiple_of(local_pair * 128, 128), 128), :
                    ] = key_grad[:, columns].astype(bfloat)
                    dk[
                        part,
                        d % 2,
                        d // 2,
                        pl.ds(pl.multiple_of(256 + local_pair * 128, 128), 128),
                        :,
                    ] = value_grad[:, columns].astype(bfloat)

            loop(2, one_pair)
            first_step(part)
            if part > 0:
                second_step(part - 1)
            work[part]()
        second_step(2)
        third_step(0)
        work[3]()
        third_step(1)
        third_step(2)
        exchange_start(j, gsrc.at[j])
        if layer == 1:
            got_qkv.wait()
        else:
            reloads["qkv"].wait()
        return dot_rows(gsrc[j, :, : 3 * D], w_qkv[...])

    dk_sent = []
    reloads = {}

    def part0():
        gathers[0].second()
        gathers[1].second()
        exchange_start(3, act_hbm)
        gathers[4].first()
        for k in range(3):
            reshard.append(
                p.push(
                    up_grad_hbm.at[:, row_block(p.others[k], 192), :],
                    expert_up_out.at[:, :, lane_block(s, 768)],
                    us.at[k],
                    ur.at[k],
                    (e, p.others[k]),
                )
            )
        reshard_own.append(
            load(
                up_grad_hbm.at[:, row_block(s, 192), :],
                expert_up_out.at[:, :, lane_block(s, 768)],
                6,
            )
        )

    def part1():
        gathers[0].third()
        gathers[1].third()
        peaks.middle(peak_m)

    def part2():
        gathers[4].second()
        gathers[2].first()
        gathers[3].first()

    def part3():
        gathers[4].third()
        peaks.finish(peak_m, peak_out)

    reshard, reshard_own = [], []
    mid_grad = mid_grad_ref[...]
    normed_grad = attention(1, mid_grad, [part0, part1, part2, part3])
    reloads["kv"] = load(kv_hbm.at[0], kv, 7)
    reloads["probs"] = load(probs_hbm.at[0], probs, 8)
    got_up = load(up_hbm, w_wide, 4)
    input_grad, gain_grad = norm_pull(one_ref[...], gains_ref[1:2, :], normed_grad)
    early[...] = small_ref[...]
    early[17:18, :] = gain_grad
    layer_grad[...] = mid_grad + input_grad
    branch = layer_grad[...].astype(bfloat)
    xg[5, own_rows, :] = branch
    gathers[5].first()
    got_down.wait()

    def slope_part(i):
        lanes = lane_block(i, 512)
        act_grad = dot_rows(xg[5, own_rows, :], w_down[row_block(i, 512), :])
        gsrc[2, :, lanes] = (act_grad * gelu_slope(pre_ref[:, lanes])).astype(bfloat)

    loop(6, slope_part)
    exchange_start(2, gsrc.at[2])
    gathers[2].second()
    gathers[3].second()
    gathers[5].second()
    got_up.wait()
    dense_grad = dot_rows(gsrc[2], w_wide[...])
    reloads["out"] = load(proj0_hbm, w_out, 9)
    reloads["qkv"] = load(qkv0_hbm, w_qkv, 10)
    input_grad, gain_grad = norm_pull(mid_ref[...], gains_ref[2:3, :], dense_grad)
    early[18:19, :] = gain_grad
    layer_grad[...] = layer_grad[...] + input_grad
    small = SmallReduce(
        p, early, early_z, early_p, jnp.add, (szs.at[1], szr.at[1], sps.at[1], spr.at[1])
    )
    small.start()
    gathers[0].done()
    gathers[1].done()
    tile_attention(1)

    def part4():
        gathers[5].third()
        gathers[2].third()
        gathers[3].third()
        gathers[4].done()
        tile_up()

    def part5():
        gathers[5].done()
        tile_down()
        z_finish(0, zb.at[0], zin.at[0], 192, att_out.at[1])
        gather_att1.first()
        small.middle(early_m)

    def part6():
        z_finish(2, zb.at[2], zin.at[2], 192, up_out)
        gather_up.first()
        gather_att1.second()

    def part7():
        z_finish(3, zb_down, zin_down, 96, down_out)
        gather_down.first()
        gather_up.second()
        gather_att1.third()

    normed_grad = attention(0, layer_grad[...], [part4, part5, part6, part7])
    input_grad, gain_grad = norm_pull(
        hidden_ref[...].astype(single), gains_ref[0:1, :], normed_grad
    )
    hidden_grad_out[...] = layer_grad[...] + input_grad
    late[...] = jnp.zeros_like(late)
    for i in range(6):
        late[i : i + 1, :] = gain_grad[:, 128 * i : 128 * (i + 1)]
    late[8:32, :NB] = lax.dot_general(
        biases[...],
        marks_ref[...].astype(single),
        (((1,), (1,)), ((), ())),
        precision=lax.Precision.HIGHEST,
        preferred_element_type=single,
    )
    tail = SmallReduce(
        p, late, late_z, late_p, jnp.add, (szs.at[2], szr.at[2], sps.at[2], spr.at[2])
    )
    tail.start()
    gathers[2].done()
    gathers[3].done()
    tile_attention(0)
    gather_down.second()
    gather_up.third()
    small.finish(early_m, small_out)
    gather_down.third()
    tail.middle(late_m)
    z_finish(1, zb.at[1], zin.at[1], 192, att_out.at[0])
    gather_att0.first()
    gather_att1.done()
    gather_up.done()
    gather_down.done()
    gather_att0.second()
    gather_att0.third()
    tail.finish(late_m, late_out)
    for copy in reshard:
        copy.wait_recv()
    reshard_own[0].wait()
    gather_att0.done()
    for copy in p.sent + dk_sent:
        copy.wait_send()


def backward(
    mid_grad, layer_one, hidden, mid, gains, normed, queries, attended, dense_normed, act, pre_act,
    marks, small, peak_rows, weights, kv, probs, up_grad,
):
    length = T * lax.axis_size("expert")
    vmem = pl.BlockSpec(memory_space=VMEM)
    anywhere = pl.BlockSpec(memory_space=ANY)
    shape = jax.ShapeDtypeStruct
    ff = pre_act.shape[1]
    sem = pltpu.SemaphoreType.DMA
    peak_shape, early_shape, late_shape = (2 * H, 128), small.shape, (32, 128)
    return pl.pallas_call(
        backward_kernel,
        name="backward_layers",
        out_shape=(
            shape((T, D), single),
            shape((2, 8, 192, 384), bfloat),
            shape((8, 192, 384), bfloat),
            shape((8, 96, D), bfloat),
            shape(early_shape, single),
            shape(late_shape, single),
            shape(peak_shape, single),
            shape((EXP_DEV, 192, ff), bfloat),
        ),
        in_specs=[vmem] * 10 + [anywhere] * 13,
        out_specs=(vmem,) * 7 + (anywhere,),
        scratch_shapes=[
            VMEM((D, ff), bfloat),
            VMEM((ff, D), bfloat),
            VMEM((3, length, 512), bfloat),
            VMEM((H * T, length), bfloat),
            VMEM((6, length, D), bfloat),
            VMEM((4, length, 384), bfloat),
            VMEM((3, T, 4 * D), bfloat),
            VMEM((3, D, 384), bfloat),
            VMEM((3, 3, 192, 384), bfloat),
            VMEM((384, D), bfloat),
            VMEM((3, 96, D), bfloat),
            VMEM((2 * T, length), single),
            VMEM((2 * T, length), bfloat),
            VMEM((3, 2, 4, 512, 128), bfloat),
            VMEM((2, 3, 4, 512, 128), bfloat),
            VMEM((2, 3, 3, 512, 128), bfloat),
            VMEM((T, D), bfloat),
            VMEM((T, D), single),
            VMEM((2 * H, TOE), single),
            VMEM(early_shape, single),
            VMEM((3,) + early_shape, single),
            VMEM((7,) + early_shape, single),
            VMEM(early_shape, single),
            VMEM(late_shape, single),
            VMEM((3,) + late_shape, single),
            VMEM((7,) + late_shape, single),
            VMEM(late_shape, single),
            VMEM((3,) + peak_shape, single),
            VMEM((7,) + peak_shape, single),
            VMEM(peak_shape, single),
            sem((10, 7)), sem((10, 7)),
            sem((4, 7)), sem((4, 7)),
            sem((4, 3)), sem((4, 3)),
            sem((2, 3)), sem((2, 3)),
            sem((2, 3, 3)), sem((2, 3, 3)),
            sem((3, 3)), sem((3, 3)),
            sem((3, 7)), sem((3, 7)),
            sem((3,)), sem((3,)),
            sem((17,)),
        ],
        compiler_params=pltpu.CompilerParams(
            collective_id=3, has_side_effects=True, vmem_limit_bytes=60 * 2**20
        ),
    )(
        mid_grad, layer_one, hidden, mid, gains, queries, pre_act, marks, small, peak_rows, normed,
        attended, dense_normed, act, *weights, kv, probs, up_grad,
    )


def experts_kernel(
    normed_ref,
    mid_ref,
    gains_ref,
    router_ref,
    router_turned_ref,
    slots_ref,
    slot_columns_ref,
    own_cot_ref,
    cot_hbm,
    up_hbm,
    down_hbm,
    hidden_out,
    mid_grad_out,
    small_out,
    up_grad_out,
    down_grad_out,
    normed_all,
    cots,
    w_up,
    w_down,
    rows,
    gated,
    gates,
    acts,
    pre_grads,
    raw,
    row_send,
    out_send,
    row_back,
    out_back,
    slot_grads,
    slot_z,
    slot_sum,
    slot_plane,
    row_part,
    out_part,
    row_z,
    out_z,
    ns,
    nr,
    gs,
    gr,
    rs,
    rr,
    os,
    orr,
    ss,
    sr,
    ps,
    pr,
    rzs,
    rzr,
    ozs,
    ozr,
    loads,
):
    p = Plane()
    e, s = p.e, p.s
    groups = [s] + [lax.rem(s + 4 - k, 4) for k in range(1, 4)]

    def load(source, target, i):
        copy = pltpu.make_async_copy(source, target, loads.at[i])
        copy.start()
        return copy

    got_cots = [load(cot_hbm.at[groups[k]], cots.at[k], k) for k in range(2)]
    got_up = load(up_hbm, w_up, 4)
    got_down = load(down_hbm, w_down, 5)
    normed_all[s, e] = normed_ref[...]
    greet([(d, s) for d in p.around] + [(e, other) for other in p.others])
    mine = normed_all.at[s, e]
    for k in range(3):
        p.push(mine, mine, ns.at[k], nr.at[k], (e, p.others[k]))

    def gather(k):
        g = groups[k]
        return PlaneGather(p, lambda who: normed_all.at[g, who], gs.at[k], gr.at[k])

    gathers = [gather(k) for k in range(4)]
    gathers[0].first()

    ids = 2 * e * CAP + lax.broadcasted_iota(jnp.int32, (2 * CAP, T), 0)
    expert_low = CAP * lax.broadcasted_iota(jnp.int32, (16, T), 0)

    def route_masks(g, who):
        at = (g * 8 + who) * 2
        first, second = slots_ref[pl.ds(at, 1), :], slots_ref[pl.ds(at + 1, 1), :]
        return first, second, ids == first, ids == second

    def select_cots(k):
        g = groups[k]
        got_cots[k].wait()

        def one(who):
            _, _, mark0, mark1 = route_masks(g, who)
            mark = jnp.where(mark0 | mark1, 1.0, 0.0).astype(bfloat)
            picked = jnp.dot(mark, cots[k % 2, who], preferred_element_type=single).astype(bfloat)
            for j in range(2):
                raw[j, g, row_block(who, CAP), :] = picked[j * CAP : (j + 1) * CAP]

        loop(8, one)
        if k < 2:
            got_cots.append(load(cot_hbm.at[groups[k + 2]], cots.at[k], k + 2))

    def select_rows(k):
        g = groups[k]

        def one(who):
            slot0, slot1, mark0, mark1 = route_masks(g, who)
            block = normed_all[g, who]
            mark = jnp.where(mark0 | mark1, 1.0, 0.0).astype(bfloat)
            picked = jnp.dot(mark, block, preferred_element_type=single).astype(bfloat)
            logits = dot_rows(router_turned_ref[...], block)
            chosen = [
                jnp.sum(
                    jnp.where((slot >= expert_low) & (slot < expert_low + CAP), logits, 0.0),
                    axis=0,
                    keepdims=True,
                )
                for slot in (slot0, slot1)
            ]
            top = jnp.maximum(chosen[0], chosen[1])
            weight = [jnp.exp(value - top) for value in chosen]
            total = weight[0] + weight[1]
            gate = jnp.sum(
                jnp.where(mark0, weight[0] / total, 0.0) + jnp.where(mark1, weight[1] / total, 0.0),
                axis=1,
                keepdims=True,
            )
            for j in range(2):
                part = slice(j * CAP, (j + 1) * CAP)
                rows[j, g, row_block(who, CAP), :] = picked[part]
                gates[j, g, row_block(who, CAP), :] = jnp.broadcast_to(gate[part], (CAP, 128))

        loop(8, one)

    def compute(k):
        g = groups[k]

        def one(j):
            before = jnp.dot(rows[j, g], w_up[j], preferred_element_type=single)
            act = jax.nn.gelu(before).astype(bfloat)
            acts[j, g] = act
            gate = gates[j, g][:, :1]
            cot = raw[j, g].astype(single)
            weighted = (gate * cot).astype(bfloat)
            gated[j, g] = weighted
            act_grad = dot_rows(weighted, w_down[j])
            pre_grad = (act_grad * gelu_slope(before)).astype(bfloat)
            pre_grads[j, g] = pre_grad
            row_grad = dot_rows(pre_grad, w_up[j])
            row_send[g, j] = row_grad.astype(bfloat).reshape(8, CAP, D)
            out = jnp.dot(act, w_down[j], preferred_element_type=single)
            out_send[g, j] = (gate * out).astype(bfloat).reshape(8, CAP, D)
            slot_grads[g, pl.ds(j, 1), :] = lax.dot_general(
                jnp.ones((8, D), single),
                out * cot,
                (((1,), (1,)), ((), ())),
                precision=lax.Precision.HIGHEST,
                preferred_element_type=single,
            )[:1]

        loop(2, one)

    def give_back(k, source, target, send_sems, recv_sems):
        g = groups[k]
        target[g, e] = source[g, :, e]
        for i, d in enumerate(p.around):
            p.push(
                source.at[g, :, d], target.at[g, e], send_sems.at[k, i], recv_sems.at[k, i], (d, s)
            )

    def step(k):
        select_rows(k)
        compute(k)
        give_back(k, row_send, row_back, rs, rr)

    def arrive(k):
        p.arrived(mine, nr.at[k - 1])
        gathers[k].first()

    slot_grads[...] = jnp.zeros_like(slot_grads)
    select_cots(0)
    gathers[0].second()
    arrive(1)
    gathers[0].third()
    gathers[1].second()
    arrive(2)
    gathers[0].done()
    gathers[1].third()
    gathers[2].second()
    arrive(3)
    got_up.wait()
    got_down.wait()
    step(0)
    gathers[2].third()
    gathers[3].second()
    select_cots(1)
    gathers[1].done()
    step(1)
    gathers[3].third()
    select_cots(2)
    gathers[2].done()
    step(2)
    select_cots(3)
    gathers[3].done()
    step(3)
    for k in range(4):
        give_back(k, out_send, out_back, os, orr)
    for k in range(3):
        p.push(
            slot_grads.at[p.others[k]], slot_z.at[k], ss.at[k], sr.at[k], (e, p.others[k])
        )

    def weight_grads(i):
        j = i // 3
        lanes = lane_block(lax.rem(i, 3), 256)
        inputs = rows[j].reshape(4 * 8 * CAP, D)
        up_grad_out[j, :, lanes] = dot_columns(
            inputs, pre_grads[j, :, :, lanes].reshape(4 * 8 * CAP, 256)
        ).astype(bfloat)
        inputs = acts[j].reshape(4 * 8 * CAP, -1)
        down_grad_out[j, :, lanes] = dot_columns(
            inputs, gated[j, :, :, lanes].reshape(4 * 8 * CAP, 256)
        )

    loop(3, weight_grads)
    total = slot_grads[s]
    for k in range(3):
        p.arrived(slot_z.at[k], sr.at[k])
        total = total + slot_z[k]
    slot_sum[...] = total
    slot_plane[e] = total
    for i, d in enumerate(p.around):
        p.push(slot_sum, slot_plane.at[e], ps.at[i], pr.at[i], (d, s))

    slot_lanes = lax.broadcasted_iota(jnp.int32, (T, 16 * CAP), 1)

    def collect(k, back, recv_sems, part, z_in, z_send, z_recv):
        g = groups[k]
        for i in range(7):
            p.arrived(back.at[g, e], recv_sems.at[k, i])
        columns = slot_columns_ref[g]
        marks = jnp.where(
            (columns[:, :1] == slot_lanes) | (columns[:, 1:2] == slot_lanes), 1.0, 0.0
        ).astype(bfloat)
        combined = jnp.dot(
            marks, back[g].reshape(16 * CAP, D), preferred_element_type=single
        )
        part[g] = combined.astype(bfloat)
        if k:
            p.push(part.at[g], z_in.at[k - 1], z_send.at[k - 1], z_recv.at[k - 1], (e, g))

    for k in (1, 2, 3, 0):
        collect(k, row_back, rr, row_part, row_z, rzs, rzr)

    def weight_later(i):
        weight_grads(i + 3)

    loop(3, weight_later)

    for i in range(7):
        p.arrived(slot_sum, pr.at[i])
    turned = pltpu.roll(
        slot_plane[...].reshape(64, 8 * CAP), lax.rem(8 * CAP - CAP * e, 8 * CAP), 1
    )
    logits = jnp.dot(normed_ref[...], router_ref[...], preferred_element_type=single)
    columns = slot_columns_ref[s]
    expert_lanes = CAP * lax.broadcasted_iota(jnp.int32, (T, 16), 1)
    picks, chosen, grads = [], [], []
    small_lanes = lax.broadcasted_iota(jnp.int32, (T, CAP), 1)
    for r in range(2):
        slot = columns[:, r : r + 1]
        picks.append((slot >= expert_lanes) & (slot < expert_lanes + CAP))
        chosen.append(jnp.sum(jnp.where(picks[r], logits, 0.0), axis=1, keepdims=True))
        found = jnp.zeros((T, CAP), single)
        for who in range(8):
            for j in range(2):
                values = turned[8 * who + j : 8 * who + j + 1, :CAP]
                found = found + jnp.where(slot - (2 * who + j) * CAP == small_lanes, values, 0.0)
        grads.append(jnp.sum(found, axis=1, keepdims=True))
    top = jnp.maximum(chosen[0], chosen[1])
    weight = [jnp.exp(value - top) for value in chosen]
    total = weight[0] + weight[1]
    weight = [value / total for value in weight]
    mean = weight[0] * grads[0] + weight[1] * grads[1]
    logit_grad = jnp.zeros((T, 16), single)
    for r in range(2):
        logit_grad = logit_grad + jnp.where(picks[r], weight[r] * (grads[r] - mean), 0.0)
    logit_grad = logit_grad.astype(bfloat)
    small_out[...] = jnp.zeros_like(small_out)
    small_out[:16, :] = dot_columns(logit_grad, normed_ref[...])
    normed_grad = jnp.dot(logit_grad, router_turned_ref[...], preferred_element_type=single)
    normed_grad = normed_grad + row_part[s].astype(single)
    for k in range(3):
        p.arrived(row_z.at[k], rzr.at[k])
        normed_grad = normed_grad + row_z[k].astype(single)
    input_grad, gain_grad = norm_pull(mid_ref[...], gains_ref[3:4, :], normed_grad)
    small_out[16:17, :] = gain_grad
    mid_grad_out[...] = own_cot_ref[...].astype(single) + input_grad

    for k in (1, 2, 3, 0):
        collect(k, out_back, orr, out_part, out_z, ozs, ozr)
    result = mid_ref[...] + out_part[s].astype(single)
    for k in range(3):
        p.arrived(out_z.at[k], ozr.at[k])
        result = result + out_z[k].astype(single)
    hidden_out[...] = result.astype(bfloat)
    for copy in p.sent:
        copy.wait_send()


def run_experts(
    normed, mid, gains, router, slots, slot_columns, own_cot, cots, up_own, expert_down
):
    vmem = pl.BlockSpec(memory_space=VMEM)
    anywhere = pl.BlockSpec(memory_space=ANY)
    shape = jax.ShapeDtypeStruct
    width = expert_down.shape[1]
    sem = pltpu.SemaphoreType.DMA
    per_expert = (EXP_DEV, 4, 8 * CAP)
    sends = (4, EXP_DEV, 8, CAP, D)
    backs = (4, 8, EXP_DEV, CAP, D)
    return pl.pallas_call(
        experts_kernel,
        name="experts",
        out_shape=(
            shape((T, D), bfloat),
            shape((T, D), single),
            shape((24, D), single),
            shape((EXP_DEV, D, width), bfloat),
            shape((EXP_DEV, width, D), single),
        ),
        in_specs=[vmem] * 8 + [anywhere] * 3,
        out_specs=(vmem,) * 5,
        scratch_shapes=[
            VMEM((4, 8, T, D), bfloat),
            VMEM((2, 8, T, D), bfloat),
            VMEM((EXP_DEV, D, width), bfloat),
            VMEM((EXP_DEV, width, D), bfloat),
            VMEM(per_expert + (D,), bfloat),
            VMEM(per_expert + (D,), bfloat),
            VMEM(per_expert + (128,), single),
            VMEM(per_expert + (width,), bfloat),
            VMEM(per_expert + (width,), bfloat),
            VMEM(per_expert + (D,), bfloat),
            VMEM(sends, bfloat),
            VMEM(sends, bfloat),
            VMEM(backs, bfloat),
            VMEM(backs, bfloat),
            VMEM((4, 8, 8 * CAP), single),
            VMEM((3, 8, 8 * CAP), single),
            VMEM((8, 8 * CAP), single),
            VMEM((8, 8, 8 * CAP), single),
            VMEM((4, T, D), bfloat),
            VMEM((4, T, D), bfloat),
            VMEM((3, T, D), bfloat),
            VMEM((3, T, D), bfloat),
            sem((3,)), sem((3,)),
            sem((4, 7)), sem((4, 7)),
            sem((4, 7)), sem((4, 7)),
            sem((4, 7)), sem((4, 7)),
            sem((3,)), sem((3,)),
            sem((7,)), sem((7,)),
            sem((3,)), sem((3,)),
            sem((3,)), sem((3,)),
            sem((6,)),
        ],
        compiler_params=pltpu.CompilerParams(
            collective_id=4, has_side_effects=True, vmem_limit_bytes=60 * 2**20
        ),
    )(
        normed, mid, gains, router, router.T, slots, slot_columns, own_cot, cots, up_own,
        expert_down,
    )


def shards(
    hidden_in,
    attn_gain,
    qkv_weight,
    out_weight,
    rel_bias,
    bucket_table,
    mlp_gain,
    mlp_up,
    mlp_down,
    router_weight,
    expert_up,
    expert_down,
    routes,
    out_grad,
):
    block_rows = hidden_in.shape[1]
    length = bucket_table.shape[0]
    experts = lax.axis_size("expert")
    groups = lax.axis_size("shard")
    here = lax.axis_index("shard")
    expert_total = EXP_DEV * experts
    capacity = 4 * block_rows // expert_total

    expert_ids = jnp.arange(expert_total, dtype=jnp.int32)
    flat_routes = routes.reshape(-1)
    marks = (flat_routes[:, None] == expert_ids).astype(bfloat)
    earlier = jnp.tri(2 * block_rows, k=-1, dtype=bfloat)
    rank = jnp.sum(matmul(earlier, marks) * marks.astype(single), axis=1).astype(jnp.int32)
    slots = (flat_routes * capacity + rank).reshape(block_rows, 2).T

    small = jnp.concatenate(
        [attn_gain.reshape(-1), mlp_gain.reshape(-1), rel_bias.reshape(-1), router_weight.reshape(-1)]
    ).astype(single)
    part = D // groups
    used = small.shape[0]
    small = jnp.pad(small, (0, -used % 1024)).reshape(-1, 128)
    small, slots_all = gather_small(small, slots)
    slot_columns = lax.dynamic_index_in_dim(
        slots_all, lax.axis_index("expert"), 1, keepdims=False
    ).transpose(0, 2, 1)
    small = small.reshape(groups, -1)
    cuts = [0, 4 * part, 4 * part + 2 * (NB // groups) * H, used]
    gains, bias_weights, router_full = (small[:, cuts[i] : cuts[i + 1]] for i in range(3))
    gains = gains.reshape(groups, 4, part).transpose(1, 0, 2).reshape(4, D)
    bias_weights = (
        bias_weights.reshape(groups, 2, NB // groups, H).transpose(1, 0, 2, 3).reshape(2, NB, H)
    )
    router_full = router_full.reshape(D, expert_total).astype(bfloat)

    distances = lax.axis_index("expert") * block_rows + block_rows - 1 - jnp.arange(TOE)
    buckets = jnp.take(bucket_table, jnp.clip(distances, 0, length - 1))
    toeplitz_marks = (buckets[None] == jnp.arange(NB, dtype=jnp.int32)[:, None]).astype(bfloat)
    table = jnp.einsum(
        "lbh,bm->lhm", bias_weights.astype(bfloat), toeplitz_marks, preferred_element_type=single
    ).reshape(2 * H, TOE)

    (
        normed, queries, attended, mid, dense_normed, pre_act, activation, layer_one, peak_rows,
        moe_normed, qkv0, qkv1, projection0, projection1, dense_up, dense_down, kv, probs, up_own,
        upstream_all,
    ) = forward(
        hidden_in.reshape(block_rows, D), gains, table, qkv_weight, out_weight, mlp_up, mlp_down,
        expert_up, out_grad.reshape(block_rows, D),
    )
    hidden_out, mid_grad, small_in, up_grad, expert_down_grad = run_experts(
        moe_normed, mid[1], gains, router_full, slots_all.reshape(-1, block_rows), slot_columns,
        out_grad.reshape(block_rows, D), upstream_all, up_own, expert_down,
    )
    hidden_grad, attention_sum, up_sum, down_sum, small_sum, late_sum, peaks, expert_up_low = (
        backward(
            mid_grad, layer_one, hidden_in.reshape(block_rows, D), mid[0], gains, normed, queries,
            attended, dense_normed, spread(activation), pre_act, toeplitz_marks, small_in,
            peak_rows, (qkv0, qkv1, projection0, projection1, dense_up, dense_down), kv, probs,
            up_grad,
        )
    )
    attention_sum = (
        attention_sum.transpose(0, 2, 1, 3).reshape(2, part, 4 * D).astype(single)
    )
    mlp_up_grad = up_sum.transpose(1, 0, 2).reshape(part, -1).astype(single)
    mlp_down_grad = down_sum.reshape(-1, D).astype(single)

    def columns(rows):
        return lax.dynamic_slice_in_dim(rows, here * part, part, rows.ndim - 1)

    first_gain = late_sum[:6].reshape(1, D)
    rows = columns(small_sum)
    gain_rows = columns(first_gain)
    biases = lax.dynamic_slice_in_dim(late_sum[8:32], here * (NB // groups), NB // groups, 1)
    clip_scales = jnp.sqrt(clip_limit / jnp.maximum(peaks[:, 0].reshape(2, H), clip_limit))
    return (
        hidden_out.reshape(hidden_in.shape),
        hidden_grad.reshape(hidden_in.shape),
        jnp.concatenate([gain_rows, rows[expert_total + 1 : expert_total + 2]]),
        attention_sum[:, :, : 3 * D],
        attention_sum[:, :, 3 * D :],
        biases.reshape(2, H, NB // groups).transpose(0, 2, 1),
        jnp.stack([rows[expert_total + 2], rows[expert_total]]),
        mlp_up_grad,
        mlp_down_grad,
        rows[:expert_total].T,
        expert_up_low.astype(single),
        expert_down_grad,
        clip_scales,
    )


def solution(mesh):
    tokens = P("shard", "expert", None, None)
    columns = P(None, "shard")
    layers = P(None, "shard", None)
    rows = P("shard", None)
    owned = P("expert", "shard", None)
    in_specs = (
        tokens, columns, layers, layers, layers, P(), columns, rows, rows, rows, owned, owned,
        tokens, tokens,
    )
    out_specs = (
        tokens, tokens, columns, layers, layers, layers, columns, rows, rows, rows, owned, owned,
        P(),
    )
    sized = mesh.shape["expert"] == 8 and mesh.shape["shard"] == 4
    part = shards if sized else plain_shards
    return jax.shard_map(part, mesh=mesh, in_specs=in_specs, out_specs=out_specs, check_vma=False)
```

```python
import functools
import math

import jax
import jax.numpy as jnp
from jax import lax
from jax.experimental import pallas as pl
from jax.experimental.pallas import tpu as pltpu
from jax.sharding import PartitionSpec as P

D = 768
H = 12
HD = 64
NB = 32
EXP_DEV = 2

epsilon = 1e-06
clip_limit = 6.0
bfloat = jnp.bfloat16
single = jnp.float32


def rms_norm(inputs, norm_gain):
    return (
        inputs * lax.rsqrt(jnp.mean(inputs * inputs, axis=-1, keepdims=True) + epsilon) * norm_gain
    )


def norm_back(inputs, norm_gain, upstream):
    _, pullback = jax.vjp(rms_norm, inputs, norm_gain)
    return pullback(upstream)


def gelu_back(pre_values, upstream):
    _, pullback = jax.vjp(jax.nn.gelu, pre_values)
    return pullback(upstream)[0]


def matmul(left, right):
    return jnp.dot(left, right, preferred_element_type=single)


def shard_shift(block, amount):
    count = lax.axis_size("shard")
    return lax.ppermute(block, "shard", [(i, (i + amount) % count) for i in range(count)])


def gather_shard(block):
    count = lax.axis_size("shard")
    here = lax.axis_index("shard")
    result = jnp.zeros((count,) + block.shape, block.dtype)
    for step in range(count):
        piece = block if step == 0 else shard_shift(block, step)
        result = lax.dynamic_update_slice_in_dim(result, piece[None], (here - step) % count, 0)
    return result


def scatter_shard(blocks, sent=bfloat):
    count = lax.axis_size("shard")
    here = lax.axis_index("shard")
    total = lax.dynamic_index_in_dim(blocks, here, 0, keepdims=False).astype(single)
    for step in range(1, count):
        part = lax.dynamic_index_in_dim(blocks, (here + step) % count, 0, keepdims=False)
        total = total + shard_shift(part.astype(sent), step).astype(single)
    return total


def spread(columns):
    experts, shard_count = lax.axis_size("expert"), lax.axis_size("shard")
    rows, width = columns.shape
    cut = columns.reshape(rows, shard_count, experts, width // (shard_count * experts))
    return cut.transpose(0, 2, 1, 3).reshape(rows, width)


def unspread(columns):
    experts, shard_count = lax.axis_size("expert"), lax.axis_size("shard")
    rows, width = columns.shape
    cut = columns.reshape(rows, experts, shard_count, width // (shard_count * experts))
    return cut.transpose(0, 2, 1, 3).reshape(rows, width)


def gather_weight(block):
    part = block.shape[0] // lax.axis_size("expert")
    own = lax.dynamic_slice_in_dim(block, lax.axis_index("expert") * part, part, 0)
    column = gather_shard(own).reshape(-1, block.shape[1])
    return lax.all_gather(column, "expert", axis=0, tiled=True)


def reduce_weight(grad):
    part = lax.psum_scatter(grad.astype(bfloat), "expert", scatter_dimension=0, tiled=True)
    blocks = part.reshape((lax.axis_size("shard"), -1) + part.shape[1:])
    own = scatter_shard(blocks).astype(bfloat)
    return lax.all_gather(own, "expert", axis=0, tiled=True).astype(single)


def bucket_marks(distance, lower, upper):
    inside = (distance[None] >= lower[:, None, None]) & (distance[None] < upper[:, None, None])
    return inside.astype(bfloat)


def position_bias(marks, bias_pair):
    return jnp.einsum("bij,bh->hij", marks, bias_pair, preferred_element_type=single)


def attention_forward(hidden, norm_gain, qkv, projection, bias_pair, geometry):
    distance, marks, scale = geometry
    rows = hidden.shape[0]
    normalized = spread(rms_norm(hidden, norm_gain).astype(bfloat))
    packed = matmul(normalized, qkv).astype(bfloat)
    key_value = lax.all_gather(packed[:, D:], "expert", axis=0, tiled=True)
    shifted = position_bias(marks, bias_pair)
    causal = distance >= 0
    queries = packed[:, :D].reshape(rows, H, HD)
    keys = key_value[:, :D].reshape(-1, H, HD)
    values = key_value[:, D:].reshape(-1, H, HD)
    raw_scores = jnp.einsum("ihd,jhd->hij", queries, keys, preferred_element_type=single) * scale
    head_peak = jnp.max(jnp.where(causal[None], raw_scores, -jnp.inf), axis=(1, 2))
    masked = jnp.where(causal[None], raw_scores + shifted, -jnp.inf)
    softmax_top = jnp.max(masked, axis=-1, keepdims=True)
    exponent = jnp.exp(masked - softmax_top)
    softmax_sum = jnp.sum(exponent, axis=-1, keepdims=True)
    probs = (exponent / softmax_sum).astype(bfloat)
    log_total = softmax_top[..., 0] + jnp.log(softmax_sum[..., 0])
    attended = jnp.einsum("hij,jhd->ihd", probs, values, preferred_element_type=single)
    attended = spread(attended.astype(bfloat).reshape(rows, D))
    saved = (normalized, packed, key_value, log_total, attended)
    return hidden + matmul(attended, projection), head_peak, saved


def attention_backward(
    upstream, hidden, norm_gain, qkv, projection, bias_pair, geometry, saved
):
    distance, marks, scale = geometry
    normalized, packed, key_value, log_total, attended = saved
    rows = hidden.shape[0]
    branch_grad = upstream.astype(bfloat)
    projection_grad = matmul(attended.T, branch_grad)
    attended_grad = unspread(matmul(branch_grad, projection.T).astype(bfloat))
    shifted = position_bias(marks, bias_pair)
    causal = distance >= 0
    queries = packed[:, :D].reshape(rows, H, HD)
    keys = key_value[:, :D].reshape(-1, H, HD)
    values = key_value[:, D:].reshape(-1, H, HD)
    grad_heads = attended_grad.reshape(rows, H, HD)
    raw_scores = jnp.einsum("ihd,jhd->hij", queries, keys, preferred_element_type=single) * scale
    probs = jnp.where(causal[None], jnp.exp(raw_scores + shifted - log_total[..., None]), 0.0)
    prob_grad = jnp.einsum("ihd,jhd->hij", grad_heads, values, preferred_element_type=single)
    row_dot = jnp.sum(prob_grad * probs, axis=-1)
    score_grad = (probs * (prob_grad - row_dot[..., None])).astype(bfloat)
    query_grad = jnp.einsum("hij,jhd->ihd", score_grad, keys, preferred_element_type=single) * scale
    query_grad = query_grad.astype(bfloat).reshape(rows, D)
    bias_grad = jnp.einsum("hij,bij->bh", score_grad, marks, preferred_element_type=single)
    key_grad = (
        jnp.einsum("hij,ihd->jhd", score_grad, queries, preferred_element_type=single) * scale
    )
    value_grad = jnp.einsum(
        "hij,ihd->jhd", probs.astype(bfloat), grad_heads, preferred_element_type=single
    )
    pair = jnp.concatenate([key_grad.reshape(-1, D), value_grad.reshape(-1, D)], axis=-1)
    pair_grad = lax.psum_scatter(pair.astype(bfloat), "expert", scatter_dimension=0, tiled=True)
    packed_grad = jnp.concatenate([query_grad, pair_grad], axis=-1)
    qkv_grad = matmul(normalized.T, packed_grad)
    normed_grad = unspread(matmul(packed_grad, qkv.T))
    input_grad, gain_grad = norm_back(hidden, norm_gain, normed_grad)
    return upstream + input_grad, gain_grad, qkv_grad, projection_grad, bias_grad


def exchange(blocks):
    return lax.all_to_all(blocks, "expert", split_axis=0, concat_axis=0, tiled=True)


def plain_shards(
    hidden_in,
    attn_gain,
    qkv_weight,
    out_weight,
    rel_bias,
    bucket_table,
    mlp_gain,
    mlp_up,
    mlp_down,
    router_weight,
    expert_up,
    expert_down,
    routes,
    out_grad,
):
    block_rows = hidden_in.shape[1]
    length = bucket_table.shape[0]
    experts = lax.axis_size("expert")
    groups = lax.axis_size("shard")
    here = lax.axis_index("shard")
    expert_total = EXP_DEV * experts
    capacity = 4 * block_rows // expert_total
    width = expert_down.shape[1]
    scale = 1.0 / math.sqrt(HD)

    small = jnp.concatenate(
        [attn_gain.reshape(-1), mlp_gain.reshape(-1), rel_bias.reshape(-1), router_weight.reshape(-1)]
    )
    small = gather_shard(small)
    part = D // groups
    cuts = [0, 2 * part, 4 * part, 4 * part + 2 * (NB // groups) * H, small.shape[1]]
    gain_attn, gain_mlp, bias_weights, router_full = (
        small[:, cuts[i] : cuts[i + 1]] for i in range(4)
    )
    gain_attn = gain_attn.reshape(groups, 2, part).transpose(1, 0, 2).reshape(2, D).astype(single)
    gain_mlp = gain_mlp.reshape(groups, 2, part).transpose(1, 0, 2).reshape(2, D).astype(single)
    bias_weights = (
        bias_weights.reshape(groups, 2, NB // groups, H).transpose(1, 0, 2, 3).reshape(2, NB, H)
    )
    router_full = router_full.reshape(D, expert_total)

    first = gather_weight(jnp.concatenate([qkv_weight[0], out_weight[0]], axis=1))
    dense_up = gather_weight(mlp_up)
    dense_down = gather_weight(mlp_down)
    second = gather_weight(jnp.concatenate([qkv_weight[1], out_weight[1]], axis=1))
    qkv = (first[:, : 3 * D], second[:, : 3 * D])
    projection = (first[:, 3 * D :], second[:, 3 * D :])

    up_own = jnp.zeros((EXP_DEV, groups, part, width), bfloat)
    for step in range(groups):
        target = (here + step) % groups
        piece = lax.dynamic_slice_in_dim(expert_up, target * width, width, 2)
        if step:
            piece = shard_shift(piece, step)
        up_own = lax.dynamic_update_slice_in_dim(up_own, piece[:, None], (here - step) % groups, 1)
    up_own = up_own.reshape(EXP_DEV, D, width)

    route_rows = gather_shard(routes.reshape(block_rows, 2))
    upstream_all = gather_shard(out_grad.reshape(block_rows, D))
    expert_ids = jnp.arange(expert_total, dtype=jnp.int32)
    flat_routes = route_rows.reshape(groups, -1)
    marks = (flat_routes[:, :, None] == expert_ids).astype(jnp.int32)
    rank = jnp.sum((jnp.cumsum(marks, axis=1) - marks) * marks, axis=2)
    slot_of_route = flat_routes * capacity + rank
    slot_ids = jnp.arange(expert_total * capacity, dtype=jnp.int32)
    slot_marks = (slot_of_route[:, :, None] == slot_ids).astype(bfloat)
    token_marks = jnp.sum(
        slot_marks.reshape(groups, block_rows, 2, -1).astype(single), axis=2
    ).astype(bfloat)

    def dispatch(rows):
        slots = jnp.einsum("gts,gtd->gsd", token_marks, rows, preferred_element_type=single)
        slots = slots.astype(bfloat).reshape(groups, experts, EXP_DEV, capacity, D)
        return exchange(slots.transpose(1, 2, 0, 3, 4)).reshape(
            experts, EXP_DEV, groups * capacity, D
        )

    def collect(blocks):
        back = exchange(blocks.astype(bfloat)).reshape(experts, EXP_DEV, groups, capacity, D)
        return back.transpose(2, 0, 1, 3, 4).reshape(groups, expert_total * capacity, D)

    owner_rows = dispatch(upstream_all)

    own_positions = lax.axis_index("expert") * block_rows + jnp.arange(block_rows, dtype=jnp.int32)
    distance = own_positions[:, None] - jnp.arange(length, dtype=jnp.int32)[None, :]
    bounds = jnp.sum(
        (bucket_table[:, None] < jnp.arange(NB + 1, dtype=jnp.int32)[None, :]).astype(jnp.int32),
        axis=0,
    )
    geometry = (distance, bucket_marks(distance, bounds[:NB], bounds[1:]), scale)

    hidden_zero = hidden_in.reshape(block_rows, D).astype(single)
    mid_first, peak_first, saved_first = attention_forward(
        hidden_zero, gain_attn[0], qkv[0], projection[0], bias_weights[0], geometry
    )
    dense_normed = spread(rms_norm(mid_first, gain_mlp[0]).astype(bfloat))
    pre_act = matmul(dense_normed, dense_up)
    activation = spread(jax.nn.gelu(pre_act).astype(bfloat))
    layer_one = mid_first + matmul(activation, dense_down)
    mid_second, peak_second, saved_second = attention_forward(
        layer_one, gain_attn[1], qkv[1], projection[1], bias_weights[1], geometry
    )

    moe_normed = rms_norm(mid_second, gain_mlp[1]).astype(bfloat)
    normed_all = gather_shard(moe_normed)
    received = dispatch(normed_all)
    router_logits = jnp.einsum("gtd,de->gte", normed_all, router_full, preferred_element_type=single)
    selected = (route_rows[..., None] == expert_ids).astype(single)
    gates_all = jax.nn.softmax(jnp.sum(selected * router_logits[:, :, None, :], axis=-1), axis=-1)
    slot_gates = jnp.sum(
        gates_all.reshape(groups, -1)[:, :, None] * (slot_of_route[:, :, None] == slot_ids), axis=1
    )
    owner_gates = exchange(
        slot_gates.reshape(groups, experts, EXP_DEV, capacity).transpose(1, 2, 0, 3)
    ).reshape(experts, EXP_DEV, groups * capacity)

    expert_pre = jnp.einsum("sjcd,jdf->sjcf", received, up_own, preferred_element_type=single)
    expert_act = jax.nn.gelu(expert_pre).astype(bfloat)
    expert_out = jnp.einsum(
        "sjcf,jfd->sjcd", expert_act, expert_down, preferred_element_type=single
    )
    owner_grad = (owner_gates[..., None] * owner_rows.astype(single)).astype(bfloat)
    act_grad = jnp.einsum("sjcd,jfd->sjcf", owner_grad, expert_down, preferred_element_type=single)
    pre_grad = gelu_back(expert_pre, act_grad).astype(bfloat)
    row_grad = jnp.einsum("sjcf,jdf->sjcd", pre_grad, up_own, preferred_element_type=single)

    returned = collect(expert_out)
    back_rows = collect(row_grad)
    expert_down_grad = jnp.einsum(
        "sjcf,sjcd->jfd", expert_act, owner_grad, preferred_element_type=single
    )
    up_grad = jnp.einsum(
        "sjcd,sjcf->jdf", received, pre_grad, preferred_element_type=single
    ).astype(bfloat)

    route_out = jnp.einsum("grs,gsd->grd", slot_marks, returned, preferred_element_type=single)
    route_out = route_out.reshape(groups, block_rows, 2, D)
    gate_grad = scatter_shard(
        jnp.sum(route_out * upstream_all[:, :, None, :].astype(single), axis=-1), single
    )
    mixed = scatter_shard(jnp.sum(gates_all[..., None] * route_out, axis=2))
    hidden_out = (mid_second + mixed).astype(bfloat).reshape(hidden_in.shape)

    gates = lax.dynamic_index_in_dim(gates_all, here, 0, keepdims=False)
    own_selected = lax.dynamic_index_in_dim(selected, here, 0, keepdims=False)
    upstream = out_grad.reshape(block_rows, D).astype(single)
    chosen_grad = gates * (gate_grad - jnp.sum(gates * gate_grad, axis=-1, keepdims=True))
    logit_grad = jnp.sum(chosen_grad[:, :, None] * own_selected, axis=1).astype(bfloat)
    router_grad = matmul(moe_normed.T, logit_grad)
    row_terms = jnp.einsum("gts,gsd->gtd", token_marks, back_rows, preferred_element_type=single)
    normed_grad = matmul(logit_grad, router_full.T) + scatter_shard(row_terms)
    moe_input_grad, moe_gain_grad = norm_back(mid_second, gain_mlp[1], normed_grad)
    mid_grad = upstream + moe_input_grad

    up_grad = up_grad.reshape(EXP_DEV, groups, part, width)
    expert_up_grad = jnp.zeros((EXP_DEV, part, groups * width), single)
    for step in range(groups):
        piece = lax.dynamic_index_in_dim(up_grad, (here + step) % groups, 1, keepdims=False)
        if step:
            piece = shard_shift(piece, step)
        expert_up_grad = lax.dynamic_update_slice_in_dim(
            expert_up_grad, piece.astype(single), ((here - step) % groups) * width, 2
        )

    layer_grad, gain_second, qkv_second, projection_second, bias_second = attention_backward(
        mid_grad, layer_one, gain_attn[1], qkv[1], projection[1], bias_weights[1], geometry,
        saved_second,
    )
    second_grad = reduce_weight(jnp.concatenate([qkv_second, projection_second], axis=1))
    dense_branch = layer_grad.astype(bfloat)
    mlp_down_grad = reduce_weight(matmul(activation.T, dense_branch))
    hidden_act_grad = unspread(matmul(dense_branch, dense_down.T))
    pre_act_grad = gelu_back(pre_act, hidden_act_grad).astype(bfloat)
    mlp_up_grad = reduce_weight(matmul(dense_normed.T, pre_act_grad))
    dense_normed_grad = unspread(matmul(pre_act_grad, dense_up.T))
    dense_input_grad, dense_gain_grad = norm_back(mid_first, gain_mlp[0], dense_normed_grad)
    first_grad = layer_grad + dense_input_grad
    input_grad, gain_first, qkv_first, projection_first, bias_first = attention_backward(
        first_grad, hidden_zero, gain_attn[0], qkv[0], projection[0], bias_weights[0], geometry,
        saved_first,
    )
    first_weight_grad = reduce_weight(jnp.concatenate([qkv_first, projection_first], axis=1))

    gains = jnp.stack([gain_first, gain_second, dense_gain_grad, moe_gain_grad])
    biases = jnp.stack([bias_first, bias_second])
    small_grad = jnp.concatenate(
        [
            gains.reshape(4, groups, part).transpose(1, 0, 2).reshape(groups, -1),
            biases.reshape(2, groups, NB // groups, H).transpose(1, 0, 2, 3).reshape(groups, -1),
            router_grad.reshape(groups, -1),
        ],
        axis=1,
    )
    small_grad = lax.psum(scatter_shard(small_grad, single), "expert")
    gain_cut = 4 * part
    bias_cut = gain_cut + 2 * (NB // groups) * H
    own_gains = small_grad[:gain_cut].reshape(4, part)
    peaks = lax.pmax(jnp.stack([peak_first, peak_second]), ("expert", "shard"))
    clip_scales = jnp.sqrt(clip_limit / jnp.maximum(peaks, clip_limit))
    return (
        hidden_out,
        input_grad.reshape(hidden_in.shape),
        own_gains[:2],
        jnp.stack([first_weight_grad[:, : 3 * D], second_grad[:, : 3 * D]]),
        jnp.stack([first_weight_grad[:, 3 * D :], second_grad[:, 3 * D :]]),
        small_grad[gain_cut:bias_cut].reshape(2, NB // groups, H),
        own_gains[2:],
        mlp_up_grad,
        mlp_down_grad,
        small_grad[bias_cut:].reshape(part, expert_total),
        expert_up_grad,
        expert_down_grad,
        clip_scales,
    )


MESH = pl.DeviceIdType.MESH
ANY = pl.ANY
VMEM = pltpu.VMEM


def place():
    return lax.axis_index("expert"), lax.axis_index("shard")


def greet(devices):
    barrier = pltpu.get_barrier_semaphore()
    for device in devices:
        pl.semaphore_signal(barrier, inc=1, device_id=device, device_id_type=MESH)
    pl.semaphore_wait(barrier, len(devices))


def push(sent, source, target, send_sem, recv_sem, device):
    copy = pltpu.make_async_remote_copy(
        src_ref=source,
        dst_ref=target,
        send_sem=send_sem,
        recv_sem=recv_sem,
        device_id=device,
        device_id_type=MESH,
    )
    copy.start()
    sent.append(copy)
    return copy


def norm_rows(inputs, gain):
    return inputs * lax.rsqrt(jnp.mean(inputs * inputs, axis=-1, keepdims=True) + epsilon) * gain


def dot_rows(left, right):
    return lax.dot_general(left, right, (((1,), (1,)), ((), ())), preferred_element_type=single)


def dot_columns(left, right):
    return lax.dot_general(left, right, (((0,), (0,)), ((), ())), preferred_element_type=single)


def loop(count, body):
    def step(i, carry):
        body(i)
        return carry

    lax.fori_loop(0, count, step, 0)


def lane_block(i, width):
    return pl.ds(pl.multiple_of(i * width, 128), width)


def row_block(i, height):
    return pl.ds(pl.multiple_of(i * height, height), height)


T = 128
PAIRS = H // 2
TOE = 1152
CAP = 32


class Plane:
    def __init__(self):
        self.e, self.s = place()
        e = self.e
        self.core = lax.rem(e, 2)
        self.quarter = e // 2
        self.at_x = e + 2 - 4 * lax.rem(self.quarter, 2)
        self.at_y = lax.rem(e + 4, 8)
        self.at_core = e + 1 - 2 * self.core
        self.inward = jnp.where(self.core == 0, self.at_x, self.at_y)
        self.onward = jnp.where(self.core == 0, self.at_y, self.at_x)
        self.diagonal = self.inward + self.onward - e
        self.others = [lax.rem(self.s + k, 4) for k in range(1, 4)]
        self.around = [lax.rem(e + k, 8) for k in range(1, 8)]
        self.sent = []

    def push(self, source, target, send_sem, recv_sem, device):
        return push(self.sent, source, target, send_sem, recv_sem, device)

    def arrived(self, view, recv_sem):
        pltpu.make_async_remote_copy(
            src_ref=view,
            dst_ref=view,
            send_sem=recv_sem,
            recv_sem=recv_sem,
            device_id=(self.at_core, self.s),
            device_id_type=MESH,
        ).wait_recv()


class PlaneGather:
    def __init__(self, plane, view, send_sems, recv_sems):
        self.plane, self.view, self.ss, self.rs = plane, view, send_sems, recv_sems

    def _push(self, who, i, target):
        p = self.plane
        block = self.view(who)
        p.push(block, block, self.ss.at[i], self.rs.at[i], (target, p.s))

    def first(self):
        p = self.plane
        self._push(p.e, 0, p.at_x)
        self._push(p.e, 1, p.at_y)
        self._push(p.e, 3, p.at_core)

    def second(self):
        p = self.plane
        p.arrived(self.view(p.inward), self.rs.at[p.core])
        self._push(p.inward, 2, p.onward)
        self._push(p.inward, 4, p.at_core)

    def third(self):
        p = self.plane
        p.arrived(self.view(p.onward), self.rs.at[1 - p.core])
        self._push(p.onward, 5, p.at_core)
        p.arrived(self.view(p.diagonal), self.rs.at[2])
        self._push(p.diagonal, 6, p.at_core)

    def done(self):
        for i in range(3, 7):
            self.plane.arrived(self.view(self.plane.e), self.rs.at[i])


def forward_kernel(
    hidden_ref,
    small_ref,
    buckets_ref,
    routes_ref,
    qkv_hbm,
    out_hbm,
    up_hbm,
    down_hbm,
    expert_up_hbm,
    cot_hbm,
    normed_out,
    query_out,
    attended_out,
    mid_first_out,
    mid_second_out,
    dense_normed_out,
    pre_out,
    act_out,
    one_out,
    peak_out,
    moe_normed_out,
    gains_ref,
    router_out,
    slots_out,
    qkv0_out,
    qkv1_out,
    proj0_out,
    proj1_out,
    up_out,
    down_out,
    kv_out,
    probs_out,
    up_own,
    cot_all,
    small_all,
    table_ref,
    slots_own,
    act,
    w_qkv0,
    w_qkv1,
    w_out0,
    w_out1,
    w_up,
    w_down,
    kv,
    probs,
    scores,
    zs,
    zr,
    f1s,
    f1r,
    f2s,
    f2r,
    cs,
    cr,
    locals_sem,
    k1s,
    k1r,
    k2s,
    k2r,
    kcs,
    kcr,
    us,
    ur,
    gs,
    gr,
    ns,
    nr,
    outs_sem,
    small_s,
    small_r,
    slot_zs,
    slot_zr,
    slot_ps,
    slot_pr,
):
    e, s = place()
    core = lax.rem(e, 2)
    quarter = e // 2
    at_x = e + 2 - 4 * lax.rem(quarter, 2)
    at_y = lax.rem(e + 4, 8)
    at_core = e + 1 - 2 * core
    inward = jnp.where(core == 0, at_x, at_y)
    onward = jnp.where(core == 0, at_y, at_x)
    others = [lax.rem(s + k, 4) for k in range(1, 4)]
    sources = [lax.rem(s + 4 - k, 4) for k in range(1, 4)]
    sent = []
    kept = []

    def local(source, target, sem):
        copy = pltpu.make_async_copy(source, target, sem)
        copy.start()
        return copy

    chunks = [
        (qkv_hbm.at[0], w_qkv0, 48, 1152),
        (out_hbm.at[0], w_out0, 48, 384),
        (up_hbm, w_up, 48, 1536),
        (down_hbm, w_down, 192, 384),
        (qkv_hbm.at[1], w_qkv1, 48, 1152),
        (out_hbm.at[1], w_out1, 48, 384),
    ]

    def block(target, who, position, height, half, width):
        rows = pl.ds(pl.multiple_of(position * 4 * height + who * height, height), height)
        return target.at[rows, lane_block(half, width)]

    def cot_block(g, who):
        return cot_all.at[g, who]

    stage1, stage2, stage3, stage4, own = {}, {}, {}, {}, {}

    def z_send(c):
        source, target, height, width = chunks[c]
        piece = source.at[row_block(quarter, height), lane_block(core, width)]
        mine = block(target, quarter, s, height, core, width)
        stage1[c] = [
            push(sent, piece, mine, zs.at[c, k], zr.at[c, k], (e, others[k])) for k in range(3)
        ]
        own[c] = local(source, target.at[row_block(s, 4 * height), :], locals_sem.at[c])

    def plane_send(c):
        _, target, height, width = chunks[c]
        stage2[c] = []
        for k in range(3):
            stage1[c][k].wait_recv()
            mine = block(target, quarter, sources[k], height, core, width)
            stage2[c].append(
                [
                    push(sent, mine, mine, f1s.at[c, k, i], f1r.at[c, k, i], (partner, s))
                    for i, partner in enumerate((at_x, at_y))
                ]
            )

    def plane_forward(c):
        _, target, height, width = chunks[c]
        stage3[c] = []
        for k in range(3):
            pltpu.make_async_remote_copy(
                src_ref=block(target, quarter, sources[k], height, core, width),
                dst_ref=block(target, quarter, sources[k], height, core, width),
                send_sem=f1s.at[c, k, core],
                recv_sem=f1r.at[c, k, core],
                device_id=(inward, s),
                device_id_type=MESH,
            ).wait_recv()
            theirs = block(target, inward // 2, sources[k], height, core, width)
            stage3[c].append(
                push(sent, theirs, theirs, f2s.at[c, k], f2r.at[c, k], (onward, s))
            )

    def core_send(c):
        _, target, height, width = chunks[c]
        stage4[c] = []
        for k in range(3):
            pltpu.make_async_remote_copy(
                src_ref=block(target, quarter, sources[k], height, core, width),
                dst_ref=block(target, quarter, sources[k], height, core, width),
                send_sem=f1s.at[c, k, 1 - core],
                recv_sem=f1r.at[c, k, 1 - core],
                device_id=(onward, s),
                device_id_type=MESH,
            ).wait_recv()
            stage3[c][k].wait_recv()
            half = target.at[row_block(sources[k], 4 * height), lane_block(core, width)]
            stage4[c].append(push(sent, half, half, cs.at[c, k], cr.at[c, k], (at_core, s)))

    weight_outs = [qkv0_out, proj0_out, up_out, down_out, qkv1_out, proj1_out]

    def ready(c):
        for k in range(3):
            stage4[c][k].wait_recv()
        own[c].wait()
        kept.append(local(chunks[c][1], weight_outs[c], outs_sem.at[c]))

    plane = Plane()
    cot_groups = [s] + sources
    cot_gathers = [
        PlaneGather(plane, functools.partial(cot_block, g), ns.at[k], nr.at[k])
        for k, g in enumerate(cot_groups)
    ]

    def cot_first(k):
        plane.arrived(cot_block(s, e), gr.at[k - 1])
        cot_gathers[k].first()

    experts = lax.broadcasted_iota(jnp.int32, (16, T), 0)
    chosen = [experts == routes_ref[r : r + 1, :] for r in range(2)]
    marks = jnp.where(chosen[0] | chosen[1], 1.0, 0.0).astype(bfloat)
    earlier = jnp.where(
        lax.broadcasted_iota(jnp.int32, (T, T), 0) < lax.broadcasted_iota(jnp.int32, (T, T), 1),
        1.0,
        0.0,
    ).astype(bfloat)
    before = jnp.dot(marks, earlier, preferred_element_type=single)
    slots_own[...] = jnp.zeros_like(slots_own)
    for r in range(2):
        rank = jnp.sum(jnp.where(chosen[r], before, 0.0), axis=0, keepdims=True)
        slots_own[r : r + 1, :] = routes_ref[r : r + 1, :] * CAP + rank.astype(jnp.int32)
    slots_out[s, e] = slots_own[...]
    own_cot = local(cot_hbm, cot_block(s, e), gs.at[3])
    small_all[s] = small_ref[...]

    greet([(d, s) for d in plane.around] + [(e, other) for other in others])
    smalls = [
        push(sent, small_ref, small_all.at[s], small_s.at[k], small_r.at[k], (e, others[k]))
        for k in range(3)
    ]
    z_send(0)
    for k in range(3):
        push(sent, slots_own, slots_out.at[s, e], slot_zs.at[k], slot_zr.at[k], (e, others[k]))
    own_cot.wait()
    cot_gathers[0].first()
    z_send(1)
    z_send(2)
    reshard = []

    def bulk():
        for c in range(3, 6):
            z_send(c)
        for k in range(3):
            push(sent, cot_hbm, cot_block(s, e), gs.at[k], gr.at[k], (e, others[k]))
        reshard.extend([
            push(
                sent,
                expert_up_hbm.at[:, :, lane_block(others[k], 768)],
                up_own.at[:, row_block(s, 192), :],
                us.at[k],
                ur.at[k],
                (e, others[k]),
            )
            for k in range(3)
        ])
        kept.append(
            local(
                expert_up_hbm.at[:, :, lane_block(s, 768)],
                up_own.at[:, row_block(s, 192), :],
                us.at[3],
            )
        )

    def slots_plane():
        for k in range(3):
            plane.arrived(slots_own, slot_zr.at[k])
        column = slots_out.at[:, e]
        for k, d in enumerate(plane.around):
            push(sent, column, column, slot_ps.at[k], slot_pr.at[k], (d, s))

    for copy in smalls:
        copy.wait_recv()
    biases = []
    for z in range(4):
        lanes = slice(192 * z, 192 * (z + 1))
        gains_ref[:, lanes] = small_all[z, :4, :192]
        router_out[:, lanes] = small_all[z, 16:32, :192].astype(bfloat)
        biases.append(small_all[z, 8:16, : 2 * H])
    bucket_marks_here = jnp.where(
        lax.broadcasted_iota(jnp.int32, (NB, TOE), 0) == buckets_ref[...], 1.0, 0.0
    ).astype(bfloat)
    table_ref[...] = dot_columns(jnp.concatenate(biases).astype(bfloat), bucket_marks_here)

    def attention(layer, inputs, w_qkv, w_out, work):
        normed = norm_rows(inputs, gains_ref[pl.ds(layer, 1), :]).astype(bfloat)
        normed_out[layer] = normed
        if layer == 0:
            plane_send(0)
            plane_forward(0)
            plane_send(1)
            core_send(0)
            plane_forward(1)
            ready(0)
            bulk()
        else:
            ready(4)
        own_rows = row_block(e, T)
        first, second, third = [], [], []
        for part in range(3):
            x = normed_out[layer]
            for i, base in enumerate((D, 2 * D)):
                columns = w_qkv[:, base + 256 * part : base + 256 * (part + 1)]
                kv[layer, part, own_rows, 256 * i : 256 * (i + 1)] = jnp.dot(
                    x, columns, preferred_element_type=single
                ).astype(bfloat)
            mine = kv.at[layer, part, own_rows, :]
            first.append(
                [
                    push(sent, mine, mine, k1s.at[layer, part, i], k1r.at[layer, part, i], (p, s))
                    for i, p in enumerate((at_x, at_y))
                ]
            )
            third.append(
                [
                    push(
                        sent, mine, mine, kcs.at[layer, part, 0], kcr.at[layer, part, 0],
                        (at_core, s),
                    )
                ]
            )
        query_out[layer] = jnp.dot(
            normed_out[layer], w_qkv[:, :D], preferred_element_type=single
        ).astype(bfloat)
        if work:
            work[0]()
        at_diagonal = inward + onward - e
        for part in range(3):
            pltpu.make_async_remote_copy(
                src_ref=kv.at[layer, part, own_rows, :],
                dst_ref=kv.at[layer, part, own_rows, :],
                send_sem=k1s.at[layer, part, core],
                recv_sem=k1r.at[layer, part, core],
                device_id=(inward, s),
                device_id_type=MESH,
            ).wait_recv()
            theirs = kv.at[layer, part, row_block(inward, T), :]
            second.append(
                push(
                    sent, theirs, theirs, k2s.at[layer, part], k2r.at[layer, part], (onward, s)
                )
            )
            third[part].append(
                push(
                    sent, theirs, theirs, kcs.at[layer, part, 1], kcr.at[layer, part, 1],
                    (at_core, s),
                )
            )
        if work:
            work[1]()
        for part in range(3):
            pltpu.make_async_remote_copy(
                src_ref=kv.at[layer, part, own_rows, :],
                dst_ref=kv.at[layer, part, own_rows, :],
                send_sem=k1s.at[layer, part, 1 - core],
                recv_sem=k1r.at[layer, part, 1 - core],
                device_id=(onward, s),
                device_id_type=MESH,
            ).wait_recv()
            theirs = kv.at[layer, part, row_block(onward, T), :]
            third[part].append(
                push(
                    sent, theirs, theirs, kcs.at[layer, part, 2], kcr.at[layer, part, 2],
                    (at_core, s),
                )
            )
            second[part].wait_recv()
            theirs = kv.at[layer, part, row_block(at_diagonal, T), :]
            third[part].append(
                push(
                    sent, theirs, theirs, kcs.at[layer, part, 3], kcr.at[layer, part, 3],
                    (at_core, s),
                )
            )
        for part in range(3):
            for i in range(4):
                third[part][i].wait_recv()

            def one_pair(local_pair):
                pair = 2 * part + local_pair
                lanes = lane_block(pair, 128)
                queries = query_out[layer, :, lanes]
                lane = lax.broadcasted_iota(jnp.int32, (T, 128), 1)
                zero = jnp.zeros_like(queries)
                both = jnp.concatenate(
                    [jnp.where(lane < HD, queries, zero), jnp.where(lane >= HD, queries, zero)]
                )
                keys = kv[layer, part, :, lane_block(local_pair, 128)]
                scores[...] = dot_rows(both, keys) * (1.0 / math.sqrt(HD))
                for half in range(2):
                    head = 2 * pair + half
                    toeplitz = table_ref[pl.ds(layer * H + head, 1), :]
                    peak = jnp.full((1, 1), -jnp.inf, single)
                    for rows in range(0, T, 32):
                        raw = scores[half * T + rows : half * T + rows + 32, :]
                        row = e * T + rows + lax.broadcasted_iota(jnp.int32, raw.shape, 0)
                        causal = row >= lax.broadcasted_iota(jnp.int32, raw.shape, 1)
                        shifted = pltpu.roll(
                            jnp.broadcast_to(toeplitz, (32, TOE)),
                            TOE - (T - 1) + rows,
                            1,
                            stride=1,
                            stride_axis=0,
                        )[:, : raw.shape[1]]
                        peak = jnp.maximum(
                            peak, jnp.max(jnp.where(causal, raw, -jnp.inf), keepdims=True)
                        )
                        masked = jnp.where(causal, raw + shifted, -jnp.inf)
                        top = jnp.max(masked, axis=-1, keepdims=True)
                        exponent = jnp.exp(masked - top)
                        total = jnp.sum(exponent, axis=-1, keepdims=True)
                        probs[layer, pl.ds(pl.multiple_of(head * T + rows, 32), 32), :] = (
                            exponent / total
                        ).astype(bfloat)
                    peak_out[pl.ds(layer * H + head, 1), :] = jnp.broadcast_to(peak, (1, 128))
                values = kv[layer, part, :, pl.ds(pl.multiple_of(256 + local_pair * 128, 128), 128)]
                mixed = jnp.dot(
                    probs[layer, pl.ds(pl.multiple_of(pair * 2 * T, 2 * T), 2 * T), :],
                    values,
                    preferred_element_type=single,
                )
                attended_out[layer, :, lanes] = jnp.where(
                    lane < HD, mixed[:T], mixed[T:]
                ).astype(bfloat)

            loop(2, one_pair)
            if work:
                work[2 + part]()
        kept.append(local(kv.at[layer], kv_out.at[layer], outs_sem.at[6 + layer]))
        kept.append(local(probs.at[layer], probs_out.at[layer], outs_sem.at[8 + layer]))

    def work0():
        plane_send(2)
        slots_plane()

    def work1():
        cot_gathers[0].second()

    def work2():
        core_send(1)
        plane_send(3)

    def work3():
        cot_gathers[0].third()

    def work4():
        plane_forward(2)

    hidden = hidden_ref[...].astype(single)
    attention(0, hidden, w_qkv0, w_out0, [work0, work1, work2, work3, work4])
    ready(1)
    mid_first_out[...] = hidden + jnp.dot(
        attended_out[0], w_out0[...], preferred_element_type=single
    )
    dense_normed_out[...] = norm_rows(mid_first_out[...], gains_ref[pl.ds(2, 1), :]).astype(bfloat)
    core_send(2)
    plane_forward(3)
    plane_send(4)
    plane_send(5)
    ready(2)

    def up_part(i):
        lanes = slice(768 * i, 768 * (i + 1))
        before = jnp.dot(dense_normed_out[...], w_up[:, lanes], preferred_element_type=single)
        pre_out[:, lanes] = before
        value = jax.nn.gelu(before).astype(bfloat)
        act[:, lanes] = value
        for b in range(8):
            act_out[:, 384 * b + 96 * i : 384 * b + 96 * (i + 1)] = value[:, 96 * b : 96 * (b + 1)]

    for i in range(4):
        up_part(i)
    core_send(3)
    plane_forward(4)
    plane_forward(5)
    cot_first(1)
    ready(3)
    one_out[...] = mid_first_out[...]

    def down_part(i):
        rows = row_block(i, 768)
        one_out[...] += jnp.dot(
            act[:, lane_block(i, 768)], w_down[rows, :], preferred_element_type=single
        )

    loop(4, down_part)
    core_send(4)
    core_send(5)

    def work5():
        cot_first(2)
        cot_first(3)
        cot_gathers[1].second()

    def work6():
        pass

    def work7():
        cot_gathers[1].third()
        cot_gathers[2].second()

    def work8():
        cot_gathers[2].third()
        cot_gathers[3].second()

    def work9():
        cot_gathers[3].third()

    attention(1, one_out[...], w_qkv1, w_out1, [work5, work6, work7, work8, work9])
    ready(5)
    mid_second_out[...] = one_out[...] + jnp.dot(
        attended_out[1], w_out1[...], preferred_element_type=single
    )
    moe_normed_out[...] = norm_rows(mid_second_out[...], gains_ref[pl.ds(3, 1), :]).astype(bfloat)
    for k in range(7):
        plane.arrived(slots_out.at[:, e], slot_pr.at[k])
    for gather in cot_gathers:
        gather.done()
    for copy in reshard:
        copy.wait_recv()
    for copy in kept:
        copy.wait()
    for copy in sent + plane.sent:
        copy.wait_send()


def forward(hidden, small, buckets, routes, qkv, out, up, down, expert_up, cotangent):
    length = T * lax.axis_size("expert")
    vmem = pl.BlockSpec(memory_space=VMEM)
    anywhere = pl.BlockSpec(memory_space=ANY)
    shape = jax.ShapeDtypeStruct
    ff = up.shape[1]
    sem = pltpu.SemaphoreType.DMA
    return pl.pallas_call(
        forward_kernel,
        name="forward_layers",
        out_shape=(
            shape((2, T, D), bfloat),
            shape((2, T, D), bfloat),
            shape((2, T, D), bfloat),
            shape((T, D), single),
            shape((T, D), single),
            shape((T, D), bfloat),
            shape((T, ff), single),
            shape((T, ff), bfloat),
            shape((T, D), single),
            shape((2 * H, 128), single),
            shape((T, D), bfloat),
            shape((4, D), single),
            shape((16, D), bfloat),
            shape((4, 8, 8, T), jnp.int32),
            shape((D, 3 * D), bfloat),
            shape((D, 3 * D), bfloat),
            shape((D, D), bfloat),
            shape((D, D), bfloat),
            shape((D, ff), bfloat),
            shape((ff, D), bfloat),
            shape((2, 3, length, 512), bfloat),
            shape((2, H * T, length), bfloat),
            shape((EXP_DEV, D, 768), bfloat),
            shape((4, 8, T, D), bfloat),
        ),
        in_specs=[vmem] * 4 + [anywhere] * 6,
        out_specs=(vmem,) * 14 + (anywhere,) * 10,
        scratch_shapes=[
            VMEM((4,) + small.shape, single),
            VMEM((2 * H, TOE), single),
            VMEM((8, T), jnp.int32),
            VMEM((T, ff), bfloat),
            VMEM((D, 3 * D), bfloat),
            VMEM((D, 3 * D), bfloat),
            VMEM((D, D), bfloat),
            VMEM((D, D), bfloat),
            VMEM((D, ff), bfloat),
            VMEM((ff, D), bfloat),
            VMEM((2, 3, length, 512), bfloat),
            VMEM((2, H * T, length), bfloat),
            VMEM((2 * T, length), single),
            sem((6, 3)), sem((6, 3)),
            sem((6, 3, 2)), sem((6, 3, 2)),
            sem((6, 3)), sem((6, 3)),
            sem((6, 3)), sem((6, 3)),
            sem((6,)),
            sem((2, 3, 2)), sem((2, 3, 2)),
            sem((2, 3)), sem((2, 3)),
            sem((2, 3, 4)), sem((2, 3, 4)),
            sem((4,)), sem((3,)),
            sem((4,)), sem((3,)),
            sem((4, 7)), sem((4, 7)),
            sem((10,)),
            sem((3,)), sem((3,)),
            sem((3,)), sem((3,)),
            sem((7,)), sem((7,)),
        ],
        compiler_params=pltpu.CompilerParams(
            collective_id=2, has_side_effects=True, vmem_limit_bytes=56 * 2**20
        ),
    )(hidden, small, buckets, routes, qkv, out, up, down, expert_up, cotangent)


class SmallReduce:
    def __init__(self, plane, value, z_in, plane_in, op, sems):
        self.plane, self.value, self.z_in, self.plane_in = plane, value, z_in, plane_in
        self.op, self.sems = op, sems

    def start(self):
        p = self.plane
        zs, zr, _, _ = self.sems
        for k in range(3):
            p.push(self.value, self.z_in.at[k], zs.at[k], zr.at[k], (p.e, p.others[k]))

    def middle(self, middle):
        p = self.plane
        zs, zr, ps, pr = self.sems
        total = self.value[...]
        for k in range(3):
            p.arrived(self.z_in.at[k], zr.at[k])
            total = self.op(total, self.z_in[k])
        middle[...] = total
        for k in range(7):
            p.push(middle, self.plane_in.at[k], ps.at[k], pr.at[k], (p.around[k], p.s))

    def finish(self, middle, result):
        p = self.plane
        total = middle[...]
        for k in range(7):
            p.arrived(self.plane_in.at[k], self.sems[3].at[k])
            total = self.op(total, self.plane_in[k])
        result[...] = total


def norm_pull(inputs, gain, upstream):
    inverse = lax.rsqrt(jnp.mean(inputs * inputs, axis=-1, keepdims=True) + epsilon)
    scaled = upstream * gain
    inner = jnp.mean(scaled * inputs, axis=-1, keepdims=True)
    gain_grad = jnp.sum(upstream * inputs * inverse, axis=0, keepdims=True)
    return inverse * scaled - inputs * (inverse * inverse * inverse * inner), gain_grad


def gelu_both(value):
    root = math.sqrt(2.0 / math.pi)
    squared = value * value
    bend = jnp.tanh(root * value * (1.0 + 0.044715 * squared))
    half = 0.5 * (1.0 + bend)
    slope = half + 0.5 * value * (1.0 - bend * bend) * (root * (1.0 + 3 * 0.044715 * squared))
    return value * half, slope


def gelu_slope(value):
    root = math.sqrt(2.0 / math.pi)
    squared = value * value
    bend = jnp.tanh(root * value * (1.0 + 0.044715 * squared))
    return 0.5 * (1.0 + bend) + 0.5 * value * (1.0 - bend * bend) * root * (
        1.0 + 3 * 0.044715 * squared
    )


def backward_kernel(
    mid_grad_ref,
    one_ref,
    hidden_ref,
    mid_ref,
    gains_ref,
    query_ref,
    pre_ref,
    buckets_ref,
    small_ref,
    peak_ref,
    early_hbm,
    normed_hbm,
    attended_hbm,
    dense_normed_hbm,
    act_hbm,
    qkv0_hbm,
    qkv1_hbm,
    proj0_hbm,
    proj1_hbm,
    up_hbm,
    down_hbm,
    kv_hbm,
    probs_hbm,
    up_grad_hbm,
    hidden_grad_out,
    att_out,
    up_out,
    down_out,
    small_out,
    late_out,
    peak_out,
    expert_up_out,
    w_wide,
    w_down,
    kv,
    probs,
    xg,
    gx,
    gsrc,
    zb,
    zin,
    zb_down,
    zin_down,
    slopes,
    score_low,
    dk,
    cin,
    rin,
    attended_grad,
    layer_grad,
    biases,
    early,
    early_z,
    early_p,
    early_m,
    late,
    late_z,
    late_p,
    late_m,
    peak_z,
    peak_p,
    peak_m,
    gs,
    gr,
    xs,
    xr,
    zs,
    zr,
    dcs,
    dcr,
    drs,
    drr,
    szs,
    szr,
    sps,
    spr,
    us,
    ur,
    loads,
):
    p = Plane()
    e, s, core = p.e, p.s, p.core
    own_rows = row_block(e, T)

    def load(source, target, i):
        copy = pltpu.make_async_copy(source, target, loads.at[i])
        copy.start()
        return copy

    own_parts = [
        load(source, xg.at[n, own_rows, :], 11 + n)
        for n, source in ((2, normed_hbm.at[0]), (3, attended_hbm.at[0]), (4, dense_normed_hbm))
    ]
    got_early = load(early_hbm, xg.at[0:2], 12)
    own_act = load(act_hbm.at[:, lane_block(e, 384)], gx.at[3, own_rows, :], 16)
    greet([(d, s) for d in p.around] + [(e, other) for other in p.others])

    w_qkv = w_wide.at[:, : 3 * D]
    w_out = w_wide.at[:, 3 * D :]
    got_out = load(proj1_hbm, w_out, 0)
    got_kv = load(kv_hbm.at[1], kv, 2)
    got_probs = load(probs_hbm.at[1], probs, 3)
    got_qkv = load(qkv1_hbm, w_qkv, 1)
    got_down = load(down_hbm, w_down, 5)

    peaks = SmallReduce(
        p, peak_ref, peak_z, peak_p, jnp.maximum, (szs.at[0], szr.at[0], sps.at[0], spr.at[0])
    )
    peaks.start()

    def rows_gather(n):
        return PlaneGather(
            p, lambda who: xg.at[n, row_block(who, T), :], gs.at[n], gr.at[n]
        )

    gathers = {n: rows_gather(n) for n in range(2, 6)}
    def exchange_start(j, source):
        if j == 3:
            own_act.wait()
        else:
            gx[j, own_rows, :] = source[:, lane_block(e, 384)]
        for k, d in enumerate(p.around):
            p.push(
                source.at[:, lane_block(d, 384)],
                gx.at[j, own_rows, :],
                xs.at[j, k],
                xr.at[j, k],
                (d, s),
            )

    def exchange_wait(j):
        for k in range(7):
            p.arrived(gx.at[j, own_rows, :], xr.at[j, k])

    def out_gather(j, target, height):
        return PlaneGather(
            p, lambda who: target.at[pl.ds(who, 1)], gs.at[6 + j], gr.at[6 + j]
        )

    def z_start(j, tile, received, height):
        for k in range(3):
            p.push(
                tile.at[row_block(p.others[k], height), :],
                received.at[k],
                zs.at[j, k],
                zr.at[j, k],
                (e, p.others[k]),
            )

    def z_finish(j, tile, received, height, target):
        total = tile[row_block(s, height), :].astype(single)
        for k in range(3):
            p.arrived(received.at[k], zr.at[j, k])
            total = total + received[k].astype(single)
        target[pl.ds(e, 1)] = total.astype(bfloat)[None]

    def tile_attention(layer):
        j = 1 - layer
        exchange_wait(j)
        rows = xg[2 * j + e // 6]
        for part in range(3):
            lanes = slice(128 * part, 128 * (part + 1))
            zb[j, :, lanes] = dot_columns(rows, gx[j, :, lanes]).astype(bfloat)
        z_start(j, zb.at[j], zin.at[j], 192)

    def tile_up():
        exchange_wait(2)
        for part in range(3):
            lanes = slice(128 * part, 128 * (part + 1))
            zb[2, :, lanes] = dot_columns(xg[4], gx[2, :, lanes]).astype(bfloat)
        z_start(2, zb.at[2], zin.at[2], 192)

    def tile_down():
        exchange_wait(3)
        for part in range(3):
            lanes = slice(128 * part, 128 * (part + 1))
            zb_down[lanes, :] = dot_columns(gx[3, :, lanes], xg[5]).astype(bfloat)
        z_start(3, zb_down, zin_down, 96)

    gather_att1 = out_gather(0, att_out.at[1], 192)
    gather_att0 = out_gather(1, att_out.at[0], 192)
    gather_up = out_gather(2, up_out, 192)
    gather_down = out_gather(3, down_out, 96)

    scale = 1.0 / math.sqrt(HD)

    def attention(layer, upstream, work):
        j = 1 - layer
        grads = gsrc.at[j]
        branch = upstream.astype(bfloat)
        grads[:, 3 * D :] = branch
        got_out_now = got_out if layer == 1 else reloads["out"]
        got_out_now.wait()
        attended_grad[...] = dot_rows(branch, w_out[...]).astype(bfloat)
        if layer == 1:
            got_kv.wait()
            got_probs.wait()
        else:
            reloads["kv"].wait()
            reloads["probs"].wait()
            for copy in dk_sent:
                copy.wait_send()
            dk_sent.clear()

        def first_step(part):
            push(
                dk_sent,
                dk.at[part, 1 - core],
                cin.at[layer, part],
                dcs.at[layer, part],
                dcr.at[layer, part],
                (p.at_core, s),
            )

        def second_step(part):
            p.arrived(cin.at[layer, part], dcr.at[layer, part])
            for q in range(4):
                dk[part, core, q] = (
                    dk[part, core, q].astype(single) + cin[layer, part, q].astype(single)
                ).astype(bfloat)
            for k, d in enumerate((p.at_x, p.at_y, p.diagonal)):
                push(
                    dk_sent,
                    dk.at[part, core, d // 2],
                    rin.at[layer, part, k],
                    drs.at[layer, part, k],
                    drr.at[layer, part, k],
                    (d, s),
                )

        def third_step(part):
            total = dk[part, core, p.quarter].astype(single)
            for k in range(3):
                p.arrived(rin.at[layer, part, k], drr.at[layer, part, k])
                total = total + rin[layer, part, k].astype(single)
            turned = total.T.astype(bfloat)
            grads[:, D + 256 * part : D + 256 * (part + 1)] = turned[:, :256]
            grads[:, 2 * D + 256 * part : 2 * D + 256 * (part + 1)] = turned[:, 256:]

        if layer == 1:
            exchange_start(3, act_hbm)

        for part in range(3):

            def one_pair(local_pair):
                pair = 2 * part + local_pair
                lanes = lane_block(pair, 128)
                lane = lax.broadcasted_iota(jnp.int32, (T, 128), 1)

                def split(value):
                    zero = jnp.zeros_like(value)
                    return jnp.concatenate(
                        [jnp.where(lane < HD, value, zero), jnp.where(lane >= HD, value, zero)]
                    )

                queries = split(query_ref[layer, :, lanes])
                outputs = split(attended_grad[:, lanes])
                keys = kv[part, :, lane_block(local_pair, 128)]
                values = kv[part, :, pl.ds(pl.multiple_of(256 + local_pair * 128, 128), 128)]
                slopes[...] = dot_rows(outputs, values)
                pair_rows = pl.ds(pl.multiple_of(pair * 2 * T, 2 * T), 2 * T)
                for half in range(2):
                    head = 2 * pair + half
                    gathered = jnp.zeros((8, TOE), single)
                    for rows in range(0, T, 32):
                        at = half * T + rows
                        prob = probs[
                            pl.ds(pl.multiple_of(head * T + rows, 32), 32), :
                        ].astype(single)
                        slope = slopes[at : at + 32, :]
                        inner = jnp.sum(prob * slope, axis=-1, keepdims=True)
                        low = (prob * (slope - inner)).astype(bfloat)
                        score_low[at : at + 32, :] = low
                        fold = jnp.concatenate(
                            [low.astype(single), jnp.zeros((32, TOE - low.shape[1]), single)],
                            axis=1,
                        )
                        fold = pltpu.roll(fold[:16], 16, 1) + fold[16:]
                        fold = pltpu.roll(fold[:8], 8, 1) + fold[8:]
                        if rows < T - 32:
                            fold = pltpu.roll(fold, T - 32 - rows, 1)
                        gathered = gathered + fold
                    fold = pltpu.roll(gathered[:4], 4, 1) + gathered[4:]
                    fold = pltpu.roll(fold[:2], 2, 1) + fold[2:]
                    fold = pltpu.roll(fold[:1], 1, 1) + fold[1:]
                    biases[pl.ds(layer * H + head, 1), :] = fold
                mixed = jnp.dot(score_low[...], keys, preferred_element_type=single) * scale
                grads[:, lanes] = jnp.where(lane < HD, mixed[:T], mixed[T:]).astype(bfloat)
                key_grad = dot_columns(queries, score_low[...]) * scale
                value_grad = dot_columns(outputs, probs[pair_rows, :])
                for d in range(8):
                    columns = slice(128 * d, 128 * (d + 1))
                    dk[
                        part, d % 2, d // 2, pl.ds(pl.multiple_of(local_pair * 128, 128), 128), :
                    ] = key_grad[:, columns].astype(bfloat)
                    dk[
                        part,
                        d % 2,
                        d // 2,
                        pl.ds(pl.multiple_of(256 + local_pair * 128, 128), 128),
                        :,
                    ] = value_grad[:, columns].astype(bfloat)

            loop(2, one_pair)
            first_step(part)
            if part > 0:
                second_step(part - 1)
            work[part]()
        second_step(2)
        third_step(0)
        work[3]()
        third_step(1)
        third_step(2)
        exchange_start(j, gsrc.at[j])
        if layer == 1:
            got_qkv.wait()
        else:
            reloads["qkv"].wait()
        return dot_rows(gsrc[j, :, : 3 * D], w_qkv[...])

    dk_sent = []
    reloads = {}

    def part0():
        for k in range(3):
            reshard.append(
                p.push(
                    up_grad_hbm.at[:, row_block(p.others[k], 192), :],
                    expert_up_out.at[:, :, lane_block(s, 768)],
                    us.at[k],
                    ur.at[k],
                    (e, p.others[k]),
                )
            )
        reshard_own.append(
            load(
                up_grad_hbm.at[:, row_block(s, 192), :],
                expert_up_out.at[:, :, lane_block(s, 768)],
                6,
            )
        )

    def part1():
        peaks.middle(peak_m)

    def part2():
        for copy in own_parts:
            copy.wait()

    def part3():
        gathers[4].first()
        peaks.finish(peak_m, peak_out)

    reshard, reshard_own = [], []
    mid_grad = mid_grad_ref[...]
    normed_grad = attention(1, mid_grad, [part0, part1, part2, part3])
    reloads["kv"] = load(kv_hbm.at[0], kv, 7)
    reloads["probs"] = load(probs_hbm.at[0], probs, 8)
    got_up = load(up_hbm, w_wide, 4)
    input_grad, gain_grad = norm_pull(one_ref[...], gains_ref[1:2, :], normed_grad)
    early[...] = small_ref[...]
    early[17:18, :] = gain_grad
    layer_grad[...] = mid_grad + input_grad
    branch = layer_grad[...].astype(bfloat)
    xg[5, own_rows, :] = branch
    gathers[5].first()
    got_down.wait()

    def slope_part(i):
        lanes = lane_block(i, 512)
        act_grad = dot_rows(xg[5, own_rows, :], w_down[row_block(i, 512), :])
        gsrc[2, :, lanes] = (act_grad * gelu_slope(pre_ref[:, lanes])).astype(bfloat)

    loop(6, slope_part)
    exchange_start(2, gsrc.at[2])
    gathers[4].second()
    gathers[5].second()
    got_up.wait()
    dense_grad = dot_rows(gsrc[2], w_wide[...])
    reloads["out"] = load(proj0_hbm, w_out, 9)
    reloads["qkv"] = load(qkv0_hbm, w_qkv, 10)
    input_grad, gain_grad = norm_pull(mid_ref[...], gains_ref[2:3, :], dense_grad)
    early[18:19, :] = gain_grad
    layer_grad[...] = layer_grad[...] + input_grad
    small = SmallReduce(
        p, early, early_z, early_p, jnp.add, (szs.at[1], szr.at[1], sps.at[1], spr.at[1])
    )
    small.start()
    gathers[4].third()
    gathers[5].third()
    got_early.wait()
    tile_attention(1)

    def part4():
        gathers[4].done()
        tile_up()

    def part5():
        gathers[5].done()
        tile_down()

    def part6():
        small.middle(early_m)

    def part7():
        gathers[2].first()
        gathers[3].first()
        z_finish(0, zb.at[0], zin.at[0], 192, att_out.at[1])
        gather_att1.first()

    normed_grad = attention(0, layer_grad[...], [part4, part5, part6, part7])
    input_grad, gain_grad = norm_pull(
        hidden_ref[...].astype(single), gains_ref[0:1, :], normed_grad
    )
    hidden_grad_out[...] = layer_grad[...] + input_grad
    late[...] = jnp.zeros_like(late)
    for i in range(6):
        late[i : i + 1, :] = gain_grad[:, 128 * i : 128 * (i + 1)]
    late[8:32, :NB] = lax.dot_general(
        biases[...],
        jnp.where(lax.broadcasted_iota(jnp.int32, (NB, TOE), 0) == buckets_ref[...], 1.0, 0.0),
        (((1,), (1,)), ((), ())),
        precision=lax.Precision.HIGHEST,
        preferred_element_type=single,
    )
    tail = SmallReduce(
        p, late, late_z, late_p, jnp.add, (szs.at[2], szr.at[2], sps.at[2], spr.at[2])
    )
    tail.start()
    gathers[2].second()
    gathers[3].second()
    z_finish(2, zb.at[2], zin.at[2], 192, up_out)
    gather_up.first()
    gather_att1.second()
    gathers[2].third()
    gathers[3].third()
    z_finish(3, zb_down, zin_down, 96, down_out)
    gather_down.first()
    gather_att1.third()
    gather_up.second()
    gathers[2].done()
    gathers[3].done()
    tile_attention(0)
    tail.middle(late_m)
    small.finish(early_m, small_out)
    gather_up.third()
    gather_down.second()
    gather_down.third()
    z_finish(1, zb.at[1], zin.at[1], 192, att_out.at[0])
    gather_att0.first()
    gather_att1.done()
    gather_up.done()
    gather_down.done()
    gather_att0.second()
    gather_att0.third()
    tail.finish(late_m, late_out)
    for copy in reshard:
        copy.wait_recv()
    reshard_own[0].wait()
    gather_att0.done()
    for copy in p.sent + dk_sent:
        copy.wait_send()


def backward(
    mid_grad, layer_one, hidden, mid, gains, normed, queries, attended, dense_normed, act, pre_act,
    buckets, small, peak_rows, early_rows, weights, kv, probs, up_grad,
):
    length = T * lax.axis_size("expert")
    vmem = pl.BlockSpec(memory_space=VMEM)
    anywhere = pl.BlockSpec(memory_space=ANY)
    shape = jax.ShapeDtypeStruct
    ff = pre_act.shape[1]
    sem = pltpu.SemaphoreType.DMA
    peak_shape, early_shape, late_shape = (2 * H, 128), small.shape, (32, 128)
    return pl.pallas_call(
        backward_kernel,
        name="backward_layers",
        out_shape=(
            shape((T, D), single),
            shape((2, 8, 192, 384), bfloat),
            shape((8, 192, 384), bfloat),
            shape((8, 96, D), bfloat),
            shape(early_shape, single),
            shape(late_shape, single),
            shape(peak_shape, single),
            shape((EXP_DEV, 192, ff), bfloat),
        ),
        in_specs=[vmem] * 10 + [anywhere] * 14,
        out_specs=(vmem,) * 7 + (anywhere,),
        scratch_shapes=[
            VMEM((D, ff), bfloat),
            VMEM((ff, D), bfloat),
            VMEM((3, length, 512), bfloat),
            VMEM((H * T, length), bfloat),
            VMEM((6, length, D), bfloat),
            VMEM((4, length, 384), bfloat),
            VMEM((3, T, 4 * D), bfloat),
            VMEM((3, D, 384), bfloat),
            VMEM((3, 3, 192, 384), bfloat),
            VMEM((384, D), bfloat),
            VMEM((3, 96, D), bfloat),
            VMEM((2 * T, length), single),
            VMEM((2 * T, length), bfloat),
            VMEM((3, 2, 4, 512, 128), bfloat),
            VMEM((2, 3, 4, 512, 128), bfloat),
            VMEM((2, 3, 3, 512, 128), bfloat),
            VMEM((T, D), bfloat),
            VMEM((T, D), single),
            VMEM((2 * H, TOE), single),
            VMEM(early_shape, single),
            VMEM((3,) + early_shape, single),
            VMEM((7,) + early_shape, single),
            VMEM(early_shape, single),
            VMEM(late_shape, single),
            VMEM((3,) + late_shape, single),
            VMEM((7,) + late_shape, single),
            VMEM(late_shape, single),
            VMEM((3,) + peak_shape, single),
            VMEM((7,) + peak_shape, single),
            VMEM(peak_shape, single),
            sem((10, 7)), sem((10, 7)),
            sem((4, 7)), sem((4, 7)),
            sem((4, 3)), sem((4, 3)),
            sem((2, 3)), sem((2, 3)),
            sem((2, 3, 3)), sem((2, 3, 3)),
            sem((3, 3)), sem((3, 3)),
            sem((3, 7)), sem((3, 7)),
            sem((3,)), sem((3,)),
            sem((17,)),
        ],
        compiler_params=pltpu.CompilerParams(
            collective_id=3, has_side_effects=True, vmem_limit_bytes=60 * 2**20
        ),
    )(
        mid_grad, layer_one, hidden, mid, gains, queries, pre_act, buckets, small, peak_rows,
        early_rows.reshape(2, length, D), normed, attended, dense_normed, act, *weights, kv, probs, up_grad,
    )


def experts_kernel(
    normed_ref,
    mid_ref,
    gains_ref,
    router_turned_ref,
    slots_ref,
    own_cot_ref,
    cot_hbm,
    up_hbm,
    down_hbm,
    normed_hbm,
    attended_hbm,
    hidden_out,
    mid_grad_out,
    small_out,
    up_grad_out,
    down_grad_out,
    early_rows,
    normed_all,
    cots,
    w_up,
    w_down,
    rows,
    gated,
    gates,
    acts,
    pre_grads,
    raw,
    row_send,
    out_send,
    row_back,
    out_back,
    slot_grads,
    slot_z,
    slot_sum,
    slot_plane,
    row_part,
    out_part,
    row_z,
    out_z,
    ns,
    nr,
    gs,
    gr,
    rs,
    rr,
    os,
    orr,
    ss,
    sr,
    ps,
    pr,
    rzs,
    rzr,
    ozs,
    ozr,
    loads,
    early_s,
    early_r,
):
    p = Plane()
    e, s = p.e, p.s
    groups = [s] + [lax.rem(s + 4 - k, 4) for k in range(1, 4)]

    def load(source, target, i):
        copy = pltpu.make_async_copy(source, target, loads.at[i])
        copy.start()
        return copy

    got_cots = [load(cot_hbm.at[groups[k]], cots.at[k], k) for k in range(2)]
    got_up = load(up_hbm, w_up, 4)
    got_down = load(down_hbm, w_down, 5)
    own_early = [
        load(source.at[1], early_rows.at[i, e], 6 + i)
        for i, source in enumerate((normed_hbm, attended_hbm))
    ]
    normed_all[s, e] = normed_ref[...]
    greet([(d, s) for d in p.around] + [(e, other) for other in p.others])
    mine = normed_all.at[s, e]
    for k in range(3):
        p.push(mine, mine, ns.at[k], nr.at[k], (e, p.others[k]))

    def gather(k):
        g = groups[k]
        return PlaneGather(p, lambda who: normed_all.at[g, who], gs.at[k], gr.at[k])

    gathers = [gather(k) for k in range(4)]
    gathers[0].first()
    early = [
        PlaneGather(
            p, functools.partial(lambda i, who: early_rows.at[i, who], i), early_s.at[i], early_r.at[i]
        )
        for i in range(2)
    ]
    for i in range(2):
        own_early[i].wait()
        early[i].first()

    ids = 2 * e * CAP + lax.broadcasted_iota(jnp.int32, (2 * CAP, T), 0)
    expert_low = CAP * lax.broadcasted_iota(jnp.int32, (16, T), 0)

    def route_masks(g, who):
        both = slots_ref[g, who]
        first, second = both[:1], both[1:2]
        return first, second, ids == first, ids == second

    def select_cots(k):
        g = groups[k]
        got_cots[k].wait()

        def one(who):
            _, _, mark0, mark1 = route_masks(g, who)
            mark = jnp.where(mark0 | mark1, 1.0, 0.0).astype(bfloat)
            picked = jnp.dot(mark, cots[k % 2, who], preferred_element_type=single).astype(bfloat)
            for j in range(2):
                raw[j, g, row_block(who, CAP), :] = picked[j * CAP : (j + 1) * CAP]

        for who in range(8):
            one(who)
        if k < 2:
            got_cots.append(load(cot_hbm.at[groups[k + 2]], cots.at[k], k + 2))

    def select_rows(k):
        g = groups[k]

        def one(who):
            slot0, slot1, mark0, mark1 = route_masks(g, who)
            block = normed_all[g, who]
            mark = jnp.where(mark0 | mark1, 1.0, 0.0).astype(bfloat)
            picked = jnp.dot(mark, block, preferred_element_type=single).astype(bfloat)
            logits = dot_rows(router_turned_ref[...], block)
            chosen = [
                jnp.sum(
                    jnp.where((slot >= expert_low) & (slot < expert_low + CAP), logits, 0.0),
                    axis=0,
                    keepdims=True,
                )
                for slot in (slot0, slot1)
            ]
            top = jnp.maximum(chosen[0], chosen[1])
            weight = [jnp.exp(value - top) for value in chosen]
            total = weight[0] + weight[1]
            gate = jnp.sum(
                jnp.where(mark0, weight[0] / total, 0.0) + jnp.where(mark1, weight[1] / total, 0.0),
                axis=1,
                keepdims=True,
            )
            for j in range(2):
                part = slice(j * CAP, (j + 1) * CAP)
                rows[j, g, row_block(who, CAP), :] = picked[part]
                gates[j, g, row_block(who, CAP), :] = jnp.broadcast_to(gate[part], (CAP, 128))

        for who in range(8):
            one(who)

    def compute(k):
        g = groups[k]

        def one(j):
            before = jnp.dot(rows[j, g], w_up[j], preferred_element_type=single)
            act, slope = gelu_both(before)
            act = act.astype(bfloat)
            acts[j, g] = act
            gate = gates[j, g][:, :1]
            cot = raw[j, g].astype(single)
            weighted = (gate * cot).astype(bfloat)
            gated[j, g] = weighted
            act_grad = dot_rows(weighted, w_down[j])
            pre_grad = (act_grad * slope).astype(bfloat)
            pre_grads[j, g] = pre_grad
            row_grad = dot_rows(pre_grad, w_up[j])
            row_send[g, j] = row_grad.astype(bfloat).reshape(8, CAP, D)
            out = jnp.dot(act, w_down[j], preferred_element_type=single)
            out_send[g, j] = (gate * out).astype(bfloat).reshape(8, CAP, D)
            product = out * cot
            folded = product[:, :128]
            for i in range(1, D // 128):
                folded = folded + product[:, 128 * i : 128 * (i + 1)]
            slot_grads[g, j : j + 1, :] = jnp.sum(folded.T, axis=0, keepdims=True)

        for j in range(2):
            one(j)

    def give_back(k, source, target, send_sems, recv_sems):
        g = groups[k]
        target[g, e] = source[g, :, e]
        for i, d in enumerate(p.around):
            p.push(
                source.at[g, :, d], target.at[g, e], send_sems.at[k, i], recv_sems.at[k, i], (d, s)
            )

    def step(k):
        select_rows(k)
        compute(k)

    def arrive(k):
        p.arrived(mine, nr.at[k - 1])
        gathers[k].first()

    slot_grads[...] = jnp.zeros_like(slot_grads)
    select_cots(0)
    gathers[0].second()
    arrive(1)
    gathers[0].third()
    arrive(2)
    early[0].second()
    early[1].second()
    arrive(3)
    gathers[0].done()
    gathers[1].second()
    got_up.wait()
    got_down.wait()
    step(0)
    gathers[1].third()
    gathers[2].second()
    gathers[3].second()
    early[0].third()
    early[1].third()
    select_cots(1)
    gathers[1].done()
    step(1)
    give_back(1, row_send, row_back, rs, rr)
    gathers[2].third()
    gathers[3].third()
    select_cots(2)
    gathers[2].done()
    step(2)
    give_back(2, row_send, row_back, rs, rr)
    select_cots(3)
    gathers[3].done()
    step(3)
    give_back(3, row_send, row_back, rs, rr)
    for k in (1, 2, 3):
        give_back(k, out_send, out_back, os, orr)
    give_back(0, row_send, row_back, rs, rr)
    give_back(0, out_send, out_back, os, orr)
    for k in range(3):
        p.push(
            slot_grads.at[p.others[k]], slot_z.at[k], ss.at[k], sr.at[k], (e, p.others[k])
        )

    def weight_grads(i):
        j = i // 3
        lanes = lane_block(lax.rem(i, 3), 256)
        inputs = rows[j].reshape(4 * 8 * CAP, D)
        up_grad_out[j, :, lanes] = dot_columns(
            inputs, pre_grads[j, :, :, lanes].reshape(4 * 8 * CAP, 256)
        ).astype(bfloat)
        inputs = acts[j].reshape(4 * 8 * CAP, -1)
        down_grad_out[j, :, lanes] = dot_columns(
            inputs, gated[j, :, :, lanes].reshape(4 * 8 * CAP, 256)
        ).astype(bfloat)

    loop(3, weight_grads)
    total = slot_grads[s]
    for k in range(3):
        p.arrived(slot_z.at[k], sr.at[k])
        total = total + slot_z[k]
    slot_sum[...] = total
    slot_plane[e] = total
    for i, d in enumerate(p.around):
        p.push(slot_sum, slot_plane.at[e], ps.at[i], pr.at[i], (d, s))

    slot_lanes = lax.broadcasted_iota(jnp.int32, (T, 16 * CAP), 1)

    def slot_columns(g):
        return slots_ref[g, e].astype(single).T.astype(jnp.int32)

    def collect(k, back, recv_sems, part, z_in, z_send, z_recv):
        g = groups[k]
        for i in range(7):
            p.arrived(back.at[g, e], recv_sems.at[k, i])
        columns = slot_columns(g)
        marks = jnp.where(
            (columns[:, :1] == slot_lanes) | (columns[:, 1:2] == slot_lanes), 1.0, 0.0
        ).astype(bfloat)
        combined = jnp.dot(
            marks, back[g].reshape(16 * CAP, D), preferred_element_type=single
        )
        part[g] = combined.astype(bfloat)
        if k:
            p.push(part.at[g], z_in.at[k - 1], z_send.at[k - 1], z_recv.at[k - 1], (e, g))

    for k in (1, 2, 3):
        collect(k, row_back, rr, row_part, row_z, rzs, rzr)

    def weight_later(i):
        weight_grads(i + 3)

    loop(3, weight_later)

    for i in range(7):
        p.arrived(slot_sum, pr.at[i])
    turned = pltpu.roll(
        slot_plane[...].reshape(64, 8 * CAP), lax.rem(8 * CAP - CAP * e, 8 * CAP), 1
    )
    logits = dot_rows(normed_ref[...], router_turned_ref[...])
    columns = slot_columns(s)
    expert_lanes = CAP * lax.broadcasted_iota(jnp.int32, (T, 16), 1)
    picks, chosen, grads = [], [], []
    small_lanes = lax.broadcasted_iota(jnp.int32, (T, CAP), 1)
    for r in range(2):
        slot = columns[:, r : r + 1]
        picks.append((slot >= expert_lanes) & (slot < expert_lanes + CAP))
        chosen.append(jnp.sum(jnp.where(picks[r], logits, 0.0), axis=1, keepdims=True))
        found = jnp.zeros((T, CAP), single)
        for who in range(8):
            for j in range(2):
                values = turned[8 * who + j : 8 * who + j + 1, :CAP]
                found = found + jnp.where(slot - (2 * who + j) * CAP == small_lanes, values, 0.0)
        grads.append(jnp.sum(found, axis=1, keepdims=True))
    top = jnp.maximum(chosen[0], chosen[1])
    weight = [jnp.exp(value - top) for value in chosen]
    total = weight[0] + weight[1]
    weight = [value / total for value in weight]
    mean = weight[0] * grads[0] + weight[1] * grads[1]
    logit_grad = jnp.zeros((T, 16), single)
    for r in range(2):
        logit_grad = logit_grad + jnp.where(picks[r], weight[r] * (grads[r] - mean), 0.0)
    logit_grad = logit_grad.astype(bfloat)
    small_out[...] = jnp.zeros_like(small_out)
    small_out[:16, :] = dot_columns(logit_grad, normed_ref[...])
    normed_grad = jnp.dot(logit_grad, router_turned_ref[...], preferred_element_type=single)
    for k in (1, 2, 3):
        collect(k, out_back, orr, out_part, out_z, ozs, ozr)
    collect(0, row_back, rr, row_part, row_z, rzs, rzr)
    normed_grad = normed_grad + row_part[s].astype(single)
    for k in range(3):
        p.arrived(row_z.at[k], rzr.at[k])
        normed_grad = normed_grad + row_z[k].astype(single)
    input_grad, gain_grad = norm_pull(mid_ref[...], gains_ref[3:4, :], normed_grad)
    small_out[16:17, :] = gain_grad
    mid_grad_out[...] = own_cot_ref[...].astype(single) + input_grad

    collect(0, out_back, orr, out_part, out_z, ozs, ozr)
    result = mid_ref[...] + out_part[s].astype(single)
    for k in range(3):
        p.arrived(out_z.at[k], ozr.at[k])
        result = result + out_z[k].astype(single)
    hidden_out[...] = result.astype(bfloat)
    for gather in early:
        gather.done()
    for copy in p.sent:
        copy.wait_send()


def run_experts(
    moe_normed, mid, gains, router, slots, own_cot, cots, up_own, expert_down, normed, attended
):
    vmem = pl.BlockSpec(memory_space=VMEM)
    anywhere = pl.BlockSpec(memory_space=ANY)
    shape = jax.ShapeDtypeStruct
    width = expert_down.shape[1]
    sem = pltpu.SemaphoreType.DMA
    per_expert = (EXP_DEV, 4, 8 * CAP)
    sends = (4, EXP_DEV, 8, CAP, D)
    backs = (4, 8, EXP_DEV, CAP, D)
    return pl.pallas_call(
        experts_kernel,
        name="experts",
        out_shape=(
            shape((T, D), bfloat),
            shape((T, D), single),
            shape((24, D), single),
            shape((EXP_DEV, D, width), bfloat),
            shape((EXP_DEV, width, D), bfloat),
            shape((2, 8, T, D), bfloat),
        ),
        in_specs=[vmem] * 6 + [anywhere] * 5,
        out_specs=(vmem,) * 5 + (anywhere,),
        scratch_shapes=[
            VMEM((4, 8, T, D), bfloat),
            VMEM((2, 8, T, D), bfloat),
            VMEM((EXP_DEV, D, width), bfloat),
            VMEM((EXP_DEV, width, D), bfloat),
            VMEM(per_expert + (D,), bfloat),
            VMEM(per_expert + (D,), bfloat),
            VMEM(per_expert + (128,), single),
            VMEM(per_expert + (width,), bfloat),
            VMEM(per_expert + (width,), bfloat),
            VMEM(per_expert + (D,), bfloat),
            VMEM(sends, bfloat),
            VMEM(sends, bfloat),
            VMEM(backs, bfloat),
            VMEM(backs, bfloat),
            VMEM((4, 8, 8 * CAP), single),
            VMEM((3, 8, 8 * CAP), single),
            VMEM((8, 8 * CAP), single),
            VMEM((8, 8, 8 * CAP), single),
            VMEM((4, T, D), bfloat),
            VMEM((4, T, D), bfloat),
            VMEM((3, T, D), bfloat),
            VMEM((3, T, D), bfloat),
            sem((3,)), sem((3,)),
            sem((4, 7)), sem((4, 7)),
            sem((4, 7)), sem((4, 7)),
            sem((4, 7)), sem((4, 7)),
            sem((3,)), sem((3,)),
            sem((7,)), sem((7,)),
            sem((3,)), sem((3,)),
            sem((3,)), sem((3,)),
            sem((8,)),
            sem((2, 7)), sem((2, 7)),
        ],
        compiler_params=pltpu.CompilerParams(
            collective_id=4, has_side_effects=True, vmem_limit_bytes=60 * 2**20
        ),
    )(
        moe_normed, mid, gains, router, slots, own_cot, cots, up_own, expert_down, normed, attended
    )


def finish_kernel(
    att_hbm,
    up_hbm,
    down_hbm,
    expert_up_hbm,
    expert_down_hbm,
    small_hbm,
    late_hbm,
    peak_hbm,
    grad_hbm,
    result_hbm,
    qkv_out,
    out_out,
    up_out,
    down_out,
    expert_up_out,
    expert_down_out,
    attn_gain_out,
    mlp_gain_out,
    bias_out,
    router_out,
    clip_out,
    grad_out,
    result_out,
    att,
    up,
    down,
    expert_up,
    expert_down,
    small_ref,
    late_ref,
    peak_ref,
    grad,
    qkv_wide,
    out_wide,
    up_wide,
    down_wide,
    expert_up_wide,
    expert_down_wide,
    turned,
    in_sems,
    out_sems,
):
    s = lax.axis_index("shard")

    def start(source, target, sem):
        copy = pltpu.make_async_copy(source, target, sem)
        copy.start()
        return copy

    got = [
        start(source, target, in_sems.at[i])
        for i, (source, target) in enumerate(
            (
                (expert_down_hbm, expert_down),
                (expert_up_hbm, expert_up),
                (att_hbm, att),
                (up_hbm, up),
                (down_hbm, down),
                (grad_hbm, grad),
                (small_hbm, small_ref),
                (late_hbm, late_ref),
                (peak_hbm, peak_ref),
                (result_hbm, result_out),
            )
        )
    ]
    put = []

    def widen(i):
        rows = row_block(i, 128)
        for j in range(EXP_DEV):
            expert_down_wide[j, rows, :] = expert_down[j, rows, :].astype(single)

    def widen_up(i):
        lanes = lane_block(i, 384)
        for j in range(EXP_DEV):
            expert_up_wide[j, :, lanes] = expert_up[j, :, lanes].astype(single)

    def widen_down(i):
        down_wide[row_block(i, 96), :] = down[i].astype(single)

    got[0].wait()
    loop(expert_down.shape[1] // 128, widen)
    put.append(start(expert_down_wide, expert_down_out, out_sems.at[0]))
    got[1].wait()
    loop(expert_up.shape[2] // 384, widen_up)
    put.append(start(expert_up_wide, expert_up_out, out_sems.at[1]))
    got[2].wait()
    for layer in range(2):
        for b in range(6):
            qkv_wide[layer, :, 384 * b : 384 * (b + 1)] = att[layer, b].astype(single)
        for b in range(2):
            out_wide[layer, :, 384 * b : 384 * (b + 1)] = att[layer, 6 + b].astype(single)
    put.append(start(qkv_wide, qkv_out, out_sems.at[2]))
    put.append(start(out_wide, out_out, out_sems.at[3]))
    got[3].wait()
    for b in range(8):
        up_wide[:, 384 * b : 384 * (b + 1)] = up[b].astype(single)
    put.append(start(up_wide, up_out, out_sems.at[4]))
    got[4].wait()
    loop(8, widen_down)
    put.append(start(down_wide, down_out, out_sems.at[5]))

    for copy in got[5:]:
        copy.wait()
    grad_out[...] = grad[...][:, None, :]
    part = D // 4
    back = lax.rem(D - part * s, D)
    first_gain = jnp.concatenate([late_ref[i : i + 1, :] for i in range(6)], axis=1)
    gains = jnp.concatenate([first_gain, small_ref[16:19, :], jnp.zeros((4, D), single)])
    gains = pltpu.roll(gains, back, 1)[:, :part]
    attn_gain_out[0:1, :] = gains[0:1]
    attn_gain_out[1:2, :] = gains[2:3]
    mlp_gain_out[0:1, :] = gains[3:4]
    mlp_gain_out[1:2, :] = gains[1:2]
    turned[:, :16] = small_ref[:16, :].T
    router_out[...] = turned[row_block(s, part), :16].T
    turned[:128, : 2 * H] = late_ref[8:32, :].T
    biases = turned[row_block(s, 8), : 2 * H]
    peaks = peak_ref[...].T[:1, :]
    clips = jnp.sqrt(clip_limit / jnp.maximum(peaks, clip_limit))
    for layer in range(2):
        bias_out[layer] = biases[:, layer * H : (layer + 1) * H]
        clip_out[layer : layer + 1, :] = clips[:, layer * H : (layer + 1) * H]
    for copy in put:
        copy.wait()


def finish(att, up, down, expert_up, expert_down, small, late, peaks, grad, result):
    vmem = pl.BlockSpec(memory_space=VMEM)
    anywhere = pl.BlockSpec(memory_space=ANY)
    loaded = (att, up, down, expert_up, expert_down, small, late, peaks, grad)
    sem = pltpu.SemaphoreType.DMA
    wide = (
        (2, 192, 3 * D), (2, 192, D), (192, 8 * 384), (8 * 96, D), expert_up.shape,
        expert_down.shape,
    )
    return pl.pallas_call(
        finish_kernel,
        name="finish",
        out_shape=tuple(
            jax.ShapeDtypeStruct(dims, single)
            for dims in wide + ((2, 192), (2, 192), (2, 8, H), (16, 192), (2, H), (T, 1, D))
        )
        + (jax.ShapeDtypeStruct(result.shape, bfloat),),
        in_specs=[anywhere] * 10,
        out_specs=(anywhere,) * 6 + (vmem,) * 7,
        scratch_shapes=[VMEM(item.shape, item.dtype) for item in loaded]
        + [VMEM(dims, single) for dims in wide]
        + [VMEM((D, 128), single), sem((10,)), sem((6,))],
        compiler_params=pltpu.CompilerParams(vmem_limit_bytes=60 * 2**20),
    )(*loaded, result)


def shards(
    hidden_in,
    attn_gain,
    qkv_weight,
    out_weight,
    rel_bias,
    bucket_table,
    mlp_gain,
    mlp_up,
    mlp_down,
    router_weight,
    expert_up,
    expert_down,
    routes,
    out_grad,
):
    block_rows = hidden_in.shape[1]
    length = bucket_table.shape[0]
    groups = lax.axis_size("shard")

    def block(values):
        return jnp.pad(values, ((0, -values.shape[0] % 8), (0, 256 - values.shape[1])))

    part = D // groups
    small = jnp.concatenate(
        [
            block(jnp.concatenate([attn_gain, mlp_gain])),
            block(rel_bias.transpose(1, 0, 2).reshape(NB // groups, 2 * H)),
            block(router_weight.T),
        ]
    ).astype(single)
    backward_table = jnp.pad(bucket_table[::-1], (0, TOE))
    buckets = lax.dynamic_slice_in_dim(
        backward_table, length - block_rows * (lax.axis_index("expert") + 1), TOE
    )[None]
    cotangent = out_grad.reshape(block_rows, D)
    (
        normed, queries, attended, mid_first, mid_second, dense_normed, pre_act, activation, layer_one, peak_rows,
        moe_normed, gains, router, slots, qkv0, qkv1, projection0, projection1, dense_up,
        dense_down, kv, probs, up_own, cotangents,
    ) = forward(
        hidden_in.reshape(block_rows, D), small, buckets, routes.reshape(block_rows, 2).T,
        qkv_weight, out_weight, mlp_up, mlp_down, expert_up, cotangent,
    )
    hidden_out, mid_grad, small_in, up_grad, expert_down_low, early_rows = run_experts(
        moe_normed, mid_second, gains, router, slots, cotangent, cotangents, up_own, expert_down,
        normed, attended,
    )
    hidden_grad, attention_sum, up_sum, down_sum, small_sum, late_sum, peaks, expert_up_low = (
        backward(
            mid_grad, layer_one, hidden_in.reshape(block_rows, D), mid_first, gains, normed, queries,
            attended, dense_normed, activation, pre_act, buckets, small_in, peak_rows,
            early_rows, (qkv0, qkv1, projection0, projection1, dense_up, dense_down), kv, probs,
            up_grad,
        )
    )
    (
        qkv_grad, out_weight_grad, mlp_up_grad, mlp_down_grad, expert_up_grad, expert_down_grad,
        attn_gain_grad, mlp_gain_grad, rel_bias_grad, router_grad, clip_scales, hidden_grad, hidden_out,
    ) = finish(
        attention_sum, up_sum, down_sum, expert_up_low, expert_down_low, small_sum, late_sum, peaks,
        hidden_grad, hidden_out,
    )
    return (
        hidden_out.reshape(hidden_in.shape),
        hidden_grad.reshape(hidden_in.shape),
        attn_gain_grad,
        qkv_grad,
        out_weight_grad,
        rel_bias_grad,
        mlp_gain_grad,
        mlp_up_grad,
        mlp_down_grad,
        router_grad.T,
        expert_up_grad,
        expert_down_grad,
        clip_scales,
    )


def solution(mesh):
    tokens = P("shard", "expert", None, None)
    columns = P(None, "shard")
    layers = P(None, "shard", None)
    rows = P("shard", None)
    owned = P("expert", "shard", None)
    in_specs = (
        tokens, columns, layers, layers, layers, P(), columns, rows, rows, rows, owned, owned,
        tokens, tokens,
    )
    out_specs = (
        tokens, tokens, columns, layers, layers, layers, columns, rows, rows, rows, owned, owned,
        P(),
    )
    sized = mesh.shape["expert"] == 8 and mesh.shape["shard"] == 4
    part = shards if sized else plain_shards
    return jax.shard_map(part, mesh=mesh, in_specs=in_specs, out_specs=out_specs, check_vma=False)
```

```python
import functools
import math

import jax
import jax.numpy as jnp
from jax import lax
from jax.experimental import pallas as pl
from jax.experimental.pallas import tpu as pltpu
from jax.sharding import PartitionSpec as P

D = 768
H = 12
HD = 64
NB = 32
EXP_DEV = 2

epsilon = 1e-06
clip_limit = 6.0
bfloat = jnp.bfloat16
single = jnp.float32


def rms_norm(inputs, norm_gain):
    return (
        inputs * lax.rsqrt(jnp.mean(inputs * inputs, axis=-1, keepdims=True) + epsilon) * norm_gain
    )


def norm_back(inputs, norm_gain, upstream):
    _, pullback = jax.vjp(rms_norm, inputs, norm_gain)
    return pullback(upstream)


def gelu_back(pre_values, upstream):
    _, pullback = jax.vjp(jax.nn.gelu, pre_values)
    return pullback(upstream)[0]


def matmul(left, right):
    return jnp.dot(left, right, preferred_element_type=single)


def shard_shift(block, amount):
    count = lax.axis_size("shard")
    return lax.ppermute(block, "shard", [(i, (i + amount) % count) for i in range(count)])


def gather_shard(block):
    count = lax.axis_size("shard")
    here = lax.axis_index("shard")
    result = jnp.zeros((count,) + block.shape, block.dtype)
    for step in range(count):
        piece = block if step == 0 else shard_shift(block, step)
        result = lax.dynamic_update_slice_in_dim(result, piece[None], (here - step) % count, 0)
    return result


def scatter_shard(blocks, sent=bfloat):
    count = lax.axis_size("shard")
    here = lax.axis_index("shard")
    total = lax.dynamic_index_in_dim(blocks, here, 0, keepdims=False).astype(single)
    for step in range(1, count):
        part = lax.dynamic_index_in_dim(blocks, (here + step) % count, 0, keepdims=False)
        total = total + shard_shift(part.astype(sent), step).astype(single)
    return total


def spread(columns):
    experts, shard_count = lax.axis_size("expert"), lax.axis_size("shard")
    rows, width = columns.shape
    cut = columns.reshape(rows, shard_count, experts, width // (shard_count * experts))
    return cut.transpose(0, 2, 1, 3).reshape(rows, width)


def unspread(columns):
    experts, shard_count = lax.axis_size("expert"), lax.axis_size("shard")
    rows, width = columns.shape
    cut = columns.reshape(rows, experts, shard_count, width // (shard_count * experts))
    return cut.transpose(0, 2, 1, 3).reshape(rows, width)


def gather_weight(block):
    part = block.shape[0] // lax.axis_size("expert")
    own = lax.dynamic_slice_in_dim(block, lax.axis_index("expert") * part, part, 0)
    column = gather_shard(own).reshape(-1, block.shape[1])
    return lax.all_gather(column, "expert", axis=0, tiled=True)


def reduce_weight(grad):
    part = lax.psum_scatter(grad.astype(bfloat), "expert", scatter_dimension=0, tiled=True)
    blocks = part.reshape((lax.axis_size("shard"), -1) + part.shape[1:])
    own = scatter_shard(blocks).astype(bfloat)
    return lax.all_gather(own, "expert", axis=0, tiled=True).astype(single)


def bucket_marks(distance, lower, upper):
    inside = (distance[None] >= lower[:, None, None]) & (distance[None] < upper[:, None, None])
    return inside.astype(bfloat)


def position_bias(marks, bias_pair):
    return jnp.einsum("bij,bh->hij", marks, bias_pair, preferred_element_type=single)


def attention_forward(hidden, norm_gain, qkv, projection, bias_pair, geometry):
    distance, marks, scale = geometry
    rows = hidden.shape[0]
    normalized = spread(rms_norm(hidden, norm_gain).astype(bfloat))
    packed = matmul(normalized, qkv).astype(bfloat)
    key_value = lax.all_gather(packed[:, D:], "expert", axis=0, tiled=True)
    shifted = position_bias(marks, bias_pair)
    causal = distance >= 0
    queries = packed[:, :D].reshape(rows, H, HD)
    keys = key_value[:, :D].reshape(-1, H, HD)
    values = key_value[:, D:].reshape(-1, H, HD)
    raw_scores = jnp.einsum("ihd,jhd->hij", queries, keys, preferred_element_type=single) * scale
    head_peak = jnp.max(jnp.where(causal[None], raw_scores, -jnp.inf), axis=(1, 2))
    masked = jnp.where(causal[None], raw_scores + shifted, -jnp.inf)
    softmax_top = jnp.max(masked, axis=-1, keepdims=True)
    exponent = jnp.exp(masked - softmax_top)
    softmax_sum = jnp.sum(exponent, axis=-1, keepdims=True)
    probs = (exponent / softmax_sum).astype(bfloat)
    log_total = softmax_top[..., 0] + jnp.log(softmax_sum[..., 0])
    attended = jnp.einsum("hij,jhd->ihd", probs, values, preferred_element_type=single)
    attended = spread(attended.astype(bfloat).reshape(rows, D))
    saved = (normalized, packed, key_value, log_total, attended)
    return hidden + matmul(attended, projection), head_peak, saved


def attention_backward(
    upstream, hidden, norm_gain, qkv, projection, bias_pair, geometry, saved
):
    distance, marks, scale = geometry
    normalized, packed, key_value, log_total, attended = saved
    rows = hidden.shape[0]
    branch_grad = upstream.astype(bfloat)
    projection_grad = matmul(attended.T, branch_grad)
    attended_grad = unspread(matmul(branch_grad, projection.T).astype(bfloat))
    shifted = position_bias(marks, bias_pair)
    causal = distance >= 0
    queries = packed[:, :D].reshape(rows, H, HD)
    keys = key_value[:, :D].reshape(-1, H, HD)
    values = key_value[:, D:].reshape(-1, H, HD)
    grad_heads = attended_grad.reshape(rows, H, HD)
    raw_scores = jnp.einsum("ihd,jhd->hij", queries, keys, preferred_element_type=single) * scale
    probs = jnp.where(causal[None], jnp.exp(raw_scores + shifted - log_total[..., None]), 0.0)
    prob_grad = jnp.einsum("ihd,jhd->hij", grad_heads, values, preferred_element_type=single)
    row_dot = jnp.sum(prob_grad * probs, axis=-1)
    score_grad = (probs * (prob_grad - row_dot[..., None])).astype(bfloat)
    query_grad = jnp.einsum("hij,jhd->ihd", score_grad, keys, preferred_element_type=single) * scale
    query_grad = query_grad.astype(bfloat).reshape(rows, D)
    bias_grad = jnp.einsum("hij,bij->bh", score_grad, marks, preferred_element_type=single)
    key_grad = (
        jnp.einsum("hij,ihd->jhd", score_grad, queries, preferred_element_type=single) * scale
    )
    value_grad = jnp.einsum(
        "hij,ihd->jhd", probs.astype(bfloat), grad_heads, preferred_element_type=single
    )
    pair = jnp.concatenate([key_grad.reshape(-1, D), value_grad.reshape(-1, D)], axis=-1)
    pair_grad = lax.psum_scatter(pair.astype(bfloat), "expert", scatter_dimension=0, tiled=True)
    packed_grad = jnp.concatenate([query_grad, pair_grad], axis=-1)
    qkv_grad = matmul(normalized.T, packed_grad)
    normed_grad = unspread(matmul(packed_grad, qkv.T))
    input_grad, gain_grad = norm_back(hidden, norm_gain, normed_grad)
    return upstream + input_grad, gain_grad, qkv_grad, projection_grad, bias_grad


def exchange(blocks):
    return lax.all_to_all(blocks, "expert", split_axis=0, concat_axis=0, tiled=True)


def plain_shards(
    hidden_in,
    attn_gain,
    qkv_weight,
    out_weight,
    rel_bias,
    bucket_table,
    mlp_gain,
    mlp_up,
    mlp_down,
    router_weight,
    expert_up,
    expert_down,
    routes,
    out_grad,
):
    block_rows = hidden_in.shape[1]
    length = bucket_table.shape[0]
    experts = lax.axis_size("expert")
    groups = lax.axis_size("shard")
    here = lax.axis_index("shard")
    expert_total = EXP_DEV * experts
    capacity = 4 * block_rows // expert_total
    width = expert_down.shape[1]
    scale = 1.0 / math.sqrt(HD)

    small = jnp.concatenate(
        [attn_gain.reshape(-1), mlp_gain.reshape(-1), rel_bias.reshape(-1), router_weight.reshape(-1)]
    )
    small = gather_shard(small)
    part = D // groups
    cuts = [0, 2 * part, 4 * part, 4 * part + 2 * (NB // groups) * H, small.shape[1]]
    gain_attn, gain_mlp, bias_weights, router_full = (
        small[:, cuts[i] : cuts[i + 1]] for i in range(4)
    )
    gain_attn = gain_attn.reshape(groups, 2, part).transpose(1, 0, 2).reshape(2, D).astype(single)
    gain_mlp = gain_mlp.reshape(groups, 2, part).transpose(1, 0, 2).reshape(2, D).astype(single)
    bias_weights = (
        bias_weights.reshape(groups, 2, NB // groups, H).transpose(1, 0, 2, 3).reshape(2, NB, H)
    )
    router_full = router_full.reshape(D, expert_total)

    first = gather_weight(jnp.concatenate([qkv_weight[0], out_weight[0]], axis=1))
    dense_up = gather_weight(mlp_up)
    dense_down = gather_weight(mlp_down)
    second = gather_weight(jnp.concatenate([qkv_weight[1], out_weight[1]], axis=1))
    qkv = (first[:, : 3 * D], second[:, : 3 * D])
    projection = (first[:, 3 * D :], second[:, 3 * D :])

    up_own = jnp.zeros((EXP_DEV, groups, part, width), bfloat)
    for step in range(groups):
        target = (here + step) % groups
        piece = lax.dynamic_slice_in_dim(expert_up, target * width, width, 2)
        if step:
            piece = shard_shift(piece, step)
        up_own = lax.dynamic_update_slice_in_dim(up_own, piece[:, None], (here - step) % groups, 1)
    up_own = up_own.reshape(EXP_DEV, D, width)

    route_rows = gather_shard(routes.reshape(block_rows, 2))
    upstream_all = gather_shard(out_grad.reshape(block_rows, D))
    expert_ids = jnp.arange(expert_total, dtype=jnp.int32)
    flat_routes = route_rows.reshape(groups, -1)
    marks = (flat_routes[:, :, None] == expert_ids).astype(jnp.int32)
    rank = jnp.sum((jnp.cumsum(marks, axis=1) - marks) * marks, axis=2)
    slot_of_route = flat_routes * capacity + rank
    slot_ids = jnp.arange(expert_total * capacity, dtype=jnp.int32)
    slot_marks = (slot_of_route[:, :, None] == slot_ids).astype(bfloat)
    token_marks = jnp.sum(
        slot_marks.reshape(groups, block_rows, 2, -1).astype(single), axis=2
    ).astype(bfloat)

    def dispatch(rows):
        slots = jnp.einsum("gts,gtd->gsd", token_marks, rows, preferred_element_type=single)
        slots = slots.astype(bfloat).reshape(groups, experts, EXP_DEV, capacity, D)
        return exchange(slots.transpose(1, 2, 0, 3, 4)).reshape(
            experts, EXP_DEV, groups * capacity, D
        )

    def collect(blocks):
        back = exchange(blocks.astype(bfloat)).reshape(experts, EXP_DEV, groups, capacity, D)
        return back.transpose(2, 0, 1, 3, 4).reshape(groups, expert_total * capacity, D)

    owner_rows = dispatch(upstream_all)

    own_positions = lax.axis_index("expert") * block_rows + jnp.arange(block_rows, dtype=jnp.int32)
    distance = own_positions[:, None] - jnp.arange(length, dtype=jnp.int32)[None, :]
    bounds = jnp.sum(
        (bucket_table[:, None] < jnp.arange(NB + 1, dtype=jnp.int32)[None, :]).astype(jnp.int32),
        axis=0,
    )
    geometry = (distance, bucket_marks(distance, bounds[:NB], bounds[1:]), scale)

    hidden_zero = hidden_in.reshape(block_rows, D).astype(single)
    mid_first, peak_first, saved_first = attention_forward(
        hidden_zero, gain_attn[0], qkv[0], projection[0], bias_weights[0], geometry
    )
    dense_normed = spread(rms_norm(mid_first, gain_mlp[0]).astype(bfloat))
    pre_act = matmul(dense_normed, dense_up)
    activation = spread(jax.nn.gelu(pre_act).astype(bfloat))
    layer_one = mid_first + matmul(activation, dense_down)
    mid_second, peak_second, saved_second = attention_forward(
        layer_one, gain_attn[1], qkv[1], projection[1], bias_weights[1], geometry
    )

    moe_normed = rms_norm(mid_second, gain_mlp[1]).astype(bfloat)
    normed_all = gather_shard(moe_normed)
    received = dispatch(normed_all)
    router_logits = jnp.einsum("gtd,de->gte", normed_all, router_full, preferred_element_type=single)
    selected = (route_rows[..., None] == expert_ids).astype(single)
    gates_all = jax.nn.softmax(jnp.sum(selected * router_logits[:, :, None, :], axis=-1), axis=-1)
    slot_gates = jnp.sum(
        gates_all.reshape(groups, -1)[:, :, None] * (slot_of_route[:, :, None] == slot_ids), axis=1
    )
    owner_gates = exchange(
        slot_gates.reshape(groups, experts, EXP_DEV, capacity).transpose(1, 2, 0, 3)
    ).reshape(experts, EXP_DEV, groups * capacity)

    expert_pre = jnp.einsum("sjcd,jdf->sjcf", received, up_own, preferred_element_type=single)
    expert_act = jax.nn.gelu(expert_pre).astype(bfloat)
    expert_out = jnp.einsum(
        "sjcf,jfd->sjcd", expert_act, expert_down, preferred_element_type=single
    )
    owner_grad = (owner_gates[..., None] * owner_rows.astype(single)).astype(bfloat)
    act_grad = jnp.einsum("sjcd,jfd->sjcf", owner_grad, expert_down, preferred_element_type=single)
    pre_grad = gelu_back(expert_pre, act_grad).astype(bfloat)
    row_grad = jnp.einsum("sjcf,jdf->sjcd", pre_grad, up_own, preferred_element_type=single)

    returned = collect(expert_out)
    back_rows = collect(row_grad)
    expert_down_grad = jnp.einsum(
        "sjcf,sjcd->jfd", expert_act, owner_grad, preferred_element_type=single
    )
    up_grad = jnp.einsum(
        "sjcd,sjcf->jdf", received, pre_grad, preferred_element_type=single
    ).astype(bfloat)

    route_out = jnp.einsum("grs,gsd->grd", slot_marks, returned, preferred_element_type=single)
    route_out = route_out.reshape(groups, block_rows, 2, D)
    gate_grad = scatter_shard(
        jnp.sum(route_out * upstream_all[:, :, None, :].astype(single), axis=-1), single
    )
    mixed = scatter_shard(jnp.sum(gates_all[..., None] * route_out, axis=2))
    hidden_out = (mid_second + mixed).astype(bfloat).reshape(hidden_in.shape)

    gates = lax.dynamic_index_in_dim(gates_all, here, 0, keepdims=False)
    own_selected = lax.dynamic_index_in_dim(selected, here, 0, keepdims=False)
    upstream = out_grad.reshape(block_rows, D).astype(single)
    chosen_grad = gates * (gate_grad - jnp.sum(gates * gate_grad, axis=-1, keepdims=True))
    logit_grad = jnp.sum(chosen_grad[:, :, None] * own_selected, axis=1).astype(bfloat)
    router_grad = matmul(moe_normed.T, logit_grad)
    row_terms = jnp.einsum("gts,gsd->gtd", token_marks, back_rows, preferred_element_type=single)
    normed_grad = matmul(logit_grad, router_full.T) + scatter_shard(row_terms)
    moe_input_grad, moe_gain_grad = norm_back(mid_second, gain_mlp[1], normed_grad)
    mid_grad = upstream + moe_input_grad

    up_grad = up_grad.reshape(EXP_DEV, groups, part, width)
    expert_up_grad = jnp.zeros((EXP_DEV, part, groups * width), single)
    for step in range(groups):
        piece = lax.dynamic_index_in_dim(up_grad, (here + step) % groups, 1, keepdims=False)
        if step:
            piece = shard_shift(piece, step)
        expert_up_grad = lax.dynamic_update_slice_in_dim(
            expert_up_grad, piece.astype(single), ((here - step) % groups) * width, 2
        )

    layer_grad, gain_second, qkv_second, projection_second, bias_second = attention_backward(
        mid_grad, layer_one, gain_attn[1], qkv[1], projection[1], bias_weights[1], geometry,
        saved_second,
    )
    second_grad = reduce_weight(jnp.concatenate([qkv_second, projection_second], axis=1))
    dense_branch = layer_grad.astype(bfloat)
    mlp_down_grad = reduce_weight(matmul(activation.T, dense_branch))
    hidden_act_grad = unspread(matmul(dense_branch, dense_down.T))
    pre_act_grad = gelu_back(pre_act, hidden_act_grad).astype(bfloat)
    mlp_up_grad = reduce_weight(matmul(dense_normed.T, pre_act_grad))
    dense_normed_grad = unspread(matmul(pre_act_grad, dense_up.T))
    dense_input_grad, dense_gain_grad = norm_back(mid_first, gain_mlp[0], dense_normed_grad)
    first_grad = layer_grad + dense_input_grad
    input_grad, gain_first, qkv_first, projection_first, bias_first = attention_backward(
        first_grad, hidden_zero, gain_attn[0], qkv[0], projection[0], bias_weights[0], geometry,
        saved_first,
    )
    first_weight_grad = reduce_weight(jnp.concatenate([qkv_first, projection_first], axis=1))

    gains = jnp.stack([gain_first, gain_second, dense_gain_grad, moe_gain_grad])
    biases = jnp.stack([bias_first, bias_second])
    small_grad = jnp.concatenate(
        [
            gains.reshape(4, groups, part).transpose(1, 0, 2).reshape(groups, -1),
            biases.reshape(2, groups, NB // groups, H).transpose(1, 0, 2, 3).reshape(groups, -1),
            router_grad.reshape(groups, -1),
        ],
        axis=1,
    )
    small_grad = lax.psum(scatter_shard(small_grad, single), "expert")
    gain_cut = 4 * part
    bias_cut = gain_cut + 2 * (NB // groups) * H
    own_gains = small_grad[:gain_cut].reshape(4, part)
    peaks = lax.pmax(jnp.stack([peak_first, peak_second]), ("expert", "shard"))
    clip_scales = jnp.sqrt(clip_limit / jnp.maximum(peaks, clip_limit))
    return (
        hidden_out,
        input_grad.reshape(hidden_in.shape),
        own_gains[:2],
        jnp.stack([first_weight_grad[:, : 3 * D], second_grad[:, : 3 * D]]),
        jnp.stack([first_weight_grad[:, 3 * D :], second_grad[:, 3 * D :]]),
        small_grad[gain_cut:bias_cut].reshape(2, NB // groups, H),
        own_gains[2:],
        mlp_up_grad,
        mlp_down_grad,
        small_grad[bias_cut:].reshape(part, expert_total),
        expert_up_grad,
        expert_down_grad,
        clip_scales,
    )


MESH = pl.DeviceIdType.MESH
ANY = pl.ANY
VMEM = pltpu.VMEM


def place():
    return lax.axis_index("expert"), lax.axis_index("shard")


def greet(devices):
    barrier = pltpu.get_barrier_semaphore()
    for device in devices:
        pl.semaphore_signal(barrier, inc=1, device_id=device, device_id_type=MESH)
    pl.semaphore_wait(barrier, len(devices))


def push(sent, source, target, send_sem, recv_sem, device):
    copy = pltpu.make_async_remote_copy(
        src_ref=source,
        dst_ref=target,
        send_sem=send_sem,
        recv_sem=recv_sem,
        device_id=device,
        device_id_type=MESH,
    )
    copy.start()
    sent.append(copy)
    return copy


def norm_rows(inputs, gain):
    return inputs * lax.rsqrt(jnp.mean(inputs * inputs, axis=-1, keepdims=True) + epsilon) * gain


def dot_rows(left, right):
    return lax.dot_general(left, right, (((1,), (1,)), ((), ())), preferred_element_type=single)


def dot_columns(left, right):
    return lax.dot_general(left, right, (((0,), (0,)), ((), ())), preferred_element_type=single)


def loop(count, body):
    def step(i, carry):
        body(i)
        return carry

    lax.fori_loop(0, count, step, 0)


def lane_block(i, width):
    return pl.ds(pl.multiple_of(i * width, 128), width)


def row_block(i, height):
    return pl.ds(pl.multiple_of(i * height, height), height)


T = 128
PAIRS = H // 2
TOE = 1152
CAP = 32


class Plane:
    def __init__(self):
        self.e, self.s = place()
        e = self.e
        self.core = lax.rem(e, 2)
        self.quarter = e // 2
        self.at_x = e + 2 - 4 * lax.rem(self.quarter, 2)
        self.at_y = lax.rem(e + 4, 8)
        self.at_core = e + 1 - 2 * self.core
        self.inward = jnp.where(self.core == 0, self.at_x, self.at_y)
        self.onward = jnp.where(self.core == 0, self.at_y, self.at_x)
        self.diagonal = self.inward + self.onward - e
        self.others = [lax.rem(self.s + k, 4) for k in range(1, 4)]
        self.around = [lax.rem(e + k, 8) for k in range(1, 8)]
        self.sent = []

    def push(self, source, target, send_sem, recv_sem, device):
        return push(self.sent, source, target, send_sem, recv_sem, device)

    def arrived(self, view, recv_sem):
        pltpu.make_async_remote_copy(
            src_ref=view,
            dst_ref=view,
            send_sem=recv_sem,
            recv_sem=recv_sem,
            device_id=(self.at_core, self.s),
            device_id_type=MESH,
        ).wait_recv()


class PlaneGather:
    def __init__(self, plane, view, send_sems, recv_sems):
        self.plane, self.view, self.ss, self.rs = plane, view, send_sems, recv_sems

    def _push(self, who, i, target):
        p = self.plane
        block = self.view(who)
        p.push(block, block, self.ss.at[i], self.rs.at[i], (target, p.s))

    def first(self):
        p = self.plane
        self._push(p.e, 0, p.at_x)
        self._push(p.e, 1, p.at_y)
        self._push(p.e, 3, p.at_core)

    def second(self):
        p = self.plane
        p.arrived(self.view(p.inward), self.rs.at[p.core])
        self._push(p.inward, 2, p.onward)
        self._push(p.inward, 4, p.at_core)

    def third(self):
        p = self.plane
        p.arrived(self.view(p.onward), self.rs.at[1 - p.core])
        self._push(p.onward, 5, p.at_core)
        p.arrived(self.view(p.diagonal), self.rs.at[2])
        self._push(p.diagonal, 6, p.at_core)

    def done(self):
        for i in range(3, 7):
            self.plane.arrived(self.view(self.plane.e), self.rs.at[i])


def forward_kernel(
    hidden_ref,
    small_ref,
    buckets_ref,
    routes_ref,
    qkv_hbm,
    out_hbm,
    up_hbm,
    down_hbm,
    expert_up_hbm,
    cot_hbm,
    normed_out,
    query_out,
    attended_out,
    mid_first_out,
    mid_second_out,
    dense_normed_out,
    pre_out,
    act_out,
    one_out,
    peak_out,
    moe_normed_out,
    gains_ref,
    router_out,
    slots_out,
    qkv0_out,
    qkv1_out,
    proj0_out,
    proj1_out,
    up_out,
    down_out,
    kv_out,
    probs_out,
    up_own,
    cot_all,
    small_all,
    table_ref,
    slots_own,
    act,
    w_qkv0,
    w_qkv1,
    w_out0,
    w_out1,
    w_up,
    w_down,
    kv,
    probs,
    scores,
    zs,
    zr,
    f1s,
    f1r,
    f2s,
    f2r,
    cs,
    cr,
    locals_sem,
    k1s,
    k1r,
    k2s,
    k2r,
    kcs,
    kcr,
    us,
    ur,
    gs,
    gr,
    ns,
    nr,
    outs_sem,
    small_s,
    small_r,
    slot_zs,
    slot_zr,
    slot_ps,
    slot_pr,
):
    e, s = place()
    core = lax.rem(e, 2)
    quarter = e // 2
    at_x = e + 2 - 4 * lax.rem(quarter, 2)
    at_y = lax.rem(e + 4, 8)
    at_core = e + 1 - 2 * core
    inward = jnp.where(core == 0, at_x, at_y)
    onward = jnp.where(core == 0, at_y, at_x)
    others = [lax.rem(s + k, 4) for k in range(1, 4)]
    sources = [lax.rem(s + 4 - k, 4) for k in range(1, 4)]
    sent = []
    kept = []

    def local(source, target, sem):
        copy = pltpu.make_async_copy(source, target, sem)
        copy.start()
        return copy

    chunks = [
        (qkv_hbm.at[0], w_qkv0, 48, 1152),
        (out_hbm.at[0], w_out0, 48, 384),
        (up_hbm, w_up, 48, 1536),
        (down_hbm, w_down, 192, 384),
        (qkv_hbm.at[1], w_qkv1, 48, 1152),
        (out_hbm.at[1], w_out1, 48, 384),
    ]

    def block(target, who, position, height, half, width):
        rows = pl.ds(pl.multiple_of(position * 4 * height + who * height, height), height)
        return target.at[rows, lane_block(half, width)]

    def cot_block(g, who):
        return cot_all.at[g, who]

    stage1, stage2, stage3, stage4, own = {}, {}, {}, {}, {}

    def z_send(c):
        source, target, height, width = chunks[c]
        piece = source.at[row_block(quarter, height), lane_block(core, width)]
        mine = block(target, quarter, s, height, core, width)
        stage1[c] = [
            push(sent, piece, mine, zs.at[c, k], zr.at[c, k], (e, others[k])) for k in range(3)
        ]
        own[c] = local(source, target.at[row_block(s, 4 * height), :], locals_sem.at[c])

    def plane_send(c):
        _, target, height, width = chunks[c]
        stage2[c] = []
        for k in range(3):
            stage1[c][k].wait_recv()
            mine = block(target, quarter, sources[k], height, core, width)
            stage2[c].append(
                [
                    push(sent, mine, mine, f1s.at[c, k, i], f1r.at[c, k, i], (partner, s))
                    for i, partner in enumerate((at_x, at_y))
                ]
            )

    def plane_forward(c):
        _, target, height, width = chunks[c]
        stage3[c] = []
        for k in range(3):
            pltpu.make_async_remote_copy(
                src_ref=block(target, quarter, sources[k], height, core, width),
                dst_ref=block(target, quarter, sources[k], height, core, width),
                send_sem=f1s.at[c, k, core],
                recv_sem=f1r.at[c, k, core],
                device_id=(inward, s),
                device_id_type=MESH,
            ).wait_recv()
            theirs = block(target, inward // 2, sources[k], height, core, width)
            stage3[c].append(
                push(sent, theirs, theirs, f2s.at[c, k], f2r.at[c, k], (onward, s))
            )

    def core_send(c):
        _, target, height, width = chunks[c]
        stage4[c] = []
        for k in range(3):
            pltpu.make_async_remote_copy(
                src_ref=block(target, quarter, sources[k], height, core, width),
                dst_ref=block(target, quarter, sources[k], height, core, width),
                send_sem=f1s.at[c, k, 1 - core],
                recv_sem=f1r.at[c, k, 1 - core],
                device_id=(onward, s),
                device_id_type=MESH,
            ).wait_recv()
            stage3[c][k].wait_recv()
            half = target.at[row_block(sources[k], 4 * height), lane_block(core, width)]
            stage4[c].append(push(sent, half, half, cs.at[c, k], cr.at[c, k], (at_core, s)))

    weight_outs = [qkv0_out, proj0_out, up_out, down_out, qkv1_out, proj1_out]

    def ready(c):
        for k in range(3):
            stage4[c][k].wait_recv()
        own[c].wait()
        kept.append(local(chunks[c][1], weight_outs[c], outs_sem.at[c]))

    plane = Plane()
    cot_groups = [s] + sources
    cot_gathers = [
        PlaneGather(plane, functools.partial(cot_block, g), ns.at[k], nr.at[k])
        for k, g in enumerate(cot_groups)
    ]

    def cot_first(k):
        plane.arrived(cot_block(s, e), gr.at[k - 1])
        cot_gathers[k].first()

    experts = lax.broadcasted_iota(jnp.int32, (16, T), 0)
    chosen = [experts == routes_ref[r : r + 1, :] for r in range(2)]
    marks = jnp.where(chosen[0] | chosen[1], 1.0, 0.0).astype(bfloat)
    earlier = jnp.where(
        lax.broadcasted_iota(jnp.int32, (T, T), 0) < lax.broadcasted_iota(jnp.int32, (T, T), 1),
        1.0,
        0.0,
    ).astype(bfloat)
    before = jnp.dot(marks, earlier, preferred_element_type=single)
    slots_own[...] = jnp.zeros_like(slots_own)
    for r in range(2):
        rank = jnp.sum(jnp.where(chosen[r], before, 0.0), axis=0, keepdims=True)
        slots_own[r : r + 1, :] = routes_ref[r : r + 1, :] * CAP + rank.astype(jnp.int32)
    slots_out[s, e] = slots_own[...]
    own_cot = local(cot_hbm, cot_block(s, e), gs.at[3])
    small_all[s] = small_ref[...]

    greet([(d, s) for d in plane.around] + [(e, other) for other in others])
    smalls = [
        push(sent, small_ref, small_all.at[s], small_s.at[k], small_r.at[k], (e, others[k]))
        for k in range(3)
    ]
    z_send(0)
    for k in range(3):
        push(sent, slots_own, slots_out.at[s, e], slot_zs.at[k], slot_zr.at[k], (e, others[k]))
    own_cot.wait()
    cot_gathers[0].first()
    z_send(1)
    z_send(2)
    reshard = []

    def bulk():
        for c in range(3, 6):
            z_send(c)
        for k in range(3):
            push(sent, cot_hbm, cot_block(s, e), gs.at[k], gr.at[k], (e, others[k]))
        reshard.extend([
            push(
                sent,
                expert_up_hbm.at[:, :, lane_block(others[k], 768)],
                up_own.at[:, row_block(s, 192), :],
                us.at[k],
                ur.at[k],
                (e, others[k]),
            )
            for k in range(3)
        ])
        kept.append(
            local(
                expert_up_hbm.at[:, :, lane_block(s, 768)],
                up_own.at[:, row_block(s, 192), :],
                us.at[3],
            )
        )

    def slots_plane():
        for k in range(3):
            plane.arrived(slots_own, slot_zr.at[k])
        column = slots_out.at[:, e]
        for k, d in enumerate(plane.around):
            push(sent, column, column, slot_ps.at[k], slot_pr.at[k], (d, s))

    for copy in smalls:
        copy.wait_recv()
    biases = []
    for z in range(4):
        lanes = slice(192 * z, 192 * (z + 1))
        gains_ref[:, lanes] = small_all[z, :4, :192]
        router_out[:, lanes] = small_all[z, 16:32, :192].astype(bfloat)
        biases.append(small_all[z, 8:16, : 2 * H])
    bucket_marks_here = jnp.where(
        lax.broadcasted_iota(jnp.int32, (NB, TOE), 0) == buckets_ref[...], 1.0, 0.0
    ).astype(bfloat)
    table_ref[...] = dot_columns(jnp.concatenate(biases).astype(bfloat), bucket_marks_here)

    def attention(layer, inputs, w_qkv, w_out, work):
        normed = norm_rows(inputs, gains_ref[pl.ds(layer, 1), :]).astype(bfloat)
        normed_out[layer] = normed
        if layer == 0:
            plane_send(0)
            plane_forward(0)
            plane_send(1)
            core_send(0)
            plane_forward(1)
            ready(0)
            bulk()
        else:
            ready(4)
        own_rows = row_block(e, T)
        first, second, third = [], [], []
        for part in range(3):
            x = normed_out[layer]
            for i, base in enumerate((D, 2 * D)):
                columns = w_qkv[:, base + 256 * part : base + 256 * (part + 1)]
                kv[layer, part, own_rows, 256 * i : 256 * (i + 1)] = jnp.dot(
                    x, columns, preferred_element_type=single
                ).astype(bfloat)
            mine = kv.at[layer, part, own_rows, :]
            first.append(
                [
                    push(sent, mine, mine, k1s.at[layer, part, i], k1r.at[layer, part, i], (p, s))
                    for i, p in enumerate((at_x, at_y))
                ]
            )
            third.append(
                [
                    push(
                        sent, mine, mine, kcs.at[layer, part, 0], kcr.at[layer, part, 0],
                        (at_core, s),
                    )
                ]
            )
        query_out[layer] = jnp.dot(
            normed_out[layer], w_qkv[:, :D], preferred_element_type=single
        ).astype(bfloat)
        if work:
            work[0]()
        at_diagonal = inward + onward - e
        for part in range(3):
            pltpu.make_async_remote_copy(
                src_ref=kv.at[layer, part, own_rows, :],
                dst_ref=kv.at[layer, part, own_rows, :],
                send_sem=k1s.at[layer, part, core],
                recv_sem=k1r.at[layer, part, core],
                device_id=(inward, s),
                device_id_type=MESH,
            ).wait_recv()
            theirs = kv.at[layer, part, row_block(inward, T), :]
            second.append(
                push(
                    sent, theirs, theirs, k2s.at[layer, part], k2r.at[layer, part], (onward, s)
                )
            )
            third[part].append(
                push(
                    sent, theirs, theirs, kcs.at[layer, part, 1], kcr.at[layer, part, 1],
                    (at_core, s),
                )
            )
        if work:
            work[1]()
        for part in range(3):
            pltpu.make_async_remote_copy(
                src_ref=kv.at[layer, part, own_rows, :],
                dst_ref=kv.at[layer, part, own_rows, :],
                send_sem=k1s.at[layer, part, 1 - core],
                recv_sem=k1r.at[layer, part, 1 - core],
                device_id=(onward, s),
                device_id_type=MESH,
            ).wait_recv()
            theirs = kv.at[layer, part, row_block(onward, T), :]
            third[part].append(
                push(
                    sent, theirs, theirs, kcs.at[layer, part, 2], kcr.at[layer, part, 2],
                    (at_core, s),
                )
            )
            second[part].wait_recv()
            theirs = kv.at[layer, part, row_block(at_diagonal, T), :]
            third[part].append(
                push(
                    sent, theirs, theirs, kcs.at[layer, part, 3], kcr.at[layer, part, 3],
                    (at_core, s),
                )
            )
        for part in range(3):
            for i in range(4):
                third[part][i].wait_recv()

            def one_pair(local_pair):
                pair = 2 * part + local_pair
                lanes = lane_block(pair, 128)
                queries = query_out[layer, :, lanes]
                lane = lax.broadcasted_iota(jnp.int32, (T, 128), 1)
                zero = jnp.zeros_like(queries)
                both = jnp.concatenate(
                    [jnp.where(lane < HD, queries, zero), jnp.where(lane >= HD, queries, zero)]
                )
                keys = kv[layer, part, :, lane_block(local_pair, 128)]
                scores[...] = dot_rows(both, keys) * (1.0 / math.sqrt(HD))
                for half in range(2):
                    head = 2 * pair + half
                    toeplitz = table_ref[pl.ds(layer * H + head, 1), :]
                    peak = jnp.full((1, 1), -jnp.inf, single)
                    for rows in range(0, T, 32):
                        raw = scores[half * T + rows : half * T + rows + 32, :]
                        row = e * T + rows + lax.broadcasted_iota(jnp.int32, raw.shape, 0)
                        causal = row >= lax.broadcasted_iota(jnp.int32, raw.shape, 1)
                        shifted = pltpu.roll(
                            jnp.broadcast_to(toeplitz, (32, TOE)),
                            TOE - (T - 1) + rows,
                            1,
                            stride=1,
                            stride_axis=0,
                        )[:, : raw.shape[1]]
                        peak = jnp.maximum(
                            peak, jnp.max(jnp.where(causal, raw, -jnp.inf), keepdims=True)
                        )
                        masked = jnp.where(causal, raw + shifted, -jnp.inf)
                        top = jnp.max(masked, axis=-1, keepdims=True)
                        exponent = jnp.exp(masked - top)
                        total = jnp.sum(exponent, axis=-1, keepdims=True)
                        probs[layer, pl.ds(pl.multiple_of(head * T + rows, 32), 32), :] = (
                            exponent / total
                        ).astype(bfloat)
                    peak_out[pl.ds(layer * H + head, 1), :] = jnp.broadcast_to(peak, (1, 128))
                values = kv[layer, part, :, pl.ds(pl.multiple_of(256 + local_pair * 128, 128), 128)]
                mixed = jnp.dot(
                    probs[layer, pl.ds(pl.multiple_of(pair * 2 * T, 2 * T), 2 * T), :],
                    values,
                    preferred_element_type=single,
                )
                attended_out[layer, :, lanes] = jnp.where(
                    lane < HD, mixed[:T], mixed[T:]
                ).astype(bfloat)

            loop(2, one_pair)
            if work:
                work[2 + part]()
        kept.append(local(kv.at[layer], kv_out.at[layer], outs_sem.at[6 + layer]))
        kept.append(local(probs.at[layer], probs_out.at[layer], outs_sem.at[8 + layer]))

    def work0():
        plane_send(2)
        slots_plane()

    def work1():
        cot_gathers[0].second()

    def work2():
        core_send(1)
        plane_send(3)

    def work3():
        cot_gathers[0].third()

    def work4():
        plane_forward(2)

    hidden = hidden_ref[...].astype(single)
    attention(0, hidden, w_qkv0, w_out0, [work0, work1, work2, work3, work4])
    ready(1)
    mid_first_out[...] = hidden + jnp.dot(
        attended_out[0], w_out0[...], preferred_element_type=single
    )
    dense_normed_out[...] = norm_rows(mid_first_out[...], gains_ref[pl.ds(2, 1), :]).astype(bfloat)
    core_send(2)
    plane_forward(3)
    plane_send(4)
    plane_send(5)
    ready(2)

    def up_part(i):
        lanes = slice(768 * i, 768 * (i + 1))
        before = jnp.dot(dense_normed_out[...], w_up[:, lanes], preferred_element_type=single)
        pre_out[:, lanes] = before
        value = jax.nn.gelu(before).astype(bfloat)
        act[:, lanes] = value
        for b in range(8):
            act_out[:, 384 * b + 96 * i : 384 * b + 96 * (i + 1)] = value[:, 96 * b : 96 * (b + 1)]

    for i in range(4):
        up_part(i)
    core_send(3)
    plane_forward(4)
    plane_forward(5)
    cot_first(1)
    ready(3)
    one_out[...] = mid_first_out[...]

    def down_part(i):
        rows = row_block(i, 768)
        one_out[...] += jnp.dot(
            act[:, lane_block(i, 768)], w_down[rows, :], preferred_element_type=single
        )

    loop(4, down_part)
    core_send(4)
    core_send(5)

    def work5():
        cot_first(2)
        cot_gathers[1].second()

    def work6():
        cot_first(3)

    def work7():
        cot_gathers[1].third()
        cot_gathers[2].second()

    def work8():
        cot_gathers[2].third()
        cot_gathers[3].second()

    def work9():
        cot_gathers[3].third()

    attention(1, one_out[...], w_qkv1, w_out1, [work5, work6, work7, work8, work9])
    ready(5)
    mid_second_out[...] = one_out[...] + jnp.dot(
        attended_out[1], w_out1[...], preferred_element_type=single
    )
    moe_normed_out[...] = norm_rows(mid_second_out[...], gains_ref[pl.ds(3, 1), :]).astype(bfloat)
    for k in range(7):
        plane.arrived(slots_out.at[:, e], slot_pr.at[k])
    for gather in cot_gathers:
        gather.done()
    for copy in reshard:
        copy.wait_recv()
    for copy in kept:
        copy.wait()
    for copy in sent + plane.sent:
        copy.wait_send()


def forward(hidden, small, buckets, routes, qkv, out, up, down, expert_up, cotangent):
    length = T * lax.axis_size("expert")
    vmem = pl.BlockSpec(memory_space=VMEM)
    anywhere = pl.BlockSpec(memory_space=ANY)
    shape = jax.ShapeDtypeStruct
    ff = up.shape[1]
    sem = pltpu.SemaphoreType.DMA
    return pl.pallas_call(
        forward_kernel,
        name="forward_layers",
        out_shape=(
            shape((2, T, D), bfloat),
            shape((2, T, D), bfloat),
            shape((2, T, D), bfloat),
            shape((T, D), single),
            shape((T, D), single),
            shape((T, D), bfloat),
            shape((T, ff), single),
            shape((T, ff), bfloat),
            shape((T, D), single),
            shape((2 * H, 128), single),
            shape((T, D), bfloat),
            shape((4, D), single),
            shape((16, D), bfloat),
            shape((4, 8, 8, T), jnp.int32),
            shape((D, 3 * D), bfloat),
            shape((D, 3 * D), bfloat),
            shape((D, D), bfloat),
            shape((D, D), bfloat),
            shape((D, ff), bfloat),
            shape((ff, D), bfloat),
            shape((2, 3, length, 512), bfloat),
            shape((2, H * T, length), bfloat),
            shape((EXP_DEV, D, 768), bfloat),
            shape((4, 8, T, D), bfloat),
        ),
        in_specs=[vmem] * 4 + [anywhere] * 6,
        out_specs=(vmem,) * 14 + (anywhere,) * 10,
        scratch_shapes=[
            VMEM((4,) + small.shape, single),
            VMEM((2 * H, TOE), single),
            VMEM((8, T), jnp.int32),
            VMEM((T, ff), bfloat),
            VMEM((D, 3 * D), bfloat),
            VMEM((D, 3 * D), bfloat),
            VMEM((D, D), bfloat),
            VMEM((D, D), bfloat),
            VMEM((D, ff), bfloat),
            VMEM((ff, D), bfloat),
            VMEM((2, 3, length, 512), bfloat),
            VMEM((2, H * T, length), bfloat),
            VMEM((2 * T, length), single),
            sem((6, 3)), sem((6, 3)),
            sem((6, 3, 2)), sem((6, 3, 2)),
            sem((6, 3)), sem((6, 3)),
            sem((6, 3)), sem((6, 3)),
            sem((6,)),
            sem((2, 3, 2)), sem((2, 3, 2)),
            sem((2, 3)), sem((2, 3)),
            sem((2, 3, 4)), sem((2, 3, 4)),
            sem((4,)), sem((3,)),
            sem((4,)), sem((3,)),
            sem((4, 7)), sem((4, 7)),
            sem((10,)),
            sem((3,)), sem((3,)),
            sem((3,)), sem((3,)),
            sem((7,)), sem((7,)),
        ],
        compiler_params=pltpu.CompilerParams(
            collective_id=2, has_side_effects=True, vmem_limit_bytes=56 * 2**20
        ),
    )(hidden, small, buckets, routes, qkv, out, up, down, expert_up, cotangent)


class SmallReduce:
    def __init__(self, plane, value, z_in, plane_in, op, sems):
        self.plane, self.value, self.z_in, self.plane_in = plane, value, z_in, plane_in
        self.op, self.sems = op, sems

    def start(self):
        p = self.plane
        zs, zr, _, _ = self.sems
        for k in range(3):
            p.push(self.value, self.z_in.at[k], zs.at[k], zr.at[k], (p.e, p.others[k]))

    def middle(self, middle):
        p = self.plane
        zs, zr, ps, pr = self.sems
        total = self.value[...]
        for k in range(3):
            p.arrived(self.z_in.at[k], zr.at[k])
            total = self.op(total, self.z_in[k])
        middle[...] = total
        for k in range(7):
            p.push(middle, self.plane_in.at[k], ps.at[k], pr.at[k], (p.around[k], p.s))

    def finish(self, middle, result):
        p = self.plane
        total = middle[...]
        for k in range(7):
            p.arrived(self.plane_in.at[k], self.sems[3].at[k])
            total = self.op(total, self.plane_in[k])
        result[...] = total


def norm_pull(inputs, gain, upstream):
    inverse = lax.rsqrt(jnp.mean(inputs * inputs, axis=-1, keepdims=True) + epsilon)
    scaled = upstream * gain
    inner = jnp.mean(scaled * inputs, axis=-1, keepdims=True)
    gain_grad = jnp.sum(upstream * inputs * inverse, axis=0, keepdims=True)
    return inverse * scaled - inputs * (inverse * inverse * inverse * inner), gain_grad


def gelu_both(value):
    root = math.sqrt(2.0 / math.pi)
    squared = value * value
    bend = jnp.tanh(root * value * (1.0 + 0.044715 * squared))
    half = 0.5 * (1.0 + bend)
    slope = half + 0.5 * value * (1.0 - bend * bend) * (root * (1.0 + 3 * 0.044715 * squared))
    return value * half, slope


def gelu_slope(value):
    root = math.sqrt(2.0 / math.pi)
    squared = value * value
    bend = jnp.tanh(root * value * (1.0 + 0.044715 * squared))
    return 0.5 * (1.0 + bend) + 0.5 * value * (1.0 - bend * bend) * root * (
        1.0 + 3 * 0.044715 * squared
    )


def backward_kernel(
    mid_grad_ref,
    one_ref,
    hidden_ref,
    mid_ref,
    gains_ref,
    query_ref,
    pre_ref,
    buckets_ref,
    small_ref,
    peak_ref,
    early_hbm,
    normed_hbm,
    attended_hbm,
    dense_normed_hbm,
    act_hbm,
    qkv0_hbm,
    qkv1_hbm,
    proj0_hbm,
    proj1_hbm,
    up_hbm,
    down_hbm,
    kv_hbm,
    probs_hbm,
    up_grad_hbm,
    hidden_grad_out,
    att_out,
    up_out,
    down_out,
    small_out,
    late_out,
    peak_out,
    expert_up_out,
    w_wide,
    w_down,
    kv,
    probs,
    xg,
    gx,
    gsrc,
    zb,
    zin,
    zb_down,
    zin_down,
    slopes,
    score_low,
    dk,
    cin,
    rin,
    attended_grad,
    layer_grad,
    biases,
    early,
    early_z,
    early_p,
    early_m,
    late,
    late_z,
    late_p,
    late_m,
    peak_z,
    peak_p,
    peak_m,
    gs,
    gr,
    xs,
    xr,
    zs,
    zr,
    dcs,
    dcr,
    drs,
    drr,
    szs,
    szr,
    sps,
    spr,
    us,
    ur,
    loads,
):
    p = Plane()
    e, s, core = p.e, p.s, p.core
    own_rows = row_block(e, T)

    def load(source, target, i):
        copy = pltpu.make_async_copy(source, target, loads.at[i])
        copy.start()
        return copy

    own_parts = [
        load(source, xg.at[n, own_rows, :], 11 + n)
        for n, source in ((2, normed_hbm.at[0]), (3, attended_hbm.at[0]), (4, dense_normed_hbm))
    ]
    got_early = load(early_hbm, xg.at[0:2], 12)
    own_act = load(act_hbm.at[:, lane_block(e, 384)], gx.at[3, own_rows, :], 16)
    greet([(d, s) for d in p.around] + [(e, other) for other in p.others])

    w_qkv = w_wide.at[:, : 3 * D]
    w_out = w_wide.at[:, 3 * D :]
    got_out = load(proj1_hbm, w_out, 0)
    got_kv = load(kv_hbm.at[1], kv, 2)
    got_probs = load(probs_hbm.at[1], probs, 3)
    got_qkv = load(qkv1_hbm, w_qkv, 1)
    got_down = load(down_hbm, w_down, 5)

    peaks = SmallReduce(
        p, peak_ref, peak_z, peak_p, jnp.maximum, (szs.at[0], szr.at[0], sps.at[0], spr.at[0])
    )
    peaks.start()

    def rows_gather(n):
        return PlaneGather(
            p, lambda who: xg.at[n, row_block(who, T), :], gs.at[n], gr.at[n]
        )

    gathers = {n: rows_gather(n) for n in range(2, 6)}
    def exchange_start(j, source):
        if j == 3:
            own_act.wait()
        else:
            gx[j, own_rows, :] = source[:, lane_block(e, 384)]
        for k, d in enumerate(p.around):
            p.push(
                source.at[:, lane_block(d, 384)],
                gx.at[j, own_rows, :],
                xs.at[j, k],
                xr.at[j, k],
                (d, s),
            )

    def exchange_wait(j):
        for k in range(7):
            p.arrived(gx.at[j, own_rows, :], xr.at[j, k])

    def out_gather(j, target, height):
        return PlaneGather(
            p, lambda who: target.at[pl.ds(who, 1)], gs.at[6 + j], gr.at[6 + j]
        )

    def z_start(j, tile, received, height):
        for k in range(3):
            p.push(
                tile.at[row_block(p.others[k], height), :],
                received.at[k],
                zs.at[j, k],
                zr.at[j, k],
                (e, p.others[k]),
            )

    def z_finish(j, tile, received, height, target):
        total = tile[row_block(s, height), :].astype(single)
        for k in range(3):
            p.arrived(received.at[k], zr.at[j, k])
            total = total + received[k].astype(single)
        target[pl.ds(e, 1)] = total.astype(bfloat)[None]

    def tile_attention(layer):
        j = 1 - layer
        exchange_wait(j)
        rows = xg[2 * j + e // 6]
        for part in range(3):
            lanes = slice(128 * part, 128 * (part + 1))
            zb[j, :, lanes] = dot_columns(rows, gx[j, :, lanes]).astype(bfloat)
        z_start(j, zb.at[j], zin.at[j], 192)

    def tile_up():
        exchange_wait(2)
        for part in range(3):
            lanes = slice(128 * part, 128 * (part + 1))
            zb[2, :, lanes] = dot_columns(xg[4], gx[2, :, lanes]).astype(bfloat)
        z_start(2, zb.at[2], zin.at[2], 192)

    def tile_down():
        exchange_wait(3)
        for part in range(3):
            lanes = slice(128 * part, 128 * (part + 1))
            zb_down[lanes, :] = dot_columns(gx[3, :, lanes], xg[5]).astype(bfloat)
        z_start(3, zb_down, zin_down, 96)

    gather_att1 = out_gather(0, att_out.at[1], 192)
    gather_att0 = out_gather(1, att_out.at[0], 192)
    gather_up = out_gather(2, up_out, 192)
    gather_down = out_gather(3, down_out, 96)

    scale = 1.0 / math.sqrt(HD)

    def attention(layer, upstream, work):
        j = 1 - layer
        grads = gsrc.at[j]
        branch = upstream.astype(bfloat)
        grads[:, 3 * D :] = branch
        got_out_now = got_out if layer == 1 else reloads["out"]
        got_out_now.wait()
        attended_grad[...] = dot_rows(branch, w_out[...]).astype(bfloat)
        if layer == 1:
            got_kv.wait()
            got_probs.wait()
        else:
            reloads["kv"].wait()
            reloads["probs"].wait()
            for copy in dk_sent:
                copy.wait_send()
            dk_sent.clear()

        def first_step(part):
            push(
                dk_sent,
                dk.at[part, 1 - core],
                cin.at[layer, part],
                dcs.at[layer, part],
                dcr.at[layer, part],
                (p.at_core, s),
            )

        def second_step(part):
            p.arrived(cin.at[layer, part], dcr.at[layer, part])
            for q in range(4):
                dk[part, core, q] = (
                    dk[part, core, q].astype(single) + cin[layer, part, q].astype(single)
                ).astype(bfloat)
            for k, d in enumerate((p.at_x, p.at_y, p.diagonal)):
                push(
                    dk_sent,
                    dk.at[part, core, d // 2],
                    rin.at[layer, part, k],
                    drs.at[layer, part, k],
                    drr.at[layer, part, k],
                    (d, s),
                )

        def third_step(part):
            total = dk[part, core, p.quarter].astype(single)
            for k in range(3):
                p.arrived(rin.at[layer, part, k], drr.at[layer, part, k])
                total = total + rin[layer, part, k].astype(single)
            turned = total.T.astype(bfloat)
            grads[:, D + 256 * part : D + 256 * (part + 1)] = turned[:, :256]
            grads[:, 2 * D + 256 * part : 2 * D + 256 * (part + 1)] = turned[:, 256:]

        if layer == 1:
            exchange_start(3, act_hbm)

        for part in range(3):

            def one_pair(local_pair):
                pair = 2 * part + local_pair
                lanes = lane_block(pair, 128)
                lane = lax.broadcasted_iota(jnp.int32, (T, 128), 1)

                def split(value):
                    zero = jnp.zeros_like(value)
                    return jnp.concatenate(
                        [jnp.where(lane < HD, value, zero), jnp.where(lane >= HD, value, zero)]
                    )

                queries = split(query_ref[layer, :, lanes])
                outputs = split(attended_grad[:, lanes])
                keys = kv[part, :, lane_block(local_pair, 128)]
                values = kv[part, :, pl.ds(pl.multiple_of(256 + local_pair * 128, 128), 128)]
                slopes[...] = dot_rows(outputs, values)
                pair_rows = pl.ds(pl.multiple_of(pair * 2 * T, 2 * T), 2 * T)
                for half in range(2):
                    head = 2 * pair + half
                    gathered = jnp.zeros((8, TOE), single)
                    for rows in range(0, T, 32):
                        at = half * T + rows
                        prob = probs[
                            pl.ds(pl.multiple_of(head * T + rows, 32), 32), :
                        ].astype(single)
                        slope = slopes[at : at + 32, :]
                        inner = jnp.sum(prob * slope, axis=-1, keepdims=True)
                        low = (prob * (slope - inner)).astype(bfloat)
                        score_low[at : at + 32, :] = low
                        fold = jnp.concatenate(
                            [low.astype(single), jnp.zeros((32, TOE - low.shape[1]), single)],
                            axis=1,
                        )
                        fold = pltpu.roll(fold[:16], 16, 1) + fold[16:]
                        fold = pltpu.roll(fold[:8], 8, 1) + fold[8:]
                        if rows < T - 32:
                            fold = pltpu.roll(fold, T - 32 - rows, 1)
                        gathered = gathered + fold
                    fold = pltpu.roll(gathered[:4], 4, 1) + gathered[4:]
                    fold = pltpu.roll(fold[:2], 2, 1) + fold[2:]
                    fold = pltpu.roll(fold[:1], 1, 1) + fold[1:]
                    biases[pl.ds(layer * H + head, 1), :] = fold
                mixed = jnp.dot(score_low[...], keys, preferred_element_type=single) * scale
                grads[:, lanes] = jnp.where(lane < HD, mixed[:T], mixed[T:]).astype(bfloat)
                key_grad = dot_columns(queries, score_low[...]) * scale
                value_grad = dot_columns(outputs, probs[pair_rows, :])
                for d in range(8):
                    columns = slice(128 * d, 128 * (d + 1))
                    dk[
                        part, d % 2, d // 2, pl.ds(pl.multiple_of(local_pair * 128, 128), 128), :
                    ] = key_grad[:, columns].astype(bfloat)
                    dk[
                        part,
                        d % 2,
                        d // 2,
                        pl.ds(pl.multiple_of(256 + local_pair * 128, 128), 128),
                        :,
                    ] = value_grad[:, columns].astype(bfloat)

            loop(2, one_pair)
            first_step(part)
            if part > 0:
                second_step(part - 1)
            work[part]()
        second_step(2)
        third_step(0)
        work[3]()
        third_step(1)
        third_step(2)
        exchange_start(j, gsrc.at[j])
        if layer == 1:
            got_qkv.wait()
        else:
            reloads["qkv"].wait()
        return dot_rows(gsrc[j, :, : 3 * D], w_qkv[...])

    dk_sent = []
    reloads = {}

    def part0():
        for k in range(3):
            reshard.append(
                p.push(
                    up_grad_hbm.at[:, row_block(p.others[k], 192), :],
                    expert_up_out.at[:, :, lane_block(s, 768)],
                    us.at[k],
                    ur.at[k],
                    (e, p.others[k]),
                )
            )
        reshard_own.append(
            load(
                up_grad_hbm.at[:, row_block(s, 192), :],
                expert_up_out.at[:, :, lane_block(s, 768)],
                6,
            )
        )

    def part1():
        peaks.middle(peak_m)

    def part2():
        for copy in own_parts:
            copy.wait()

    def part3():
        gathers[4].first()
        peaks.finish(peak_m, peak_out)

    reshard, reshard_own = [], []
    mid_grad = mid_grad_ref[...]
    normed_grad = attention(1, mid_grad, [part0, part1, part2, part3])
    reloads["kv"] = load(kv_hbm.at[0], kv, 7)
    reloads["probs"] = load(probs_hbm.at[0], probs, 8)
    got_up = load(up_hbm, w_wide, 4)
    input_grad, gain_grad = norm_pull(one_ref[...], gains_ref[1:2, :], normed_grad)
    early[...] = small_ref[...]
    early[17:18, :] = gain_grad
    layer_grad[...] = mid_grad + input_grad
    branch = layer_grad[...].astype(bfloat)
    xg[5, own_rows, :] = branch
    gathers[5].first()
    got_down.wait()

    def slope_part(i):
        lanes = lane_block(i, 512)
        act_grad = dot_rows(xg[5, own_rows, :], w_down[row_block(i, 512), :])
        gsrc[2, :, lanes] = (act_grad * gelu_slope(pre_ref[:, lanes])).astype(bfloat)

    loop(6, slope_part)
    exchange_start(2, gsrc.at[2])
    gathers[2].first()
    gathers[3].first()
    gathers[4].second()
    got_up.wait()
    dense_grad = dot_rows(gsrc[2], w_wide[...])
    reloads["out"] = load(proj0_hbm, w_out, 9)
    reloads["qkv"] = load(qkv0_hbm, w_qkv, 10)
    input_grad, gain_grad = norm_pull(mid_ref[...], gains_ref[2:3, :], dense_grad)
    early[18:19, :] = gain_grad
    layer_grad[...] = layer_grad[...] + input_grad
    small = SmallReduce(
        p, early, early_z, early_p, jnp.add, (szs.at[1], szr.at[1], sps.at[1], spr.at[1])
    )
    small.start()
    got_early.wait()
    tile_attention(1)

    def part4():
        gathers[5].second()
        gathers[4].third()

    def part5():
        gathers[2].second()
        gathers[3].second()
        small.middle(early_m)

    def part6():
        gathers[5].third()

    def part7():
        gathers[4].done()
        tile_up()
        gathers[5].done()
        tile_down()
        gathers[2].third()
        gathers[3].third()

    normed_grad = attention(0, layer_grad[...], [part4, part5, part6, part7])
    input_grad, gain_grad = norm_pull(
        hidden_ref[...].astype(single), gains_ref[0:1, :], normed_grad
    )
    hidden_grad_out[...] = layer_grad[...] + input_grad
    late[...] = jnp.zeros_like(late)
    for i in range(6):
        late[i : i + 1, :] = gain_grad[:, 128 * i : 128 * (i + 1)]
    late[8:32, :NB] = lax.dot_general(
        biases[...],
        jnp.where(lax.broadcasted_iota(jnp.int32, (NB, TOE), 0) == buckets_ref[...], 1.0, 0.0),
        (((1,), (1,)), ((), ())),
        precision=lax.Precision.HIGHEST,
        preferred_element_type=single,
    )
    tail = SmallReduce(
        p, late, late_z, late_p, jnp.add, (szs.at[2], szr.at[2], sps.at[2], spr.at[2])
    )
    tail.start()
    z_finish(0, zb.at[0], zin.at[0], 192, att_out.at[1])
    gather_att1.first()
    gathers[2].done()
    gathers[3].done()
    tile_attention(0)
    tail.middle(late_m)
    small.finish(early_m, small_out)
    z_finish(2, zb.at[2], zin.at[2], 192, up_out)
    gather_up.first()
    gather_att1.second()
    z_finish(3, zb_down, zin_down, 96, down_out)
    gather_down.first()
    gather_up.second()
    gather_att1.third()
    gather_down.second()
    gather_up.third()
    gather_down.third()
    z_finish(1, zb.at[1], zin.at[1], 192, att_out.at[0])
    gather_att0.first()
    gather_att1.done()
    gather_up.done()
    gather_down.done()
    gather_att0.second()
    gather_att0.third()
    tail.finish(late_m, late_out)
    for copy in reshard:
        copy.wait_recv()
    reshard_own[0].wait()
    gather_att0.done()
    for copy in p.sent + dk_sent:
        copy.wait_send()


def backward(
    mid_grad, layer_one, hidden, mid, gains, normed, queries, attended, dense_normed, act, pre_act,
    buckets, small, peak_rows, early_rows, weights, kv, probs, up_grad,
):
    length = T * lax.axis_size("expert")
    vmem = pl.BlockSpec(memory_space=VMEM)
    anywhere = pl.BlockSpec(memory_space=ANY)
    shape = jax.ShapeDtypeStruct
    ff = pre_act.shape[1]
    sem = pltpu.SemaphoreType.DMA
    peak_shape, early_shape, late_shape = (2 * H, 128), small.shape, (32, 128)
    return pl.pallas_call(
        backward_kernel,
        name="backward_layers",
        out_shape=(
            shape((T, D), single),
            shape((2, 8, 192, 384), bfloat),
            shape((8, 192, 384), bfloat),
            shape((8, 96, D), bfloat),
            shape(early_shape, single),
            shape(late_shape, single),
            shape(peak_shape, single),
            shape((EXP_DEV, 192, ff), bfloat),
        ),
        in_specs=[vmem] * 10 + [anywhere] * 14,
        out_specs=(vmem,) * 7 + (anywhere,),
        scratch_shapes=[
            VMEM((D, ff), bfloat),
            VMEM((ff, D), bfloat),
            VMEM((3, length, 512), bfloat),
            VMEM((H * T, length), bfloat),
            VMEM((6, length, D), bfloat),
            VMEM((4, length, 384), bfloat),
            VMEM((3, T, 4 * D), bfloat),
            VMEM((3, D, 384), bfloat),
            VMEM((3, 3, 192, 384), bfloat),
            VMEM((384, D), bfloat),
            VMEM((3, 96, D), bfloat),
            VMEM((2 * T, length), single),
            VMEM((2 * T, length), bfloat),
            VMEM((3, 2, 4, 512, 128), bfloat),
            VMEM((2, 3, 4, 512, 128), bfloat),
            VMEM((2, 3, 3, 512, 128), bfloat),
            VMEM((T, D), bfloat),
            VMEM((T, D), single),
            VMEM((2 * H, TOE), single),
            VMEM(early_shape, single),
            VMEM((3,) + early_shape, single),
            VMEM((7,) + early_shape, single),
            VMEM(early_shape, single),
            VMEM(late_shape, single),
            VMEM((3,) + late_shape, single),
            VMEM((7,) + late_shape, single),
            VMEM(late_shape, single),
            VMEM((3,) + peak_shape, single),
            VMEM((7,) + peak_shape, single),
            VMEM(peak_shape, single),
            sem((10, 7)), sem((10, 7)),
            sem((4, 7)), sem((4, 7)),
            sem((4, 3)), sem((4, 3)),
            sem((2, 3)), sem((2, 3)),
            sem((2, 3, 3)), sem((2, 3, 3)),
            sem((3, 3)), sem((3, 3)),
            sem((3, 7)), sem((3, 7)),
            sem((3,)), sem((3,)),
            sem((17,)),
        ],
        compiler_params=pltpu.CompilerParams(
            collective_id=3, has_side_effects=True, vmem_limit_bytes=60 * 2**20
        ),
    )(
        mid_grad, layer_one, hidden, mid, gains, queries, pre_act, buckets, small, peak_rows,
        early_rows.reshape(2, length, D), normed, attended, dense_normed, act, *weights, kv, probs, up_grad,
    )


def experts_kernel(
    normed_ref,
    mid_ref,
    gains_ref,
    router_turned_ref,
    slots_ref,
    own_cot_ref,
    cot_hbm,
    up_hbm,
    down_hbm,
    normed_hbm,
    attended_hbm,
    hidden_out,
    mid_grad_out,
    small_out,
    up_grad_out,
    down_grad_out,
    early_rows,
    normed_all,
    cots,
    w_up,
    w_down,
    rows,
    gated,
    gates,
    acts,
    pre_grads,
    raw,
    row_send,
    out_send,
    row_back,
    out_back,
    out_ahead_in,
    slot_grads,
    slot_z,
    slot_sum,
    slot_plane,
    row_part,
    out_part,
    row_z,
    out_z,
    ns,
    nr,
    gs,
    gr,
    rs,
    rr,
    os,
    orr,
    ss,
    sr,
    ps,
    pr,
    rzs,
    rzr,
    ozs,
    ozr,
    loads,
    early_s,
    early_r,
    oas,
    oar,
):
    p = Plane()
    e, s = p.e, p.s
    groups = [s] + [lax.rem(s + 4 - k, 4) for k in range(1, 4)]

    def load(source, target, i):
        copy = pltpu.make_async_copy(source, target, loads.at[i])
        copy.start()
        return copy

    got_cots = [load(cot_hbm.at[groups[k]], cots.at[k], k) for k in range(2)]
    got_up = load(up_hbm, w_up, 4)
    got_down = load(down_hbm, w_down, 5)
    own_early = [
        load(source.at[1], early_rows.at[i, e], 6 + i)
        for i, source in enumerate((normed_hbm, attended_hbm))
    ]
    normed_all[s, e] = normed_ref[...]
    greet([(d, s) for d in p.around] + [(e, other) for other in p.others])
    mine = normed_all.at[s, e]
    for k in range(3):
        p.push(mine, mine, ns.at[k], nr.at[k], (e, p.others[k]))

    def gather(k):
        g = groups[k]
        return PlaneGather(p, lambda who: normed_all.at[g, who], gs.at[k], gr.at[k])

    gathers = [gather(k) for k in range(4)]
    gathers[0].first()
    early = [
        PlaneGather(
            p, functools.partial(lambda i, who: early_rows.at[i, who], i), early_s.at[i], early_r.at[i]
        )
        for i in range(2)
    ]
    for i in range(2):
        own_early[i].wait()
        early[i].first()

    ids = 2 * e * CAP + lax.broadcasted_iota(jnp.int32, (2 * CAP, T), 0)
    expert_low = CAP * lax.broadcasted_iota(jnp.int32, (16, T), 0)

    def route_masks(g, who):
        both = slots_ref[g, who]
        first, second = both[:1], both[1:2]
        return first, second, ids == first, ids == second

    def select_cots(k):
        g = groups[k]
        got_cots[k].wait()

        def one(who):
            _, _, mark0, mark1 = route_masks(g, who)
            mark = jnp.where(mark0 | mark1, 1.0, 0.0).astype(bfloat)
            picked = jnp.dot(mark, cots[k % 2, who], preferred_element_type=single).astype(bfloat)
            for j in range(2):
                raw[j, g, row_block(who, CAP), :] = picked[j * CAP : (j + 1) * CAP]

        for who in range(8):
            one(who)
        if k < 2:
            got_cots.append(load(cot_hbm.at[groups[k + 2]], cots.at[k], k + 2))

    def select_rows(k):
        g = groups[k]

        def one(who):
            slot0, slot1, mark0, mark1 = route_masks(g, who)
            block = normed_all[g, who]
            mark = jnp.where(mark0 | mark1, 1.0, 0.0).astype(bfloat)
            picked = jnp.dot(mark, block, preferred_element_type=single).astype(bfloat)
            logits = dot_rows(router_turned_ref[...], block)
            chosen = [
                jnp.sum(
                    jnp.where((slot >= expert_low) & (slot < expert_low + CAP), logits, 0.0),
                    axis=0,
                    keepdims=True,
                )
                for slot in (slot0, slot1)
            ]
            top = jnp.maximum(chosen[0], chosen[1])
            weight = [jnp.exp(value - top) for value in chosen]
            total = weight[0] + weight[1]
            gate = jnp.sum(
                jnp.where(mark0, weight[0] / total, 0.0) + jnp.where(mark1, weight[1] / total, 0.0),
                axis=1,
                keepdims=True,
            )
            for j in range(2):
                part = slice(j * CAP, (j + 1) * CAP)
                rows[j, g, row_block(who, CAP), :] = picked[part]
                gates[j, g, row_block(who, CAP), :] = jnp.broadcast_to(gate[part], (CAP, 128))

        for who in range(8):
            one(who)

    def compute(k):
        g = groups[k]

        def one(j):
            before = jnp.dot(rows[j, g], w_up[j], preferred_element_type=single)
            act, slope = gelu_both(before)
            act = act.astype(bfloat)
            acts[j, g] = act
            gate = gates[j, g][:, :1]
            cot = raw[j, g].astype(single)
            weighted = (gate * cot).astype(bfloat)
            gated[j, g] = weighted
            act_grad = dot_rows(weighted, w_down[j])
            pre_grad = (act_grad * slope).astype(bfloat)
            pre_grads[j, g] = pre_grad
            row_grad = dot_rows(pre_grad, w_up[j])
            row_send[g, j] = row_grad.astype(bfloat).reshape(8, CAP, D)
            out = jnp.dot(act, w_down[j], preferred_element_type=single)
            out_send[g, j] = (gate * out).astype(bfloat).reshape(8, CAP, D)
            product = out * cot
            folded = product[:, :128]
            for i in range(1, D // 128):
                folded = folded + product[:, 128 * i : 128 * (i + 1)]
            slot_grads[g, j : j + 1, :] = jnp.sum(folded.T, axis=0, keepdims=True)

        for j in range(2):
            one(j)

    def give_back(k, source, target, send_sems, recv_sems):
        g = groups[k]
        slot = k if source is row_send else k // 2
        target[slot, e] = source[g, :, e]
        for i, d in enumerate(p.around):
            p.push(
                source.at[g, :, d], target.at[slot, e], send_sems.at[k, i], recv_sems.at[k, i],
                (d, s),
            )

    def out_ahead(k):
        g = groups[k]
        i = k // 2
        p.push(out_send.at[g], out_ahead_in.at[i], oas.at[i], oar.at[i], (e, g))

    def step(k):
        select_rows(k)
        compute(k)

    def arrive(k):
        p.arrived(mine, nr.at[k - 1])
        gathers[k].first()

    slot_grads[...] = jnp.zeros_like(slot_grads)
    select_cots(0)
    gathers[0].second()
    arrive(1)
    gathers[0].third()
    arrive(2)
    early[0].second()
    early[1].second()
    arrive(3)
    gathers[0].done()
    gathers[1].second()
    got_up.wait()
    got_down.wait()
    step(0)
    gathers[1].third()
    gathers[2].second()
    gathers[3].second()
    early[0].third()
    early[1].third()
    select_cots(1)
    gathers[1].done()
    step(1)
    give_back(1, row_send, row_back, rs, rr)
    out_ahead(1)
    gathers[2].third()
    gathers[3].third()
    select_cots(2)
    gathers[2].done()
    step(2)
    give_back(2, row_send, row_back, rs, rr)
    select_cots(3)
    gathers[3].done()
    step(3)
    give_back(3, row_send, row_back, rs, rr)
    give_back(2, out_send, out_back, os, orr)
    give_back(0, row_send, row_back, rs, rr)
    for k in range(3):
        p.push(
            slot_grads.at[p.others[k]], slot_z.at[k], ss.at[k], sr.at[k], (e, p.others[k])
        )

    out_ahead(3)

    def weight_grads(i):
        j = i // 3
        lanes = lane_block(lax.rem(i, 3), 256)
        inputs = rows[j].reshape(4 * 8 * CAP, D)
        up_grad_out[j, :, lanes] = dot_columns(
            inputs, pre_grads[j, :, :, lanes].reshape(4 * 8 * CAP, 256)
        ).astype(bfloat)
        inputs = acts[j].reshape(4 * 8 * CAP, -1)
        down_grad_out[j, :, lanes] = dot_columns(
            inputs, gated[j, :, :, lanes].reshape(4 * 8 * CAP, 256)
        ).astype(bfloat)

    loop(3, weight_grads)
    total = slot_grads[s]
    for k in range(3):
        p.arrived(slot_z.at[k], sr.at[k])
        total = total + slot_z[k]
    slot_sum[...] = total
    slot_plane[e] = total
    for i, d in enumerate(p.around):
        p.push(slot_sum, slot_plane.at[e], ps.at[i], pr.at[i], (d, s))

    slot_lanes = lax.broadcasted_iota(jnp.int32, (T, 16 * CAP), 1)

    def slot_columns(g):
        return slots_ref[g, e].astype(single).T.astype(jnp.int32)

    def collect(k, back, recv_sems, part, z_in, z_send, z_recv):
        g = groups[k]
        slot = k if back is row_back else k // 2
        for i in range(7):
            p.arrived(back.at[slot, e], recv_sems.at[k, i])
        columns = slot_columns(g)
        marks = jnp.where(
            (columns[:, :1] == slot_lanes) | (columns[:, 1:2] == slot_lanes), 1.0, 0.0
        ).astype(bfloat)
        combined = jnp.dot(
            marks, back[slot].reshape(16 * CAP, D), preferred_element_type=single
        )
        part[slot] = combined.astype(bfloat)
        if k:
            i = k - 1 if back is row_back else 0
            p.push(part.at[slot], z_in.at[i], z_send.at[i], z_recv.at[i], (e, g))

    for k in (1, 2, 3):
        collect(k, row_back, rr, row_part, row_z, rzs, rzr)

    for i in range(2):
        p.arrived(out_ahead_in.at[i], oar.at[i])
    for j in range(2):
        out_send[s, j] = (
            out_send[s, j].astype(single)
            + out_ahead_in[0, j].astype(single)
            + out_ahead_in[1, j].astype(single)
        ).astype(bfloat)
    give_back(0, out_send, out_back, os, orr)

    def weight_later(i):
        weight_grads(i + 3)

    loop(3, weight_later)

    for i in range(7):
        p.arrived(slot_sum, pr.at[i])
    turned = pltpu.roll(
        slot_plane[...].reshape(64, 8 * CAP), lax.rem(8 * CAP - CAP * e, 8 * CAP), 1
    )
    logits = dot_rows(normed_ref[...], router_turned_ref[...])
    columns = slot_columns(s)
    expert_lanes = CAP * lax.broadcasted_iota(jnp.int32, (T, 16), 1)
    picks, chosen, grads = [], [], []
    small_lanes = lax.broadcasted_iota(jnp.int32, (T, CAP), 1)
    for r in range(2):
        slot = columns[:, r : r + 1]
        picks.append((slot >= expert_lanes) & (slot < expert_lanes + CAP))
        chosen.append(jnp.sum(jnp.where(picks[r], logits, 0.0), axis=1, keepdims=True))
        found = jnp.zeros((T, CAP), single)
        for who in range(8):
            for j in range(2):
                values = turned[8 * who + j : 8 * who + j + 1, :CAP]
                found = found + jnp.where(slot - (2 * who + j) * CAP == small_lanes, values, 0.0)
        grads.append(jnp.sum(found, axis=1, keepdims=True))
    top = jnp.maximum(chosen[0], chosen[1])
    weight = [jnp.exp(value - top) for value in chosen]
    total = weight[0] + weight[1]
    weight = [value / total for value in weight]
    mean = weight[0] * grads[0] + weight[1] * grads[1]
    logit_grad = jnp.zeros((T, 16), single)
    for r in range(2):
        logit_grad = logit_grad + jnp.where(picks[r], weight[r] * (grads[r] - mean), 0.0)
    logit_grad = logit_grad.astype(bfloat)
    small_out[...] = jnp.zeros_like(small_out)
    small_out[:16, :] = dot_columns(logit_grad, normed_ref[...])
    normed_grad = jnp.dot(logit_grad, router_turned_ref[...], preferred_element_type=single)
    collect(2, out_back, orr, out_part, out_z, ozs, ozr)
    collect(0, row_back, rr, row_part, row_z, rzs, rzr)
    normed_grad = normed_grad + row_part[0].astype(single)
    for k in range(3):
        p.arrived(row_z.at[k], rzr.at[k])
        normed_grad = normed_grad + row_z[k].astype(single)
    input_grad, gain_grad = norm_pull(mid_ref[...], gains_ref[3:4, :], normed_grad)
    small_out[16:17, :] = gain_grad
    mid_grad_out[...] = own_cot_ref[...].astype(single) + input_grad

    collect(0, out_back, orr, out_part, out_z, ozs, ozr)
    p.arrived(out_z.at[0], ozr.at[0])
    result = mid_ref[...] + out_part[0].astype(single) + out_z[0].astype(single)
    hidden_out[...] = result.astype(bfloat)
    for gather in early:
        gather.done()
    for copy in p.sent:
        copy.wait_send()


def run_experts(
    moe_normed, mid, gains, router, slots, own_cot, cots, up_own, expert_down, normed, attended
):
    vmem = pl.BlockSpec(memory_space=VMEM)
    anywhere = pl.BlockSpec(memory_space=ANY)
    shape = jax.ShapeDtypeStruct
    width = expert_down.shape[1]
    sem = pltpu.SemaphoreType.DMA
    per_expert = (EXP_DEV, 4, 8 * CAP)
    sends = (4, EXP_DEV, 8, CAP, D)
    backs = (4, 8, EXP_DEV, CAP, D)
    return pl.pallas_call(
        experts_kernel,
        name="experts",
        out_shape=(
            shape((T, D), bfloat),
            shape((T, D), single),
            shape((24, D), single),
            shape((EXP_DEV, D, width), bfloat),
            shape((EXP_DEV, width, D), bfloat),
            shape((2, 8, T, D), bfloat),
        ),
        in_specs=[vmem] * 6 + [anywhere] * 5,
        out_specs=(vmem,) * 5 + (anywhere,),
        scratch_shapes=[
            VMEM((4, 8, T, D), bfloat),
            VMEM((2, 8, T, D), bfloat),
            VMEM((EXP_DEV, D, width), bfloat),
            VMEM((EXP_DEV, width, D), bfloat),
            VMEM(per_expert + (D,), bfloat),
            VMEM(per_expert + (D,), bfloat),
            VMEM(per_expert + (128,), single),
            VMEM(per_expert + (width,), bfloat),
            VMEM(per_expert + (width,), bfloat),
            VMEM(per_expert + (D,), bfloat),
            VMEM(sends, bfloat),
            VMEM(sends, bfloat),
            VMEM(backs, bfloat),
            VMEM((2,) + backs[1:], bfloat),
            VMEM((2,) + sends[1:], bfloat),
            VMEM((4, 8, 8 * CAP), single),
            VMEM((3, 8, 8 * CAP), single),
            VMEM((8, 8 * CAP), single),
            VMEM((8, 8, 8 * CAP), single),
            VMEM((4, T, D), bfloat),
            VMEM((2, T, D), bfloat),
            VMEM((3, T, D), bfloat),
            VMEM((1, T, D), bfloat),
            sem((3,)), sem((3,)),
            sem((4, 7)), sem((4, 7)),
            sem((4, 7)), sem((4, 7)),
            sem((4, 7)), sem((4, 7)),
            sem((3,)), sem((3,)),
            sem((7,)), sem((7,)),
            sem((3,)), sem((3,)),
            sem((3,)), sem((3,)),
            sem((8,)),
            sem((2, 7)), sem((2, 7)),
            sem((2,)), sem((2,)),
        ],
        compiler_params=pltpu.CompilerParams(
            collective_id=4, has_side_effects=True, vmem_limit_bytes=60 * 2**20
        ),
    )(
        moe_normed, mid, gains, router, slots, own_cot, cots, up_own, expert_down, normed, attended
    )


def finish_kernel(
    att_hbm,
    up_hbm,
    down_hbm,
    expert_up_hbm,
    expert_down_hbm,
    small_hbm,
    late_hbm,
    peak_hbm,
    grad_hbm,
    result_hbm,
    qkv_out,
    out_out,
    up_out,
    down_out,
    expert_up_out,
    expert_down_out,
    attn_gain_out,
    mlp_gain_out,
    bias_out,
    router_out,
    clip_out,
    grad_out,
    result_out,
    att,
    up,
    down,
    expert_up,
    expert_down,
    small_ref,
    late_ref,
    peak_ref,
    grad,
    qkv_wide,
    out_wide,
    up_wide,
    down_wide,
    expert_up_wide,
    expert_down_wide,
    turned,
    in_sems,
    out_sems,
):
    s = lax.axis_index("shard")

    def start(source, target, sem):
        copy = pltpu.make_async_copy(source, target, sem)
        copy.start()
        return copy

    got = [
        start(source, target, in_sems.at[i])
        for i, (source, target) in enumerate(
            (
                (expert_down_hbm, expert_down),
                (expert_up_hbm, expert_up),
                (att_hbm, att),
                (up_hbm, up),
                (down_hbm, down),
                (grad_hbm, grad),
                (small_hbm, small_ref),
                (late_hbm, late_ref),
                (peak_hbm, peak_ref),
                (result_hbm, result_out),
            )
        )
    ]
    put = []

    def widen(i):
        rows = row_block(i, 128)
        for j in range(EXP_DEV):
            expert_down_wide[j, rows, :] = expert_down[j, rows, :].astype(single)

    def widen_up(i):
        lanes = lane_block(i, 384)
        for j in range(EXP_DEV):
            expert_up_wide[j, :, lanes] = expert_up[j, :, lanes].astype(single)

    def widen_down(i):
        down_wide[row_block(i, 96), :] = down[i].astype(single)

    got[0].wait()
    loop(expert_down.shape[1] // 128, widen)
    put.append(start(expert_down_wide, expert_down_out, out_sems.at[0]))
    got[1].wait()
    loop(expert_up.shape[2] // 384, widen_up)
    put.append(start(expert_up_wide, expert_up_out, out_sems.at[1]))
    got[2].wait()
    for layer in range(2):
        for b in range(6):
            qkv_wide[layer, :, 384 * b : 384 * (b + 1)] = att[layer, b].astype(single)
        for b in range(2):
            out_wide[layer, :, 384 * b : 384 * (b + 1)] = att[layer, 6 + b].astype(single)
    put.append(start(qkv_wide, qkv_out, out_sems.at[2]))
    put.append(start(out_wide, out_out, out_sems.at[3]))
    got[3].wait()
    for b in range(8):
        up_wide[:, 384 * b : 384 * (b + 1)] = up[b].astype(single)
    put.append(start(up_wide, up_out, out_sems.at[4]))
    got[4].wait()
    loop(8, widen_down)
    put.append(start(down_wide, down_out, out_sems.at[5]))

    for copy in got[5:]:
        copy.wait()
    grad_out[...] = grad[...][:, None, :]
    part = D // 4
    back = lax.rem(D - part * s, D)
    first_gain = jnp.concatenate([late_ref[i : i + 1, :] for i in range(6)], axis=1)
    gains = jnp.concatenate([first_gain, small_ref[16:19, :], jnp.zeros((4, D), single)])
    gains = pltpu.roll(gains, back, 1)[:, :part]
    attn_gain_out[0:1, :] = gains[0:1]
    attn_gain_out[1:2, :] = gains[2:3]
    mlp_gain_out[0:1, :] = gains[3:4]
    mlp_gain_out[1:2, :] = gains[1:2]
    turned[:, :16] = small_ref[:16, :].T
    router_out[...] = turned[row_block(s, part), :16].T
    turned[:128, : 2 * H] = late_ref[8:32, :].T
    biases = turned[row_block(s, 8), : 2 * H]
    peaks = peak_ref[...].T[:1, :]
    clips = jnp.sqrt(clip_limit / jnp.maximum(peaks, clip_limit))
    for layer in range(2):
        bias_out[layer] = biases[:, layer * H : (layer + 1) * H]
        clip_out[layer : layer + 1, :] = clips[:, layer * H : (layer + 1) * H]
    for copy in put:
        copy.wait()


def finish(att, up, down, expert_up, expert_down, small, late, peaks, grad, result):
    vmem = pl.BlockSpec(memory_space=VMEM)
    anywhere = pl.BlockSpec(memory_space=ANY)
    loaded = (att, up, down, expert_up, expert_down, small, late, peaks, grad)
    sem = pltpu.SemaphoreType.DMA
    wide = (
        (2, 192, 3 * D), (2, 192, D), (192, 8 * 384), (8 * 96, D), expert_up.shape,
        expert_down.shape,
    )
    return pl.pallas_call(
        finish_kernel,
        name="finish",
        out_shape=tuple(
            jax.ShapeDtypeStruct(dims, single)
            for dims in wide + ((2, 192), (2, 192), (2, 8, H), (16, 192), (2, H), (T, 1, D))
        )
        + (jax.ShapeDtypeStruct(result.shape, bfloat),),
        in_specs=[anywhere] * 10,
        out_specs=(anywhere,) * 6 + (vmem,) * 7,
        scratch_shapes=[VMEM(item.shape, item.dtype) for item in loaded]
        + [VMEM(dims, single) for dims in wide]
        + [VMEM((D, 128), single), sem((10,)), sem((6,))],
        compiler_params=pltpu.CompilerParams(vmem_limit_bytes=60 * 2**20),
    )(*loaded, result)


def shards(
    hidden_in,
    attn_gain,
    qkv_weight,
    out_weight,
    rel_bias,
    bucket_table,
    mlp_gain,
    mlp_up,
    mlp_down,
    router_weight,
    expert_up,
    expert_down,
    routes,
    out_grad,
):
    block_rows = hidden_in.shape[1]
    length = bucket_table.shape[0]
    groups = lax.axis_size("shard")

    def block(values):
        return jnp.pad(values, ((0, -values.shape[0] % 8), (0, 256 - values.shape[1])))

    part = D // groups
    small = jnp.concatenate(
        [
            block(jnp.concatenate([attn_gain, mlp_gain])),
            block(rel_bias.transpose(1, 0, 2).reshape(NB // groups, 2 * H)),
            block(router_weight.T),
        ]
    ).astype(single)
    backward_table = jnp.pad(bucket_table[::-1], (0, TOE))
    buckets = lax.dynamic_slice_in_dim(
        backward_table, length - block_rows * (lax.axis_index("expert") + 1), TOE
    )[None]
    cotangent = out_grad.reshape(block_rows, D)
    (
        normed, queries, attended, mid_first, mid_second, dense_normed, pre_act, activation, layer_one, peak_rows,
        moe_normed, gains, router, slots, qkv0, qkv1, projection0, projection1, dense_up,
        dense_down, kv, probs, up_own, cotangents,
    ) = forward(
        hidden_in.reshape(block_rows, D), small, buckets, routes.reshape(block_rows, 2).T,
        qkv_weight, out_weight, mlp_up, mlp_down, expert_up, cotangent,
    )
    hidden_out, mid_grad, small_in, up_grad, expert_down_low, early_rows = run_experts(
        moe_normed, mid_second, gains, router, slots, cotangent, cotangents, up_own, expert_down,
        normed, attended,
    )
    hidden_grad, attention_sum, up_sum, down_sum, small_sum, late_sum, peaks, expert_up_low = (
        backward(
            mid_grad, layer_one, hidden_in.reshape(block_rows, D), mid_first, gains, normed, queries,
            attended, dense_normed, activation, pre_act, buckets, small_in, peak_rows,
            early_rows, (qkv0, qkv1, projection0, projection1, dense_up, dense_down), kv, probs,
            up_grad,
        )
    )
    (
        qkv_grad, out_weight_grad, mlp_up_grad, mlp_down_grad, expert_up_grad, expert_down_grad,
        attn_gain_grad, mlp_gain_grad, rel_bias_grad, router_grad, clip_scales, hidden_grad, hidden_out,
    ) = finish(
        attention_sum, up_sum, down_sum, expert_up_low, expert_down_low, small_sum, late_sum, peaks,
        hidden_grad, hidden_out,
    )
    return (
        hidden_out.reshape(hidden_in.shape),
        hidden_grad.reshape(hidden_in.shape),
        attn_gain_grad,
        qkv_grad,
        out_weight_grad,
        rel_bias_grad,
        mlp_gain_grad,
        mlp_up_grad,
        mlp_down_grad,
        router_grad.T,
        expert_up_grad,
        expert_down_grad,
        clip_scales,
    )


def solution(mesh):
    tokens = P("shard", "expert", None, None)
    columns = P(None, "shard")
    layers = P(None, "shard", None)
    rows = P("shard", None)
    owned = P("expert", "shard", None)
    in_specs = (
        tokens, columns, layers, layers, layers, P(), columns, rows, rows, rows, owned, owned,
        tokens, tokens,
    )
    out_specs = (
        tokens, tokens, columns, layers, layers, layers, columns, rows, rows, rows, owned, owned,
        P(),
    )
    sized = mesh.shape["expert"] == 8 and mesh.shape["shard"] == 4
    part = shards if sized else plain_shards
    return jax.shard_map(part, mesh=mesh, in_specs=in_specs, out_specs=out_specs, check_vma=False)
```

```python
import functools
import math

import jax
import jax.numpy as jnp
from jax import lax
from jax.experimental import pallas as pl
from jax.experimental.pallas import tpu as pltpu
from jax.sharding import PartitionSpec as P

D = 768
H = 12
HD = 64
NB = 32
EXP_DEV = 2

epsilon = 1e-06
clip_limit = 6.0
bfloat = jnp.bfloat16
single = jnp.float32


def rms_norm(inputs, norm_gain):
    return (
        inputs * lax.rsqrt(jnp.mean(inputs * inputs, axis=-1, keepdims=True) + epsilon) * norm_gain
    )


def norm_back(inputs, norm_gain, upstream):
    _, pullback = jax.vjp(rms_norm, inputs, norm_gain)
    return pullback(upstream)


def gelu_back(pre_values, upstream):
    _, pullback = jax.vjp(jax.nn.gelu, pre_values)
    return pullback(upstream)[0]


def matmul(left, right):
    return jnp.dot(left, right, preferred_element_type=single)


def shard_shift(block, amount):
    count = lax.axis_size("shard")
    return lax.ppermute(block, "shard", [(i, (i + amount) % count) for i in range(count)])


def gather_shard(block):
    count = lax.axis_size("shard")
    here = lax.axis_index("shard")
    result = jnp.zeros((count,) + block.shape, block.dtype)
    for step in range(count):
        piece = block if step == 0 else shard_shift(block, step)
        result = lax.dynamic_update_slice_in_dim(result, piece[None], (here - step) % count, 0)
    return result


def scatter_shard(blocks, sent=bfloat):
    count = lax.axis_size("shard")
    here = lax.axis_index("shard")
    total = lax.dynamic_index_in_dim(blocks, here, 0, keepdims=False).astype(single)
    for step in range(1, count):
        part = lax.dynamic_index_in_dim(blocks, (here + step) % count, 0, keepdims=False)
        total = total + shard_shift(part.astype(sent), step).astype(single)
    return total


def spread(columns):
    experts, shard_count = lax.axis_size("expert"), lax.axis_size("shard")
    rows, width = columns.shape
    cut = columns.reshape(rows, shard_count, experts, width // (shard_count * experts))
    return cut.transpose(0, 2, 1, 3).reshape(rows, width)


def unspread(columns):
    experts, shard_count = lax.axis_size("expert"), lax.axis_size("shard")
    rows, width = columns.shape
    cut = columns.reshape(rows, experts, shard_count, width // (shard_count * experts))
    return cut.transpose(0, 2, 1, 3).reshape(rows, width)


def gather_weight(block):
    part = block.shape[0] // lax.axis_size("expert")
    own = lax.dynamic_slice_in_dim(block, lax.axis_index("expert") * part, part, 0)
    column = gather_shard(own).reshape(-1, block.shape[1])
    return lax.all_gather(column, "expert", axis=0, tiled=True)


def reduce_weight(grad):
    part = lax.psum_scatter(grad.astype(bfloat), "expert", scatter_dimension=0, tiled=True)
    blocks = part.reshape((lax.axis_size("shard"), -1) + part.shape[1:])
    own = scatter_shard(blocks).astype(bfloat)
    return lax.all_gather(own, "expert", axis=0, tiled=True).astype(single)


def bucket_marks(distance, lower, upper):
    inside = (distance[None] >= lower[:, None, None]) & (distance[None] < upper[:, None, None])
    return inside.astype(bfloat)


def position_bias(marks, bias_pair):
    return jnp.einsum("bij,bh->hij", marks, bias_pair, preferred_element_type=single)


def attention_forward(hidden, norm_gain, qkv, projection, bias_pair, geometry):
    distance, marks, scale = geometry
    rows = hidden.shape[0]
    normalized = spread(rms_norm(hidden, norm_gain).astype(bfloat))
    packed = matmul(normalized, qkv).astype(bfloat)
    key_value = lax.all_gather(packed[:, D:], "expert", axis=0, tiled=True)
    shifted = position_bias(marks, bias_pair)
    causal = distance >= 0
    queries = packed[:, :D].reshape(rows, H, HD)
    keys = key_value[:, :D].reshape(-1, H, HD)
    values = key_value[:, D:].reshape(-1, H, HD)
    raw_scores = jnp.einsum("ihd,jhd->hij", queries, keys, preferred_element_type=single) * scale
    head_peak = jnp.max(jnp.where(causal[None], raw_scores, -jnp.inf), axis=(1, 2))
    masked = jnp.where(causal[None], raw_scores + shifted, -jnp.inf)
    softmax_top = jnp.max(masked, axis=-1, keepdims=True)
    exponent = jnp.exp(masked - softmax_top)
    softmax_sum = jnp.sum(exponent, axis=-1, keepdims=True)
    probs = (exponent / softmax_sum).astype(bfloat)
    log_total = softmax_top[..., 0] + jnp.log(softmax_sum[..., 0])
    attended = jnp.einsum("hij,jhd->ihd", probs, values, preferred_element_type=single)
    attended = spread(attended.astype(bfloat).reshape(rows, D))
    saved = (normalized, packed, key_value, log_total, attended)
    return hidden + matmul(attended, projection), head_peak, saved


def attention_backward(
    upstream, hidden, norm_gain, qkv, projection, bias_pair, geometry, saved
):
    distance, marks, scale = geometry
    normalized, packed, key_value, log_total, attended = saved
    rows = hidden.shape[0]
    branch_grad = upstream.astype(bfloat)
    projection_grad = matmul(attended.T, branch_grad)
    attended_grad = unspread(matmul(branch_grad, projection.T).astype(bfloat))
    shifted = position_bias(marks, bias_pair)
    causal = distance >= 0
    queries = packed[:, :D].reshape(rows, H, HD)
    keys = key_value[:, :D].reshape(-1, H, HD)
    values = key_value[:, D:].reshape(-1, H, HD)
    grad_heads = attended_grad.reshape(rows, H, HD)
    raw_scores = jnp.einsum("ihd,jhd->hij", queries, keys, preferred_element_type=single) * scale
    probs = jnp.where(causal[None], jnp.exp(raw_scores + shifted - log_total[..., None]), 0.0)
    prob_grad = jnp.einsum("ihd,jhd->hij", grad_heads, values, preferred_element_type=single)
    row_dot = jnp.sum(prob_grad * probs, axis=-1)
    score_grad = (probs * (prob_grad - row_dot[..., None])).astype(bfloat)
    query_grad = jnp.einsum("hij,jhd->ihd", score_grad, keys, preferred_element_type=single) * scale
    query_grad = query_grad.astype(bfloat).reshape(rows, D)
    bias_grad = jnp.einsum("hij,bij->bh", score_grad, marks, preferred_element_type=single)
    key_grad = (
        jnp.einsum("hij,ihd->jhd", score_grad, queries, preferred_element_type=single) * scale
    )
    value_grad = jnp.einsum(
        "hij,ihd->jhd", probs.astype(bfloat), grad_heads, preferred_element_type=single
    )
    pair = jnp.concatenate([key_grad.reshape(-1, D), value_grad.reshape(-1, D)], axis=-1)
    pair_grad = lax.psum_scatter(pair.astype(bfloat), "expert", scatter_dimension=0, tiled=True)
    packed_grad = jnp.concatenate([query_grad, pair_grad], axis=-1)
    qkv_grad = matmul(normalized.T, packed_grad)
    normed_grad = unspread(matmul(packed_grad, qkv.T))
    input_grad, gain_grad = norm_back(hidden, norm_gain, normed_grad)
    return upstream + input_grad, gain_grad, qkv_grad, projection_grad, bias_grad


def exchange(blocks):
    return lax.all_to_all(blocks, "expert", split_axis=0, concat_axis=0, tiled=True)


def plain_shards(
    hidden_in,
    attn_gain,
    qkv_weight,
    out_weight,
    rel_bias,
    bucket_table,
    mlp_gain,
    mlp_up,
    mlp_down,
    router_weight,
    expert_up,
    expert_down,
    routes,
    out_grad,
):
    block_rows = hidden_in.shape[1]
    length = bucket_table.shape[0]
    experts = lax.axis_size("expert")
    groups = lax.axis_size("shard")
    here = lax.axis_index("shard")
    expert_total = EXP_DEV * experts
    capacity = 4 * block_rows // expert_total
    width = expert_down.shape[1]
    scale = 1.0 / math.sqrt(HD)

    small = jnp.concatenate(
        [attn_gain.reshape(-1), mlp_gain.reshape(-1), rel_bias.reshape(-1), router_weight.reshape(-1)]
    )
    small = gather_shard(small)
    part = D // groups
    cuts = [0, 2 * part, 4 * part, 4 * part + 2 * (NB // groups) * H, small.shape[1]]
    gain_attn, gain_mlp, bias_weights, router_full = (
        small[:, cuts[i] : cuts[i + 1]] for i in range(4)
    )
    gain_attn = gain_attn.reshape(groups, 2, part).transpose(1, 0, 2).reshape(2, D).astype(single)
    gain_mlp = gain_mlp.reshape(groups, 2, part).transpose(1, 0, 2).reshape(2, D).astype(single)
    bias_weights = (
        bias_weights.reshape(groups, 2, NB // groups, H).transpose(1, 0, 2, 3).reshape(2, NB, H)
    )
    router_full = router_full.reshape(D, expert_total)

    first = gather_weight(jnp.concatenate([qkv_weight[0], out_weight[0]], axis=1))
    dense_up = gather_weight(mlp_up)
    dense_down = gather_weight(mlp_down)
    second = gather_weight(jnp.concatenate([qkv_weight[1], out_weight[1]], axis=1))
    qkv = (first[:, : 3 * D], second[:, : 3 * D])
    projection = (first[:, 3 * D :], second[:, 3 * D :])

    up_own = jnp.zeros((EXP_DEV, groups, part, width), bfloat)
    for step in range(groups):
        target = (here + step) % groups
        piece = lax.dynamic_slice_in_dim(expert_up, target * width, width, 2)
        if step:
            piece = shard_shift(piece, step)
        up_own = lax.dynamic_update_slice_in_dim(up_own, piece[:, None], (here - step) % groups, 1)
    up_own = up_own.reshape(EXP_DEV, D, width)

    route_rows = gather_shard(routes.reshape(block_rows, 2))
    upstream_all = gather_shard(out_grad.reshape(block_rows, D))
    expert_ids = jnp.arange(expert_total, dtype=jnp.int32)
    flat_routes = route_rows.reshape(groups, -1)
    marks = (flat_routes[:, :, None] == expert_ids).astype(jnp.int32)
    rank = jnp.sum((jnp.cumsum(marks, axis=1) - marks) * marks, axis=2)
    slot_of_route = flat_routes * capacity + rank
    slot_ids = jnp.arange(expert_total * capacity, dtype=jnp.int32)
    slot_marks = (slot_of_route[:, :, None] == slot_ids).astype(bfloat)
    token_marks = jnp.sum(
        slot_marks.reshape(groups, block_rows, 2, -1).astype(single), axis=2
    ).astype(bfloat)

    def dispatch(rows):
        slots = jnp.einsum("gts,gtd->gsd", token_marks, rows, preferred_element_type=single)
        slots = slots.astype(bfloat).reshape(groups, experts, EXP_DEV, capacity, D)
        return exchange(slots.transpose(1, 2, 0, 3, 4)).reshape(
            experts, EXP_DEV, groups * capacity, D
        )

    def collect(blocks):
        back = exchange(blocks.astype(bfloat)).reshape(experts, EXP_DEV, groups, capacity, D)
        return back.transpose(2, 0, 1, 3, 4).reshape(groups, expert_total * capacity, D)

    owner_rows = dispatch(upstream_all)

    own_positions = lax.axis_index("expert") * block_rows + jnp.arange(block_rows, dtype=jnp.int32)
    distance = own_positions[:, None] - jnp.arange(length, dtype=jnp.int32)[None, :]
    bounds = jnp.sum(
        (bucket_table[:, None] < jnp.arange(NB + 1, dtype=jnp.int32)[None, :]).astype(jnp.int32),
        axis=0,
    )
    geometry = (distance, bucket_marks(distance, bounds[:NB], bounds[1:]), scale)

    hidden_zero = hidden_in.reshape(block_rows, D).astype(single)
    mid_first, peak_first, saved_first = attention_forward(
        hidden_zero, gain_attn[0], qkv[0], projection[0], bias_weights[0], geometry
    )
    dense_normed = spread(rms_norm(mid_first, gain_mlp[0]).astype(bfloat))
    pre_act = matmul(dense_normed, dense_up)
    activation = spread(jax.nn.gelu(pre_act).astype(bfloat))
    layer_one = mid_first + matmul(activation, dense_down)
    mid_second, peak_second, saved_second = attention_forward(
        layer_one, gain_attn[1], qkv[1], projection[1], bias_weights[1], geometry
    )

    moe_normed = rms_norm(mid_second, gain_mlp[1]).astype(bfloat)
    normed_all = gather_shard(moe_normed)
    received = dispatch(normed_all)
    router_logits = jnp.einsum("gtd,de->gte", normed_all, router_full, preferred_element_type=single)
    selected = (route_rows[..., None] == expert_ids).astype(single)
    gates_all = jax.nn.softmax(jnp.sum(selected * router_logits[:, :, None, :], axis=-1), axis=-1)
    slot_gates = jnp.sum(
        gates_all.reshape(groups, -1)[:, :, None] * (slot_of_route[:, :, None] == slot_ids), axis=1
    )
    owner_gates = exchange(
        slot_gates.reshape(groups, experts, EXP_DEV, capacity).transpose(1, 2, 0, 3)
    ).reshape(experts, EXP_DEV, groups * capacity)

    expert_pre = jnp.einsum("sjcd,jdf->sjcf", received, up_own, preferred_element_type=single)
    expert_act = jax.nn.gelu(expert_pre).astype(bfloat)
    expert_out = jnp.einsum(
        "sjcf,jfd->sjcd", expert_act, expert_down, preferred_element_type=single
    )
    owner_grad = (owner_gates[..., None] * owner_rows.astype(single)).astype(bfloat)
    act_grad = jnp.einsum("sjcd,jfd->sjcf", owner_grad, expert_down, preferred_element_type=single)
    pre_grad = gelu_back(expert_pre, act_grad).astype(bfloat)
    row_grad = jnp.einsum("sjcf,jdf->sjcd", pre_grad, up_own, preferred_element_type=single)

    returned = collect(expert_out)
    back_rows = collect(row_grad)
    expert_down_grad = jnp.einsum(
        "sjcf,sjcd->jfd", expert_act, owner_grad, preferred_element_type=single
    )
    up_grad = jnp.einsum(
        "sjcd,sjcf->jdf", received, pre_grad, preferred_element_type=single
    ).astype(bfloat)

    route_out = jnp.einsum("grs,gsd->grd", slot_marks, returned, preferred_element_type=single)
    route_out = route_out.reshape(groups, block_rows, 2, D)
    gate_grad = scatter_shard(
        jnp.sum(route_out * upstream_all[:, :, None, :].astype(single), axis=-1), single
    )
    mixed = scatter_shard(jnp.sum(gates_all[..., None] * route_out, axis=2))
    hidden_out = (mid_second + mixed).astype(bfloat).reshape(hidden_in.shape)

    gates = lax.dynamic_index_in_dim(gates_all, here, 0, keepdims=False)
    own_selected = lax.dynamic_index_in_dim(selected, here, 0, keepdims=False)
    upstream = out_grad.reshape(block_rows, D).astype(single)
    chosen_grad = gates * (gate_grad - jnp.sum(gates * gate_grad, axis=-1, keepdims=True))
    logit_grad = jnp.sum(chosen_grad[:, :, None] * own_selected, axis=1).astype(bfloat)
    router_grad = matmul(moe_normed.T, logit_grad)
    row_terms = jnp.einsum("gts,gsd->gtd", token_marks, back_rows, preferred_element_type=single)
    normed_grad = matmul(logit_grad, router_full.T) + scatter_shard(row_terms)
    moe_input_grad, moe_gain_grad = norm_back(mid_second, gain_mlp[1], normed_grad)
    mid_grad = upstream + moe_input_grad

    up_grad = up_grad.reshape(EXP_DEV, groups, part, width)
    expert_up_grad = jnp.zeros((EXP_DEV, part, groups * width), single)
    for step in range(groups):
        piece = lax.dynamic_index_in_dim(up_grad, (here + step) % groups, 1, keepdims=False)
        if step:
            piece = shard_shift(piece, step)
        expert_up_grad = lax.dynamic_update_slice_in_dim(
            expert_up_grad, piece.astype(single), ((here - step) % groups) * width, 2
        )

    layer_grad, gain_second, qkv_second, projection_second, bias_second = attention_backward(
        mid_grad, layer_one, gain_attn[1], qkv[1], projection[1], bias_weights[1], geometry,
        saved_second,
    )
    second_grad = reduce_weight(jnp.concatenate([qkv_second, projection_second], axis=1))
    dense_branch = layer_grad.astype(bfloat)
    mlp_down_grad = reduce_weight(matmul(activation.T, dense_branch))
    hidden_act_grad = unspread(matmul(dense_branch, dense_down.T))
    pre_act_grad = gelu_back(pre_act, hidden_act_grad).astype(bfloat)
    mlp_up_grad = reduce_weight(matmul(dense_normed.T, pre_act_grad))
    dense_normed_grad = unspread(matmul(pre_act_grad, dense_up.T))
    dense_input_grad, dense_gain_grad = norm_back(mid_first, gain_mlp[0], dense_normed_grad)
    first_grad = layer_grad + dense_input_grad
    input_grad, gain_first, qkv_first, projection_first, bias_first = attention_backward(
        first_grad, hidden_zero, gain_attn[0], qkv[0], projection[0], bias_weights[0], geometry,
        saved_first,
    )
    first_weight_grad = reduce_weight(jnp.concatenate([qkv_first, projection_first], axis=1))

    gains = jnp.stack([gain_first, gain_second, dense_gain_grad, moe_gain_grad])
    biases = jnp.stack([bias_first, bias_second])
    small_grad = jnp.concatenate(
        [
            gains.reshape(4, groups, part).transpose(1, 0, 2).reshape(groups, -1),
            biases.reshape(2, groups, NB // groups, H).transpose(1, 0, 2, 3).reshape(groups, -1),
            router_grad.reshape(groups, -1),
        ],
        axis=1,
    )
    small_grad = lax.psum(scatter_shard(small_grad, single), "expert")
    gain_cut = 4 * part
    bias_cut = gain_cut + 2 * (NB // groups) * H
    own_gains = small_grad[:gain_cut].reshape(4, part)
    peaks = lax.pmax(jnp.stack([peak_first, peak_second]), ("expert", "shard"))
    clip_scales = jnp.sqrt(clip_limit / jnp.maximum(peaks, clip_limit))
    return (
        hidden_out,
        input_grad.reshape(hidden_in.shape),
        own_gains[:2],
        jnp.stack([first_weight_grad[:, : 3 * D], second_grad[:, : 3 * D]]),
        jnp.stack([first_weight_grad[:, 3 * D :], second_grad[:, 3 * D :]]),
        small_grad[gain_cut:bias_cut].reshape(2, NB // groups, H),
        own_gains[2:],
        mlp_up_grad,
        mlp_down_grad,
        small_grad[bias_cut:].reshape(part, expert_total),
        expert_up_grad,
        expert_down_grad,
        clip_scales,
    )


MESH = pl.DeviceIdType.MESH
ANY = pl.ANY
VMEM = pltpu.VMEM


def place():
    return lax.axis_index("expert"), lax.axis_index("shard")


def greet(devices):
    barrier = pltpu.get_barrier_semaphore()
    for device in devices:
        pl.semaphore_signal(barrier, inc=1, device_id=device, device_id_type=MESH)
    pl.semaphore_wait(barrier, len(devices))


def push(sent, source, target, send_sem, recv_sem, device):
    copy = pltpu.make_async_remote_copy(
        src_ref=source,
        dst_ref=target,
        send_sem=send_sem,
        recv_sem=recv_sem,
        device_id=device,
        device_id_type=MESH,
    )
    copy.start()
    sent.append(copy)
    return copy


def norm_rows(inputs, gain):
    return inputs * lax.rsqrt(jnp.mean(inputs * inputs, axis=-1, keepdims=True) + epsilon) * gain


def dot_rows(left, right):
    return lax.dot_general(left, right, (((1,), (1,)), ((), ())), preferred_element_type=single)


def dot_columns(left, right):
    return lax.dot_general(left, right, (((0,), (0,)), ((), ())), preferred_element_type=single)


def loop(count, body):
    def step(i, carry):
        body(i)
        return carry

    lax.fori_loop(0, count, step, 0)


def lane_block(i, width):
    return pl.ds(pl.multiple_of(i * width, 128), width)


def row_block(i, height):
    return pl.ds(pl.multiple_of(i * height, height), height)


T = 128
PAIRS = H // 2
TOE = 1152
CAP = 32


class Plane:
    def __init__(self):
        self.e, self.s = place()
        e = self.e
        self.core = lax.rem(e, 2)
        self.quarter = e // 2
        self.at_x = e + 2 - 4 * lax.rem(self.quarter, 2)
        self.at_y = lax.rem(e + 4, 8)
        self.at_core = e + 1 - 2 * self.core
        self.inward = jnp.where(self.core == 0, self.at_x, self.at_y)
        self.onward = jnp.where(self.core == 0, self.at_y, self.at_x)
        self.diagonal = self.inward + self.onward - e
        self.others = [lax.rem(self.s + k, 4) for k in range(1, 4)]
        self.around = [lax.rem(e + k, 8) for k in range(1, 8)]
        z = self.s
        first = jnp.where(z == 0, 1, jnp.where(z == 1, 2, jnp.where(z == 2, 1, 2)))
        second = jnp.where(z == 0, 2, jnp.where(z == 1, 0, jnp.where(z == 2, 3, 1)))
        self.near = [first, second, 6 - z - first - second]
        self.to_k = [lax.rem(other - z + 4, 4) - 1 for other in self.near]
        self.from_k = [lax.rem(z - other + 4, 4) - 1 for other in self.near]
        self.sent = []

    def push(self, source, target, send_sem, recv_sem, device):
        return push(self.sent, source, target, send_sem, recv_sem, device)

    def arrived(self, view, recv_sem):
        pltpu.make_async_remote_copy(
            src_ref=view,
            dst_ref=view,
            send_sem=recv_sem,
            recv_sem=recv_sem,
            device_id=(self.at_core, self.s),
            device_id_type=MESH,
        ).wait_recv()


class PlaneGather:
    def __init__(self, plane, view, send_sems, recv_sems):
        self.plane, self.view, self.ss, self.rs = plane, view, send_sems, recv_sems

    def _push(self, who, i, target):
        p = self.plane
        block = self.view(who)
        p.push(block, block, self.ss.at[i], self.rs.at[i], (target, p.s))

    def first(self):
        p = self.plane
        self._push(p.e, 0, p.at_x)
        self._push(p.e, 1, p.at_y)
        self._push(p.e, 3, p.at_core)

    def second(self):
        p = self.plane
        p.arrived(self.view(p.inward), self.rs.at[p.core])
        self._push(p.inward, 2, p.onward)
        self._push(p.inward, 4, p.at_core)

    def third(self):
        p = self.plane
        p.arrived(self.view(p.onward), self.rs.at[1 - p.core])
        self._push(p.onward, 5, p.at_core)
        p.arrived(self.view(p.diagonal), self.rs.at[2])
        self._push(p.diagonal, 6, p.at_core)

    def done(self):
        for i in range(3, 7):
            self.plane.arrived(self.view(self.plane.e), self.rs.at[i])


class PlaneSum:
    def __init__(self, plane, parts, core_in, chips_in, send_sems, recv_sems):
        self.plane, self.parts, self.core_in, self.chips_in = plane, parts, core_in, chips_in
        self.ss, self.rs = send_sems, recv_sems

    def give(self):
        p = self.plane
        p.push(
            self.parts.at[1 - p.core], self.core_in, self.ss.at[0], self.rs.at[0], (p.at_core, p.s)
        )

    def pass_on(self):
        p = self.plane
        p.arrived(self.core_in, self.rs.at[0])
        for q in range(4):
            self.parts[p.core, q] = (
                self.parts[p.core, q].astype(single) + self.core_in[q].astype(single)
            ).astype(bfloat)
        for k, d in enumerate((p.at_x, p.at_y, p.diagonal)):
            p.push(
                self.parts.at[p.core, d // 2],
                self.chips_in.at[k],
                self.ss.at[1 + k],
                self.rs.at[1 + k],
                (d, p.s),
            )

    def result(self):
        p = self.plane
        total = self.parts[p.core, p.quarter].astype(single)
        for k in range(3):
            p.arrived(self.chips_in.at[k], self.rs.at[1 + k])
            total = total + self.chips_in[k].astype(single)
        return total


def forward_kernel(
    hidden_ref,
    attn_gain_ref,
    mlp_gain_ref,
    rel_bias_ref,
    router_ref,
    buckets_ref,
    routes_ref,
    qkv_hbm,
    out_hbm,
    up_hbm,
    down_hbm,
    expert_up_hbm,
    cot_hbm,
    normed_out,
    query_out,
    attended_out,
    mid_first_out,
    mid_second_out,
    dense_normed_out,
    pre_out,
    act_out,
    one_out,
    peak_out,
    moe_normed_out,
    gains_ref,
    router_out,
    slots_out,
    qkv0_out,
    qkv1_out,
    proj0_out,
    proj1_out,
    up_out,
    down_out,
    kv_out,
    probs_out,
    up_own,
    cot_all,
    dense_rows_out,
    small_ref,
    small_all,
    table_ref,
    slots_own,
    up_shard,
    up_turned,
    dense_rows,
    sums,
    sums_core,
    sums_chips,
    w_qkv0,
    w_qkv1,
    w_out0,
    w_out1,
    w_up,
    w_down,
    kv,
    probs,
    scores,
    zs,
    zr,
    f1s,
    f1r,
    f2s,
    f2r,
    cs,
    cr,
    locals_sem,
    k1s,
    k1r,
    k2s,
    k2r,
    kcs,
    kcr,
    us,
    ur,
    gs,
    gr,
    ns,
    nr,
    outs_sem,
    small_s,
    small_r,
    slot_zs,
    slot_zr,
    slot_ps,
    slot_pr,
    dense_s,
    dense_r,
    sum_s,
    sum_r,
):
    e, s = place()
    core = lax.rem(e, 2)
    quarter = e // 2
    at_x = e + 2 - 4 * lax.rem(quarter, 2)
    at_y = lax.rem(e + 4, 8)
    at_core = e + 1 - 2 * core
    inward = jnp.where(core == 0, at_x, at_y)
    onward = jnp.where(core == 0, at_y, at_x)
    others = [lax.rem(s + k, 4) for k in range(1, 4)]
    plane = Plane()
    near, to_k, from_k = plane.near, plane.to_k, plane.from_k
    sources = near
    sent = []
    kept = []

    def local(source, target, sem):
        copy = pltpu.make_async_copy(source, target, sem)
        copy.start()
        return copy

    chunks = [
        (qkv_hbm.at[0], w_qkv0, 48, 1152),
        (out_hbm.at[0], w_out0, 48, 384),
        None,
        None,
        (qkv_hbm.at[1], w_qkv1, 48, 1152),
        (out_hbm.at[1], w_out1, 48, 384),
    ]

    def block(target, who, position, height, half, width):
        rows = pl.ds(pl.multiple_of(position * 4 * height + who * height, height), height)
        return target.at[rows, lane_block(half, width)]

    def cot_block(g, who):
        return cot_all.at[g, who]

    stage1, stage2, stage3, stage4, own = {}, {}, {}, {}, {}

    def z_send(c):
        source, target, height, width = chunks[c]
        piece = source.at[row_block(quarter, height), lane_block(core, width)]
        mine = block(target, quarter, s, height, core, width)
        stage1[c] = [
            push(sent, piece, mine, zs.at[c, to_k[i]], zr.at[c, to_k[i]], (e, near[i]))
            for i in range(3)
        ]
        own[c] = local(source, target.at[row_block(s, 4 * height), :], locals_sem.at[c])

    got_shard = local(up_hbm, up_shard, outs_sem.at[11])

    def turn_shard():
        got_shard.wait()
        for b in range(8):
            for z in range(4):
                up_turned[:, 384 * b + 96 * z : 384 * b + 96 * (z + 1)] = up_shard[
                    :, 768 * z + 96 * b : 768 * z + 96 * (b + 1)
                ]

    def unit_send(c):
        target, height = ((w_up, 192), (w_down, 96))[c - 2]
        piece = up_turned.at[:, lane_block(e, 384)] if c == 2 else down_hbm.at[row_block(e, 96), :]
        mine = target.at[row_block(s, height), :]
        stage1[c] = [
            push(sent, piece, mine, zs.at[c, to_k[i]], zr.at[c, to_k[i]], (e, near[i]))
            for i in range(3)
        ]
        own[c] = local(piece, mine, locals_sem.at[c])

    def units_ready(c):
        for copy in stage1[c]:
            copy.wait_recv()
        own[c].wait()
        kept.append(local((w_up, w_down)[c - 2], weight_outs[c], outs_sem.at[c]))

    def plane_send(c):
        _, target, height, width = chunks[c]
        stage2[c] = []
        for k in range(3):
            mine = block(target, quarter, sources[k], height, core, width)
            plane.arrived(mine, zr.at[c, from_k[k]])
            stage2[c].append(
                [
                    push(sent, mine, mine, f1s.at[c, k, i], f1r.at[c, k, i], (partner, s))
                    for i, partner in enumerate((at_x, at_y))
                ]
            )

    def plane_forward(c):
        _, target, height, width = chunks[c]
        stage3[c] = []
        for k in range(3):
            pltpu.make_async_remote_copy(
                src_ref=block(target, quarter, sources[k], height, core, width),
                dst_ref=block(target, quarter, sources[k], height, core, width),
                send_sem=f1s.at[c, k, core],
                recv_sem=f1r.at[c, k, core],
                device_id=(inward, s),
                device_id_type=MESH,
            ).wait_recv()
            theirs = block(target, inward // 2, sources[k], height, core, width)
            stage3[c].append(
                push(sent, theirs, theirs, f2s.at[c, k], f2r.at[c, k], (onward, s))
            )

    def core_send(c):
        _, target, height, width = chunks[c]
        stage4[c] = []
        for k in range(3):
            pltpu.make_async_remote_copy(
                src_ref=block(target, quarter, sources[k], height, core, width),
                dst_ref=block(target, quarter, sources[k], height, core, width),
                send_sem=f1s.at[c, k, 1 - core],
                recv_sem=f1r.at[c, k, 1 - core],
                device_id=(onward, s),
                device_id_type=MESH,
            ).wait_recv()
            stage3[c][k].wait_recv()
            half = target.at[row_block(sources[k], 4 * height), lane_block(core, width)]
            stage4[c].append(push(sent, half, half, cs.at[c, k], cr.at[c, k], (at_core, s)))

    weight_outs = [qkv0_out, proj0_out, up_out, down_out, qkv1_out, proj1_out]

    def ready(c):
        for k in range(3):
            stage4[c][k].wait_recv()
        own[c].wait()
        kept.append(local(chunks[c][1], weight_outs[c], outs_sem.at[c]))

    cot_groups = [s] + sources
    cot_gathers = [
        PlaneGather(plane, functools.partial(cot_block, g), ns.at[k], nr.at[k])
        for k, g in enumerate(cot_groups)
    ]

    def cot_first(k):
        plane.arrived(cot_block(s, e), gr.at[from_k[k - 1]])
        cot_gathers[k].first()

    experts = lax.broadcasted_iota(jnp.int32, (16, T), 0)
    chosen = [experts == routes_ref[r : r + 1, :] for r in range(2)]
    marks = jnp.where(chosen[0] | chosen[1], 1.0, 0.0).astype(bfloat)
    earlier = jnp.where(
        lax.broadcasted_iota(jnp.int32, (T, T), 0) < lax.broadcasted_iota(jnp.int32, (T, T), 1),
        1.0,
        0.0,
    ).astype(bfloat)
    before = jnp.dot(marks, earlier, preferred_element_type=single)
    slots_own[...] = jnp.zeros_like(slots_own)
    for r in range(2):
        rank = jnp.sum(jnp.where(chosen[r], before, 0.0), axis=0, keepdims=True)
        slots_own[r : r + 1, :] = routes_ref[r : r + 1, :] * CAP + rank.astype(jnp.int32)
    slots_out[s, e] = slots_own[...]
    own_cot = local(cot_hbm, cot_block(s, e), gs.at[3])
    part = D // 4
    small_ref[...] = jnp.zeros_like(small_ref)
    small_ref[0:2, :part] = attn_gain_ref[...].astype(single)
    small_ref[2:4, :part] = mlp_gain_ref[...].astype(single)
    for layer in range(2):
        small_ref[8:16, layer * H : (layer + 1) * H] = rel_bias_ref[layer].astype(single)
    small_ref[16:32, :part] = router_ref[...].astype(single)
    small_all[s] = small_ref[...]

    greet([(d, s) for d in plane.around] + [(e, other) for other in others])
    smalls = [
        push(sent, small_ref, small_all.at[s], small_s.at[k], small_r.at[k], (e, others[k]))
        for k in range(3)
    ]
    z_send(0)
    for k in range(3):
        push(sent, slots_own, slots_out.at[s, e], slot_zs.at[k], slot_zr.at[k], (e, others[k]))
    own_cot.wait()
    cot_gathers[0].first()
    z_send(1)
    turn_shard()
    unit_send(2)
    reshard = []

    def bulk():
        z_send(4)
        z_send(5)
        unit_send(3)
        for i in range(3):
            push(sent, cot_hbm, cot_block(s, e), gs.at[to_k[i]], gr.at[to_k[i]], (e, near[i]))
        kept.append(
            local(
                expert_up_hbm.at[:, :, lane_block(s, 768)],
                up_own.at[:, row_block(s, 192), :],
                us.at[3],
            )
        )

    def slots_plane():
        for k in range(3):
            plane.arrived(slots_own, slot_zr.at[k])
        column = slots_out.at[:, e]
        for k, d in enumerate(plane.around):
            push(sent, column, column, slot_ps.at[k], slot_pr.at[k], (d, s))

    for copy in smalls:
        copy.wait_recv()
    biases = []
    for z in range(4):
        lanes = slice(192 * z, 192 * (z + 1))
        gains_ref[:, lanes] = small_all[z, :4, :192]
        router_out[:, lanes] = small_all[z, 16:32, :192].astype(bfloat)
        biases.append(small_all[z, 8:16, : 2 * H])
    bucket_marks_here = jnp.where(
        lax.broadcasted_iota(jnp.int32, (NB, TOE), 0) == buckets_ref[...], 1.0, 0.0
    ).astype(bfloat)
    table_ref[...] = dot_columns(jnp.concatenate(biases).astype(bfloat), bucket_marks_here)

    def attention(layer, inputs, w_qkv, w_out, work):
        normed = norm_rows(inputs, gains_ref[pl.ds(layer, 1), :]).astype(bfloat)
        normed_out[layer] = normed
        if layer == 0:
            plane_send(0)
            plane_forward(0)
            plane_send(1)
            core_send(0)
            plane_forward(1)
            ready(0)
            bulk()
        else:
            ready(4)
        own_rows = row_block(e, T)
        first, second, third = [], [], []
        for part in range(3):
            x = normed_out[layer]
            for i, base in enumerate((D, 2 * D)):
                columns = w_qkv[:, base + 256 * part : base + 256 * (part + 1)]
                kv[layer, part, own_rows, 256 * i : 256 * (i + 1)] = jnp.dot(
                    x, columns, preferred_element_type=single
                ).astype(bfloat)
            mine = kv.at[layer, part, own_rows, :]
            first.append(
                [
                    push(sent, mine, mine, k1s.at[layer, part, i], k1r.at[layer, part, i], (p, s))
                    for i, p in enumerate((at_x, at_y))
                ]
            )
            third.append(
                [
                    push(
                        sent, mine, mine, kcs.at[layer, part, 0], kcr.at[layer, part, 0],
                        (at_core, s),
                    )
                ]
            )
        query_out[layer] = jnp.dot(
            normed_out[layer], w_qkv[:, :D], preferred_element_type=single
        ).astype(bfloat)
        if work:
            work[0]()
        at_diagonal = inward + onward - e
        for part in range(3):
            pltpu.make_async_remote_copy(
                src_ref=kv.at[layer, part, own_rows, :],
                dst_ref=kv.at[layer, part, own_rows, :],
                send_sem=k1s.at[layer, part, core],
                recv_sem=k1r.at[layer, part, core],
                device_id=(inward, s),
                device_id_type=MESH,
            ).wait_recv()
            theirs = kv.at[layer, part, row_block(inward, T), :]
            second.append(
                push(
                    sent, theirs, theirs, k2s.at[layer, part], k2r.at[layer, part], (onward, s)
                )
            )
            third[part].append(
                push(
                    sent, theirs, theirs, kcs.at[layer, part, 1], kcr.at[layer, part, 1],
                    (at_core, s),
                )
            )
        if work:
            work[1]()
        for part in range(3):
            pltpu.make_async_remote_copy(
                src_ref=kv.at[layer, part, own_rows, :],
                dst_ref=kv.at[layer, part, own_rows, :],
                send_sem=k1s.at[layer, part, 1 - core],
                recv_sem=k1r.at[layer, part, 1 - core],
                device_id=(onward, s),
                device_id_type=MESH,
            ).wait_recv()
            theirs = kv.at[layer, part, row_block(onward, T), :]
            third[part].append(
                push(
                    sent, theirs, theirs, kcs.at[layer, part, 2], kcr.at[layer, part, 2],
                    (at_core, s),
                )
            )
            second[part].wait_recv()
            theirs = kv.at[layer, part, row_block(at_diagonal, T), :]
            third[part].append(
                push(
                    sent, theirs, theirs, kcs.at[layer, part, 3], kcr.at[layer, part, 3],
                    (at_core, s),
                )
            )
        for part in range(3):
            for i in range(4):
                third[part][i].wait_recv()

            def one_pair(local_pair):
                pair = 2 * part + local_pair
                lanes = lane_block(pair, 128)
                queries = query_out[layer, :, lanes]
                lane = lax.broadcasted_iota(jnp.int32, (T, 128), 1)
                zero = jnp.zeros_like(queries)
                both = jnp.concatenate(
                    [jnp.where(lane < HD, queries, zero), jnp.where(lane >= HD, queries, zero)]
                )
                keys = kv[layer, part, :, lane_block(local_pair, 128)]
                scores[...] = dot_rows(both, keys) * (1.0 / math.sqrt(HD))
                for half in range(2):
                    head = 2 * pair + half
                    toeplitz = table_ref[pl.ds(layer * H + head, 1), :]
                    peak = jnp.full((1, 1), -jnp.inf, single)
                    for rows in range(0, T, 32):
                        raw = scores[half * T + rows : half * T + rows + 32, :]
                        row = e * T + rows + lax.broadcasted_iota(jnp.int32, raw.shape, 0)
                        causal = row >= lax.broadcasted_iota(jnp.int32, raw.shape, 1)
                        shifted = pltpu.roll(
                            jnp.broadcast_to(toeplitz, (32, TOE)),
                            TOE - (T - 1) + rows,
                            1,
                            stride=1,
                            stride_axis=0,
                        )[:, : raw.shape[1]]
                        peak = jnp.maximum(
                            peak, jnp.max(jnp.where(causal, raw, -jnp.inf), keepdims=True)
                        )
                        masked = jnp.where(causal, raw + shifted, -jnp.inf)
                        top = jnp.max(masked, axis=-1, keepdims=True)
                        exponent = jnp.exp(masked - top)
                        total = jnp.sum(exponent, axis=-1, keepdims=True)
                        probs[layer, pl.ds(pl.multiple_of(head * T + rows, 32), 32), :] = (
                            exponent / total
                        ).astype(bfloat)
                    peak_out[pl.ds(layer * H + head, 1), :] = jnp.broadcast_to(peak, (1, 128))
                values = kv[layer, part, :, pl.ds(pl.multiple_of(256 + local_pair * 128, 128), 128)]
                mixed = jnp.dot(
                    probs[layer, pl.ds(pl.multiple_of(pair * 2 * T, 2 * T), 2 * T), :],
                    values,
                    preferred_element_type=single,
                )
                attended_out[layer, :, lanes] = jnp.where(
                    lane < HD, mixed[:T], mixed[T:]
                ).astype(bfloat)

            loop(2, one_pair)
            if work:
                work[2 + part]()
        kept.append(local(kv.at[layer], kv_out.at[layer], outs_sem.at[6 + layer]))
        kept.append(local(probs.at[layer], probs_out.at[layer], outs_sem.at[8 + layer]))

    def work0():
        slots_plane()

    def work1():
        cot_gathers[0].second()

    def work2():
        core_send(1)
        plane_send(4)

    def work3():
        cot_gathers[0].third()
        plane_send(5)

    def work4():
        plane_forward(4)

    hidden = hidden_ref[...].astype(single)
    attention(0, hidden, w_qkv0, w_out0, [work0, work1, work2, work3, work4])
    ready(1)
    mid_first_out[...] = hidden + jnp.dot(
        attended_out[0], w_out0[...], preferred_element_type=single
    )
    dense_normed_out[...] = norm_rows(mid_first_out[...], gains_ref[pl.ds(2, 1), :]).astype(bfloat)
    reshard.extend([
        push(
            sent,
            expert_up_hbm.at[:, :, lane_block(near[i], 768)],
            up_own.at[:, row_block(s, 192), :],
            us.at[to_k[i]],
            ur.at[to_k[i]],
            (e, near[i]),
        )
        for i in range(3)
    ])
    dense_rows[e] = dense_normed_out[...]
    dense = PlaneGather(plane, lambda who: dense_rows.at[who], dense_s, dense_r)
    dense.first()
    plane_forward(5)
    core_send(4)
    dense.second()
    core_send(5)
    units_ready(2)
    units_ready(3)
    dense.third()
    dense.done()
    kept.append(local(dense_rows, dense_rows_out, outs_sem.at[10]))
    reduce = PlaneSum(plane, sums, sums_core, sums_chips, sum_s, sum_r)

    def units(c, q):
        who = 2 * q + c
        rows = row_block(who, T)
        before = jnp.dot(dense_rows[who], w_up[...], preferred_element_type=single)
        pre_out[rows, :] = before
        act = jax.nn.gelu(before).astype(bfloat)
        act_out[rows, :] = act
        sums[c, q] = jnp.dot(act, w_down[...], preferred_element_type=single).astype(bfloat)

    for q in range(4):
        units(1 - core, q)
    reduce.give()
    for q in range(4):
        units(core, q)
    reduce.pass_on()
    cot_first(1)
    one_out[...] = mid_first_out[...] + reduce.result()

    def work5():
        cot_first(2)
        cot_gathers[1].second()

    def work6():
        cot_first(3)

    def work7():
        cot_gathers[1].third()
        cot_gathers[2].second()

    def work8():
        cot_gathers[2].third()
        cot_gathers[3].second()

    def work9():
        cot_gathers[3].third()

    attention(1, one_out[...], w_qkv1, w_out1, [work5, work6, work7, work8, work9])
    ready(5)
    mid_second_out[...] = one_out[...] + jnp.dot(
        attended_out[1], w_out1[...], preferred_element_type=single
    )
    moe_normed_out[...] = norm_rows(mid_second_out[...], gains_ref[pl.ds(3, 1), :]).astype(bfloat)
    for k in range(7):
        plane.arrived(slots_out.at[:, e], slot_pr.at[k])
    for gather in cot_gathers:
        gather.done()
    for copy in reshard:
        copy.wait_recv()
    for copy in kept:
        copy.wait()
    for copy in sent + plane.sent:
        copy.wait_send()


def forward(
    hidden, attn_gain, mlp_gain, rel_bias, router, buckets, routes, qkv, out, up, down, expert_up,
    cotangent,
):
    length = T * lax.axis_size("expert")
    vmem = pl.BlockSpec(memory_space=VMEM)
    anywhere = pl.BlockSpec(memory_space=ANY)
    shape = jax.ShapeDtypeStruct
    sem = pltpu.SemaphoreType.DMA
    return pl.pallas_call(
        forward_kernel,
        name="forward_layers",
        out_shape=(
            shape((2, T, D), bfloat),
            shape((2, T, D), bfloat),
            shape((2, T, D), bfloat),
            shape((T, D), single),
            shape((T, D), single),
            shape((T, D), bfloat),
            shape((length, 384), single),
            shape((length, 384), bfloat),
            shape((T, D), single),
            shape((2 * H, 128), single),
            shape((T, D), bfloat),
            shape((4, D), single),
            shape((16, D), bfloat),
            shape((4, 8, 8, T), jnp.int32),
            shape((D, 3 * D), bfloat),
            shape((D, 3 * D), bfloat),
            shape((D, D), bfloat),
            shape((D, D), bfloat),
            shape((D, 384), bfloat),
            shape((384, D), bfloat),
            shape((2, 3, length, 512), bfloat),
            shape((2, H * T, length), bfloat),
            shape((EXP_DEV, D, 768), bfloat),
            shape((4, 8, T, D), bfloat),
            shape((8, T, D), bfloat),
        ),
        in_specs=[vmem] * 7 + [anywhere] * 6,
        out_specs=(vmem,) * 14 + (anywhere,) * 11,
        scratch_shapes=[
            VMEM((32, 256), single),
            VMEM((4, 32, 256), single),
            VMEM((2 * H, TOE), single),
            VMEM((8, T), jnp.int32),
            VMEM(up.shape, bfloat),
            VMEM(up.shape, bfloat),
            VMEM((8, T, D), bfloat),
            VMEM((2, 4, T, D), bfloat),
            VMEM((4, T, D), bfloat),
            VMEM((3, T, D), bfloat),
            VMEM((D, 3 * D), bfloat),
            VMEM((D, 3 * D), bfloat),
            VMEM((D, D), bfloat),
            VMEM((D, D), bfloat),
            VMEM((D, 384), bfloat),
            VMEM((384, D), bfloat),
            VMEM((2, 3, length, 512), bfloat),
            VMEM((2, H * T, length), bfloat),
            VMEM((2 * T, length), single),
            sem((6, 3)), sem((6, 3)),
            sem((6, 3, 2)), sem((6, 3, 2)),
            sem((6, 3)), sem((6, 3)),
            sem((6, 3)), sem((6, 3)),
            sem((6,)),
            sem((2, 3, 2)), sem((2, 3, 2)),
            sem((2, 3)), sem((2, 3)),
            sem((2, 3, 4)), sem((2, 3, 4)),
            sem((4,)), sem((3,)),
            sem((4,)), sem((3,)),
            sem((4, 7)), sem((4, 7)),
            sem((12,)),
            sem((3,)), sem((3,)),
            sem((3,)), sem((3,)),
            sem((7,)), sem((7,)),
            sem((7,)), sem((7,)),
            sem((4,)), sem((4,)),
        ],
        compiler_params=pltpu.CompilerParams(
            collective_id=2, has_side_effects=True, vmem_limit_bytes=56 * 2**20
        ),
    )(
        hidden, attn_gain, mlp_gain, rel_bias, router, buckets, routes, qkv, out, up, down,
        expert_up, cotangent,
    )


class SmallReduce:
    def __init__(self, plane, value, z_in, plane_in, op, sems):
        self.plane, self.value, self.z_in, self.plane_in = plane, value, z_in, plane_in
        self.op, self.sems = op, sems

    def start(self):
        p = self.plane
        zs, zr, _, _ = self.sems
        for k in range(3):
            p.push(self.value, self.z_in.at[k], zs.at[k], zr.at[k], (p.e, p.others[k]))

    def middle(self, middle):
        p = self.plane
        zs, zr, ps, pr = self.sems
        total = self.value[...]
        for k in range(3):
            p.arrived(self.z_in.at[k], zr.at[k])
            total = self.op(total, self.z_in[k])
        middle[...] = total
        for k in range(7):
            p.push(middle, self.plane_in.at[k], ps.at[k], pr.at[k], (p.around[k], p.s))

    def finish(self, middle, result):
        p = self.plane
        total = middle[...]
        for k in range(7):
            p.arrived(self.plane_in.at[k], self.sems[3].at[k])
            total = self.op(total, self.plane_in[k])
        result[...] = total


def norm_pull(inputs, gain, upstream):
    inverse = lax.rsqrt(jnp.mean(inputs * inputs, axis=-1, keepdims=True) + epsilon)
    scaled = upstream * gain
    inner = jnp.mean(scaled * inputs, axis=-1, keepdims=True)
    gain_grad = jnp.sum(upstream * inputs * inverse, axis=0, keepdims=True)
    return inverse * scaled - inputs * (inverse * inverse * inverse * inner), gain_grad


def gelu_both(value):
    root = math.sqrt(2.0 / math.pi)
    squared = value * value
    bend = jnp.tanh(root * value * (1.0 + 0.044715 * squared))
    half = 0.5 * (1.0 + bend)
    slope = half + 0.5 * value * (1.0 - bend * bend) * (root * (1.0 + 3 * 0.044715 * squared))
    return value * half, slope


def gelu_slope(value):
    root = math.sqrt(2.0 / math.pi)
    squared = value * value
    bend = jnp.tanh(root * value * (1.0 + 0.044715 * squared))
    return 0.5 * (1.0 + bend) + 0.5 * value * (1.0 - bend * bend) * root * (
        1.0 + 3 * 0.044715 * squared
    )


def backward_kernel(
    mid_grad_ref,
    one_ref,
    hidden_ref,
    mid_ref,
    gains_ref,
    query_ref,
    pre_ref,
    buckets_ref,
    small_ref,
    peak_ref,
    early_hbm,
    normed_hbm,
    attended_hbm,
    dense_rows_hbm,
    act_hbm,
    qkv0_hbm,
    qkv1_hbm,
    proj0_hbm,
    proj1_hbm,
    up_hbm,
    down_hbm,
    kv_hbm,
    probs_hbm,
    up_grad_hbm,
    hidden_grad_out,
    att_out,
    up_out,
    down_out,
    small_out,
    late_out,
    peak_out,
    expert_up_out,
    w_wide,
    w_up,
    w_down,
    sums,
    sums_core,
    sums_chips,
    kv,
    probs,
    xg,
    gx,
    gsrc,
    zb,
    zin,
    zb_down,
    zin_down,
    slopes,
    score_low,
    dk,
    cin,
    rin,
    attended_grad,
    layer_grad,
    biases,
    early,
    early_z,
    early_p,
    early_m,
    late,
    late_z,
    late_p,
    late_m,
    peak_z,
    peak_p,
    peak_m,
    gs,
    gr,
    xs,
    xr,
    zs,
    zr,
    dcs,
    dcr,
    drs,
    drr,
    szs,
    szr,
    sps,
    spr,
    us,
    ur,
    loads,
    sum_s,
    sum_r,
):
    p = Plane()
    e, s, core = p.e, p.s, p.core
    own_rows = row_block(e, T)

    def load(source, target, i):
        copy = pltpu.make_async_copy(source, target, loads.at[i])
        copy.start()
        return copy

    own_parts = [
        load(source, xg.at[n, own_rows, :], 11 + n)
        for n, source in ((2, normed_hbm.at[0]), (3, attended_hbm.at[0]))
    ]
    got_early = load(early_hbm, xg.at[0:2], 12)
    got_act = load(act_hbm, gx.at[3], 16)
    got_dense = load(dense_rows_hbm, xg.at[4], 9)
    greet([(d, s) for d in p.around] + [(e, other) for other in p.others])

    w_qkv = w_wide.at[:, : 3 * D]
    w_out = w_wide.at[:, 3 * D :]
    got_out = load(proj1_hbm, w_out, 0)
    got_kv = load(kv_hbm.at[1], kv, 2)
    got_probs = load(probs_hbm.at[1], probs, 3)
    got_qkv = load(qkv1_hbm, w_qkv, 1)
    got_down = load(down_hbm, w_down, 5)
    got_up = load(up_hbm, w_up, 4)

    peaks = SmallReduce(
        p, peak_ref, peak_z, peak_p, jnp.maximum, (szs.at[0], szr.at[0], sps.at[0], spr.at[0])
    )
    peaks.start()

    def rows_gather(n):
        return PlaneGather(
            p, lambda who: xg.at[n, row_block(who, T), :], gs.at[n], gr.at[n]
        )

    gathers = {n: rows_gather(n) for n in range(2, 6)}
    def exchange_start(j, source):
        gx[j, own_rows, :] = source[:, lane_block(e, 384)]
        for k, d in enumerate(p.around):
            p.push(
                source.at[:, lane_block(d, 384)],
                gx.at[j, own_rows, :],
                xs.at[j, k],
                xr.at[j, k],
                (d, s),
            )

    def exchange_wait(j):
        for k in range(7):
            p.arrived(gx.at[j, own_rows, :], xr.at[j, k])

    def out_gather(j, target, height):
        return PlaneGather(
            p, lambda who: target.at[pl.ds(who, 1)], gs.at[6 + j], gr.at[6 + j]
        )

    def z_start(j, tile, received, height):
        for i, k in enumerate(p.to_k):
            p.push(
                tile.at[row_block(p.near[i], height), :],
                received.at[k],
                zs.at[j, k],
                zr.at[j, k],
                (e, p.near[i]),
            )

    def z_finish(j, tile, received, height, target):
        total = tile[row_block(s, height), :].astype(single)
        for k in range(3):
            p.arrived(received.at[k], zr.at[j, k])
            total = total + received[k].astype(single)
        target[pl.ds(e, 1)] = total.astype(bfloat)[None]

    def tile_attention(layer):
        j = 1 - layer
        exchange_wait(j)
        rows = xg[2 * j + e // 6]
        for part in range(3):
            lanes = slice(128 * part, 128 * (part + 1))
            zb[j, :, lanes] = dot_columns(rows, gx[j, :, lanes]).astype(bfloat)
        z_start(j, zb.at[j], zin.at[j], 192)

    def tile_up():
        for part in range(3):
            lanes = slice(128 * part, 128 * (part + 1))
            zb[2, :, lanes] = dot_columns(xg[4], gx[2, :, lanes]).astype(bfloat)
        z_start(2, zb.at[2], zin.at[2], 192)

    def tile_down():
        for part in range(3):
            lanes = slice(128 * part, 128 * (part + 1))
            zb_down[lanes, :] = dot_columns(gx[3, :, lanes], xg[5]).astype(bfloat)
        z_start(3, zb_down, zin_down, 96)

    gather_att1 = out_gather(0, att_out.at[1], 192)
    gather_att0 = out_gather(1, att_out.at[0], 192)
    gather_up = out_gather(2, up_out, 192)
    gather_down = out_gather(3, down_out, 96)

    scale = 1.0 / math.sqrt(HD)

    def attention(layer, upstream, work):
        j = 1 - layer
        grads = gsrc.at[j]
        branch = upstream.astype(bfloat)
        grads[:, 3 * D :] = branch
        got_out_now = got_out if layer == 1 else reloads["out"]
        got_out_now.wait()
        attended_grad[...] = dot_rows(branch, w_out[...]).astype(bfloat)
        if layer == 1:
            got_kv.wait()
            got_probs.wait()
        else:
            reloads["kv"].wait()
            reloads["probs"].wait()
            for copy in dk_sent:
                copy.wait_send()
            dk_sent.clear()

        def first_step(part):
            push(
                dk_sent,
                dk.at[part, 1 - core],
                cin.at[layer, part],
                dcs.at[layer, part],
                dcr.at[layer, part],
                (p.at_core, s),
            )

        def second_step(part):
            p.arrived(cin.at[layer, part], dcr.at[layer, part])
            for q in range(4):
                dk[part, core, q] = (
                    dk[part, core, q].astype(single) + cin[layer, part, q].astype(single)
                ).astype(bfloat)
            for k, d in enumerate((p.at_x, p.at_y, p.diagonal)):
                push(
                    dk_sent,
                    dk.at[part, core, d // 2],
                    rin.at[layer, part, k],
                    drs.at[layer, part, k],
                    drr.at[layer, part, k],
                    (d, s),
                )

        def third_step(part):
            total = dk[part, core, p.quarter].astype(single)
            for k in range(3):
                p.arrived(rin.at[layer, part, k], drr.at[layer, part, k])
                total = total + rin[layer, part, k].astype(single)
            turned = total.T.astype(bfloat)
            grads[:, D + 256 * part : D + 256 * (part + 1)] = turned[:, :256]
            grads[:, 2 * D + 256 * part : 2 * D + 256 * (part + 1)] = turned[:, 256:]

        if layer == 1:
            for copy in own_parts:
                copy.wait()
            gathers[2].first()
            gathers[3].first()

        for part in range(3):

            def one_pair(local_pair):
                pair = 2 * part + local_pair
                lanes = lane_block(pair, 128)
                lane = lax.broadcasted_iota(jnp.int32, (T, 128), 1)

                def split(value):
                    zero = jnp.zeros_like(value)
                    return jnp.concatenate(
                        [jnp.where(lane < HD, value, zero), jnp.where(lane >= HD, value, zero)]
                    )

                queries = split(query_ref[layer, :, lanes])
                outputs = split(attended_grad[:, lanes])
                keys = kv[part, :, lane_block(local_pair, 128)]
                values = kv[part, :, pl.ds(pl.multiple_of(256 + local_pair * 128, 128), 128)]
                slopes[...] = dot_rows(outputs, values)
                pair_rows = pl.ds(pl.multiple_of(pair * 2 * T, 2 * T), 2 * T)
                for half in range(2):
                    head = 2 * pair + half
                    gathered = jnp.zeros((8, TOE), single)
                    for rows in range(0, T, 32):
                        at = half * T + rows
                        prob = probs[
                            pl.ds(pl.multiple_of(head * T + rows, 32), 32), :
                        ].astype(single)
                        slope = slopes[at : at + 32, :]
                        inner = jnp.sum(prob * slope, axis=-1, keepdims=True)
                        low = (prob * (slope - inner)).astype(bfloat)
                        score_low[at : at + 32, :] = low
                        fold = jnp.concatenate(
                            [low.astype(single), jnp.zeros((32, TOE - low.shape[1]), single)],
                            axis=1,
                        )
                        fold = pltpu.roll(fold[:16], 16, 1) + fold[16:]
                        fold = pltpu.roll(fold[:8], 8, 1) + fold[8:]
                        if rows < T - 32:
                            fold = pltpu.roll(fold, T - 32 - rows, 1)
                        gathered = gathered + fold
                    fold = pltpu.roll(gathered[:4], 4, 1) + gathered[4:]
                    fold = pltpu.roll(fold[:2], 2, 1) + fold[2:]
                    fold = pltpu.roll(fold[:1], 1, 1) + fold[1:]
                    biases[pl.ds(layer * H + head, 1), :] = fold
                mixed = jnp.dot(score_low[...], keys, preferred_element_type=single) * scale
                grads[:, lanes] = jnp.where(lane < HD, mixed[:T], mixed[T:]).astype(bfloat)
                key_grad = dot_columns(queries, score_low[...]) * scale
                value_grad = dot_columns(outputs, probs[pair_rows, :])
                for d in range(8):
                    columns = slice(128 * d, 128 * (d + 1))
                    dk[
                        part, d % 2, d // 2, pl.ds(pl.multiple_of(local_pair * 128, 128), 128), :
                    ] = key_grad[:, columns].astype(bfloat)
                    dk[
                        part,
                        d % 2,
                        d // 2,
                        pl.ds(pl.multiple_of(256 + local_pair * 128, 128), 128),
                        :,
                    ] = value_grad[:, columns].astype(bfloat)

            loop(2, one_pair)
            first_step(part)
            if part > 0:
                second_step(part - 1)
            work[part]()
        second_step(2)
        third_step(0)
        work[3]()
        third_step(1)
        third_step(2)
        if layer == 0:
            exchange_start(j, gsrc.at[j])
        if layer == 1:
            got_qkv.wait()
        else:
            reloads["qkv"].wait()
        return dot_rows(gsrc[j, :, : 3 * D], w_qkv[...])

    dk_sent = []
    reloads = {}

    def part0():
        for i, k in enumerate(p.to_k):
            reshard.append(
                p.push(
                    up_grad_hbm.at[:, row_block(p.near[i], 192), :],
                    expert_up_out.at[:, :, lane_block(s, 768)],
                    us.at[k],
                    ur.at[k],
                    (e, p.near[i]),
                )
            )
        reshard_own.append(
            load(
                up_grad_hbm.at[:, row_block(s, 192), :],
                expert_up_out.at[:, :, lane_block(s, 768)],
                6,
            )
        )

    def part1():
        gathers[2].second()
        gathers[3].second()
        peaks.middle(peak_m)

    def part2():
        pass

    def part3():
        gathers[2].third()
        gathers[3].third()
        peaks.finish(peak_m, peak_out)

    reshard, reshard_own = [], []
    mid_grad = mid_grad_ref[...]
    normed_grad = attention(1, mid_grad, [part0, part1, part2, part3])
    reloads["kv"] = load(kv_hbm.at[0], kv, 7)
    reloads["probs"] = load(probs_hbm.at[0], probs, 8)
    reloads["out"] = load(proj0_hbm, w_out, 17)
    reloads["qkv"] = load(qkv0_hbm, w_qkv, 10)
    input_grad, gain_grad = norm_pull(one_ref[...], gains_ref[1:2, :], normed_grad)
    early[...] = small_ref[...]
    early[17:18, :] = gain_grad
    layer_grad[...] = mid_grad + input_grad
    branch = layer_grad[...].astype(bfloat)
    xg[5, own_rows, :] = branch
    gathers[5].first()
    got_down.wait()
    got_up.wait()
    gathers[5].second()
    gathers[5].third()
    gathers[5].done()
    reduce = PlaneSum(p, sums, sums_core, sums_chips, sum_s, sum_r)

    def units(c, q):
        rows = row_block(2 * q + c, T)
        act_grad = dot_rows(xg[5, rows, :], w_down[...])
        pre_grad = (act_grad * gelu_slope(pre_ref[rows, :])).astype(bfloat)
        gx[2, rows, :] = pre_grad
        sums[c, q] = dot_rows(pre_grad, w_up[...]).astype(bfloat)

    for q in range(4):
        units(1 - core, q)
    reduce.give()
    for q in range(4):
        units(core, q)
    reduce.pass_on()
    input_grad, gain_grad = norm_pull(mid_ref[...], gains_ref[2:3, :], reduce.result())
    early[18:19, :] = gain_grad
    layer_grad[...] = layer_grad[...] + input_grad
    small = SmallReduce(
        p, early, early_z, early_p, jnp.add, (szs.at[1], szr.at[1], sps.at[1], spr.at[1])
    )
    small.start()
    got_early.wait()
    got_dense.wait()
    got_act.wait()

    def part4():
        exchange_start(0, gsrc.at[0])

    def part5():
        small.middle(early_m)

    def part6():
        tile_up()

    def part7():
        tile_down()
        tile_attention(1)

    normed_grad = attention(0, layer_grad[...], [part4, part5, part6, part7])
    input_grad, gain_grad = norm_pull(
        hidden_ref[...].astype(single), gains_ref[0:1, :], normed_grad
    )
    hidden_grad_out[...] = layer_grad[...] + input_grad
    late[...] = jnp.zeros_like(late)
    for i in range(6):
        late[i : i + 1, :] = gain_grad[:, 128 * i : 128 * (i + 1)]
    late[8:32, :NB] = lax.dot_general(
        biases[...],
        jnp.where(lax.broadcasted_iota(jnp.int32, (NB, TOE), 0) == buckets_ref[...], 1.0, 0.0),
        (((1,), (1,)), ((), ())),
        precision=lax.Precision.HIGHEST,
        preferred_element_type=single,
    )
    tail = SmallReduce(
        p, late, late_z, late_p, jnp.add, (szs.at[2], szr.at[2], sps.at[2], spr.at[2])
    )
    tail.start()
    z_finish(2, zb.at[2], zin.at[2], 192, up_out)
    gather_up.first()
    z_finish(3, zb_down, zin_down, 96, down_out)
    gather_down.first()
    z_finish(0, zb.at[0], zin.at[0], 192, att_out.at[1])
    gather_att1.first()
    gathers[2].done()
    gathers[3].done()
    tile_attention(0)
    tail.middle(late_m)
    small.finish(early_m, small_out)
    gather_att1.second()
    gather_up.second()
    gather_down.second()
    gather_att1.third()
    gather_up.third()
    gather_down.third()
    z_finish(1, zb.at[1], zin.at[1], 192, att_out.at[0])
    gather_att0.first()
    gather_att1.done()
    gather_up.done()
    gather_down.done()
    gather_att0.second()
    gather_att0.third()
    tail.finish(late_m, late_out)
    for copy in reshard:
        copy.wait_recv()
    reshard_own[0].wait()
    gather_att0.done()
    for copy in p.sent + dk_sent:
        copy.wait_send()


def backward(
    mid_grad, layer_one, hidden, mid, gains, normed, queries, attended, dense_rows, act, pre_act,
    buckets, small, peak_rows, early_rows, weights, kv, probs, up_grad,
):
    length = T * lax.axis_size("expert")
    vmem = pl.BlockSpec(memory_space=VMEM)
    anywhere = pl.BlockSpec(memory_space=ANY)
    shape = jax.ShapeDtypeStruct
    ff = up_grad.shape[2] * 4
    sem = pltpu.SemaphoreType.DMA
    peak_shape, early_shape, late_shape = (2 * H, 128), small.shape, (32, 128)
    return pl.pallas_call(
        backward_kernel,
        name="backward_layers",
        out_shape=(
            shape((T, D), single),
            shape((2, 8, 192, 384), bfloat),
            shape((8, 192, 384), bfloat),
            shape((8, 96, D), bfloat),
            shape(early_shape, single),
            shape(late_shape, single),
            shape(peak_shape, single),
            shape((EXP_DEV, 192, ff), bfloat),
        ),
        in_specs=[vmem] * 10 + [anywhere] * 14,
        out_specs=(vmem,) * 7 + (anywhere,),
        scratch_shapes=[
            VMEM((D, 4 * D), bfloat),
            VMEM((D, 384), bfloat),
            VMEM((384, D), bfloat),
            VMEM((2, 4, T, D), bfloat),
            VMEM((4, T, D), bfloat),
            VMEM((3, T, D), bfloat),
            VMEM((3, length, 512), bfloat),
            VMEM((H * T, length), bfloat),
            VMEM((6, length, D), bfloat),
            VMEM((4, length, 384), bfloat),
            VMEM((2, T, 4 * D), bfloat),
            VMEM((3, D, 384), bfloat),
            VMEM((3, 3, 192, 384), bfloat),
            VMEM((384, D), bfloat),
            VMEM((3, 96, D), bfloat),
            VMEM((2 * T, length), single),
            VMEM((2 * T, length), bfloat),
            VMEM((3, 2, 4, 512, 128), bfloat),
            VMEM((2, 3, 4, 512, 128), bfloat),
            VMEM((2, 3, 3, 512, 128), bfloat),
            VMEM((T, D), bfloat),
            VMEM((T, D), single),
            VMEM((2 * H, TOE), single),
            VMEM(early_shape, single),
            VMEM((3,) + early_shape, single),
            VMEM((7,) + early_shape, single),
            VMEM(early_shape, single),
            VMEM(late_shape, single),
            VMEM((3,) + late_shape, single),
            VMEM((7,) + late_shape, single),
            VMEM(late_shape, single),
            VMEM((3,) + peak_shape, single),
            VMEM((7,) + peak_shape, single),
            VMEM(peak_shape, single),
            sem((10, 7)), sem((10, 7)),
            sem((4, 7)), sem((4, 7)),
            sem((4, 3)), sem((4, 3)),
            sem((2, 3)), sem((2, 3)),
            sem((2, 3, 3)), sem((2, 3, 3)),
            sem((3, 3)), sem((3, 3)),
            sem((3, 7)), sem((3, 7)),
            sem((3,)), sem((3,)),
            sem((18,)),
            sem((4,)), sem((4,)),
        ],
        compiler_params=pltpu.CompilerParams(
            collective_id=3, has_side_effects=True, vmem_limit_bytes=60 * 2**20
        ),
    )(
        mid_grad, layer_one, hidden, mid, gains, queries, pre_act, buckets, small, peak_rows,
        early_rows.reshape(2, length, D), normed, attended, dense_rows.reshape(length, D), act, *weights, kv, probs, up_grad,
    )


def experts_kernel(
    normed_ref,
    mid_ref,
    gains_ref,
    router_turned_ref,
    slots_ref,
    own_cot_ref,
    cot_hbm,
    up_hbm,
    down_hbm,
    normed_hbm,
    attended_hbm,
    hidden_out,
    mid_grad_out,
    small_out,
    up_grad_out,
    down_grad_out,
    early_rows,
    normed_all,
    cots,
    w_up,
    w_down,
    rows,
    gated,
    gates,
    acts,
    pre_grads,
    raw,
    row_send,
    out_send,
    row_back,
    out_back,
    out_ahead_in,
    slot_grads,
    slot_z,
    slot_sum,
    slot_plane,
    row_part,
    out_part,
    row_z,
    out_z,
    ns,
    nr,
    gs,
    gr,
    rs,
    rr,
    os,
    orr,
    ss,
    sr,
    ps,
    pr,
    rzs,
    rzr,
    ozs,
    ozr,
    loads,
    early_s,
    early_r,
    oas,
    oar,
):
    p = Plane()
    e, s = p.e, p.s
    groups = [s] + [lax.rem(s + 4 - k, 4) for k in range(1, 4)]

    def load(source, target, i):
        copy = pltpu.make_async_copy(source, target, loads.at[i])
        copy.start()
        return copy

    got_cots = [load(cot_hbm.at[groups[k]], cots.at[k], k) for k in range(2)]
    got_up = load(up_hbm, w_up, 4)
    got_down = load(down_hbm, w_down, 5)
    own_early = [
        load(source.at[1], early_rows.at[i, e], 6 + i)
        for i, source in enumerate((normed_hbm, attended_hbm))
    ]
    normed_all[s, e] = normed_ref[...]
    greet([(d, s) for d in p.around] + [(e, other) for other in p.others])
    mine = normed_all.at[s, e]
    for i, k in enumerate(p.to_k):
        p.push(mine, mine, ns.at[k], nr.at[k], (e, p.near[i]))

    def gather(k):
        g = groups[k]
        return PlaneGather(p, lambda who: normed_all.at[g, who], gs.at[k], gr.at[k])

    gathers = [gather(k) for k in range(4)]
    gathers[0].first()
    early = [
        PlaneGather(
            p, functools.partial(lambda i, who: early_rows.at[i, who], i), early_s.at[i], early_r.at[i]
        )
        for i in range(2)
    ]
    for i in range(2):
        own_early[i].wait()
        early[i].first()

    ids = 2 * e * CAP + lax.broadcasted_iota(jnp.int32, (2 * CAP, T), 0)
    expert_low = CAP * lax.broadcasted_iota(jnp.int32, (16, T), 0)

    def route_masks(g, who):
        both = slots_ref[g, who]
        first, second = both[:1], both[1:2]
        return first, second, ids == first, ids == second

    def select_cots(k):
        g = groups[k]
        got_cots[k].wait()

        def one(who):
            _, _, mark0, mark1 = route_masks(g, who)
            mark = jnp.where(mark0 | mark1, 1.0, 0.0).astype(bfloat)
            picked = jnp.dot(mark, cots[k % 2, who], preferred_element_type=single).astype(bfloat)
            for j in range(2):
                raw[j, g, row_block(who, CAP), :] = picked[j * CAP : (j + 1) * CAP]

        for who in range(8):
            one(who)
        if k < 2:
            got_cots.append(load(cot_hbm.at[groups[k + 2]], cots.at[k], k + 2))

    def select_rows(k):
        g = groups[k]

        def one(who):
            slot0, slot1, mark0, mark1 = route_masks(g, who)
            block = normed_all[g, who]
            mark = jnp.where(mark0 | mark1, 1.0, 0.0).astype(bfloat)
            picked = jnp.dot(mark, block, preferred_element_type=single).astype(bfloat)
            logits = dot_rows(router_turned_ref[...], block)
            chosen = [
                jnp.sum(
                    jnp.where((slot >= expert_low) & (slot < expert_low + CAP), logits, 0.0),
                    axis=0,
                    keepdims=True,
                )
                for slot in (slot0, slot1)
            ]
            top = jnp.maximum(chosen[0], chosen[1])
            weight = [jnp.exp(value - top) for value in chosen]
            total = weight[0] + weight[1]
            gate = jnp.sum(
                jnp.where(mark0, weight[0] / total, 0.0) + jnp.where(mark1, weight[1] / total, 0.0),
                axis=1,
                keepdims=True,
            )
            for j in range(2):
                part = slice(j * CAP, (j + 1) * CAP)
                rows[j, g, row_block(who, CAP), :] = picked[part]
                gates[j, g, row_block(who, CAP), :] = jnp.broadcast_to(gate[part], (CAP, 128))

        for who in range(8):
            one(who)

    def compute(k):
        g = groups[k]

        def one(j):
            before = jnp.dot(rows[j, g], w_up[j], preferred_element_type=single)
            act, slope = gelu_both(before)
            act = act.astype(bfloat)
            acts[j, g] = act
            gate = gates[j, g][:, :1]
            cot = raw[j, g].astype(single)
            weighted = (gate * cot).astype(bfloat)
            gated[j, g] = weighted
            act_grad = dot_rows(weighted, w_down[j])
            pre_grad = (act_grad * slope).astype(bfloat)
            pre_grads[j, g] = pre_grad
            row_grad = dot_rows(pre_grad, w_up[j])
            row_send[g, j] = row_grad.astype(bfloat).reshape(8, CAP, D)
            out = jnp.dot(act, w_down[j], preferred_element_type=single)
            out_send[g, j] = (gate * out).astype(bfloat).reshape(8, CAP, D)
            product = out * cot
            folded = product[:, :128]
            for i in range(1, D // 128):
                folded = folded + product[:, 128 * i : 128 * (i + 1)]
            slot_grads[g, j : j + 1, :] = jnp.sum(folded.T, axis=0, keepdims=True)

        for j in range(2):
            one(j)

    def give_back(k, source, target, send_sems, recv_sems):
        g = groups[k]
        slot = k if source is row_send else k // 2
        target[slot, e] = source[g, :, e]
        for i, d in enumerate(p.around):
            p.push(
                source.at[g, :, d], target.at[slot, e], send_sems.at[k, i], recv_sems.at[k, i],
                (d, s),
            )

    def out_ahead(k):
        g = groups[k]
        i = k // 2
        p.push(out_send.at[g], out_ahead_in.at[i], oas.at[i], oar.at[i], (e, g))

    def step(k):
        select_rows(k)
        compute(k)

    def arrive(k):
        p.arrived(mine, nr.at[k - 1])
        gathers[k].first()

    slot_grads[...] = jnp.zeros_like(slot_grads)
    select_cots(0)
    gathers[0].second()
    arrive(1)
    gathers[0].third()
    arrive(2)
    early[0].second()
    early[1].second()
    arrive(3)
    gathers[0].done()
    gathers[1].second()
    got_up.wait()
    got_down.wait()
    step(0)
    gathers[1].third()
    gathers[2].second()
    gathers[3].second()
    early[0].third()
    early[1].third()
    select_cots(1)
    gathers[1].done()
    step(1)
    give_back(1, row_send, row_back, rs, rr)
    out_ahead(1)
    gathers[2].third()
    gathers[3].third()
    select_cots(2)
    gathers[2].done()
    step(2)
    give_back(2, row_send, row_back, rs, rr)
    select_cots(3)
    gathers[3].done()
    step(3)
    give_back(3, row_send, row_back, rs, rr)
    give_back(2, out_send, out_back, os, orr)
    give_back(0, row_send, row_back, rs, rr)
    for k in range(3):
        p.push(
            slot_grads.at[p.others[k]], slot_z.at[k], ss.at[k], sr.at[k], (e, p.others[k])
        )

    out_ahead(3)

    def weight_grads(i):
        j = i // 3
        lanes = lane_block(lax.rem(i, 3), 256)
        inputs = rows[j].reshape(4 * 8 * CAP, D)
        up_grad_out[j, :, lanes] = dot_columns(
            inputs, pre_grads[j, :, :, lanes].reshape(4 * 8 * CAP, 256)
        ).astype(bfloat)
        inputs = acts[j].reshape(4 * 8 * CAP, -1)
        down_grad_out[j, :, lanes] = dot_columns(
            inputs, gated[j, :, :, lanes].reshape(4 * 8 * CAP, 256)
        ).astype(bfloat)

    loop(3, weight_grads)
    total = slot_grads[s]
    for k in range(3):
        p.arrived(slot_z.at[k], sr.at[k])
        total = total + slot_z[k]
    slot_sum[...] = total
    slot_plane[e] = total
    for i, d in enumerate(p.around):
        p.push(slot_sum, slot_plane.at[e], ps.at[i], pr.at[i], (d, s))

    slot_lanes = lax.broadcasted_iota(jnp.int32, (T, 16 * CAP), 1)

    def slot_columns(g):
        return slots_ref[g, e].astype(single).T.astype(jnp.int32)

    def collect(k, back, recv_sems, part, z_in, z_send, z_recv):
        g = groups[k]
        slot = k if back is row_back else k // 2
        for i in range(7):
            p.arrived(back.at[slot, e], recv_sems.at[k, i])
        columns = slot_columns(g)
        marks = jnp.where(
            (columns[:, :1] == slot_lanes) | (columns[:, 1:2] == slot_lanes), 1.0, 0.0
        ).astype(bfloat)
        combined = jnp.dot(
            marks, back[slot].reshape(16 * CAP, D), preferred_element_type=single
        )
        part[slot] = combined.astype(bfloat)
        if k:
            i = k - 1 if back is row_back else 0
            p.push(part.at[slot], z_in.at[i], z_send.at[i], z_recv.at[i], (e, g))

    for k in (1, 2, 3):
        collect(k, row_back, rr, row_part, row_z, rzs, rzr)

    for i in range(2):
        p.arrived(out_ahead_in.at[i], oar.at[i])
    for j in range(2):
        out_send[s, j] = (
            out_send[s, j].astype(single)
            + out_ahead_in[0, j].astype(single)
            + out_ahead_in[1, j].astype(single)
        ).astype(bfloat)
    give_back(0, out_send, out_back, os, orr)

    def weight_later(i):
        weight_grads(i + 3)

    loop(3, weight_later)

    for i in range(7):
        p.arrived(slot_sum, pr.at[i])
    turned = pltpu.roll(
        slot_plane[...].reshape(64, 8 * CAP), lax.rem(8 * CAP - CAP * e, 8 * CAP), 1
    )
    logits = dot_rows(normed_ref[...], router_turned_ref[...])
    columns = slot_columns(s)
    expert_lanes = CAP * lax.broadcasted_iota(jnp.int32, (T, 16), 1)
    picks, chosen, grads = [], [], []
    small_lanes = lax.broadcasted_iota(jnp.int32, (T, CAP), 1)
    for r in range(2):
        slot = columns[:, r : r + 1]
        picks.append((slot >= expert_lanes) & (slot < expert_lanes + CAP))
        chosen.append(jnp.sum(jnp.where(picks[r], logits, 0.0), axis=1, keepdims=True))
        found = jnp.zeros((T, CAP), single)
        for who in range(8):
            for j in range(2):
                values = turned[8 * who + j : 8 * who + j + 1, :CAP]
                found = found + jnp.where(slot - (2 * who + j) * CAP == small_lanes, values, 0.0)
        grads.append(jnp.sum(found, axis=1, keepdims=True))
    top = jnp.maximum(chosen[0], chosen[1])
    weight = [jnp.exp(value - top) for value in chosen]
    total = weight[0] + weight[1]
    weight = [value / total for value in weight]
    mean = weight[0] * grads[0] + weight[1] * grads[1]
    logit_grad = jnp.zeros((T, 16), single)
    for r in range(2):
        logit_grad = logit_grad + jnp.where(picks[r], weight[r] * (grads[r] - mean), 0.0)
    logit_grad = logit_grad.astype(bfloat)
    small_out[...] = jnp.zeros_like(small_out)
    small_out[:16, :] = dot_columns(logit_grad, normed_ref[...])
    normed_grad = jnp.dot(logit_grad, router_turned_ref[...], preferred_element_type=single)
    collect(2, out_back, orr, out_part, out_z, ozs, ozr)
    collect(0, row_back, rr, row_part, row_z, rzs, rzr)
    normed_grad = normed_grad + row_part[0].astype(single)
    for k in range(3):
        p.arrived(row_z.at[k], rzr.at[k])
        normed_grad = normed_grad + row_z[k].astype(single)
    input_grad, gain_grad = norm_pull(mid_ref[...], gains_ref[3:4, :], normed_grad)
    small_out[16:17, :] = gain_grad
    mid_grad_out[...] = own_cot_ref[...].astype(single) + input_grad

    collect(0, out_back, orr, out_part, out_z, ozs, ozr)
    p.arrived(out_z.at[0], ozr.at[0])
    result = mid_ref[...] + out_part[0].astype(single) + out_z[0].astype(single)
    hidden_out[...] = result.astype(bfloat)
    for gather in early:
        gather.done()
    for copy in p.sent:
        copy.wait_send()


def run_experts(
    moe_normed, mid, gains, router, slots, own_cot, cots, up_own, expert_down, normed, attended
):
    vmem = pl.BlockSpec(memory_space=VMEM)
    anywhere = pl.BlockSpec(memory_space=ANY)
    shape = jax.ShapeDtypeStruct
    width = expert_down.shape[1]
    sem = pltpu.SemaphoreType.DMA
    per_expert = (EXP_DEV, 4, 8 * CAP)
    sends = (4, EXP_DEV, 8, CAP, D)
    backs = (4, 8, EXP_DEV, CAP, D)
    return pl.pallas_call(
        experts_kernel,
        name="experts",
        out_shape=(
            shape((T, D), bfloat),
            shape((T, D), single),
            shape((24, D), single),
            shape((EXP_DEV, D, width), bfloat),
            shape((EXP_DEV, width, D), bfloat),
            shape((2, 8, T, D), bfloat),
        ),
        in_specs=[vmem] * 6 + [anywhere] * 5,
        out_specs=(vmem,) * 5 + (anywhere,),
        scratch_shapes=[
            VMEM((4, 8, T, D), bfloat),
            VMEM((2, 8, T, D), bfloat),
            VMEM((EXP_DEV, D, width), bfloat),
            VMEM((EXP_DEV, width, D), bfloat),
            VMEM(per_expert + (D,), bfloat),
            VMEM(per_expert + (D,), bfloat),
            VMEM(per_expert + (128,), single),
            VMEM(per_expert + (width,), bfloat),
            VMEM(per_expert + (width,), bfloat),
            VMEM(per_expert + (D,), bfloat),
            VMEM(sends, bfloat),
            VMEM(sends, bfloat),
            VMEM(backs, bfloat),
            VMEM((2,) + backs[1:], bfloat),
            VMEM((2,) + sends[1:], bfloat),
            VMEM((4, 8, 8 * CAP), single),
            VMEM((3, 8, 8 * CAP), single),
            VMEM((8, 8 * CAP), single),
            VMEM((8, 8, 8 * CAP), single),
            VMEM((4, T, D), bfloat),
            VMEM((2, T, D), bfloat),
            VMEM((3, T, D), bfloat),
            VMEM((1, T, D), bfloat),
            sem((3,)), sem((3,)),
            sem((4, 7)), sem((4, 7)),
            sem((4, 7)), sem((4, 7)),
            sem((4, 7)), sem((4, 7)),
            sem((3,)), sem((3,)),
            sem((7,)), sem((7,)),
            sem((3,)), sem((3,)),
            sem((3,)), sem((3,)),
            sem((8,)),
            sem((2, 7)), sem((2, 7)),
            sem((2,)), sem((2,)),
        ],
        compiler_params=pltpu.CompilerParams(
            collective_id=4, has_side_effects=True, vmem_limit_bytes=60 * 2**20
        ),
    )(
        moe_normed, mid, gains, router, slots, own_cot, cots, up_own, expert_down, normed, attended
    )


def finish_kernel(
    att_hbm,
    up_hbm,
    down_hbm,
    expert_up_hbm,
    expert_down_hbm,
    small_hbm,
    late_hbm,
    peak_hbm,
    grad_hbm,
    result_hbm,
    qkv_out,
    out_out,
    up_out,
    down_out,
    expert_up_out,
    expert_down_out,
    attn_gain_out,
    mlp_gain_out,
    bias_out,
    router_out,
    clip_out,
    grad_out,
    result_out,
    att,
    up,
    down,
    expert_up,
    expert_down,
    small_ref,
    late_ref,
    peak_ref,
    grad,
    qkv_wide,
    out_wide,
    up_wide,
    down_wide,
    expert_up_wide,
    expert_down_wide,
    turned,
    in_sems,
    out_sems,
):
    s = lax.axis_index("shard")

    def start(source, target, sem):
        copy = pltpu.make_async_copy(source, target, sem)
        copy.start()
        return copy

    got = [
        start(source, target, in_sems.at[i])
        for i, (source, target) in enumerate(
            (
                (expert_down_hbm, expert_down),
                (expert_up_hbm, expert_up),
                (att_hbm, att),
                (up_hbm, up),
                (down_hbm, down),
                (grad_hbm, grad),
                (small_hbm, small_ref),
                (late_hbm, late_ref),
                (peak_hbm, peak_ref),
                (result_hbm, result_out),
            )
        )
    ]
    put = []

    def widen(i):
        rows = row_block(i, 128)
        for j in range(EXP_DEV):
            expert_down_wide[j, rows, :] = expert_down[j, rows, :].astype(single)

    def widen_up(i):
        lanes = lane_block(i, 384)
        for j in range(EXP_DEV):
            expert_up_wide[j, :, lanes] = expert_up[j, :, lanes].astype(single)

    def widen_down(i):
        down_wide[row_block(i, 96), :] = down[i].astype(single)

    got[0].wait()
    loop(expert_down.shape[1] // 128, widen)
    put.append(start(expert_down_wide, expert_down_out, out_sems.at[0]))
    got[1].wait()
    loop(expert_up.shape[2] // 384, widen_up)
    put.append(start(expert_up_wide, expert_up_out, out_sems.at[1]))
    got[2].wait()
    for layer in range(2):
        for b in range(6):
            qkv_wide[layer, :, 384 * b : 384 * (b + 1)] = att[layer, b].astype(single)
        for b in range(2):
            out_wide[layer, :, 384 * b : 384 * (b + 1)] = att[layer, 6 + b].astype(single)
    put.append(start(qkv_wide, qkv_out, out_sems.at[2]))
    put.append(start(out_wide, out_out, out_sems.at[3]))
    got[3].wait()
    for b in range(8):
        for z in range(4):
            up_wide[:, 768 * z + 96 * b : 768 * z + 96 * (b + 1)] = up[
                b, :, 96 * z : 96 * (z + 1)
            ].astype(single)
    put.append(start(up_wide, up_out, out_sems.at[4]))
    got[4].wait()
    loop(8, widen_down)
    put.append(start(down_wide, down_out, out_sems.at[5]))

    for copy in got[5:]:
        copy.wait()
    grad_out[...] = grad[...][:, None, :]
    part = D // 4
    back = lax.rem(D - part * s, D)
    first_gain = jnp.concatenate([late_ref[i : i + 1, :] for i in range(6)], axis=1)
    gains = jnp.concatenate([first_gain, small_ref[16:19, :], jnp.zeros((4, D), single)])
    gains = pltpu.roll(gains, back, 1)[:, :part]
    attn_gain_out[0:1, :] = gains[0:1]
    attn_gain_out[1:2, :] = gains[2:3]
    mlp_gain_out[0:1, :] = gains[3:4]
    mlp_gain_out[1:2, :] = gains[1:2]
    turned[:, :16] = small_ref[:16, :].T
    router_out[...] = turned[row_block(s, part), :16].T
    turned[:128, : 2 * H] = late_ref[8:32, :].T
    biases = turned[row_block(s, 8), : 2 * H]
    peaks = peak_ref[...].T[:1, :]
    clips = jnp.sqrt(clip_limit / jnp.maximum(peaks, clip_limit))
    for layer in range(2):
        bias_out[layer] = biases[:, layer * H : (layer + 1) * H]
        clip_out[layer : layer + 1, :] = clips[:, layer * H : (layer + 1) * H]
    for copy in put:
        copy.wait()


def finish(att, up, down, expert_up, expert_down, small, late, peaks, grad, result):
    vmem = pl.BlockSpec(memory_space=VMEM)
    anywhere = pl.BlockSpec(memory_space=ANY)
    loaded = (att, up, down, expert_up, expert_down, small, late, peaks, grad)
    sem = pltpu.SemaphoreType.DMA
    wide = (
        (2, 192, 3 * D), (2, 192, D), (192, 8 * 384), (8 * 96, D), expert_up.shape,
        expert_down.shape,
    )
    return pl.pallas_call(
        finish_kernel,
        name="finish",
        out_shape=tuple(
            jax.ShapeDtypeStruct(dims, single)
            for dims in wide + ((2, 192), (2, 192), (2, 8, H), (16, 192), (2, H), (T, 1, D))
        )
        + (jax.ShapeDtypeStruct(result.shape, bfloat),),
        in_specs=[anywhere] * 10,
        out_specs=(anywhere,) * 6 + (vmem,) * 7,
        scratch_shapes=[VMEM(item.shape, item.dtype) for item in loaded]
        + [VMEM(dims, single) for dims in wide]
        + [VMEM((D, 128), single), sem((10,)), sem((6,))],
        compiler_params=pltpu.CompilerParams(vmem_limit_bytes=60 * 2**20),
    )(*loaded, result)


def shards(
    hidden_in,
    attn_gain,
    qkv_weight,
    out_weight,
    rel_bias,
    bucket_table,
    mlp_gain,
    mlp_up,
    mlp_down,
    router_weight,
    expert_up,
    expert_down,
    routes,
    out_grad,
):
    block_rows = hidden_in.shape[1]
    length = bucket_table.shape[0]
    groups = lax.axis_size("shard")

    backward_table = jnp.pad(bucket_table[::-1], (0, TOE))
    buckets = lax.dynamic_slice_in_dim(
        backward_table, length - block_rows * (lax.axis_index("expert") + 1), TOE
    )[None]
    cotangent = out_grad.reshape(block_rows, D)
    (
        normed, queries, attended, mid_first, mid_second, dense_normed, pre_act, activation, layer_one, peak_rows,
        moe_normed, gains, router, slots, qkv0, qkv1, projection0, projection1, dense_up,
        dense_down, kv, probs, up_own, cotangents, dense_rows,
    ) = forward(
        hidden_in.reshape(block_rows, D), attn_gain, mlp_gain, rel_bias, router_weight.T, buckets,
        routes.reshape(block_rows, 2).T,
        qkv_weight, out_weight, mlp_up, mlp_down, expert_up, cotangent,
    )
    hidden_out, mid_grad, small_in, up_grad, expert_down_low, early_rows = run_experts(
        moe_normed, mid_second, gains, router, slots, cotangent, cotangents, up_own, expert_down,
        normed, attended,
    )
    hidden_grad, attention_sum, up_sum, down_sum, small_sum, late_sum, peaks, expert_up_low = (
        backward(
            mid_grad, layer_one, hidden_in.reshape(block_rows, D), mid_first, gains, normed, queries,
            attended, dense_rows, activation, pre_act, buckets, small_in, peak_rows,
            early_rows, (qkv0, qkv1, projection0, projection1, dense_up, dense_down), kv, probs,
            up_grad,
        )
    )
    (
        qkv_grad, out_weight_grad, mlp_up_grad, mlp_down_grad, expert_up_grad, expert_down_grad,
        attn_gain_grad, mlp_gain_grad, rel_bias_grad, router_grad, clip_scales, hidden_grad, hidden_out,
    ) = finish(
        attention_sum, up_sum, down_sum, expert_up_low, expert_down_low, small_sum, late_sum, peaks,
        hidden_grad, hidden_out,
    )
    return (
        hidden_out.reshape(hidden_in.shape),
        hidden_grad.reshape(hidden_in.shape),
        attn_gain_grad,
        qkv_grad,
        out_weight_grad,
        rel_bias_grad,
        mlp_gain_grad,
        mlp_up_grad,
        mlp_down_grad,
        router_grad.T,
        expert_up_grad,
        expert_down_grad,
        clip_scales,
    )


def solution(mesh):
    tokens = P("shard", "expert", None, None)
    columns = P(None, "shard")
    layers = P(None, "shard", None)
    rows = P("shard", None)
    owned = P("expert", "shard", None)
    in_specs = (
        tokens, columns, layers, layers, layers, P(), columns, rows, rows, rows, owned, owned,
        tokens, tokens,
    )
    out_specs = (
        tokens, tokens, columns, layers, layers, layers, columns, rows, rows, rows, owned, owned,
        P(),
    )
    sized = mesh.shape["expert"] == 8 and mesh.shape["shard"] == 4
    part = shards if sized else plain_shards
    return jax.shard_map(part, mesh=mesh, in_specs=in_specs, out_specs=out_specs, check_vma=False)
```

```python
import functools
import math

import jax
import jax.numpy as jnp
from jax import lax
from jax.experimental import pallas as pl
from jax.experimental.pallas import tpu as pltpu
from jax.sharding import PartitionSpec as P

D = 768
H = 12
HD = 64
NB = 32
EXP_DEV = 2

epsilon = 1e-06
clip_limit = 6.0
bfloat = jnp.bfloat16
single = jnp.float32


def rms_norm(inputs, norm_gain):
    return (
        inputs * lax.rsqrt(jnp.mean(inputs * inputs, axis=-1, keepdims=True) + epsilon) * norm_gain
    )


def norm_back(inputs, norm_gain, upstream):
    _, pullback = jax.vjp(rms_norm, inputs, norm_gain)
    return pullback(upstream)


def gelu_back(pre_values, upstream):
    _, pullback = jax.vjp(jax.nn.gelu, pre_values)
    return pullback(upstream)[0]


def matmul(left, right):
    return jnp.dot(left, right, preferred_element_type=single)


def shard_shift(block, amount):
    count = lax.axis_size("shard")
    return lax.ppermute(block, "shard", [(i, (i + amount) % count) for i in range(count)])


def gather_shard(block):
    count = lax.axis_size("shard")
    here = lax.axis_index("shard")
    result = jnp.zeros((count,) + block.shape, block.dtype)
    for step in range(count):
        piece = block if step == 0 else shard_shift(block, step)
        result = lax.dynamic_update_slice_in_dim(result, piece[None], (here - step) % count, 0)
    return result


def scatter_shard(blocks, sent=bfloat):
    count = lax.axis_size("shard")
    here = lax.axis_index("shard")
    total = lax.dynamic_index_in_dim(blocks, here, 0, keepdims=False).astype(single)
    for step in range(1, count):
        part = lax.dynamic_index_in_dim(blocks, (here + step) % count, 0, keepdims=False)
        total = total + shard_shift(part.astype(sent), step).astype(single)
    return total


def spread(columns):
    experts, shard_count = lax.axis_size("expert"), lax.axis_size("shard")
    rows, width = columns.shape
    cut = columns.reshape(rows, shard_count, experts, width // (shard_count * experts))
    return cut.transpose(0, 2, 1, 3).reshape(rows, width)


def unspread(columns):
    experts, shard_count = lax.axis_size("expert"), lax.axis_size("shard")
    rows, width = columns.shape
    cut = columns.reshape(rows, experts, shard_count, width // (shard_count * experts))
    return cut.transpose(0, 2, 1, 3).reshape(rows, width)


def gather_weight(block):
    part = block.shape[0] // lax.axis_size("expert")
    own = lax.dynamic_slice_in_dim(block, lax.axis_index("expert") * part, part, 0)
    column = gather_shard(own).reshape(-1, block.shape[1])
    return lax.all_gather(column, "expert", axis=0, tiled=True)


def reduce_weight(grad):
    part = lax.psum_scatter(grad.astype(bfloat), "expert", scatter_dimension=0, tiled=True)
    blocks = part.reshape((lax.axis_size("shard"), -1) + part.shape[1:])
    own = scatter_shard(blocks).astype(bfloat)
    return lax.all_gather(own, "expert", axis=0, tiled=True).astype(single)


def bucket_marks(distance, lower, upper):
    inside = (distance[None] >= lower[:, None, None]) & (distance[None] < upper[:, None, None])
    return inside.astype(bfloat)


def position_bias(marks, bias_pair):
    return jnp.einsum("bij,bh->hij", marks, bias_pair, preferred_element_type=single)


def attention_forward(hidden, norm_gain, qkv, projection, bias_pair, geometry):
    distance, marks, scale = geometry
    rows = hidden.shape[0]
    normalized = spread(rms_norm(hidden, norm_gain).astype(bfloat))
    packed = matmul(normalized, qkv).astype(bfloat)
    key_value = lax.all_gather(packed[:, D:], "expert", axis=0, tiled=True)
    shifted = position_bias(marks, bias_pair)
    causal = distance >= 0
    queries = packed[:, :D].reshape(rows, H, HD)
    keys = key_value[:, :D].reshape(-1, H, HD)
    values = key_value[:, D:].reshape(-1, H, HD)
    raw_scores = jnp.einsum("ihd,jhd->hij", queries, keys, preferred_element_type=single) * scale
    head_peak = jnp.max(jnp.where(causal[None], raw_scores, -jnp.inf), axis=(1, 2))
    masked = jnp.where(causal[None], raw_scores + shifted, -jnp.inf)
    softmax_top = jnp.max(masked, axis=-1, keepdims=True)
    exponent = jnp.exp(masked - softmax_top)
    softmax_sum = jnp.sum(exponent, axis=-1, keepdims=True)
    probs = (exponent / softmax_sum).astype(bfloat)
    log_total = softmax_top[..., 0] + jnp.log(softmax_sum[..., 0])
    attended = jnp.einsum("hij,jhd->ihd", probs, values, preferred_element_type=single)
    attended = spread(attended.astype(bfloat).reshape(rows, D))
    saved = (normalized, packed, key_value, log_total, attended)
    return hidden + matmul(attended, projection), head_peak, saved


def attention_backward(
    upstream, hidden, norm_gain, qkv, projection, bias_pair, geometry, saved
):
    distance, marks, scale = geometry
    normalized, packed, key_value, log_total, attended = saved
    rows = hidden.shape[0]
    branch_grad = upstream.astype(bfloat)
    projection_grad = matmul(attended.T, branch_grad)
    attended_grad = unspread(matmul(branch_grad, projection.T).astype(bfloat))
    shifted = position_bias(marks, bias_pair)
    causal = distance >= 0
    queries = packed[:, :D].reshape(rows, H, HD)
    keys = key_value[:, :D].reshape(-1, H, HD)
    values = key_value[:, D:].reshape(-1, H, HD)
    grad_heads = attended_grad.reshape(rows, H, HD)
    raw_scores = jnp.einsum("ihd,jhd->hij", queries, keys, preferred_element_type=single) * scale
    probs = jnp.where(causal[None], jnp.exp(raw_scores + shifted - log_total[..., None]), 0.0)
    prob_grad = jnp.einsum("ihd,jhd->hij", grad_heads, values, preferred_element_type=single)
    row_dot = jnp.sum(prob_grad * probs, axis=-1)
    score_grad = (probs * (prob_grad - row_dot[..., None])).astype(bfloat)
    query_grad = jnp.einsum("hij,jhd->ihd", score_grad, keys, preferred_element_type=single) * scale
    query_grad = query_grad.astype(bfloat).reshape(rows, D)
    bias_grad = jnp.einsum("hij,bij->bh", score_grad, marks, preferred_element_type=single)
    key_grad = (
        jnp.einsum("hij,ihd->jhd", score_grad, queries, preferred_element_type=single) * scale
    )
    value_grad = jnp.einsum(
        "hij,ihd->jhd", probs.astype(bfloat), grad_heads, preferred_element_type=single
    )
    pair = jnp.concatenate([key_grad.reshape(-1, D), value_grad.reshape(-1, D)], axis=-1)
    pair_grad = lax.psum_scatter(pair.astype(bfloat), "expert", scatter_dimension=0, tiled=True)
    packed_grad = jnp.concatenate([query_grad, pair_grad], axis=-1)
    qkv_grad = matmul(normalized.T, packed_grad)
    normed_grad = unspread(matmul(packed_grad, qkv.T))
    input_grad, gain_grad = norm_back(hidden, norm_gain, normed_grad)
    return upstream + input_grad, gain_grad, qkv_grad, projection_grad, bias_grad


def exchange(blocks):
    return lax.all_to_all(blocks, "expert", split_axis=0, concat_axis=0, tiled=True)


def plain_shards(
    hidden_in,
    attn_gain,
    qkv_weight,
    out_weight,
    rel_bias,
    bucket_table,
    mlp_gain,
    mlp_up,
    mlp_down,
    router_weight,
    expert_up,
    expert_down,
    routes,
    out_grad,
):
    block_rows = hidden_in.shape[1]
    length = bucket_table.shape[0]
    experts = lax.axis_size("expert")
    groups = lax.axis_size("shard")
    here = lax.axis_index("shard")
    expert_total = EXP_DEV * experts
    capacity = 4 * block_rows // expert_total
    width = expert_down.shape[1]
    scale = 1.0 / math.sqrt(HD)

    small = jnp.concatenate(
        [attn_gain.reshape(-1), mlp_gain.reshape(-1), rel_bias.reshape(-1), router_weight.reshape(-1)]
    )
    small = gather_shard(small)
    part = D // groups
    cuts = [0, 2 * part, 4 * part, 4 * part + 2 * (NB // groups) * H, small.shape[1]]
    gain_attn, gain_mlp, bias_weights, router_full = (
        small[:, cuts[i] : cuts[i + 1]] for i in range(4)
    )
    gain_attn = gain_attn.reshape(groups, 2, part).transpose(1, 0, 2).reshape(2, D).astype(single)
    gain_mlp = gain_mlp.reshape(groups, 2, part).transpose(1, 0, 2).reshape(2, D).astype(single)
    bias_weights = (
        bias_weights.reshape(groups, 2, NB // groups, H).transpose(1, 0, 2, 3).reshape(2, NB, H)
    )
    router_full = router_full.reshape(D, expert_total)

    first = gather_weight(jnp.concatenate([qkv_weight[0], out_weight[0]], axis=1))
    dense_up = gather_weight(mlp_up)
    dense_down = gather_weight(mlp_down)
    second = gather_weight(jnp.concatenate([qkv_weight[1], out_weight[1]], axis=1))
    qkv = (first[:, : 3 * D], second[:, : 3 * D])
    projection = (first[:, 3 * D :], second[:, 3 * D :])

    up_own = jnp.zeros((EXP_DEV, groups, part, width), bfloat)
    for step in range(groups):
        target = (here + step) % groups
        piece = lax.dynamic_slice_in_dim(expert_up, target * width, width, 2)
        if step:
            piece = shard_shift(piece, step)
        up_own = lax.dynamic_update_slice_in_dim(up_own, piece[:, None], (here - step) % groups, 1)
    up_own = up_own.reshape(EXP_DEV, D, width)

    route_rows = gather_shard(routes.reshape(block_rows, 2))
    upstream_all = gather_shard(out_grad.reshape(block_rows, D))
    expert_ids = jnp.arange(expert_total, dtype=jnp.int32)
    flat_routes = route_rows.reshape(groups, -1)
    marks = (flat_routes[:, :, None] == expert_ids).astype(jnp.int32)
    rank = jnp.sum((jnp.cumsum(marks, axis=1) - marks) * marks, axis=2)
    slot_of_route = flat_routes * capacity + rank
    slot_ids = jnp.arange(expert_total * capacity, dtype=jnp.int32)
    slot_marks = (slot_of_route[:, :, None] == slot_ids).astype(bfloat)
    token_marks = jnp.sum(
        slot_marks.reshape(groups, block_rows, 2, -1).astype(single), axis=2
    ).astype(bfloat)

    def dispatch(rows):
        slots = jnp.einsum("gts,gtd->gsd", token_marks, rows, preferred_element_type=single)
        slots = slots.astype(bfloat).reshape(groups, experts, EXP_DEV, capacity, D)
        return exchange(slots.transpose(1, 2, 0, 3, 4)).reshape(
            experts, EXP_DEV, groups * capacity, D
        )

    def collect(blocks):
        back = exchange(blocks.astype(bfloat)).reshape(experts, EXP_DEV, groups, capacity, D)
        return back.transpose(2, 0, 1, 3, 4).reshape(groups, expert_total * capacity, D)

    owner_rows = dispatch(upstream_all)

    own_positions = lax.axis_index("expert") * block_rows + jnp.arange(block_rows, dtype=jnp.int32)
    distance = own_positions[:, None] - jnp.arange(length, dtype=jnp.int32)[None, :]
    bounds = jnp.sum(
        (bucket_table[:, None] < jnp.arange(NB + 1, dtype=jnp.int32)[None, :]).astype(jnp.int32),
        axis=0,
    )
    geometry = (distance, bucket_marks(distance, bounds[:NB], bounds[1:]), scale)

    hidden_zero = hidden_in.reshape(block_rows, D).astype(single)
    mid_first, peak_first, saved_first = attention_forward(
        hidden_zero, gain_attn[0], qkv[0], projection[0], bias_weights[0], geometry
    )
    dense_normed = spread(rms_norm(mid_first, gain_mlp[0]).astype(bfloat))
    pre_act = matmul(dense_normed, dense_up)
    activation = spread(jax.nn.gelu(pre_act).astype(bfloat))
    layer_one = mid_first + matmul(activation, dense_down)
    mid_second, peak_second, saved_second = attention_forward(
        layer_one, gain_attn[1], qkv[1], projection[1], bias_weights[1], geometry
    )

    moe_normed = rms_norm(mid_second, gain_mlp[1]).astype(bfloat)
    normed_all = gather_shard(moe_normed)
    received = dispatch(normed_all)
    router_logits = jnp.einsum("gtd,de->gte", normed_all, router_full, preferred_element_type=single)
    selected = (route_rows[..., None] == expert_ids).astype(single)
    gates_all = jax.nn.softmax(jnp.sum(selected * router_logits[:, :, None, :], axis=-1), axis=-1)
    slot_gates = jnp.sum(
        gates_all.reshape(groups, -1)[:, :, None] * (slot_of_route[:, :, None] == slot_ids), axis=1
    )
    owner_gates = exchange(
        slot_gates.reshape(groups, experts, EXP_DEV, capacity).transpose(1, 2, 0, 3)
    ).reshape(experts, EXP_DEV, groups * capacity)

    expert_pre = jnp.einsum("sjcd,jdf->sjcf", received, up_own, preferred_element_type=single)
    expert_act = jax.nn.gelu(expert_pre).astype(bfloat)
    expert_out = jnp.einsum(
        "sjcf,jfd->sjcd", expert_act, expert_down, preferred_element_type=single
    )
    owner_grad = (owner_gates[..., None] * owner_rows.astype(single)).astype(bfloat)
    act_grad = jnp.einsum("sjcd,jfd->sjcf", owner_grad, expert_down, preferred_element_type=single)
    pre_grad = gelu_back(expert_pre, act_grad).astype(bfloat)
    row_grad = jnp.einsum("sjcf,jdf->sjcd", pre_grad, up_own, preferred_element_type=single)

    returned = collect(expert_out)
    back_rows = collect(row_grad)
    expert_down_grad = jnp.einsum(
        "sjcf,sjcd->jfd", expert_act, owner_grad, preferred_element_type=single
    )
    up_grad = jnp.einsum(
        "sjcd,sjcf->jdf", received, pre_grad, preferred_element_type=single
    ).astype(bfloat)

    route_out = jnp.einsum("grs,gsd->grd", slot_marks, returned, preferred_element_type=single)
    route_out = route_out.reshape(groups, block_rows, 2, D)
    gate_grad = scatter_shard(
        jnp.sum(route_out * upstream_all[:, :, None, :].astype(single), axis=-1), single
    )
    mixed = scatter_shard(jnp.sum(gates_all[..., None] * route_out, axis=2))
    hidden_out = (mid_second + mixed).astype(bfloat).reshape(hidden_in.shape)

    gates = lax.dynamic_index_in_dim(gates_all, here, 0, keepdims=False)
    own_selected = lax.dynamic_index_in_dim(selected, here, 0, keepdims=False)
    upstream = out_grad.reshape(block_rows, D).astype(single)
    chosen_grad = gates * (gate_grad - jnp.sum(gates * gate_grad, axis=-1, keepdims=True))
    logit_grad = jnp.sum(chosen_grad[:, :, None] * own_selected, axis=1).astype(bfloat)
    router_grad = matmul(moe_normed.T, logit_grad)
    row_terms = jnp.einsum("gts,gsd->gtd", token_marks, back_rows, preferred_element_type=single)
    normed_grad = matmul(logit_grad, router_full.T) + scatter_shard(row_terms)
    moe_input_grad, moe_gain_grad = norm_back(mid_second, gain_mlp[1], normed_grad)
    mid_grad = upstream + moe_input_grad

    up_grad = up_grad.reshape(EXP_DEV, groups, part, width)
    expert_up_grad = jnp.zeros((EXP_DEV, part, groups * width), single)
    for step in range(groups):
        piece = lax.dynamic_index_in_dim(up_grad, (here + step) % groups, 1, keepdims=False)
        if step:
            piece = shard_shift(piece, step)
        expert_up_grad = lax.dynamic_update_slice_in_dim(
            expert_up_grad, piece.astype(single), ((here - step) % groups) * width, 2
        )

    layer_grad, gain_second, qkv_second, projection_second, bias_second = attention_backward(
        mid_grad, layer_one, gain_attn[1], qkv[1], projection[1], bias_weights[1], geometry,
        saved_second,
    )
    second_grad = reduce_weight(jnp.concatenate([qkv_second, projection_second], axis=1))
    dense_branch = layer_grad.astype(bfloat)
    mlp_down_grad = reduce_weight(matmul(activation.T, dense_branch))
    hidden_act_grad = unspread(matmul(dense_branch, dense_down.T))
    pre_act_grad = gelu_back(pre_act, hidden_act_grad).astype(bfloat)
    mlp_up_grad = reduce_weight(matmul(dense_normed.T, pre_act_grad))
    dense_normed_grad = unspread(matmul(pre_act_grad, dense_up.T))
    dense_input_grad, dense_gain_grad = norm_back(mid_first, gain_mlp[0], dense_normed_grad)
    first_grad = layer_grad + dense_input_grad
    input_grad, gain_first, qkv_first, projection_first, bias_first = attention_backward(
        first_grad, hidden_zero, gain_attn[0], qkv[0], projection[0], bias_weights[0], geometry,
        saved_first,
    )
    first_weight_grad = reduce_weight(jnp.concatenate([qkv_first, projection_first], axis=1))

    gains = jnp.stack([gain_first, gain_second, dense_gain_grad, moe_gain_grad])
    biases = jnp.stack([bias_first, bias_second])
    small_grad = jnp.concatenate(
        [
            gains.reshape(4, groups, part).transpose(1, 0, 2).reshape(groups, -1),
            biases.reshape(2, groups, NB // groups, H).transpose(1, 0, 2, 3).reshape(groups, -1),
            router_grad.reshape(groups, -1),
        ],
        axis=1,
    )
    small_grad = lax.psum(scatter_shard(small_grad, single), "expert")
    gain_cut = 4 * part
    bias_cut = gain_cut + 2 * (NB // groups) * H
    own_gains = small_grad[:gain_cut].reshape(4, part)
    peaks = lax.pmax(jnp.stack([peak_first, peak_second]), ("expert", "shard"))
    clip_scales = jnp.sqrt(clip_limit / jnp.maximum(peaks, clip_limit))
    return (
        hidden_out,
        input_grad.reshape(hidden_in.shape),
        own_gains[:2],
        jnp.stack([first_weight_grad[:, : 3 * D], second_grad[:, : 3 * D]]),
        jnp.stack([first_weight_grad[:, 3 * D :], second_grad[:, 3 * D :]]),
        small_grad[gain_cut:bias_cut].reshape(2, NB // groups, H),
        own_gains[2:],
        mlp_up_grad,
        mlp_down_grad,
        small_grad[bias_cut:].reshape(part, expert_total),
        expert_up_grad,
        expert_down_grad,
        clip_scales,
    )


MESH = pl.DeviceIdType.MESH
ANY = pl.ANY
VMEM = pltpu.VMEM


def place():
    return lax.axis_index("expert"), lax.axis_index("shard")


def greet(devices):
    barrier = pltpu.get_barrier_semaphore()
    for device in devices:
        pl.semaphore_signal(barrier, inc=1, device_id=device, device_id_type=MESH)
    pl.semaphore_wait(barrier, len(devices))


def push(sent, source, target, send_sem, recv_sem, device):
    copy = pltpu.make_async_remote_copy(
        src_ref=source,
        dst_ref=target,
        send_sem=send_sem,
        recv_sem=recv_sem,
        device_id=device,
        device_id_type=MESH,
    )
    copy.start()
    sent.append(copy)
    return copy


def norm_rows(inputs, gain):
    return inputs * lax.rsqrt(jnp.mean(inputs * inputs, axis=-1, keepdims=True) + epsilon) * gain


def dot_rows(left, right):
    return lax.dot_general(left, right, (((1,), (1,)), ((), ())), preferred_element_type=single)


def dot_columns(left, right):
    return lax.dot_general(left, right, (((0,), (0,)), ((), ())), preferred_element_type=single)


def loop(count, body):
    def step(i, carry):
        body(i)
        return carry

    lax.fori_loop(0, count, step, 0)


def lane_block(i, width):
    return pl.ds(pl.multiple_of(i * width, 128), width)


def row_block(i, height):
    return pl.ds(pl.multiple_of(i * height, height), height)


T = 128
PAIRS = H // 2
TOE = 1152
CAP = 32


class Plane:
    def __init__(self):
        self.e, self.s = place()
        e = self.e
        self.core = lax.rem(e, 2)
        self.quarter = e // 2
        self.at_x = e + 2 - 4 * lax.rem(self.quarter, 2)
        self.at_y = lax.rem(e + 4, 8)
        self.at_core = e + 1 - 2 * self.core
        self.inward = jnp.where(self.core == 0, self.at_x, self.at_y)
        self.onward = jnp.where(self.core == 0, self.at_y, self.at_x)
        self.diagonal = self.inward + self.onward - e
        self.others = [lax.rem(self.s + k, 4) for k in range(1, 4)]
        self.around = [lax.rem(e + k, 8) for k in range(1, 8)]
        z = self.s
        first = jnp.where(z == 0, 1, jnp.where(z == 1, 2, jnp.where(z == 2, 1, 2)))
        second = jnp.where(z == 0, 2, jnp.where(z == 1, 0, jnp.where(z == 2, 3, 1)))
        self.near = [first, second, 6 - z - first - second]
        self.to_k = [lax.rem(other - z + 4, 4) - 1 for other in self.near]
        self.from_k = [lax.rem(z - other + 4, 4) - 1 for other in self.near]
        self.sent = []

    def push(self, source, target, send_sem, recv_sem, device):
        return push(self.sent, source, target, send_sem, recv_sem, device)

    def arrived(self, view, recv_sem):
        pltpu.make_async_remote_copy(
            src_ref=view,
            dst_ref=view,
            send_sem=recv_sem,
            recv_sem=recv_sem,
            device_id=(self.at_core, self.s),
            device_id_type=MESH,
        ).wait_recv()


class PlaneGather:
    def __init__(self, plane, view, send_sems, recv_sems):
        self.plane, self.view, self.ss, self.rs = plane, view, send_sems, recv_sems

    def _push(self, who, i, target):
        p = self.plane
        block = self.view(who)
        p.push(block, block, self.ss.at[i], self.rs.at[i], (target, p.s))

    def first(self):
        p = self.plane
        self._push(p.e, 0, p.at_x)
        self._push(p.e, 1, p.at_y)
        self._push(p.e, 3, p.at_core)

    def second(self):
        p = self.plane
        p.arrived(self.view(p.inward), self.rs.at[p.core])
        self._push(p.inward, 2, p.onward)
        self._push(p.inward, 4, p.at_core)

    def third(self):
        p = self.plane
        p.arrived(self.view(p.onward), self.rs.at[1 - p.core])
        self._push(p.onward, 5, p.at_core)
        p.arrived(self.view(p.diagonal), self.rs.at[2])
        self._push(p.diagonal, 6, p.at_core)

    def done(self):
        for i in range(3, 7):
            self.plane.arrived(self.view(self.plane.e), self.rs.at[i])


class PlaneSum:
    def __init__(self, plane, parts, core_in, chips_in, send_sems, recv_sems):
        self.plane, self.parts, self.core_in, self.chips_in = plane, parts, core_in, chips_in
        self.ss, self.rs = send_sems, recv_sems

    def give(self):
        p = self.plane
        p.push(
            self.parts.at[1 - p.core], self.core_in, self.ss.at[0], self.rs.at[0], (p.at_core, p.s)
        )

    def pass_on(self):
        p = self.plane
        p.arrived(self.core_in, self.rs.at[0])
        for q in range(4):
            self.parts[p.core, q] = (
                self.parts[p.core, q].astype(single) + self.core_in[q].astype(single)
            ).astype(bfloat)
        for k, d in enumerate((p.at_x, p.at_y, p.diagonal)):
            p.push(
                self.parts.at[p.core, d // 2],
                self.chips_in.at[k],
                self.ss.at[1 + k],
                self.rs.at[1 + k],
                (d, p.s),
            )

    def result(self):
        p = self.plane
        total = self.parts[p.core, p.quarter].astype(single)
        for k in range(3):
            p.arrived(self.chips_in.at[k], self.rs.at[1 + k])
            total = total + self.chips_in[k].astype(single)
        return total


def forward_kernel(
    hidden_ref,
    attn_gain_ref,
    mlp_gain_ref,
    rel_bias_ref,
    router_ref,
    buckets_ref,
    routes_ref,
    qkv_hbm,
    out_hbm,
    up_hbm,
    down_hbm,
    expert_up_hbm,
    cot_hbm,
    normed_out,
    query_out,
    attended_out,
    mid_first_out,
    mid_second_out,
    dense_normed_out,
    one_out,
    peak_out,
    moe_normed_out,
    gains_ref,
    router_out,
    slots_out,
    qkv0_out,
    qkv1_out,
    proj0_out,
    proj1_out,
    up_out,
    down_out,
    kv_out,
    probs_out,
    up_own,
    cot_all,
    dense_rows_out,
    pre_hbm,
    act_hbm,
    small_ref,
    small_all,
    table_ref,
    slots_own,
    up_shard,
    up_turned,
    pre_out,
    act_out,
    dense_rows,
    sums,
    sums_core,
    sums_chips,
    w_qkv0,
    w_qkv1,
    w_out0,
    w_out1,
    w_up,
    w_down,
    kv,
    probs,
    scores,
    zs,
    zr,
    f1s,
    f1r,
    f2s,
    f2r,
    cs,
    cr,
    locals_sem,
    k1s,
    k1r,
    k2s,
    k2r,
    kcs,
    kcr,
    us,
    ur,
    gs,
    gr,
    ns,
    nr,
    outs_sem,
    small_s,
    small_r,
    slot_zs,
    slot_zr,
    slot_ps,
    slot_pr,
    dense_s,
    dense_r,
    sum_s,
    sum_r,
):
    e, s = place()
    core = lax.rem(e, 2)
    quarter = e // 2
    at_x = e + 2 - 4 * lax.rem(quarter, 2)
    at_y = lax.rem(e + 4, 8)
    at_core = e + 1 - 2 * core
    inward = jnp.where(core == 0, at_x, at_y)
    onward = jnp.where(core == 0, at_y, at_x)
    others = [lax.rem(s + k, 4) for k in range(1, 4)]
    plane = Plane()
    near, to_k, from_k = plane.near, plane.to_k, plane.from_k
    sources = near
    sent = []
    kept = []

    def local(source, target, sem):
        copy = pltpu.make_async_copy(source, target, sem)
        copy.start()
        return copy

    chunks = [
        (qkv_hbm.at[0], w_qkv0, 48, 1152),
        (out_hbm.at[0], w_out0, 48, 384),
        None,
        None,
        (qkv_hbm.at[1], w_qkv1, 48, 1152),
        (out_hbm.at[1], w_out1, 48, 384),
    ]

    def block(target, who, position, height, half, width):
        rows = pl.ds(pl.multiple_of(position * 4 * height + who * height, height), height)
        return target.at[rows, lane_block(half, width)]

    def cot_block(g, who):
        return cot_all.at[g, who]

    stage1, stage2, stage3, stage4, own = {}, {}, {}, {}, {}

    def z_send(c):
        source, target, height, width = chunks[c]
        piece = source.at[row_block(quarter, height), lane_block(core, width)]
        mine = block(target, quarter, s, height, core, width)
        stage1[c] = [
            push(sent, piece, mine, zs.at[c, to_k[i]], zr.at[c, to_k[i]], (e, near[i]))
            for i in range(3)
        ]
        own[c] = local(source, target.at[row_block(s, 4 * height), :], locals_sem.at[c])

    got_shard = local(up_hbm, up_shard, outs_sem.at[11])

    def turn_shard():
        got_shard.wait()
        for b in range(8):
            for z in range(4):
                up_turned[:, 384 * b + 96 * z : 384 * b + 96 * (z + 1)] = up_shard[
                    :, 768 * z + 96 * b : 768 * z + 96 * (b + 1)
                ]

    def unit_send(c):
        target, height = ((w_up, 192), (w_down, 96))[c - 2]
        piece = up_turned.at[:, lane_block(e, 384)] if c == 2 else down_hbm.at[row_block(e, 96), :]
        mine = target.at[row_block(s, height), :]
        stage1[c] = [
            push(sent, piece, mine, zs.at[c, to_k[i]], zr.at[c, to_k[i]], (e, near[i]))
            for i in range(3)
        ]
        own[c] = local(piece, mine, locals_sem.at[c])

    def units_ready(c):
        for copy in stage1[c]:
            copy.wait_recv()
        own[c].wait()
        kept.append(local((w_up, w_down)[c - 2], weight_outs[c], outs_sem.at[c]))

    def plane_send(c):
        _, target, height, width = chunks[c]
        stage2[c] = []
        for k in range(3):
            mine = block(target, quarter, sources[k], height, core, width)
            plane.arrived(mine, zr.at[c, from_k[k]])
            stage2[c].append(
                [
                    push(sent, mine, mine, f1s.at[c, k, i], f1r.at[c, k, i], (partner, s))
                    for i, partner in enumerate((at_x, at_y))
                ]
            )

    def plane_forward(c):
        _, target, height, width = chunks[c]
        stage3[c] = []
        for k in range(3):
            pltpu.make_async_remote_copy(
                src_ref=block(target, quarter, sources[k], height, core, width),
                dst_ref=block(target, quarter, sources[k], height, core, width),
                send_sem=f1s.at[c, k, core],
                recv_sem=f1r.at[c, k, core],
                device_id=(inward, s),
                device_id_type=MESH,
            ).wait_recv()
            theirs = block(target, inward // 2, sources[k], height, core, width)
            stage3[c].append(
                push(sent, theirs, theirs, f2s.at[c, k], f2r.at[c, k], (onward, s))
            )

    def core_send(c):
        _, target, height, width = chunks[c]
        stage4[c] = []
        for k in range(3):
            pltpu.make_async_remote_copy(
                src_ref=block(target, quarter, sources[k], height, core, width),
                dst_ref=block(target, quarter, sources[k], height, core, width),
                send_sem=f1s.at[c, k, 1 - core],
                recv_sem=f1r.at[c, k, 1 - core],
                device_id=(onward, s),
                device_id_type=MESH,
            ).wait_recv()
            stage3[c][k].wait_recv()
            half = target.at[row_block(sources[k], 4 * height), lane_block(core, width)]
            stage4[c].append(push(sent, half, half, cs.at[c, k], cr.at[c, k], (at_core, s)))

    weight_outs = [qkv0_out, proj0_out, up_out, down_out, qkv1_out, proj1_out]

    def ready(c):
        for k in range(3):
            stage4[c][k].wait_recv()
        own[c].wait()
        kept.append(local(chunks[c][1], weight_outs[c], outs_sem.at[c]))

    cot_groups = [s] + sources
    cot_gathers = [
        PlaneGather(plane, functools.partial(cot_block, g), ns.at[k], nr.at[k])
        for k, g in enumerate(cot_groups)
    ]

    def cot_first(k):
        plane.arrived(cot_block(s, e), gr.at[from_k[k - 1]])
        cot_gathers[k].first()

    experts = lax.broadcasted_iota(jnp.int32, (16, T), 0)
    chosen = [experts == routes_ref[r : r + 1, :] for r in range(2)]
    marks = jnp.where(chosen[0] | chosen[1], 1.0, 0.0).astype(bfloat)
    earlier = jnp.where(
        lax.broadcasted_iota(jnp.int32, (T, T), 0) < lax.broadcasted_iota(jnp.int32, (T, T), 1),
        1.0,
        0.0,
    ).astype(bfloat)
    before = jnp.dot(marks, earlier, preferred_element_type=single)
    slots_own[...] = jnp.zeros_like(slots_own)
    for r in range(2):
        rank = jnp.sum(jnp.where(chosen[r], before, 0.0), axis=0, keepdims=True)
        slots_own[r : r + 1, :] = routes_ref[r : r + 1, :] * CAP + rank.astype(jnp.int32)
    slots_out[s, e] = slots_own[...]
    own_cot = local(cot_hbm, cot_block(s, e), gs.at[3])
    part = D // 4
    small_ref[...] = jnp.zeros_like(small_ref)
    small_ref[0:2, :part] = attn_gain_ref[...].astype(single)
    small_ref[2:4, :part] = mlp_gain_ref[...].astype(single)
    for layer in range(2):
        small_ref[8:16, layer * H : (layer + 1) * H] = rel_bias_ref[layer].astype(single)
    small_ref[16:32, :part] = router_ref[...].astype(single)
    small_all[s] = small_ref[...]

    greet([(d, s) for d in plane.around] + [(e, other) for other in others])
    smalls = [
        push(sent, small_ref, small_all.at[s], small_s.at[k], small_r.at[k], (e, others[k]))
        for k in range(3)
    ]
    z_send(0)
    for k in range(3):
        push(sent, slots_own, slots_out.at[s, e], slot_zs.at[k], slot_zr.at[k], (e, others[k]))
    own_cot.wait()
    cot_gathers[0].first()
    z_send(1)
    turn_shard()
    unit_send(2)
    reshard = []

    def bulk():
        z_send(4)
        z_send(5)
        unit_send(3)
        for i in range(3):
            push(sent, cot_hbm, cot_block(s, e), gs.at[to_k[i]], gr.at[to_k[i]], (e, near[i]))
        kept.append(
            local(
                expert_up_hbm.at[:, :, lane_block(s, 768)],
                up_own.at[:, row_block(s, 192), :],
                us.at[3],
            )
        )

    def slots_plane():
        for k in range(3):
            plane.arrived(slots_own, slot_zr.at[k])
        column = slots_out.at[:, e]
        for k, d in enumerate(plane.around):
            push(sent, column, column, slot_ps.at[k], slot_pr.at[k], (d, s))

    for copy in smalls:
        copy.wait_recv()
    biases = []
    for z in range(4):
        lanes = slice(192 * z, 192 * (z + 1))
        gains_ref[:, lanes] = small_all[z, :4, :192]
        router_out[:, lanes] = small_all[z, 16:32, :192].astype(bfloat)
        biases.append(small_all[z, 8:16, : 2 * H])
    bucket_marks_here = jnp.where(
        lax.broadcasted_iota(jnp.int32, (NB, TOE), 0) == buckets_ref[...], 1.0, 0.0
    ).astype(bfloat)
    table_ref[...] = dot_columns(jnp.concatenate(biases).astype(bfloat), bucket_marks_here)

    def attention(layer, inputs, w_qkv, w_out, work):
        normed = norm_rows(inputs, gains_ref[pl.ds(layer, 1), :]).astype(bfloat)
        normed_out[layer] = normed
        if layer == 0:
            plane_send(0)
            plane_forward(0)
            plane_send(1)
            core_send(0)
            plane_forward(1)
            ready(0)
            bulk()
        else:
            ready(4)
        own_rows = row_block(e, T)
        first, second, third = [], [], []
        for part in range(3):
            x = normed_out[layer]
            for i, base in enumerate((D, 2 * D)):
                columns = w_qkv[:, base + 256 * part : base + 256 * (part + 1)]
                kv[layer, part, own_rows, 256 * i : 256 * (i + 1)] = jnp.dot(
                    x, columns, preferred_element_type=single
                ).astype(bfloat)
            mine = kv.at[layer, part, own_rows, :]
            first.append(
                [
                    push(sent, mine, mine, k1s.at[layer, part, i], k1r.at[layer, part, i], (p, s))
                    for i, p in enumerate((at_x, at_y))
                ]
            )
            third.append(
                [
                    push(
                        sent, mine, mine, kcs.at[layer, part, 0], kcr.at[layer, part, 0],
                        (at_core, s),
                    )
                ]
            )
        query_out[layer] = jnp.dot(
            normed_out[layer], w_qkv[:, :D], preferred_element_type=single
        ).astype(bfloat)
        if work:
            work[0]()
        at_diagonal = inward + onward - e
        for part in range(3):
            pltpu.make_async_remote_copy(
                src_ref=kv.at[layer, part, own_rows, :],
                dst_ref=kv.at[layer, part, own_rows, :],
                send_sem=k1s.at[layer, part, core],
                recv_sem=k1r.at[layer, part, core],
                device_id=(inward, s),
                device_id_type=MESH,
            ).wait_recv()
            theirs = kv.at[layer, part, row_block(inward, T), :]
            second.append(
                push(
                    sent, theirs, theirs, k2s.at[layer, part], k2r.at[layer, part], (onward, s)
                )
            )
            third[part].append(
                push(
                    sent, theirs, theirs, kcs.at[layer, part, 1], kcr.at[layer, part, 1],
                    (at_core, s),
                )
            )
        if work:
            work[1]()
        for part in range(3):
            pltpu.make_async_remote_copy(
                src_ref=kv.at[layer, part, own_rows, :],
                dst_ref=kv.at[layer, part, own_rows, :],
                send_sem=k1s.at[layer, part, 1 - core],
                recv_sem=k1r.at[layer, part, 1 - core],
                device_id=(onward, s),
                device_id_type=MESH,
            ).wait_recv()
            theirs = kv.at[layer, part, row_block(onward, T), :]
            third[part].append(
                push(
                    sent, theirs, theirs, kcs.at[layer, part, 2], kcr.at[layer, part, 2],
                    (at_core, s),
                )
            )
            second[part].wait_recv()
            theirs = kv.at[layer, part, row_block(at_diagonal, T), :]
            third[part].append(
                push(
                    sent, theirs, theirs, kcs.at[layer, part, 3], kcr.at[layer, part, 3],
                    (at_core, s),
                )
            )
        for part in range(3):
            for i in range(4):
                third[part][i].wait_recv()

            def one_pair(local_pair):
                pair = 2 * part + local_pair
                lanes = lane_block(pair, 128)
                queries = query_out[layer, :, lanes]
                lane = lax.broadcasted_iota(jnp.int32, (T, 128), 1)
                zero = jnp.zeros_like(queries)
                both = jnp.concatenate(
                    [jnp.where(lane < HD, queries, zero), jnp.where(lane >= HD, queries, zero)]
                )
                keys = kv[layer, part, :, lane_block(local_pair, 128)]
                scores[...] = dot_rows(both, keys) * (1.0 / math.sqrt(HD))
                for half in range(2):
                    head = 2 * pair + half
                    toeplitz = table_ref[pl.ds(layer * H + head, 1), :]
                    peak = jnp.full((1, 1), -jnp.inf, single)
                    for rows in range(0, T, 32):
                        raw = scores[half * T + rows : half * T + rows + 32, :]
                        row = e * T + rows + lax.broadcasted_iota(jnp.int32, raw.shape, 0)
                        causal = row >= lax.broadcasted_iota(jnp.int32, raw.shape, 1)
                        shifted = pltpu.roll(
                            jnp.broadcast_to(toeplitz, (32, TOE)),
                            TOE - (T - 1) + rows,
                            1,
                            stride=1,
                            stride_axis=0,
                        )[:, : raw.shape[1]]
                        peak = jnp.maximum(
                            peak, jnp.max(jnp.where(causal, raw, -jnp.inf), keepdims=True)
                        )
                        masked = jnp.where(causal, raw + shifted, -jnp.inf)
                        top = jnp.max(masked, axis=-1, keepdims=True)
                        exponent = jnp.exp(masked - top)
                        total = jnp.sum(exponent, axis=-1, keepdims=True)
                        probs[layer, pl.ds(pl.multiple_of(head * T + rows, 32), 32), :] = (
                            exponent / total
                        ).astype(bfloat)
                    peak_out[pl.ds(layer * H + head, 1), :] = jnp.broadcast_to(peak, (1, 128))
                values = kv[layer, part, :, pl.ds(pl.multiple_of(256 + local_pair * 128, 128), 128)]
                mixed = jnp.dot(
                    probs[layer, pl.ds(pl.multiple_of(pair * 2 * T, 2 * T), 2 * T), :],
                    values,
                    preferred_element_type=single,
                )
                attended_out[layer, :, lanes] = jnp.where(
                    lane < HD, mixed[:T], mixed[T:]
                ).astype(bfloat)

            loop(2, one_pair)
            if work:
                work[2 + part]()
        kept.append(local(kv.at[layer], kv_out.at[layer], outs_sem.at[6 + layer]))
        kept.append(local(probs.at[layer], probs_out.at[layer], outs_sem.at[8 + layer]))

    def work0():
        slots_plane()

    def work1():
        cot_gathers[0].second()

    def work2():
        core_send(1)
        plane_send(4)

    def work3():
        cot_gathers[0].third()
        plane_send(5)

    def work4():
        plane_forward(4)

    hidden = hidden_ref[...].astype(single)
    attention(0, hidden, w_qkv0, w_out0, [work0, work1, work2, work3, work4])
    ready(1)
    mid_first_out[...] = hidden + jnp.dot(
        attended_out[0], w_out0[...], preferred_element_type=single
    )
    dense_normed_out[...] = norm_rows(mid_first_out[...], gains_ref[pl.ds(2, 1), :]).astype(bfloat)
    reshard.extend([
        push(
            sent,
            expert_up_hbm.at[:, :, lane_block(near[i], 768)],
            up_own.at[:, row_block(s, 192), :],
            us.at[to_k[i]],
            ur.at[to_k[i]],
            (e, near[i]),
        )
        for i in range(3)
    ])
    dense_rows[e] = dense_normed_out[...]
    dense = PlaneGather(plane, lambda who: dense_rows.at[who], dense_s, dense_r)
    dense.first()
    plane_forward(5)
    core_send(4)
    dense.second()
    core_send(5)
    units_ready(2)
    units_ready(3)
    dense.third()
    dense.done()
    kept.append(local(dense_rows, dense_rows_out, outs_sem.at[10]))
    reduce = PlaneSum(plane, sums, sums_core, sums_chips, sum_s, sum_r)

    def units(c, q):
        who = 2 * q + c
        rows = row_block(who, T)
        before = jnp.dot(dense_rows[who], w_up[...], preferred_element_type=single)
        pre_out[rows, :] = before
        act = jax.nn.gelu(before).astype(bfloat)
        act_out[rows, :] = act
        sums[c, q] = jnp.dot(act, w_down[...], preferred_element_type=single).astype(bfloat)

    for q in range(4):
        units(1 - core, q)
    reduce.give()
    for q in range(4):
        units(core, q)
    reduce.pass_on()
    kept.append(local(pre_out, pre_hbm, outs_sem.at[12]))
    kept.append(local(act_out, act_hbm, outs_sem.at[13]))
    cot_first(1)
    one_out[...] = mid_first_out[...] + reduce.result()

    def work5():
        cot_first(2)
        cot_gathers[1].second()

    def work6():
        cot_first(3)

    def work7():
        cot_gathers[1].third()
        cot_gathers[2].second()

    def work8():
        cot_gathers[2].third()
        cot_gathers[3].second()

    def work9():
        cot_gathers[3].third()

    attention(1, one_out[...], w_qkv1, w_out1, [work5, work6, work7, work8, work9])
    ready(5)
    mid_second_out[...] = one_out[...] + jnp.dot(
        attended_out[1], w_out1[...], preferred_element_type=single
    )
    moe_normed_out[...] = norm_rows(mid_second_out[...], gains_ref[pl.ds(3, 1), :]).astype(bfloat)
    for k in range(7):
        plane.arrived(slots_out.at[:, e], slot_pr.at[k])
    for gather in cot_gathers:
        gather.done()
    for copy in reshard:
        copy.wait_recv()
    for copy in kept:
        copy.wait()
    for copy in sent + plane.sent:
        copy.wait_send()


def forward(
    hidden, attn_gain, mlp_gain, rel_bias, router, buckets, routes, qkv, out, up, down, expert_up,
    cotangent,
):
    length = T * lax.axis_size("expert")
    vmem = pl.BlockSpec(memory_space=VMEM)
    anywhere = pl.BlockSpec(memory_space=ANY)
    shape = jax.ShapeDtypeStruct
    sem = pltpu.SemaphoreType.DMA
    return pl.pallas_call(
        forward_kernel,
        name="forward_layers",
        out_shape=(
            shape((2, T, D), bfloat),
            shape((2, T, D), bfloat),
            shape((2, T, D), bfloat),
            shape((T, D), single),
            shape((T, D), single),
            shape((T, D), bfloat),
            shape((T, D), single),
            shape((2 * H, 128), single),
            shape((T, D), bfloat),
            shape((4, D), single),
            shape((16, D), bfloat),
            shape((4, 8, 8, T), jnp.int32),
            shape((D, 3 * D), bfloat),
            shape((D, 3 * D), bfloat),
            shape((D, D), bfloat),
            shape((D, D), bfloat),
            shape((D, 384), bfloat),
            shape((384, D), bfloat),
            shape((2, 3, length, 512), bfloat),
            shape((2, H * T, length), bfloat),
            shape((EXP_DEV, D, 768), bfloat),
            shape((4, 8, T, D), bfloat),
            shape((8, T, D), bfloat),
            shape((length, 384), single),
            shape((length, 384), bfloat),
        ),
        in_specs=[vmem] * 7 + [anywhere] * 6,
        out_specs=(vmem,) * 12 + (anywhere,) * 13,
        scratch_shapes=[
            VMEM((32, 256), single),
            VMEM((4, 32, 256), single),
            VMEM((2 * H, TOE), single),
            VMEM((8, T), jnp.int32),
            VMEM(up.shape, bfloat),
            VMEM(up.shape, bfloat),
            VMEM((length, 384), single),
            VMEM((length, 384), bfloat),
            VMEM((8, T, D), bfloat),
            VMEM((2, 4, T, D), bfloat),
            VMEM((4, T, D), bfloat),
            VMEM((3, T, D), bfloat),
            VMEM((D, 3 * D), bfloat),
            VMEM((D, 3 * D), bfloat),
            VMEM((D, D), bfloat),
            VMEM((D, D), bfloat),
            VMEM((D, 384), bfloat),
            VMEM((384, D), bfloat),
            VMEM((2, 3, length, 512), bfloat),
            VMEM((2, H * T, length), bfloat),
            VMEM((2 * T, length), single),
            sem((6, 3)), sem((6, 3)),
            sem((6, 3, 2)), sem((6, 3, 2)),
            sem((6, 3)), sem((6, 3)),
            sem((6, 3)), sem((6, 3)),
            sem((6,)),
            sem((2, 3, 2)), sem((2, 3, 2)),
            sem((2, 3)), sem((2, 3)),
            sem((2, 3, 4)), sem((2, 3, 4)),
            sem((4,)), sem((3,)),
            sem((4,)), sem((3,)),
            sem((4, 7)), sem((4, 7)),
            sem((14,)),
            sem((3,)), sem((3,)),
            sem((3,)), sem((3,)),
            sem((7,)), sem((7,)),
            sem((7,)), sem((7,)),
            sem((4,)), sem((4,)),
        ],
        compiler_params=pltpu.CompilerParams(
            collective_id=2, has_side_effects=True, vmem_limit_bytes=56 * 2**20
        ),
    )(
        hidden, attn_gain, mlp_gain, rel_bias, router, buckets, routes, qkv, out, up, down,
        expert_up, cotangent,
    )


class SmallReduce:
    def __init__(self, plane, value, z_in, plane_in, op, sems):
        self.plane, self.value, self.z_in, self.plane_in = plane, value, z_in, plane_in
        self.op, self.sems = op, sems

    def start(self):
        p = self.plane
        zs, zr, _, _ = self.sems
        for k in range(3):
            p.push(self.value, self.z_in.at[k], zs.at[k], zr.at[k], (p.e, p.others[k]))

    def middle(self, middle):
        p = self.plane
        zs, zr, ps, pr = self.sems
        total = self.value[...]
        for k in range(3):
            p.arrived(self.z_in.at[k], zr.at[k])
            total = self.op(total, self.z_in[k])
        middle[...] = total
        for k in range(7):
            p.push(middle, self.plane_in.at[k], ps.at[k], pr.at[k], (p.around[k], p.s))

    def finish(self, middle, result):
        p = self.plane
        total = middle[...]
        for k in range(7):
            p.arrived(self.plane_in.at[k], self.sems[3].at[k])
            total = self.op(total, self.plane_in[k])
        result[...] = total


def norm_pull(inputs, gain, upstream):
    inverse = lax.rsqrt(jnp.mean(inputs * inputs, axis=-1, keepdims=True) + epsilon)
    scaled = upstream * gain
    inner = jnp.mean(scaled * inputs, axis=-1, keepdims=True)
    gain_grad = jnp.sum(upstream * inputs * inverse, axis=0, keepdims=True)
    return inverse * scaled - inputs * (inverse * inverse * inverse * inner), gain_grad


def gelu_both(value):
    root = math.sqrt(2.0 / math.pi)
    squared = value * value
    bend = jnp.tanh(root * value * (1.0 + 0.044715 * squared))
    half = 0.5 * (1.0 + bend)
    slope = half + 0.5 * value * (1.0 - bend * bend) * (root * (1.0 + 3 * 0.044715 * squared))
    return value * half, slope


def gelu_slope(value):
    root = math.sqrt(2.0 / math.pi)
    squared = value * value
    bend = jnp.tanh(root * value * (1.0 + 0.044715 * squared))
    return 0.5 * (1.0 + bend) + 0.5 * value * (1.0 - bend * bend) * root * (
        1.0 + 3 * 0.044715 * squared
    )


def backward_kernel(
    mid_grad_ref,
    one_ref,
    hidden_ref,
    mid_ref,
    gains_ref,
    query_ref,
    pre_ref,
    buckets_ref,
    small_ref,
    peak_ref,
    normed_hbm,
    attended_hbm,
    dense_rows_hbm,
    act_hbm,
    qkv0_hbm,
    qkv1_hbm,
    proj0_hbm,
    proj1_hbm,
    up_hbm,
    down_hbm,
    kv_hbm,
    probs_hbm,
    up_grad_hbm,
    hidden_grad_out,
    att_out,
    up_out,
    down_out,
    small_out,
    late_out,
    peak_out,
    expert_up_out,
    w_wide,
    w_up,
    w_down,
    sums,
    sums_core,
    sums_chips,
    kv,
    probs,
    xg,
    gx,
    gsrc,
    zb,
    zin,
    zb_down,
    zin_down,
    slopes,
    score_low,
    dk,
    cin,
    rin,
    attended_grad,
    layer_grad,
    biases,
    early,
    early_z,
    early_p,
    early_m,
    late,
    late_z,
    late_p,
    late_m,
    peak_z,
    peak_p,
    peak_m,
    gs,
    gr,
    xs,
    xr,
    zs,
    zr,
    dcs,
    dcr,
    drs,
    drr,
    szs,
    szr,
    sps,
    spr,
    us,
    ur,
    loads,
    sum_s,
    sum_r,
):
    p = Plane()
    e, s, core = p.e, p.s, p.core
    own_rows = row_block(e, T)

    def load(source, target, i):
        copy = pltpu.make_async_copy(source, target, loads.at[i])
        copy.start()
        return copy

    own_parts = [
        load(source, xg.at[n, own_rows, :], 11 + n)
        for n, source in enumerate(
            (normed_hbm.at[1], attended_hbm.at[1], normed_hbm.at[0], attended_hbm.at[0])
        )
    ]
    got_act = load(act_hbm, gx.at[3], 16)
    got_dense = load(dense_rows_hbm, xg.at[4], 9)
    greet([(d, s) for d in p.around] + [(e, other) for other in p.others])

    w_qkv = w_wide.at[:, : 3 * D]
    w_out = w_wide.at[:, 3 * D :]
    got_out = load(proj1_hbm, w_out, 0)
    got_kv = load(kv_hbm.at[1], kv, 2)
    got_probs = load(probs_hbm.at[1], probs, 3)
    got_qkv = load(qkv1_hbm, w_qkv, 1)
    got_down = load(down_hbm, w_down, 5)
    got_up = load(up_hbm, w_up, 4)

    peaks = SmallReduce(
        p, peak_ref, peak_z, peak_p, jnp.maximum, (szs.at[0], szr.at[0], sps.at[0], spr.at[0])
    )
    peaks.start()

    def rows_gather(n):
        return PlaneGather(
            p, lambda who: xg.at[n, row_block(who, T), :], gs.at[n], gr.at[n]
        )

    gathers = {n: rows_gather(n) for n in (0, 1, 2, 3, 5)}
    def exchange_start(j, source):
        gx[j, own_rows, :] = source[:, lane_block(e, 384)]
        for k, d in enumerate(p.around):
            p.push(
                source.at[:, lane_block(d, 384)],
                gx.at[j, own_rows, :],
                xs.at[j, k],
                xr.at[j, k],
                (d, s),
            )

    def exchange_wait(j):
        for k in range(7):
            p.arrived(gx.at[j, own_rows, :], xr.at[j, k])

    def out_gather(j, target, height):
        return PlaneGather(
            p, lambda who: target.at[pl.ds(who, 1)], gs.at[6 + j], gr.at[6 + j]
        )

    def z_start(j, tile, received, height):
        for i, k in enumerate(p.to_k):
            p.push(
                tile.at[row_block(p.near[i], height), :],
                received.at[k],
                zs.at[j, k],
                zr.at[j, k],
                (e, p.near[i]),
            )

    def z_finish(j, tile, received, height, target):
        total = tile[row_block(s, height), :].astype(single)
        for k in range(3):
            p.arrived(received.at[k], zr.at[j, k])
            total = total + received[k].astype(single)
        target[pl.ds(e, 1)] = total.astype(bfloat)[None]

    def tile_attention(layer):
        j = 1 - layer
        exchange_wait(j)
        rows = xg[2 * j + e // 6]
        zb[j] = dot_columns(rows, gx[j]).astype(bfloat)
        z_start(j, zb.at[j], zin.at[j], 192)

    def tile_up():
        zb[2] = dot_columns(xg[4], gx[2]).astype(bfloat)
        z_start(2, zb.at[2], zin.at[2], 192)

    def tile_down():
        zb_down[...] = dot_columns(gx[3], xg[5]).astype(bfloat)
        z_start(3, zb_down, zin_down, 96)

    gather_att1 = out_gather(0, att_out.at[1], 192)
    gather_att0 = out_gather(1, att_out.at[0], 192)
    gather_up = out_gather(2, up_out, 192)
    gather_down = out_gather(3, down_out, 96)

    scale = 1.0 / math.sqrt(HD)

    def attention(layer, upstream, work):
        j = 1 - layer
        grads = gsrc.at[j]
        branch = upstream.astype(bfloat)
        grads[:, 3 * D :] = branch
        got_out_now = got_out if layer == 1 else reloads["out"]
        got_out_now.wait()
        attended_grad[...] = dot_rows(branch, w_out[...]).astype(bfloat)
        if layer == 1:
            got_kv.wait()
            got_probs.wait()
        else:
            reloads["kv"].wait()
            reloads["probs"].wait()
            for copy in dk_sent:
                copy.wait_send()
            dk_sent.clear()

        def first_step(part):
            push(
                dk_sent,
                dk.at[part, 1 - core],
                cin.at[layer, part],
                dcs.at[layer, part],
                dcr.at[layer, part],
                (p.at_core, s),
            )

        def second_step(part):
            p.arrived(cin.at[layer, part], dcr.at[layer, part])
            for q in range(4):
                dk[part, core, q] = (
                    dk[part, core, q].astype(single) + cin[layer, part, q].astype(single)
                ).astype(bfloat)
            for k, d in enumerate((p.at_x, p.at_y, p.diagonal)):
                push(
                    dk_sent,
                    dk.at[part, core, d // 2],
                    rin.at[layer, part, k],
                    drs.at[layer, part, k],
                    drr.at[layer, part, k],
                    (d, s),
                )

        def third_step(part):
            total = dk[part, core, p.quarter].astype(single)
            for k in range(3):
                p.arrived(rin.at[layer, part, k], drr.at[layer, part, k])
                total = total + rin[layer, part, k].astype(single)
            turned = total.T.astype(bfloat)
            grads[:, D + 256 * part : D + 256 * (part + 1)] = turned[:, :256]
            grads[:, 2 * D + 256 * part : 2 * D + 256 * (part + 1)] = turned[:, 256:]

        if layer == 1:
            for copy in own_parts:
                copy.wait()
            gathers[0].first()
            gathers[1].first()

        for part in range(3):

            def one_pair(local_pair):
                pair = 2 * part + local_pair
                lanes = lane_block(pair, 128)
                lane = lax.broadcasted_iota(jnp.int32, (T, 128), 1)

                def split(value):
                    zero = jnp.zeros_like(value)
                    return jnp.concatenate(
                        [jnp.where(lane < HD, value, zero), jnp.where(lane >= HD, value, zero)]
                    )

                queries = split(query_ref[layer, :, lanes])
                outputs = split(attended_grad[:, lanes])
                keys = kv[part, :, lane_block(local_pair, 128)]
                values = kv[part, :, pl.ds(pl.multiple_of(256 + local_pair * 128, 128), 128)]
                slopes[...] = dot_rows(outputs, values)
                pair_rows = pl.ds(pl.multiple_of(pair * 2 * T, 2 * T), 2 * T)
                for half in range(2):
                    head = 2 * pair + half
                    gathered = jnp.zeros((8, TOE), single)
                    for rows in range(0, T, 32):
                        at = half * T + rows
                        prob = probs[
                            pl.ds(pl.multiple_of(head * T + rows, 32), 32), :
                        ].astype(single)
                        slope = slopes[at : at + 32, :]
                        inner = jnp.sum(prob * slope, axis=-1, keepdims=True)
                        low = (prob * (slope - inner)).astype(bfloat)
                        score_low[at : at + 32, :] = low
                        fold = jnp.concatenate(
                            [low.astype(single), jnp.zeros((32, TOE - low.shape[1]), single)],
                            axis=1,
                        )
                        fold = pltpu.roll(fold[:16], 16, 1) + fold[16:]
                        fold = pltpu.roll(fold[:8], 8, 1) + fold[8:]
                        if rows < T - 32:
                            fold = pltpu.roll(fold, T - 32 - rows, 1)
                        gathered = gathered + fold
                    fold = pltpu.roll(gathered[:4], 4, 1) + gathered[4:]
                    fold = pltpu.roll(fold[:2], 2, 1) + fold[2:]
                    fold = pltpu.roll(fold[:1], 1, 1) + fold[1:]
                    biases[pl.ds(layer * H + head, 1), :] = fold
                mixed = jnp.dot(score_low[...], keys, preferred_element_type=single) * scale
                grads[:, lanes] = jnp.where(lane < HD, mixed[:T], mixed[T:]).astype(bfloat)
                key_grad = dot_columns(queries, score_low[...]) * scale
                value_grad = dot_columns(outputs, probs[pair_rows, :])
                for d in range(8):
                    columns = slice(128 * d, 128 * (d + 1))
                    dk[
                        part, d % 2, d // 2, pl.ds(pl.multiple_of(local_pair * 128, 128), 128), :
                    ] = key_grad[:, columns].astype(bfloat)
                    dk[
                        part,
                        d % 2,
                        d // 2,
                        pl.ds(pl.multiple_of(256 + local_pair * 128, 128), 128),
                        :,
                    ] = value_grad[:, columns].astype(bfloat)

            loop(2, one_pair)
            first_step(part)
            if part > 0:
                second_step(part - 1)
            work[part]()
        second_step(2)
        third_step(0)
        work[3]()
        third_step(1)
        third_step(2)
        if layer == 0:
            exchange_start(j, gsrc.at[j])
        if layer == 1:
            got_qkv.wait()
        else:
            reloads["qkv"].wait()
        return dot_rows(gsrc[j, :, : 3 * D], w_qkv[...])

    dk_sent = []
    reloads = {}

    def part0():
        for i, k in enumerate(p.to_k):
            reshard.append(
                p.push(
                    up_grad_hbm.at[:, row_block(p.near[i], 192), :],
                    expert_up_out.at[:, :, lane_block(s, 768)],
                    us.at[k],
                    ur.at[k],
                    (e, p.near[i]),
                )
            )
        reshard_own.append(
            load(
                up_grad_hbm.at[:, row_block(s, 192), :],
                expert_up_out.at[:, :, lane_block(s, 768)],
                6,
            )
        )

    def part1():
        gathers[0].second()
        gathers[1].second()
        peaks.middle(peak_m)

    def part2():
        pass

    def part3():
        gathers[0].third()
        gathers[1].third()
        peaks.finish(peak_m, peak_out)

    reshard, reshard_own = [], []
    mid_grad = mid_grad_ref[...]
    normed_grad = attention(1, mid_grad, [part0, part1, part2, part3])
    reloads["kv"] = load(kv_hbm.at[0], kv, 7)
    reloads["probs"] = load(probs_hbm.at[0], probs, 8)
    reloads["out"] = load(proj0_hbm, w_out, 17)
    reloads["qkv"] = load(qkv0_hbm, w_qkv, 10)
    input_grad, gain_grad = norm_pull(one_ref[...], gains_ref[1:2, :], normed_grad)
    early[...] = small_ref[...]
    early[17:18, :] = gain_grad
    layer_grad[...] = mid_grad + input_grad
    branch = layer_grad[...].astype(bfloat)
    xg[5, own_rows, :] = branch
    gathers[5].first()
    got_down.wait()
    got_up.wait()
    gathers[5].second()
    gathers[5].third()
    gathers[5].done()
    reduce = PlaneSum(p, sums, sums_core, sums_chips, sum_s, sum_r)

    def units(c, q):
        rows = row_block(2 * q + c, T)
        act_grad = dot_rows(xg[5, rows, :], w_down[...])
        pre_grad = (act_grad * gelu_slope(pre_ref[rows, :])).astype(bfloat)
        gx[2, rows, :] = pre_grad
        sums[c, q] = dot_rows(pre_grad, w_up[...]).astype(bfloat)

    for q in range(4):
        units(1 - core, q)
    reduce.give()
    for q in range(4):
        units(core, q)
    reduce.pass_on()
    gathers[2].first()
    gathers[3].first()
    input_grad, gain_grad = norm_pull(mid_ref[...], gains_ref[2:3, :], reduce.result())
    early[18:19, :] = gain_grad
    layer_grad[...] = layer_grad[...] + input_grad
    small = SmallReduce(
        p, early, early_z, early_p, jnp.add, (szs.at[1], szr.at[1], sps.at[1], spr.at[1])
    )
    small.start()
    got_dense.wait()
    got_act.wait()

    def part4():
        exchange_start(0, gsrc.at[0])

    def part5():
        gathers[2].second()
        gathers[3].second()
        small.middle(early_m)

    def part6():
        tile_up()

    def part7():
        tile_down()
        gathers[0].done()
        gathers[1].done()
        tile_attention(1)
        gathers[2].third()
        gathers[3].third()

    normed_grad = attention(0, layer_grad[...], [part4, part5, part6, part7])
    input_grad, gain_grad = norm_pull(
        hidden_ref[...].astype(single), gains_ref[0:1, :], normed_grad
    )
    hidden_grad_out[...] = layer_grad[...] + input_grad
    late[...] = jnp.zeros_like(late)
    for i in range(6):
        late[i : i + 1, :] = gain_grad[:, 128 * i : 128 * (i + 1)]
    late[8:32, :NB] = lax.dot_general(
        biases[...],
        jnp.where(lax.broadcasted_iota(jnp.int32, (NB, TOE), 0) == buckets_ref[...], 1.0, 0.0),
        (((1,), (1,)), ((), ())),
        precision=lax.Precision.HIGHEST,
        preferred_element_type=single,
    )
    tail = SmallReduce(
        p, late, late_z, late_p, jnp.add, (szs.at[2], szr.at[2], sps.at[2], spr.at[2])
    )
    tail.start()
    z_finish(2, zb.at[2], zin.at[2], 192, up_out)
    gather_up.first()
    z_finish(3, zb_down, zin_down, 96, down_out)
    gather_down.first()
    z_finish(0, zb.at[0], zin.at[0], 192, att_out.at[1])
    gather_att1.first()
    gathers[2].done()
    gathers[3].done()
    tile_attention(0)
    tail.middle(late_m)
    small.finish(early_m, small_out)
    gather_att1.second()
    gather_up.second()
    gather_down.second()
    gather_att1.third()
    gather_up.third()
    gather_down.third()
    z_finish(1, zb.at[1], zin.at[1], 192, att_out.at[0])
    gather_att0.first()
    gather_att1.done()
    gather_up.done()
    gather_down.done()
    gather_att0.second()
    gather_att0.third()
    tail.finish(late_m, late_out)
    for copy in reshard:
        copy.wait_recv()
    reshard_own[0].wait()
    gather_att0.done()
    for copy in p.sent + dk_sent:
        copy.wait_send()


def backward(
    mid_grad, layer_one, hidden, mid, gains, normed, queries, attended, dense_rows, act, pre_act,
    buckets, small, peak_rows, weights, kv, probs, up_grad,
):
    length = T * lax.axis_size("expert")
    vmem = pl.BlockSpec(memory_space=VMEM)
    anywhere = pl.BlockSpec(memory_space=ANY)
    shape = jax.ShapeDtypeStruct
    ff = up_grad.shape[2] * 4
    sem = pltpu.SemaphoreType.DMA
    peak_shape, early_shape, late_shape = (2 * H, 128), small.shape, (32, 128)
    return pl.pallas_call(
        backward_kernel,
        name="backward_layers",
        out_shape=(
            shape((T, D), single),
            shape((2, 8, 192, 384), bfloat),
            shape((8, 192, 384), bfloat),
            shape((8, 96, D), bfloat),
            shape(early_shape, single),
            shape(late_shape, single),
            shape(peak_shape, single),
            shape((EXP_DEV, 192, ff), bfloat),
        ),
        in_specs=[vmem] * 10 + [anywhere] * 13,
        out_specs=(vmem,) * 7 + (anywhere,),
        scratch_shapes=[
            VMEM((D, 4 * D), bfloat),
            VMEM((D, 384), bfloat),
            VMEM((384, D), bfloat),
            VMEM((2, 4, T, D), bfloat),
            VMEM((4, T, D), bfloat),
            VMEM((3, T, D), bfloat),
            VMEM((3, length, 512), bfloat),
            VMEM((H * T, length), bfloat),
            VMEM((6, length, D), bfloat),
            VMEM((4, length, 384), bfloat),
            VMEM((2, T, 4 * D), bfloat),
            VMEM((3, D, 384), bfloat),
            VMEM((3, 3, 192, 384), bfloat),
            VMEM((384, D), bfloat),
            VMEM((3, 96, D), bfloat),
            VMEM((2 * T, length), single),
            VMEM((2 * T, length), bfloat),
            VMEM((3, 2, 4, 512, 128), bfloat),
            VMEM((2, 3, 4, 512, 128), bfloat),
            VMEM((2, 3, 3, 512, 128), bfloat),
            VMEM((T, D), bfloat),
            VMEM((T, D), single),
            VMEM((2 * H, TOE), single),
            VMEM(early_shape, single),
            VMEM((3,) + early_shape, single),
            VMEM((7,) + early_shape, single),
            VMEM(early_shape, single),
            VMEM(late_shape, single),
            VMEM((3,) + late_shape, single),
            VMEM((7,) + late_shape, single),
            VMEM(late_shape, single),
            VMEM((3,) + peak_shape, single),
            VMEM((7,) + peak_shape, single),
            VMEM(peak_shape, single),
            sem((10, 7)), sem((10, 7)),
            sem((4, 7)), sem((4, 7)),
            sem((4, 3)), sem((4, 3)),
            sem((2, 3)), sem((2, 3)),
            sem((2, 3, 3)), sem((2, 3, 3)),
            sem((3, 3)), sem((3, 3)),
            sem((3, 7)), sem((3, 7)),
            sem((3,)), sem((3,)),
            sem((18,)),
            sem((4,)), sem((4,)),
        ],
        compiler_params=pltpu.CompilerParams(
            collective_id=3, has_side_effects=True, vmem_limit_bytes=60 * 2**20
        ),
    )(
        mid_grad, layer_one, hidden, mid, gains, queries, pre_act, buckets, small, peak_rows,
        normed, attended, dense_rows.reshape(length, D), act, *weights, kv, probs, up_grad,
    )


def experts_kernel(
    normed_ref,
    mid_ref,
    gains_ref,
    router_turned_ref,
    slots_ref,
    own_cot_ref,
    cot_hbm,
    up_hbm,
    down_hbm,
    hidden_out,
    mid_grad_out,
    small_out,
    up_grad_hbm,
    down_grad_hbm,
    up_grad_out,
    down_grad_out,
    normed_all,
    cots,
    w_up,
    w_down,
    rows,
    gated,
    gates,
    acts,
    pre_grads,
    raw,
    row_send,
    out_send,
    row_back,
    out_back,
    out_ahead_in,
    slot_grads,
    slot_z,
    slot_sum,
    slot_plane,
    row_part,
    out_part,
    row_z,
    out_z,
    ns,
    nr,
    gs,
    gr,
    rs,
    rr,
    os,
    orr,
    ss,
    sr,
    ps,
    pr,
    rzs,
    rzr,
    ozs,
    ozr,
    loads,
    oas,
    oar,
):
    p = Plane()
    e, s = p.e, p.s
    groups = [s] + [lax.rem(s + 4 - k, 4) for k in range(1, 4)]

    def load(source, target, i):
        copy = pltpu.make_async_copy(source, target, loads.at[i])
        copy.start()
        return copy

    got_cots = [load(cot_hbm.at[groups[k]], cots.at[k], k) for k in range(2)]
    got_up = load(up_hbm, w_up, 4)
    got_down = load(down_hbm, w_down, 5)
    normed_all[s, e] = normed_ref[...]
    greet([(d, s) for d in p.around] + [(e, other) for other in p.others])
    mine = normed_all.at[s, e]
    for i, k in enumerate(p.to_k):
        p.push(mine, mine, ns.at[k], nr.at[k], (e, p.near[i]))

    def gather(k):
        g = groups[k]
        return PlaneGather(p, lambda who: normed_all.at[g, who], gs.at[k], gr.at[k])

    gathers = [gather(k) for k in range(4)]
    gathers[0].first()

    ids = 2 * e * CAP + lax.broadcasted_iota(jnp.int32, (2 * CAP, T), 0)
    expert_low = CAP * lax.broadcasted_iota(jnp.int32, (16, T), 0)

    def route_masks(g, who):
        both = slots_ref[g, who]
        first, second = both[:1], both[1:2]
        return first, second, ids == first, ids == second

    def select_cots(k):
        g = groups[k]
        got_cots[k].wait()

        def one(who):
            _, _, mark0, mark1 = route_masks(g, who)
            mark = jnp.where(mark0 | mark1, 1.0, 0.0).astype(bfloat)
            picked = jnp.dot(mark, cots[k % 2, who], preferred_element_type=single).astype(bfloat)
            for j in range(2):
                raw[j, g, row_block(who, CAP), :] = picked[j * CAP : (j + 1) * CAP]

        for who in range(8):
            one(who)
        if k < 2:
            got_cots.append(load(cot_hbm.at[groups[k + 2]], cots.at[k], k + 2))

    def select_rows(k):
        g = groups[k]

        def one(who):
            slot0, slot1, mark0, mark1 = route_masks(g, who)
            block = normed_all[g, who]
            mark = jnp.where(mark0 | mark1, 1.0, 0.0).astype(bfloat)
            picked = jnp.dot(mark, block, preferred_element_type=single).astype(bfloat)
            logits = dot_rows(router_turned_ref[...], block)
            chosen = [
                jnp.sum(
                    jnp.where((slot >= expert_low) & (slot < expert_low + CAP), logits, 0.0),
                    axis=0,
                    keepdims=True,
                )
                for slot in (slot0, slot1)
            ]
            top = jnp.maximum(chosen[0], chosen[1])
            weight = [jnp.exp(value - top) for value in chosen]
            total = weight[0] + weight[1]
            gate = jnp.sum(
                jnp.where(mark0, weight[0] / total, 0.0) + jnp.where(mark1, weight[1] / total, 0.0),
                axis=1,
                keepdims=True,
            )
            for j in range(2):
                part = slice(j * CAP, (j + 1) * CAP)
                rows[j, g, row_block(who, CAP), :] = picked[part]
                gates[j, g, row_block(who, CAP), :] = jnp.broadcast_to(gate[part], (CAP, 128))

        for who in range(8):
            one(who)

    def compute(k):
        g = groups[k]

        def one(j):
            before = jnp.dot(rows[j, g], w_up[j], preferred_element_type=single)
            act, slope = gelu_both(before)
            act = act.astype(bfloat)
            acts[j, g] = act
            gate = gates[j, g][:, :1]
            cot = raw[j, g].astype(single)
            weighted = (gate * cot).astype(bfloat)
            gated[j, g] = weighted
            act_grad = dot_rows(weighted, w_down[j])
            pre_grad = (act_grad * slope).astype(bfloat)
            pre_grads[j, g] = pre_grad
            row_grad = dot_rows(pre_grad, w_up[j])
            row_send[g, j] = row_grad.astype(bfloat).reshape(8, CAP, D)
            out = jnp.dot(act, w_down[j], preferred_element_type=single)
            out_send[g, j] = (gate * out).astype(bfloat).reshape(8, CAP, D)
            product = out * cot
            folded = product[:, :128]
            for i in range(1, D // 128):
                folded = folded + product[:, 128 * i : 128 * (i + 1)]
            slot_grads[g, j : j + 1, :] = jnp.sum(folded.T, axis=0, keepdims=True)

        for j in range(2):
            one(j)

    def give_back(k, source, target, send_sems, recv_sems):
        g = groups[k]
        slot = k if source is row_send else k // 2
        target[slot, e] = source[g, :, e]
        for i, d in enumerate(p.around):
            p.push(
                source.at[g, :, d], target.at[slot, e], send_sems.at[k, i], recv_sems.at[k, i],
                (d, s),
            )

    def out_ahead(k):
        g = groups[k]
        i = k // 2
        p.push(out_send.at[g], out_ahead_in.at[i], oas.at[i], oar.at[i], (e, g))

    def step(k):
        select_rows(k)
        compute(k)

    def arrive(k):
        p.arrived(mine, nr.at[k - 1])
        gathers[k].first()

    slot_grads[...] = jnp.zeros_like(slot_grads)
    select_cots(0)
    gathers[0].second()
    arrive(1)
    gathers[0].third()
    arrive(2)
    arrive(3)
    gathers[0].done()
    gathers[1].second()
    got_up.wait()
    got_down.wait()
    step(0)
    gathers[1].third()
    gathers[2].second()
    gathers[3].second()
    select_cots(1)
    gathers[1].done()
    step(1)
    give_back(1, row_send, row_back, rs, rr)
    out_ahead(1)
    gathers[2].third()
    gathers[3].third()
    select_cots(2)
    gathers[2].done()
    step(2)
    give_back(2, row_send, row_back, rs, rr)
    select_cots(3)
    gathers[3].done()
    step(3)
    give_back(3, row_send, row_back, rs, rr)
    give_back(2, out_send, out_back, os, orr)
    give_back(0, row_send, row_back, rs, rr)
    for k in range(3):
        p.push(
            slot_grads.at[p.others[k]], slot_z.at[k], ss.at[k], sr.at[k], (e, p.others[k])
        )

    out_ahead(3)

    def weight_grads(i):
        j = i // 3
        lanes = lane_block(lax.rem(i, 3), 256)
        inputs = rows[j].reshape(4 * 8 * CAP, D)
        up_grad_out[j, :, lanes] = dot_columns(
            inputs, pre_grads[j, :, :, lanes].reshape(4 * 8 * CAP, 256)
        ).astype(bfloat)
        inputs = acts[j].reshape(4 * 8 * CAP, -1)
        down_grad_out[j, :, lanes] = dot_columns(
            inputs, gated[j, :, :, lanes].reshape(4 * 8 * CAP, 256)
        ).astype(bfloat)

    loop(3, weight_grads)
    total = slot_grads[s]
    for k in range(3):
        p.arrived(slot_z.at[k], sr.at[k])
        total = total + slot_z[k]
    slot_sum[...] = total
    slot_plane[e] = total
    for i, d in enumerate(p.around):
        p.push(slot_sum, slot_plane.at[e], ps.at[i], pr.at[i], (d, s))

    slot_lanes = lax.broadcasted_iota(jnp.int32, (T, 16 * CAP), 1)

    def slot_columns(g):
        return slots_ref[g, e].astype(single).T.astype(jnp.int32)

    def collect(k, back, recv_sems, part, z_in, z_send, z_recv):
        g = groups[k]
        slot = k if back is row_back else k // 2
        for i in range(7):
            p.arrived(back.at[slot, e], recv_sems.at[k, i])
        columns = slot_columns(g)
        marks = jnp.where(
            (columns[:, :1] == slot_lanes) | (columns[:, 1:2] == slot_lanes), 1.0, 0.0
        ).astype(bfloat)
        combined = jnp.dot(
            marks, back[slot].reshape(16 * CAP, D), preferred_element_type=single
        )
        part[slot] = combined.astype(bfloat)
        if k:
            i = k - 1 if back is row_back else 0
            p.push(part.at[slot], z_in.at[i], z_send.at[i], z_recv.at[i], (e, g))

    for k in (1, 2, 3):
        collect(k, row_back, rr, row_part, row_z, rzs, rzr)

    for i in range(2):
        p.arrived(out_ahead_in.at[i], oar.at[i])
    for j in range(2):
        out_send[s, j] = (
            out_send[s, j].astype(single)
            + out_ahead_in[0, j].astype(single)
            + out_ahead_in[1, j].astype(single)
        ).astype(bfloat)
    give_back(0, out_send, out_back, os, orr)

    def weight_later(i):
        weight_grads(i + 3)

    loop(3, weight_later)
    leaving = [load(up_grad_out, up_grad_hbm, 6), load(down_grad_out, down_grad_hbm, 7)]

    for i in range(7):
        p.arrived(slot_sum, pr.at[i])
    turned = pltpu.roll(
        slot_plane[...].reshape(64, 8 * CAP), lax.rem(8 * CAP - CAP * e, 8 * CAP), 1
    )
    logits = dot_rows(normed_ref[...], router_turned_ref[...])
    columns = slot_columns(s)
    expert_lanes = CAP * lax.broadcasted_iota(jnp.int32, (T, 16), 1)
    picks, chosen, grads = [], [], []
    small_lanes = lax.broadcasted_iota(jnp.int32, (T, CAP), 1)
    for r in range(2):
        slot = columns[:, r : r + 1]
        picks.append((slot >= expert_lanes) & (slot < expert_lanes + CAP))
        chosen.append(jnp.sum(jnp.where(picks[r], logits, 0.0), axis=1, keepdims=True))
        found = jnp.zeros((T, CAP), single)
        for who in range(8):
            for j in range(2):
                values = turned[8 * who + j : 8 * who + j + 1, :CAP]
                found = found + jnp.where(slot - (2 * who + j) * CAP == small_lanes, values, 0.0)
        grads.append(jnp.sum(found, axis=1, keepdims=True))
    top = jnp.maximum(chosen[0], chosen[1])
    weight = [jnp.exp(value - top) for value in chosen]
    total = weight[0] + weight[1]
    weight = [value / total for value in weight]
    mean = weight[0] * grads[0] + weight[1] * grads[1]
    logit_grad = jnp.zeros((T, 16), single)
    for r in range(2):
        logit_grad = logit_grad + jnp.where(picks[r], weight[r] * (grads[r] - mean), 0.0)
    logit_grad = logit_grad.astype(bfloat)
    small_out[...] = jnp.zeros_like(small_out)
    small_out[:16, :] = dot_columns(logit_grad, normed_ref[...])
    normed_grad = jnp.dot(logit_grad, router_turned_ref[...], preferred_element_type=single)
    collect(2, out_back, orr, out_part, out_z, ozs, ozr)
    collect(0, row_back, rr, row_part, row_z, rzs, rzr)
    normed_grad = normed_grad + row_part[0].astype(single)
    for k in range(3):
        p.arrived(row_z.at[k], rzr.at[k])
        normed_grad = normed_grad + row_z[k].astype(single)
    input_grad, gain_grad = norm_pull(mid_ref[...], gains_ref[3:4, :], normed_grad)
    small_out[16:17, :] = gain_grad
    mid_grad_out[...] = own_cot_ref[...].astype(single) + input_grad

    collect(0, out_back, orr, out_part, out_z, ozs, ozr)
    p.arrived(out_z.at[0], ozr.at[0])
    result = mid_ref[...] + out_part[0].astype(single) + out_z[0].astype(single)
    hidden_out[...] = result.astype(bfloat)
    for copy in leaving:
        copy.wait()
    for copy in p.sent:
        copy.wait_send()


def run_experts(
    moe_normed, mid, gains, router, slots, own_cot, cots, up_own, expert_down
):
    vmem = pl.BlockSpec(memory_space=VMEM)
    anywhere = pl.BlockSpec(memory_space=ANY)
    shape = jax.ShapeDtypeStruct
    width = expert_down.shape[1]
    sem = pltpu.SemaphoreType.DMA
    per_expert = (EXP_DEV, 4, 8 * CAP)
    sends = (4, EXP_DEV, 8, CAP, D)
    backs = (4, 8, EXP_DEV, CAP, D)
    return pl.pallas_call(
        experts_kernel,
        name="experts",
        out_shape=(
            shape((T, D), bfloat),
            shape((T, D), single),
            shape((24, D), single),
            shape((EXP_DEV, D, width), bfloat),
            shape((EXP_DEV, width, D), bfloat),
        ),
        in_specs=[vmem] * 6 + [anywhere] * 3,
        out_specs=(vmem,) * 3 + (anywhere,) * 2,
        scratch_shapes=[
            VMEM((EXP_DEV, D, width), bfloat),
            VMEM((EXP_DEV, width, D), bfloat),
            VMEM((4, 8, T, D), bfloat),
            VMEM((2, 8, T, D), bfloat),
            VMEM((EXP_DEV, D, width), bfloat),
            VMEM((EXP_DEV, width, D), bfloat),
            VMEM(per_expert + (D,), bfloat),
            VMEM(per_expert + (D,), bfloat),
            VMEM(per_expert + (128,), single),
            VMEM(per_expert + (width,), bfloat),
            VMEM(per_expert + (width,), bfloat),
            VMEM(per_expert + (D,), bfloat),
            VMEM(sends, bfloat),
            VMEM(sends, bfloat),
            VMEM(backs, bfloat),
            VMEM((2,) + backs[1:], bfloat),
            VMEM((2,) + sends[1:], bfloat),
            VMEM((4, 8, 8 * CAP), single),
            VMEM((3, 8, 8 * CAP), single),
            VMEM((8, 8 * CAP), single),
            VMEM((8, 8, 8 * CAP), single),
            VMEM((4, T, D), bfloat),
            VMEM((2, T, D), bfloat),
            VMEM((3, T, D), bfloat),
            VMEM((1, T, D), bfloat),
            sem((3,)), sem((3,)),
            sem((4, 7)), sem((4, 7)),
            sem((4, 7)), sem((4, 7)),
            sem((4, 7)), sem((4, 7)),
            sem((3,)), sem((3,)),
            sem((7,)), sem((7,)),
            sem((3,)), sem((3,)),
            sem((3,)), sem((3,)),
            sem((8,)),
            sem((2,)), sem((2,)),
        ],
        compiler_params=pltpu.CompilerParams(
            collective_id=4, has_side_effects=True, vmem_limit_bytes=60 * 2**20
        ),
    )(
        moe_normed, mid, gains, router, slots, own_cot, cots, up_own, expert_down
    )


def finish_kernel(
    att_hbm,
    up_hbm,
    down_hbm,
    expert_up_hbm,
    expert_down_hbm,
    small_hbm,
    late_hbm,
    peak_hbm,
    grad_hbm,
    result_hbm,
    qkv_out,
    out_out,
    up_out,
    down_out,
    expert_up_out,
    expert_down_out,
    attn_gain_out,
    mlp_gain_out,
    bias_out,
    router_out,
    clip_out,
    grad_out,
    result_out,
    att,
    up,
    down,
    expert_up,
    expert_down,
    small_ref,
    late_ref,
    peak_ref,
    grad,
    qkv_wide,
    out_wide,
    up_wide,
    down_wide,
    expert_up_wide,
    expert_down_wide,
    turned,
    in_sems,
    out_sems,
):
    s = lax.axis_index("shard")

    def start(source, target, sem):
        copy = pltpu.make_async_copy(source, target, sem)
        copy.start()
        return copy

    got = [
        start(source, target, in_sems.at[i])
        for i, (source, target) in enumerate(
            (
                (expert_down_hbm, expert_down),
                (expert_up_hbm, expert_up),
                (att_hbm, att),
                (up_hbm, up),
                (down_hbm, down),
                (grad_hbm, grad),
                (small_hbm, small_ref),
                (late_hbm, late_ref),
                (peak_hbm, peak_ref),
                (result_hbm, result_out),
            )
        )
    ]
    put = []

    def widen(i):
        rows = row_block(i, 128)
        for j in range(EXP_DEV):
            expert_down_wide[j, rows, :] = expert_down[j, rows, :].astype(single)

    def widen_up(i):
        lanes = lane_block(i, 384)
        for j in range(EXP_DEV):
            expert_up_wide[j, :, lanes] = expert_up[j, :, lanes].astype(single)

    def widen_down(i):
        down_wide[row_block(i, 96), :] = down[i].astype(single)

    got[0].wait()
    loop(expert_down.shape[1] // 128, widen)
    put.append(start(expert_down_wide, expert_down_out, out_sems.at[0]))
    got[1].wait()
    loop(expert_up.shape[2] // 384, widen_up)
    put.append(start(expert_up_wide, expert_up_out, out_sems.at[1]))
    got[2].wait()
    for layer in range(2):
        for b in range(6):
            qkv_wide[layer, :, 384 * b : 384 * (b + 1)] = att[layer, b].astype(single)
        for b in range(2):
            out_wide[layer, :, 384 * b : 384 * (b + 1)] = att[layer, 6 + b].astype(single)
    put.append(start(qkv_wide, qkv_out, out_sems.at[2]))
    put.append(start(out_wide, out_out, out_sems.at[3]))
    got[3].wait()
    for b in range(8):
        for z in range(4):
            up_wide[:, 768 * z + 96 * b : 768 * z + 96 * (b + 1)] = up[
                b, :, 96 * z : 96 * (z + 1)
            ].astype(single)
    put.append(start(up_wide, up_out, out_sems.at[4]))
    got[4].wait()
    loop(8, widen_down)
    put.append(start(down_wide, down_out, out_sems.at[5]))

    for copy in got[5:]:
        copy.wait()
    grad_out[...] = grad[...][:, None, :]
    part = D // 4
    back = lax.rem(D - part * s, D)
    first_gain = jnp.concatenate([late_ref[i : i + 1, :] for i in range(6)], axis=1)
    gains = jnp.concatenate([first_gain, small_ref[16:19, :], jnp.zeros((4, D), single)])
    gains = pltpu.roll(gains, back, 1)[:, :part]
    attn_gain_out[0:1, :] = gains[0:1]
    attn_gain_out[1:2, :] = gains[2:3]
    mlp_gain_out[0:1, :] = gains[3:4]
    mlp_gain_out[1:2, :] = gains[1:2]
    turned[:, :16] = small_ref[:16, :].T
    router_out[...] = turned[row_block(s, part), :16].T
    turned[:128, : 2 * H] = late_ref[8:32, :].T
    biases = turned[row_block(s, 8), : 2 * H]
    peaks = peak_ref[...].T[:1, :]
    clips = jnp.sqrt(clip_limit / jnp.maximum(peaks, clip_limit))
    for layer in range(2):
        bias_out[layer] = biases[:, layer * H : (layer + 1) * H]
        clip_out[layer : layer + 1, :] = clips[:, layer * H : (layer + 1) * H]
    for copy in put:
        copy.wait()


def finish(att, up, down, expert_up, expert_down, small, late, peaks, grad, result):
    vmem = pl.BlockSpec(memory_space=VMEM)
    anywhere = pl.BlockSpec(memory_space=ANY)
    loaded = (att, up, down, expert_up, expert_down, small, late, peaks, grad)
    sem = pltpu.SemaphoreType.DMA
    wide = (
        (2, 192, 3 * D), (2, 192, D), (192, 8 * 384), (8 * 96, D), expert_up.shape,
        expert_down.shape,
    )
    return pl.pallas_call(
        finish_kernel,
        name="finish",
        out_shape=tuple(
            jax.ShapeDtypeStruct(dims, single)
            for dims in wide + ((2, 192), (2, 192), (2, 8, H), (16, 192), (2, H), (T, 1, D))
        )
        + (jax.ShapeDtypeStruct(result.shape, bfloat),),
        in_specs=[anywhere] * 10,
        out_specs=(anywhere,) * 6 + (vmem,) * 7,
        scratch_shapes=[VMEM(item.shape, item.dtype) for item in loaded]
        + [VMEM(dims, single) for dims in wide]
        + [VMEM((D, 128), single), sem((10,)), sem((6,))],
        compiler_params=pltpu.CompilerParams(vmem_limit_bytes=60 * 2**20),
    )(*loaded, result)


def shards(
    hidden_in,
    attn_gain,
    qkv_weight,
    out_weight,
    rel_bias,
    bucket_table,
    mlp_gain,
    mlp_up,
    mlp_down,
    router_weight,
    expert_up,
    expert_down,
    routes,
    out_grad,
):
    block_rows = hidden_in.shape[1]
    length = bucket_table.shape[0]
    groups = lax.axis_size("shard")

    backward_table = jnp.pad(bucket_table[::-1], (0, TOE))
    buckets = lax.dynamic_slice_in_dim(
        backward_table, length - block_rows * (lax.axis_index("expert") + 1), TOE
    )[None]
    cotangent = out_grad.reshape(block_rows, D)
    (
        normed, queries, attended, mid_first, mid_second, dense_normed, layer_one, peak_rows,
        moe_normed, gains, router, slots, qkv0, qkv1, projection0, projection1, dense_up,
        dense_down, kv, probs, up_own, cotangents, dense_rows, pre_act, activation,
    ) = forward(
        hidden_in.reshape(block_rows, D), attn_gain, mlp_gain, rel_bias, router_weight.T, buckets,
        routes.reshape(block_rows, 2).T,
        qkv_weight, out_weight, mlp_up, mlp_down, expert_up, cotangent,
    )
    hidden_out, mid_grad, small_in, up_grad, expert_down_low = run_experts(
        moe_normed, mid_second, gains, router, slots, cotangent, cotangents, up_own, expert_down,
    )
    hidden_grad, attention_sum, up_sum, down_sum, small_sum, late_sum, peaks, expert_up_low = (
        backward(
            mid_grad, layer_one, hidden_in.reshape(block_rows, D), mid_first, gains, normed, queries,
            attended, dense_rows, activation, pre_act, buckets, small_in, peak_rows,
            (qkv0, qkv1, projection0, projection1, dense_up, dense_down), kv, probs,
            up_grad,
        )
    )
    (
        qkv_grad, out_weight_grad, mlp_up_grad, mlp_down_grad, expert_up_grad, expert_down_grad,
        attn_gain_grad, mlp_gain_grad, rel_bias_grad, router_grad, clip_scales, hidden_grad, hidden_out,
    ) = finish(
        attention_sum, up_sum, down_sum, expert_up_low, expert_down_low, small_sum, late_sum, peaks,
        hidden_grad, hidden_out,
    )
    return (
        hidden_out.reshape(hidden_in.shape),
        hidden_grad.reshape(hidden_in.shape),
        attn_gain_grad,
        qkv_grad,
        out_weight_grad,
        rel_bias_grad,
        mlp_gain_grad,
        mlp_up_grad,
        mlp_down_grad,
        router_grad.T,
        expert_up_grad,
        expert_down_grad,
        clip_scales,
    )


def solution(mesh):
    tokens = P("shard", "expert", None, None)
    columns = P(None, "shard")
    layers = P(None, "shard", None)
    rows = P("shard", None)
    owned = P("expert", "shard", None)
    in_specs = (
        tokens, columns, layers, layers, layers, P(), columns, rows, rows, rows, owned, owned,
        tokens, tokens,
    )
    out_specs = (
        tokens, tokens, columns, layers, layers, layers, columns, rows, rows, rows, owned, owned,
        P(),
    )
    sized = mesh.shape["expert"] == 8 and mesh.shape["shard"] == 4
    part = shards if sized else plain_shards
    return jax.shard_map(part, mesh=mesh, in_specs=in_specs, out_specs=out_specs, check_vma=False)
```

```python
import functools
import math

import jax
import jax.numpy as jnp
from jax import lax
from jax.experimental import pallas as pl
from jax.experimental.pallas import tpu as pltpu
from jax.sharding import PartitionSpec as P

D = 768
H = 12
HD = 64
NB = 32
EXP_DEV = 2

epsilon = 1e-06
clip_limit = 6.0
bfloat = jnp.bfloat16
single = jnp.float32


def rms_norm(inputs, norm_gain):
    return (
        inputs * lax.rsqrt(jnp.mean(inputs * inputs, axis=-1, keepdims=True) + epsilon) * norm_gain
    )


def norm_back(inputs, norm_gain, upstream):
    _, pullback = jax.vjp(rms_norm, inputs, norm_gain)
    return pullback(upstream)


def gelu_back(pre_values, upstream):
    _, pullback = jax.vjp(jax.nn.gelu, pre_values)
    return pullback(upstream)[0]


def matmul(left, right):
    return jnp.dot(left, right, preferred_element_type=single)


def shard_shift(block, amount):
    count = lax.axis_size("shard")
    return lax.ppermute(block, "shard", [(i, (i + amount) % count) for i in range(count)])


def gather_shard(block):
    count = lax.axis_size("shard")
    here = lax.axis_index("shard")
    result = jnp.zeros((count,) + block.shape, block.dtype)
    for step in range(count):
        piece = block if step == 0 else shard_shift(block, step)
        result = lax.dynamic_update_slice_in_dim(result, piece[None], (here - step) % count, 0)
    return result


def scatter_shard(blocks, sent=bfloat):
    count = lax.axis_size("shard")
    here = lax.axis_index("shard")
    total = lax.dynamic_index_in_dim(blocks, here, 0, keepdims=False).astype(single)
    for step in range(1, count):
        part = lax.dynamic_index_in_dim(blocks, (here + step) % count, 0, keepdims=False)
        total = total + shard_shift(part.astype(sent), step).astype(single)
    return total


def spread(columns):
    experts, shard_count = lax.axis_size("expert"), lax.axis_size("shard")
    rows, width = columns.shape
    cut = columns.reshape(rows, shard_count, experts, width // (shard_count * experts))
    return cut.transpose(0, 2, 1, 3).reshape(rows, width)


def unspread(columns):
    experts, shard_count = lax.axis_size("expert"), lax.axis_size("shard")
    rows, width = columns.shape
    cut = columns.reshape(rows, experts, shard_count, width // (shard_count * experts))
    return cut.transpose(0, 2, 1, 3).reshape(rows, width)


def gather_weight(block):
    part = block.shape[0] // lax.axis_size("expert")
    own = lax.dynamic_slice_in_dim(block, lax.axis_index("expert") * part, part, 0)
    column = gather_shard(own).reshape(-1, block.shape[1])
    return lax.all_gather(column, "expert", axis=0, tiled=True)


def reduce_weight(grad):
    part = lax.psum_scatter(grad.astype(bfloat), "expert", scatter_dimension=0, tiled=True)
    blocks = part.reshape((lax.axis_size("shard"), -1) + part.shape[1:])
    own = scatter_shard(blocks).astype(bfloat)
    return lax.all_gather(own, "expert", axis=0, tiled=True).astype(single)


def bucket_marks(distance, lower, upper):
    inside = (distance[None] >= lower[:, None, None]) & (distance[None] < upper[:, None, None])
    return inside.astype(bfloat)


def position_bias(marks, bias_pair):
    return jnp.einsum("bij,bh->hij", marks, bias_pair, preferred_element_type=single)


def attention_forward(hidden, norm_gain, qkv, projection, bias_pair, geometry):
    distance, marks, scale = geometry
    rows = hidden.shape[0]
    normalized = spread(rms_norm(hidden, norm_gain).astype(bfloat))
    packed = matmul(normalized, qkv).astype(bfloat)
    key_value = lax.all_gather(packed[:, D:], "expert", axis=0, tiled=True)
    shifted = position_bias(marks, bias_pair)
    causal = distance >= 0
    queries = packed[:, :D].reshape(rows, H, HD)
    keys = key_value[:, :D].reshape(-1, H, HD)
    values = key_value[:, D:].reshape(-1, H, HD)
    raw_scores = jnp.einsum("ihd,jhd->hij", queries, keys, preferred_element_type=single) * scale
    head_peak = jnp.max(jnp.where(causal[None], raw_scores, -jnp.inf), axis=(1, 2))
    masked = jnp.where(causal[None], raw_scores + shifted, -jnp.inf)
    softmax_top = jnp.max(masked, axis=-1, keepdims=True)
    exponent = jnp.exp(masked - softmax_top)
    softmax_sum = jnp.sum(exponent, axis=-1, keepdims=True)
    probs = (exponent / softmax_sum).astype(bfloat)
    log_total = softmax_top[..., 0] + jnp.log(softmax_sum[..., 0])
    attended = jnp.einsum("hij,jhd->ihd", probs, values, preferred_element_type=single)
    attended = spread(attended.astype(bfloat).reshape(rows, D))
    saved = (normalized, packed, key_value, log_total, attended)
    return hidden + matmul(attended, projection), head_peak, saved


def attention_backward(
    upstream, hidden, norm_gain, qkv, projection, bias_pair, geometry, saved
):
    distance, marks, scale = geometry
    normalized, packed, key_value, log_total, attended = saved
    rows = hidden.shape[0]
    branch_grad = upstream.astype(bfloat)
    projection_grad = matmul(attended.T, branch_grad)
    attended_grad = unspread(matmul(branch_grad, projection.T).astype(bfloat))
    shifted = position_bias(marks, bias_pair)
    causal = distance >= 0
    queries = packed[:, :D].reshape(rows, H, HD)
    keys = key_value[:, :D].reshape(-1, H, HD)
    values = key_value[:, D:].reshape(-1, H, HD)
    grad_heads = attended_grad.reshape(rows, H, HD)
    raw_scores = jnp.einsum("ihd,jhd->hij", queries, keys, preferred_element_type=single) * scale
    probs = jnp.where(causal[None], jnp.exp(raw_scores + shifted - log_total[..., None]), 0.0)
    prob_grad = jnp.einsum("ihd,jhd->hij", grad_heads, values, preferred_element_type=single)
    row_dot = jnp.sum(prob_grad * probs, axis=-1)
    score_grad = (probs * (prob_grad - row_dot[..., None])).astype(bfloat)
    query_grad = jnp.einsum("hij,jhd->ihd", score_grad, keys, preferred_element_type=single) * scale
    query_grad = query_grad.astype(bfloat).reshape(rows, D)
    bias_grad = jnp.einsum("hij,bij->bh", score_grad, marks, preferred_element_type=single)
    key_grad = (
        jnp.einsum("hij,ihd->jhd", score_grad, queries, preferred_element_type=single) * scale
    )
    value_grad = jnp.einsum(
        "hij,ihd->jhd", probs.astype(bfloat), grad_heads, preferred_element_type=single
    )
    pair = jnp.concatenate([key_grad.reshape(-1, D), value_grad.reshape(-1, D)], axis=-1)
    pair_grad = lax.psum_scatter(pair.astype(bfloat), "expert", scatter_dimension=0, tiled=True)
    packed_grad = jnp.concatenate([query_grad, pair_grad], axis=-1)
    qkv_grad = matmul(normalized.T, packed_grad)
    normed_grad = unspread(matmul(packed_grad, qkv.T))
    input_grad, gain_grad = norm_back(hidden, norm_gain, normed_grad)
    return upstream + input_grad, gain_grad, qkv_grad, projection_grad, bias_grad


def exchange(blocks):
    return lax.all_to_all(blocks, "expert", split_axis=0, concat_axis=0, tiled=True)


def plain_shards(
    hidden_in,
    attn_gain,
    qkv_weight,
    out_weight,
    rel_bias,
    bucket_table,
    mlp_gain,
    mlp_up,
    mlp_down,
    router_weight,
    expert_up,
    expert_down,
    routes,
    out_grad,
):
    block_rows = hidden_in.shape[1]
    length = bucket_table.shape[0]
    experts = lax.axis_size("expert")
    groups = lax.axis_size("shard")
    here = lax.axis_index("shard")
    expert_total = EXP_DEV * experts
    capacity = 4 * block_rows // expert_total
    width = expert_down.shape[1]
    scale = 1.0 / math.sqrt(HD)

    small = jnp.concatenate(
        [attn_gain.reshape(-1), mlp_gain.reshape(-1), rel_bias.reshape(-1), router_weight.reshape(-1)]
    )
    small = gather_shard(small)
    part = D // groups
    cuts = [0, 2 * part, 4 * part, 4 * part + 2 * (NB // groups) * H, small.shape[1]]
    gain_attn, gain_mlp, bias_weights, router_full = (
        small[:, cuts[i] : cuts[i + 1]] for i in range(4)
    )
    gain_attn = gain_attn.reshape(groups, 2, part).transpose(1, 0, 2).reshape(2, D).astype(single)
    gain_mlp = gain_mlp.reshape(groups, 2, part).transpose(1, 0, 2).reshape(2, D).astype(single)
    bias_weights = (
        bias_weights.reshape(groups, 2, NB // groups, H).transpose(1, 0, 2, 3).reshape(2, NB, H)
    )
    router_full = router_full.reshape(D, expert_total)

    first = gather_weight(jnp.concatenate([qkv_weight[0], out_weight[0]], axis=1))
    dense_up = gather_weight(mlp_up)
    dense_down = gather_weight(mlp_down)
    second = gather_weight(jnp.concatenate([qkv_weight[1], out_weight[1]], axis=1))
    qkv = (first[:, : 3 * D], second[:, : 3 * D])
    projection = (first[:, 3 * D :], second[:, 3 * D :])

    up_own = jnp.zeros((EXP_DEV, groups, part, width), bfloat)
    for step in range(groups):
        target = (here + step) % groups
        piece = lax.dynamic_slice_in_dim(expert_up, target * width, width, 2)
        if step:
            piece = shard_shift(piece, step)
        up_own = lax.dynamic_update_slice_in_dim(up_own, piece[:, None], (here - step) % groups, 1)
    up_own = up_own.reshape(EXP_DEV, D, width)

    route_rows = gather_shard(routes.reshape(block_rows, 2))
    upstream_all = gather_shard(out_grad.reshape(block_rows, D))
    expert_ids = jnp.arange(expert_total, dtype=jnp.int32)
    flat_routes = route_rows.reshape(groups, -1)
    marks = (flat_routes[:, :, None] == expert_ids).astype(jnp.int32)
    rank = jnp.sum((jnp.cumsum(marks, axis=1) - marks) * marks, axis=2)
    slot_of_route = flat_routes * capacity + rank
    slot_ids = jnp.arange(expert_total * capacity, dtype=jnp.int32)
    slot_marks = (slot_of_route[:, :, None] == slot_ids).astype(bfloat)
    token_marks = jnp.sum(
        slot_marks.reshape(groups, block_rows, 2, -1).astype(single), axis=2
    ).astype(bfloat)

    def dispatch(rows):
        slots = jnp.einsum("gts,gtd->gsd", token_marks, rows, preferred_element_type=single)
        slots = slots.astype(bfloat).reshape(groups, experts, EXP_DEV, capacity, D)
        return exchange(slots.transpose(1, 2, 0, 3, 4)).reshape(
            experts, EXP_DEV, groups * capacity, D
        )

    def collect(blocks):
        back = exchange(blocks.astype(bfloat)).reshape(experts, EXP_DEV, groups, capacity, D)
        return back.transpose(2, 0, 1, 3, 4).reshape(groups, expert_total * capacity, D)

    owner_rows = dispatch(upstream_all)

    own_positions = lax.axis_index("expert") * block_rows + jnp.arange(block_rows, dtype=jnp.int32)
    distance = own_positions[:, None] - jnp.arange(length, dtype=jnp.int32)[None, :]
    bounds = jnp.sum(
        (bucket_table[:, None] < jnp.arange(NB + 1, dtype=jnp.int32)[None, :]).astype(jnp.int32),
        axis=0,
    )
    geometry = (distance, bucket_marks(distance, bounds[:NB], bounds[1:]), scale)

    hidden_zero = hidden_in.reshape(block_rows, D).astype(single)
    mid_first, peak_first, saved_first = attention_forward(
        hidden_zero, gain_attn[0], qkv[0], projection[0], bias_weights[0], geometry
    )
    dense_normed = spread(rms_norm(mid_first, gain_mlp[0]).astype(bfloat))
    pre_act = matmul(dense_normed, dense_up)
    activation = spread(jax.nn.gelu(pre_act).astype(bfloat))
    layer_one = mid_first + matmul(activation, dense_down)
    mid_second, peak_second, saved_second = attention_forward(
        layer_one, gain_attn[1], qkv[1], projection[1], bias_weights[1], geometry
    )

    moe_normed = rms_norm(mid_second, gain_mlp[1]).astype(bfloat)
    normed_all = gather_shard(moe_normed)
    received = dispatch(normed_all)
    router_logits = jnp.einsum("gtd,de->gte", normed_all, router_full, preferred_element_type=single)
    selected = (route_rows[..., None] == expert_ids).astype(single)
    gates_all = jax.nn.softmax(jnp.sum(selected * router_logits[:, :, None, :], axis=-1), axis=-1)
    slot_gates = jnp.sum(
        gates_all.reshape(groups, -1)[:, :, None] * (slot_of_route[:, :, None] == slot_ids), axis=1
    )
    owner_gates = exchange(
        slot_gates.reshape(groups, experts, EXP_DEV, capacity).transpose(1, 2, 0, 3)
    ).reshape(experts, EXP_DEV, groups * capacity)

    expert_pre = jnp.einsum("sjcd,jdf->sjcf", received, up_own, preferred_element_type=single)
    expert_act = jax.nn.gelu(expert_pre).astype(bfloat)
    expert_out = jnp.einsum(
        "sjcf,jfd->sjcd", expert_act, expert_down, preferred_element_type=single
    )
    owner_grad = (owner_gates[..., None] * owner_rows.astype(single)).astype(bfloat)
    act_grad = jnp.einsum("sjcd,jfd->sjcf", owner_grad, expert_down, preferred_element_type=single)
    pre_grad = gelu_back(expert_pre, act_grad).astype(bfloat)
    row_grad = jnp.einsum("sjcf,jdf->sjcd", pre_grad, up_own, preferred_element_type=single)

    returned = collect(expert_out)
    back_rows = collect(row_grad)
    expert_down_grad = jnp.einsum(
        "sjcf,sjcd->jfd", expert_act, owner_grad, preferred_element_type=single
    )
    up_grad = jnp.einsum(
        "sjcd,sjcf->jdf", received, pre_grad, preferred_element_type=single
    ).astype(bfloat)

    route_out = jnp.einsum("grs,gsd->grd", slot_marks, returned, preferred_element_type=single)
    route_out = route_out.reshape(groups, block_rows, 2, D)
    gate_grad = scatter_shard(
        jnp.sum(route_out * upstream_all[:, :, None, :].astype(single), axis=-1), single
    )
    mixed = scatter_shard(jnp.sum(gates_all[..., None] * route_out, axis=2))
    hidden_out = (mid_second + mixed).astype(bfloat).reshape(hidden_in.shape)

    gates = lax.dynamic_index_in_dim(gates_all, here, 0, keepdims=False)
    own_selected = lax.dynamic_index_in_dim(selected, here, 0, keepdims=False)
    upstream = out_grad.reshape(block_rows, D).astype(single)
    chosen_grad = gates * (gate_grad - jnp.sum(gates * gate_grad, axis=-1, keepdims=True))
    logit_grad = jnp.sum(chosen_grad[:, :, None] * own_selected, axis=1).astype(bfloat)
    router_grad = matmul(moe_normed.T, logit_grad)
    row_terms = jnp.einsum("gts,gsd->gtd", token_marks, back_rows, preferred_element_type=single)
    normed_grad = matmul(logit_grad, router_full.T) + scatter_shard(row_terms)
    moe_input_grad, moe_gain_grad = norm_back(mid_second, gain_mlp[1], normed_grad)
    mid_grad = upstream + moe_input_grad

    up_grad = up_grad.reshape(EXP_DEV, groups, part, width)
    expert_up_grad = jnp.zeros((EXP_DEV, part, groups * width), single)
    for step in range(groups):
        piece = lax.dynamic_index_in_dim(up_grad, (here + step) % groups, 1, keepdims=False)
        if step:
            piece = shard_shift(piece, step)
        expert_up_grad = lax.dynamic_update_slice_in_dim(
            expert_up_grad, piece.astype(single), ((here - step) % groups) * width, 2
        )

    layer_grad, gain_second, qkv_second, projection_second, bias_second = attention_backward(
        mid_grad, layer_one, gain_attn[1], qkv[1], projection[1], bias_weights[1], geometry,
        saved_second,
    )
    second_grad = reduce_weight(jnp.concatenate([qkv_second, projection_second], axis=1))
    dense_branch = layer_grad.astype(bfloat)
    mlp_down_grad = reduce_weight(matmul(activation.T, dense_branch))
    hidden_act_grad = unspread(matmul(dense_branch, dense_down.T))
    pre_act_grad = gelu_back(pre_act, hidden_act_grad).astype(bfloat)
    mlp_up_grad = reduce_weight(matmul(dense_normed.T, pre_act_grad))
    dense_normed_grad = unspread(matmul(pre_act_grad, dense_up.T))
    dense_input_grad, dense_gain_grad = norm_back(mid_first, gain_mlp[0], dense_normed_grad)
    first_grad = layer_grad + dense_input_grad
    input_grad, gain_first, qkv_first, projection_first, bias_first = attention_backward(
        first_grad, hidden_zero, gain_attn[0], qkv[0], projection[0], bias_weights[0], geometry,
        saved_first,
    )
    first_weight_grad = reduce_weight(jnp.concatenate([qkv_first, projection_first], axis=1))

    gains = jnp.stack([gain_first, gain_second, dense_gain_grad, moe_gain_grad])
    biases = jnp.stack([bias_first, bias_second])
    small_grad = jnp.concatenate(
        [
            gains.reshape(4, groups, part).transpose(1, 0, 2).reshape(groups, -1),
            biases.reshape(2, groups, NB // groups, H).transpose(1, 0, 2, 3).reshape(groups, -1),
            router_grad.reshape(groups, -1),
        ],
        axis=1,
    )
    small_grad = lax.psum(scatter_shard(small_grad, single), "expert")
    gain_cut = 4 * part
    bias_cut = gain_cut + 2 * (NB // groups) * H
    own_gains = small_grad[:gain_cut].reshape(4, part)
    peaks = lax.pmax(jnp.stack([peak_first, peak_second]), ("expert", "shard"))
    clip_scales = jnp.sqrt(clip_limit / jnp.maximum(peaks, clip_limit))
    return (
        hidden_out,
        input_grad.reshape(hidden_in.shape),
        own_gains[:2],
        jnp.stack([first_weight_grad[:, : 3 * D], second_grad[:, : 3 * D]]),
        jnp.stack([first_weight_grad[:, 3 * D :], second_grad[:, 3 * D :]]),
        small_grad[gain_cut:bias_cut].reshape(2, NB // groups, H),
        own_gains[2:],
        mlp_up_grad,
        mlp_down_grad,
        small_grad[bias_cut:].reshape(part, expert_total),
        expert_up_grad,
        expert_down_grad,
        clip_scales,
    )


MESH = pl.DeviceIdType.MESH
ANY = pl.ANY
VMEM = pltpu.VMEM


def place():
    return lax.axis_index("expert"), lax.axis_index("shard")


def greet(devices):
    barrier = pltpu.get_barrier_semaphore()
    for device in devices:
        pl.semaphore_signal(barrier, inc=1, device_id=device, device_id_type=MESH)
    pl.semaphore_wait(barrier, len(devices))


def push(sent, source, target, send_sem, recv_sem, device):
    copy = pltpu.make_async_remote_copy(
        src_ref=source,
        dst_ref=target,
        send_sem=send_sem,
        recv_sem=recv_sem,
        device_id=device,
        device_id_type=MESH,
    )
    copy.start()
    sent.append(copy)
    return copy


def norm_rows(inputs, gain):
    return inputs * lax.rsqrt(jnp.mean(inputs * inputs, axis=-1, keepdims=True) + epsilon) * gain


def dot_rows(left, right):
    return lax.dot_general(left, right, (((1,), (1,)), ((), ())), preferred_element_type=single)


def dot_columns(left, right):
    return lax.dot_general(left, right, (((0,), (0,)), ((), ())), preferred_element_type=single)


def loop(count, body):
    def step(i, carry):
        body(i)
        return carry

    lax.fori_loop(0, count, step, 0)


def lane_block(i, width):
    return pl.ds(pl.multiple_of(i * width, 128), width)


def row_block(i, height):
    return pl.ds(pl.multiple_of(i * height, height), height)


T = 128
PAIRS = H // 2
TOE = 1152
CAP = 32


class Plane:
    def __init__(self):
        self.e, self.s = place()
        e = self.e
        self.core = lax.rem(e, 2)
        self.quarter = e // 2
        self.at_x = e + 2 - 4 * lax.rem(self.quarter, 2)
        self.at_y = lax.rem(e + 4, 8)
        self.at_core = e + 1 - 2 * self.core
        self.inward = jnp.where(self.core == 0, self.at_x, self.at_y)
        self.onward = jnp.where(self.core == 0, self.at_y, self.at_x)
        self.diagonal = self.inward + self.onward - e
        self.others = [lax.rem(self.s + k, 4) for k in range(1, 4)]
        self.around = [lax.rem(e + k, 8) for k in range(1, 8)]
        z = self.s
        first = jnp.where(z == 0, 1, jnp.where(z == 1, 2, jnp.where(z == 2, 1, 2)))
        second = jnp.where(z == 0, 2, jnp.where(z == 1, 0, jnp.where(z == 2, 3, 1)))
        self.near = [first, second, 6 - z - first - second]
        self.to_k = [lax.rem(other - z + 4, 4) - 1 for other in self.near]
        self.from_k = [lax.rem(z - other + 4, 4) - 1 for other in self.near]
        self.sent = []

    def push(self, source, target, send_sem, recv_sem, device):
        return push(self.sent, source, target, send_sem, recv_sem, device)

    def arrived(self, view, recv_sem):
        pltpu.make_async_remote_copy(
            src_ref=view,
            dst_ref=view,
            send_sem=recv_sem,
            recv_sem=recv_sem,
            device_id=(self.at_core, self.s),
            device_id_type=MESH,
        ).wait_recv()


class PlaneGather:
    def __init__(self, plane, view, send_sems, recv_sems):
        self.plane, self.view, self.ss, self.rs = plane, view, send_sems, recv_sems

    def _push(self, who, i, target):
        p = self.plane
        block = self.view(who)
        p.push(block, block, self.ss.at[i], self.rs.at[i], (target, p.s))

    def first(self):
        p = self.plane
        self._push(p.e, 0, p.at_x)
        self._push(p.e, 1, p.at_y)
        self._push(p.e, 3, p.at_core)

    def second(self):
        p = self.plane
        p.arrived(self.view(p.inward), self.rs.at[p.core])
        self._push(p.inward, 2, p.onward)
        self._push(p.inward, 4, p.at_core)

    def third(self):
        p = self.plane
        p.arrived(self.view(p.onward), self.rs.at[1 - p.core])
        self._push(p.onward, 5, p.at_core)
        p.arrived(self.view(p.diagonal), self.rs.at[2])
        self._push(p.diagonal, 6, p.at_core)

    def done(self):
        for i in range(3, 7):
            self.plane.arrived(self.view(self.plane.e), self.rs.at[i])


class PlaneSum:
    def __init__(self, plane, parts, core_in, chips_in, send_sems, recv_sems):
        self.plane, self.parts, self.core_in, self.chips_in = plane, parts, core_in, chips_in
        self.ss, self.rs = send_sems, recv_sems

    def give(self):
        p = self.plane
        p.push(
            self.parts.at[1 - p.core], self.core_in, self.ss.at[0], self.rs.at[0], (p.at_core, p.s)
        )

    def pass_on(self):
        p = self.plane
        p.arrived(self.core_in, self.rs.at[0])
        for q in range(4):
            self.parts[p.core, q] = (
                self.parts[p.core, q].astype(single) + self.core_in[q].astype(single)
            ).astype(bfloat)
        for k, d in enumerate((p.at_x, p.at_y, p.diagonal)):
            p.push(
                self.parts.at[p.core, d // 2],
                self.chips_in.at[k],
                self.ss.at[1 + k],
                self.rs.at[1 + k],
                (d, p.s),
            )

    def result(self):
        p = self.plane
        total = self.parts[p.core, p.quarter].astype(single)
        for k in range(3):
            p.arrived(self.chips_in.at[k], self.rs.at[1 + k])
            total = total + self.chips_in[k].astype(single)
        return total


def forward_kernel(
    hidden_ref,
    attn_gain_ref,
    mlp_gain_ref,
    rel_bias_ref,
    router_ref,
    buckets_ref,
    routes_ref,
    qkv_hbm,
    out_hbm,
    up_hbm,
    down_hbm,
    expert_up_hbm,
    cot_hbm,
    normed_out,
    query_out,
    attended_out,
    mid_first_out,
    mid_second_out,
    dense_normed_out,
    one_out,
    peak_out,
    moe_normed_out,
    gains_ref,
    router_out,
    slots_out,
    qkv0_out,
    qkv1_out,
    proj0_out,
    proj1_out,
    up_out,
    down_out,
    kv_out,
    probs_out,
    up_own,
    cot_all,
    dense_rows_out,
    pre_hbm,
    act_hbm,
    small_ref,
    small_all,
    table_ref,
    slots_own,
    up_shard,
    up_turned,
    pre_out,
    act_out,
    dense_rows,
    sums,
    sums_core,
    sums_chips,
    w_qkv0,
    w_qkv1,
    w_out0,
    w_out1,
    w_up,
    w_down,
    kv,
    probs,
    scores,
    zs,
    zr,
    f1s,
    f1r,
    f2s,
    f2r,
    cs,
    cr,
    locals_sem,
    k1s,
    k1r,
    k2s,
    k2r,
    kcs,
    kcr,
    us,
    ur,
    gs,
    gr,
    ns,
    nr,
    outs_sem,
    small_s,
    small_r,
    slot_zs,
    slot_zr,
    slot_ps,
    slot_pr,
    dense_s,
    dense_r,
    sum_s,
    sum_r,
):
    e, s = place()
    core = lax.rem(e, 2)
    quarter = e // 2
    at_x = e + 2 - 4 * lax.rem(quarter, 2)
    at_y = lax.rem(e + 4, 8)
    at_core = e + 1 - 2 * core
    inward = jnp.where(core == 0, at_x, at_y)
    onward = jnp.where(core == 0, at_y, at_x)
    others = [lax.rem(s + k, 4) for k in range(1, 4)]
    plane = Plane()
    near, to_k, from_k = plane.near, plane.to_k, plane.from_k
    sources = near
    sent = []
    kept = []

    def local(source, target, sem):
        copy = pltpu.make_async_copy(source, target, sem)
        copy.start()
        return copy

    chunks = [
        (qkv_hbm.at[0], w_qkv0, 48, 1152),
        (out_hbm.at[0], w_out0, 48, 384),
        None,
        None,
        (qkv_hbm.at[1], w_qkv1, 48, 1152),
        (out_hbm.at[1], w_out1, 48, 384),
    ]

    def block(target, who, position, height, half, width):
        rows = pl.ds(pl.multiple_of(position * 4 * height + who * height, height), height)
        return target.at[rows, lane_block(half, width)]

    def cot_block(g, who):
        return cot_all.at[g, who]

    stage1, stage2, stage3, stage4, own = {}, {}, {}, {}, {}

    def z_send(c):
        source, target, height, width = chunks[c]
        piece = source.at[row_block(quarter, height), lane_block(core, width)]
        mine = block(target, quarter, s, height, core, width)
        stage1[c] = [
            push(sent, piece, mine, zs.at[c, to_k[i]], zr.at[c, to_k[i]], (e, near[i]))
            for i in range(3)
        ]
        own[c] = local(source, target.at[row_block(s, 4 * height), :], locals_sem.at[c])

    got_shard = local(up_hbm, up_shard, outs_sem.at[11])

    def turn_shard():
        got_shard.wait()
        for b in range(8):
            for z in range(4):
                up_turned[:, 384 * b + 96 * z : 384 * b + 96 * (z + 1)] = up_shard[
                    :, 768 * z + 96 * b : 768 * z + 96 * (b + 1)
                ]

    def unit_send(c):
        target, height = ((w_up, 192), (w_down, 96))[c - 2]
        piece = up_turned.at[:, lane_block(e, 384)] if c == 2 else down_hbm.at[row_block(e, 96), :]
        mine = target.at[row_block(s, height), :]
        stage1[c] = [
            push(sent, piece, mine, zs.at[c, to_k[i]], zr.at[c, to_k[i]], (e, near[i]))
            for i in range(3)
        ]
        own[c] = local(piece, mine, locals_sem.at[c])

    def units_ready(c):
        for copy in stage1[c]:
            copy.wait_recv()
        own[c].wait()
        kept.append(local((w_up, w_down)[c - 2], weight_outs[c], outs_sem.at[c]))

    def plane_send(c):
        _, target, height, width = chunks[c]
        stage2[c] = []
        for k in range(3):
            mine = block(target, quarter, sources[k], height, core, width)
            plane.arrived(mine, zr.at[c, from_k[k]])
            stage2[c].append(
                [
                    push(sent, mine, mine, f1s.at[c, k, i], f1r.at[c, k, i], (partner, s))
                    for i, partner in enumerate((at_x, at_y))
                ]
            )

    def plane_forward(c):
        _, target, height, width = chunks[c]
        stage3[c] = []
        for k in range(3):
            pltpu.make_async_remote_copy(
                src_ref=block(target, quarter, sources[k], height, core, width),
                dst_ref=block(target, quarter, sources[k], height, core, width),
                send_sem=f1s.at[c, k, core],
                recv_sem=f1r.at[c, k, core],
                device_id=(inward, s),
                device_id_type=MESH,
            ).wait_recv()
            theirs = block(target, inward // 2, sources[k], height, core, width)
            stage3[c].append(
                push(sent, theirs, theirs, f2s.at[c, k], f2r.at[c, k], (onward, s))
            )

    def core_send(c):
        _, target, height, width = chunks[c]
        stage4[c] = []
        for k in range(3):
            pltpu.make_async_remote_copy(
                src_ref=block(target, quarter, sources[k], height, core, width),
                dst_ref=block(target, quarter, sources[k], height, core, width),
                send_sem=f1s.at[c, k, 1 - core],
                recv_sem=f1r.at[c, k, 1 - core],
                device_id=(onward, s),
                device_id_type=MESH,
            ).wait_recv()
            stage3[c][k].wait_recv()
            half = target.at[row_block(sources[k], 4 * height), lane_block(core, width)]
            stage4[c].append(push(sent, half, half, cs.at[c, k], cr.at[c, k], (at_core, s)))

    weight_outs = [qkv0_out, proj0_out, up_out, down_out, qkv1_out, proj1_out]

    def ready(c):
        for k in range(3):
            stage4[c][k].wait_recv()
        own[c].wait()
        kept.append(local(chunks[c][1], weight_outs[c], outs_sem.at[c]))

    cot_groups = [s] + sources
    cot_gathers = [
        PlaneGather(plane, functools.partial(cot_block, g), ns.at[k], nr.at[k])
        for k, g in enumerate(cot_groups)
    ]

    def cot_first(k):
        plane.arrived(cot_block(s, e), gr.at[from_k[k - 1]])
        cot_gathers[k].first()

    experts = lax.broadcasted_iota(jnp.int32, (16, T), 0)
    chosen = [experts == routes_ref[r : r + 1, :] for r in range(2)]
    marks = jnp.where(chosen[0] | chosen[1], 1.0, 0.0).astype(bfloat)
    earlier = jnp.where(
        lax.broadcasted_iota(jnp.int32, (T, T), 0) < lax.broadcasted_iota(jnp.int32, (T, T), 1),
        1.0,
        0.0,
    ).astype(bfloat)
    before = jnp.dot(marks, earlier, preferred_element_type=single)
    slots_own[...] = jnp.zeros_like(slots_own)
    for r in range(2):
        rank = jnp.sum(jnp.where(chosen[r], before, 0.0), axis=0, keepdims=True)
        slots_own[r : r + 1, :] = routes_ref[r : r + 1, :] * CAP + rank.astype(jnp.int32)
    slots_out[s, e] = slots_own[...]
    own_cot = local(cot_hbm, cot_block(s, e), gs.at[3])
    part = D // 4
    small_ref[...] = jnp.zeros_like(small_ref)
    small_ref[0:2, :part] = attn_gain_ref[...].astype(single)
    small_ref[2:4, :part] = mlp_gain_ref[...].astype(single)
    for layer in range(2):
        small_ref[8:16, layer * H : (layer + 1) * H] = rel_bias_ref[layer].astype(single)
    small_ref[16:32, :part] = router_ref[...].astype(single)
    small_all[s] = small_ref[...]

    greet([(d, s) for d in plane.around] + [(e, other) for other in others])
    smalls = [
        push(sent, small_ref, small_all.at[s], small_s.at[k], small_r.at[k], (e, others[k]))
        for k in range(3)
    ]
    z_send(0)
    for k in range(3):
        push(sent, slots_own, slots_out.at[s, e], slot_zs.at[k], slot_zr.at[k], (e, others[k]))
    own_cot.wait()
    cot_gathers[0].first()
    z_send(1)
    turn_shard()
    unit_send(2)
    reshard = []

    def bulk():
        z_send(4)
        z_send(5)
        unit_send(3)
        for i in range(3):
            push(sent, cot_hbm, cot_block(s, e), gs.at[to_k[i]], gr.at[to_k[i]], (e, near[i]))
        kept.append(
            local(
                expert_up_hbm.at[:, :, lane_block(s, 768)],
                up_own.at[:, row_block(s, 192), :],
                us.at[3],
            )
        )

    def slots_plane():
        for k in range(3):
            plane.arrived(slots_own, slot_zr.at[k])
        column = slots_out.at[:, e]
        for k, d in enumerate(plane.around):
            push(sent, column, column, slot_ps.at[k], slot_pr.at[k], (d, s))

    for copy in smalls:
        copy.wait_recv()
    biases = []
    for z in range(4):
        lanes = slice(192 * z, 192 * (z + 1))
        gains_ref[:, lanes] = small_all[z, :4, :192]
        router_out[:, lanes] = small_all[z, 16:32, :192].astype(bfloat)
        biases.append(small_all[z, 8:16, : 2 * H])
    bucket_marks_here = jnp.where(
        lax.broadcasted_iota(jnp.int32, (NB, TOE), 0) == buckets_ref[...], 1.0, 0.0
    ).astype(bfloat)
    table_ref[...] = dot_columns(jnp.concatenate(biases).astype(bfloat), bucket_marks_here)

    def attention(layer, inputs, w_qkv, w_out, work):
        normed = norm_rows(inputs, gains_ref[pl.ds(layer, 1), :]).astype(bfloat)
        normed_out[layer] = normed
        if layer == 0:
            plane_send(0)
            plane_forward(0)
            plane_send(1)
            core_send(0)
            plane_forward(1)
            ready(0)
            bulk()
        else:
            ready(4)
        own_rows = row_block(e, T)
        first, second, third = [], [], []
        for part in range(3):
            x = normed_out[layer]
            for i, base in enumerate((D, 2 * D)):
                columns = w_qkv[:, base + 256 * part : base + 256 * (part + 1)]
                kv[layer, part, own_rows, 256 * i : 256 * (i + 1)] = jnp.dot(
                    x, columns, preferred_element_type=single
                ).astype(bfloat)
            mine = kv.at[layer, part, own_rows, :]
            first.append(
                [
                    push(sent, mine, mine, k1s.at[layer, part, i], k1r.at[layer, part, i], (p, s))
                    for i, p in enumerate((at_x, at_y))
                ]
            )
            third.append(
                [
                    push(
                        sent, mine, mine, kcs.at[layer, part, 0], kcr.at[layer, part, 0],
                        (at_core, s),
                    )
                ]
            )
        query_out[layer] = jnp.dot(
            normed_out[layer], w_qkv[:, :D], preferred_element_type=single
        ).astype(bfloat)
        if work:
            work[0]()
        at_diagonal = inward + onward - e
        for part in range(3):
            pltpu.make_async_remote_copy(
                src_ref=kv.at[layer, part, own_rows, :],
                dst_ref=kv.at[layer, part, own_rows, :],
                send_sem=k1s.at[layer, part, core],
                recv_sem=k1r.at[layer, part, core],
                device_id=(inward, s),
                device_id_type=MESH,
            ).wait_recv()
            theirs = kv.at[layer, part, row_block(inward, T), :]
            second.append(
                push(
                    sent, theirs, theirs, k2s.at[layer, part], k2r.at[layer, part], (onward, s)
                )
            )
            third[part].append(
                push(
                    sent, theirs, theirs, kcs.at[layer, part, 1], kcr.at[layer, part, 1],
                    (at_core, s),
                )
            )
        if work:
            work[1]()
        for part in range(3):
            pltpu.make_async_remote_copy(
                src_ref=kv.at[layer, part, own_rows, :],
                dst_ref=kv.at[layer, part, own_rows, :],
                send_sem=k1s.at[layer, part, 1 - core],
                recv_sem=k1r.at[layer, part, 1 - core],
                device_id=(onward, s),
                device_id_type=MESH,
            ).wait_recv()
            theirs = kv.at[layer, part, row_block(onward, T), :]
            third[part].append(
                push(
                    sent, theirs, theirs, kcs.at[layer, part, 2], kcr.at[layer, part, 2],
                    (at_core, s),
                )
            )
            second[part].wait_recv()
            theirs = kv.at[layer, part, row_block(at_diagonal, T), :]
            third[part].append(
                push(
                    sent, theirs, theirs, kcs.at[layer, part, 3], kcr.at[layer, part, 3],
                    (at_core, s),
                )
            )
        for part in range(3):
            for i in range(4):
                third[part][i].wait_recv()

            def one_pair(local_pair):
                pair = 2 * part + local_pair
                lanes = lane_block(pair, 128)
                queries = query_out[layer, :, lanes]
                lane = lax.broadcasted_iota(jnp.int32, (T, 128), 1)
                zero = jnp.zeros_like(queries)
                both = jnp.concatenate(
                    [jnp.where(lane < HD, queries, zero), jnp.where(lane >= HD, queries, zero)]
                )
                keys = kv[layer, part, :, lane_block(local_pair, 128)]
                scores[...] = dot_rows(both, keys) * (1.0 / math.sqrt(HD))
                for half in range(2):
                    head = 2 * pair + half
                    toeplitz = table_ref[pl.ds(layer * H + head, 1), :]
                    peak = jnp.full((1, 1), -jnp.inf, single)
                    for rows in range(0, T, 32):
                        raw = scores[half * T + rows : half * T + rows + 32, :]
                        row = e * T + rows + lax.broadcasted_iota(jnp.int32, raw.shape, 0)
                        causal = row >= lax.broadcasted_iota(jnp.int32, raw.shape, 1)
                        shifted = pltpu.roll(
                            jnp.broadcast_to(toeplitz, (32, TOE)),
                            TOE - (T - 1) + rows,
                            1,
                            stride=1,
                            stride_axis=0,
                        )[:, : raw.shape[1]]
                        peak = jnp.maximum(
                            peak, jnp.max(jnp.where(causal, raw, -jnp.inf), keepdims=True)
                        )
                        masked = jnp.where(causal, raw + shifted, -jnp.inf)
                        top = jnp.max(masked, axis=-1, keepdims=True)
                        exponent = jnp.exp(masked - top)
                        total = jnp.sum(exponent, axis=-1, keepdims=True)
                        probs[layer, pl.ds(pl.multiple_of(head * T + rows, 32), 32), :] = (
                            exponent / total
                        ).astype(bfloat)
                    peak_out[pl.ds(layer * H + head, 1), :] = jnp.broadcast_to(peak, (1, 128))
                values = kv[layer, part, :, pl.ds(pl.multiple_of(256 + local_pair * 128, 128), 128)]
                mixed = jnp.dot(
                    probs[layer, pl.ds(pl.multiple_of(pair * 2 * T, 2 * T), 2 * T), :],
                    values,
                    preferred_element_type=single,
                )
                attended_out[layer, :, lanes] = jnp.where(
                    lane < HD, mixed[:T], mixed[T:]
                ).astype(bfloat)

            loop(2, one_pair)
            if work:
                work[2 + part]()
        kept.append(local(kv.at[layer], kv_out.at[layer], outs_sem.at[6 + layer]))
        kept.append(local(probs.at[layer], probs_out.at[layer], outs_sem.at[8 + layer]))

    def work0():
        slots_plane()

    def work1():
        cot_gathers[0].second()

    def work2():
        core_send(1)
        plane_send(4)

    def work3():
        cot_gathers[0].third()
        plane_send(5)

    def work4():
        plane_forward(4)

    hidden = hidden_ref[...].astype(single)
    attention(0, hidden, w_qkv0, w_out0, [work0, work1, work2, work3, work4])
    ready(1)
    mid_first_out[...] = hidden + jnp.dot(
        attended_out[0], w_out0[...], preferred_element_type=single
    )
    dense_normed_out[...] = norm_rows(mid_first_out[...], gains_ref[pl.ds(2, 1), :]).astype(bfloat)
    reshard.extend([
        push(
            sent,
            expert_up_hbm.at[:, :, lane_block(near[i], 768)],
            up_own.at[:, row_block(s, 192), :],
            us.at[to_k[i]],
            ur.at[to_k[i]],
            (e, near[i]),
        )
        for i in range(3)
    ])
    dense_rows[e] = dense_normed_out[...]
    dense = PlaneGather(plane, lambda who: dense_rows.at[who], dense_s, dense_r)
    dense.first()
    plane_forward(5)
    core_send(4)
    dense.second()
    core_send(5)
    units_ready(2)
    units_ready(3)
    dense.third()
    dense.done()
    kept.append(local(dense_rows, dense_rows_out, outs_sem.at[10]))
    reduce = PlaneSum(plane, sums, sums_core, sums_chips, sum_s, sum_r)

    def units(c, q):
        who = 2 * q + c
        rows = row_block(who, T)
        before = jnp.dot(dense_rows[who], w_up[...], preferred_element_type=single)
        pre_out[rows, :] = before
        act = jax.nn.gelu(before).astype(bfloat)
        act_out[rows, :] = act
        sums[c, q] = jnp.dot(act, w_down[...], preferred_element_type=single).astype(bfloat)

    for q in range(4):
        units(1 - core, q)
    reduce.give()
    for q in range(4):
        units(core, q)
    reduce.pass_on()
    kept.append(local(pre_out, pre_hbm, outs_sem.at[12]))
    kept.append(local(act_out, act_hbm, outs_sem.at[13]))
    cot_first(1)
    one_out[...] = mid_first_out[...] + reduce.result()

    def work5():
        cot_first(2)
        cot_gathers[1].second()

    def work6():
        cot_first(3)

    def work7():
        cot_gathers[1].third()
        cot_gathers[2].second()

    def work8():
        cot_gathers[2].third()
        cot_gathers[3].second()

    def work9():
        cot_gathers[3].third()

    attention(1, one_out[...], w_qkv1, w_out1, [work5, work6, work7, work8, work9])
    ready(5)
    mid_second_out[...] = one_out[...] + jnp.dot(
        attended_out[1], w_out1[...], preferred_element_type=single
    )
    moe_normed_out[...] = norm_rows(mid_second_out[...], gains_ref[pl.ds(3, 1), :]).astype(bfloat)
    for k in range(7):
        plane.arrived(slots_out.at[:, e], slot_pr.at[k])
    for gather in cot_gathers:
        gather.done()
    for copy in reshard:
        copy.wait_recv()
    for copy in kept:
        copy.wait()
    for copy in sent + plane.sent:
        copy.wait_send()


def forward(
    hidden, attn_gain, mlp_gain, rel_bias, router, buckets, routes, qkv, out, up, down, expert_up,
    cotangent,
):
    length = T * lax.axis_size("expert")
    vmem = pl.BlockSpec(memory_space=VMEM)
    anywhere = pl.BlockSpec(memory_space=ANY)
    shape = jax.ShapeDtypeStruct
    sem = pltpu.SemaphoreType.DMA
    return pl.pallas_call(
        forward_kernel,
        name="forward_layers",
        out_shape=(
            shape((2, T, D), bfloat),
            shape((2, T, D), bfloat),
            shape((2, T, D), bfloat),
            shape((T, D), single),
            shape((T, D), single),
            shape((T, D), bfloat),
            shape((T, D), single),
            shape((2 * H, 128), single),
            shape((T, D), bfloat),
            shape((4, D), single),
            shape((16, D), bfloat),
            shape((4, 8, 8, T), jnp.int32),
            shape((D, 3 * D), bfloat),
            shape((D, 3 * D), bfloat),
            shape((D, D), bfloat),
            shape((D, D), bfloat),
            shape((D, 384), bfloat),
            shape((384, D), bfloat),
            shape((2, 3, length, 512), bfloat),
            shape((2, H * T, length), bfloat),
            shape((EXP_DEV, D, 768), bfloat),
            shape((4, 8, T, D), bfloat),
            shape((8, T, D), bfloat),
            shape((length, 384), single),
            shape((length, 384), bfloat),
        ),
        in_specs=[vmem] * 7 + [anywhere] * 6,
        out_specs=(vmem,) * 12 + (anywhere,) * 13,
        scratch_shapes=[
            VMEM((32, 256), single),
            VMEM((4, 32, 256), single),
            VMEM((2 * H, TOE), single),
            VMEM((8, T), jnp.int32),
            VMEM(up.shape, bfloat),
            VMEM(up.shape, bfloat),
            VMEM((length, 384), single),
            VMEM((length, 384), bfloat),
            VMEM((8, T, D), bfloat),
            VMEM((2, 4, T, D), bfloat),
            VMEM((4, T, D), bfloat),
            VMEM((3, T, D), bfloat),
            VMEM((D, 3 * D), bfloat),
            VMEM((D, 3 * D), bfloat),
            VMEM((D, D), bfloat),
            VMEM((D, D), bfloat),
            VMEM((D, 384), bfloat),
            VMEM((384, D), bfloat),
            VMEM((2, 3, length, 512), bfloat),
            VMEM((2, H * T, length), bfloat),
            VMEM((2 * T, length), single),
            sem((6, 3)), sem((6, 3)),
            sem((6, 3, 2)), sem((6, 3, 2)),
            sem((6, 3)), sem((6, 3)),
            sem((6, 3)), sem((6, 3)),
            sem((6,)),
            sem((2, 3, 2)), sem((2, 3, 2)),
            sem((2, 3)), sem((2, 3)),
            sem((2, 3, 4)), sem((2, 3, 4)),
            sem((4,)), sem((3,)),
            sem((4,)), sem((3,)),
            sem((4, 7)), sem((4, 7)),
            sem((14,)),
            sem((3,)), sem((3,)),
            sem((3,)), sem((3,)),
            sem((7,)), sem((7,)),
            sem((7,)), sem((7,)),
            sem((4,)), sem((4,)),
        ],
        compiler_params=pltpu.CompilerParams(
            collective_id=2, has_side_effects=True, vmem_limit_bytes=56 * 2**20
        ),
    )(
        hidden, attn_gain, mlp_gain, rel_bias, router, buckets, routes, qkv, out, up, down,
        expert_up, cotangent,
    )


class SmallReduce:
    def __init__(self, plane, value, z_in, plane_in, op, sems):
        self.plane, self.value, self.z_in, self.plane_in = plane, value, z_in, plane_in
        self.op, self.sems = op, sems

    def start(self):
        p = self.plane
        zs, zr, _, _ = self.sems
        for k in range(3):
            p.push(self.value, self.z_in.at[k], zs.at[k], zr.at[k], (p.e, p.others[k]))

    def middle(self, middle):
        p = self.plane
        zs, zr, ps, pr = self.sems
        total = self.value[...]
        for k in range(3):
            p.arrived(self.z_in.at[k], zr.at[k])
            total = self.op(total, self.z_in[k])
        middle[...] = total
        for k in range(7):
            p.push(middle, self.plane_in.at[k], ps.at[k], pr.at[k], (p.around[k], p.s))

    def finish(self, middle, result):
        p = self.plane
        total = middle[...]
        for k in range(7):
            p.arrived(self.plane_in.at[k], self.sems[3].at[k])
            total = self.op(total, self.plane_in[k])
        result[...] = total


def norm_pull(inputs, gain, upstream):
    inverse = lax.rsqrt(jnp.mean(inputs * inputs, axis=-1, keepdims=True) + epsilon)
    scaled = upstream * gain
    inner = jnp.mean(scaled * inputs, axis=-1, keepdims=True)
    gain_grad = jnp.sum(upstream * inputs * inverse, axis=0, keepdims=True)
    return inverse * scaled - inputs * (inverse * inverse * inverse * inner), gain_grad


def gelu_both(value):
    root = math.sqrt(2.0 / math.pi)
    squared = value * value
    bend = jnp.tanh(root * value * (1.0 + 0.044715 * squared))
    half = 0.5 * (1.0 + bend)
    slope = half + 0.5 * value * (1.0 - bend * bend) * (root * (1.0 + 3 * 0.044715 * squared))
    return value * half, slope


def gelu_slope(value):
    root = math.sqrt(2.0 / math.pi)
    squared = value * value
    bend = jnp.tanh(root * value * (1.0 + 0.044715 * squared))
    return 0.5 * (1.0 + bend) + 0.5 * value * (1.0 - bend * bend) * root * (
        1.0 + 3 * 0.044715 * squared
    )


def backward_kernel(
    mid_grad_ref,
    one_ref,
    hidden_ref,
    mid_ref,
    gains_ref,
    query_ref,
    pre_ref,
    buckets_ref,
    small_ref,
    peak_ref,
    normed_hbm,
    attended_hbm,
    dense_rows_hbm,
    act_hbm,
    qkv0_hbm,
    qkv1_hbm,
    proj0_hbm,
    proj1_hbm,
    up_hbm,
    down_hbm,
    kv_hbm,
    probs_hbm,
    up_grad_hbm,
    hidden_grad_out,
    att_out,
    up_out,
    down_out,
    small_out,
    late_out,
    peak_out,
    expert_up_out,
    w_wide,
    w_up,
    w_down,
    sums,
    sums_core,
    sums_chips,
    kv,
    probs,
    xg,
    gx,
    gsrc,
    zb,
    zin,
    zb_down,
    zin_down,
    slopes,
    score_low,
    dk,
    cin,
    rin,
    attended_grad,
    layer_grad,
    biases,
    early,
    early_z,
    early_p,
    early_m,
    late,
    late_z,
    late_p,
    late_m,
    peak_z,
    peak_p,
    peak_m,
    gs,
    gr,
    xs,
    xr,
    zs,
    zr,
    dcs,
    dcr,
    drs,
    drr,
    szs,
    szr,
    sps,
    spr,
    us,
    ur,
    loads,
    sum_s,
    sum_r,
):
    p = Plane()
    e, s, core = p.e, p.s, p.core
    own_rows = row_block(e, T)

    def load(source, target, i):
        copy = pltpu.make_async_copy(source, target, loads.at[i])
        copy.start()
        return copy

    own_parts = [
        load(source, xg.at[n, own_rows, :], 11 + n)
        for n, source in enumerate(
            (normed_hbm.at[1], attended_hbm.at[1], normed_hbm.at[0], attended_hbm.at[0])
        )
    ]
    got_act = load(act_hbm, gx.at[3], 16)
    got_dense = load(dense_rows_hbm, xg.at[4], 9)
    greet([(d, s) for d in p.around] + [(e, other) for other in p.others])

    w_qkv = w_wide.at[:, : 3 * D]
    w_out = w_wide.at[:, 3 * D :]
    got_out = load(proj1_hbm, w_out, 0)
    got_kv = load(kv_hbm.at[1], kv, 2)
    got_probs = load(probs_hbm.at[1], probs, 3)
    got_qkv = load(qkv1_hbm, w_qkv, 1)
    got_down = load(down_hbm, w_down, 5)
    got_up = load(up_hbm, w_up, 4)

    peaks = SmallReduce(
        p, peak_ref, peak_z, peak_p, jnp.maximum, (szs.at[0], szr.at[0], sps.at[0], spr.at[0])
    )
    peaks.start()

    def rows_gather(n):
        return PlaneGather(
            p, lambda who: xg.at[n, row_block(who, T), :], gs.at[n], gr.at[n]
        )

    gathers = {n: rows_gather(n) for n in (0, 1, 2, 3, 5)}
    def exchange_start(j, source):
        gx[j, own_rows, :] = source[:, lane_block(e, 384)]
        for k, d in enumerate(p.around):
            p.push(
                source.at[:, lane_block(d, 384)],
                gx.at[j, own_rows, :],
                xs.at[j, k],
                xr.at[j, k],
                (d, s),
            )

    def exchange_wait(j):
        for k in range(7):
            p.arrived(gx.at[j, own_rows, :], xr.at[j, k])

    def out_gather(j, target, height):
        return PlaneGather(
            p, lambda who: target.at[pl.ds(who, 1)], gs.at[6 + j], gr.at[6 + j]
        )

    def z_start(j, tile, received, height):
        for i, k in enumerate(p.to_k):
            p.push(
                tile.at[row_block(p.near[i], height), :],
                received.at[k],
                zs.at[j, k],
                zr.at[j, k],
                (e, p.near[i]),
            )

    def z_finish(j, tile, received, height, target):
        total = tile[row_block(s, height), :].astype(single)
        for k in range(3):
            p.arrived(received.at[k], zr.at[j, k])
            total = total + received[k].astype(single)
        target[pl.ds(e, 1)] = total.astype(bfloat)[None]

    def tile_attention(layer):
        j = 1 - layer
        exchange_wait(j)
        rows = xg[2 * j + e // 6]
        zb[j] = dot_columns(rows, gx[j]).astype(bfloat)
        z_start(j, zb.at[j], zin.at[j], 192)

    def tile_up():
        zb[2] = dot_columns(xg[4], gx[2]).astype(bfloat)
        z_start(2, zb.at[2], zin.at[2], 192)

    def tile_down():
        zb_down[...] = dot_columns(gx[3], xg[5]).astype(bfloat)
        z_start(3, zb_down, zin_down, 96)

    gather_att1 = out_gather(0, att_out.at[1], 192)
    gather_att0 = out_gather(1, att_out.at[0], 192)
    gather_up = out_gather(2, up_out, 192)
    gather_down = out_gather(3, down_out, 96)

    scale = 1.0 / math.sqrt(HD)

    def attention(layer, upstream, work):
        j = 1 - layer
        grads = gsrc.at[j]
        branch = upstream.astype(bfloat)
        grads[:, 3 * D :] = branch
        got_out_now = got_out if layer == 1 else reloads["out"]
        got_out_now.wait()
        attended_grad[...] = dot_rows(branch, w_out[...]).astype(bfloat)
        if layer == 1:
            got_kv.wait()
            got_probs.wait()
        else:
            reloads["kv"].wait()
            reloads["probs"].wait()
            for copy in dk_sent:
                copy.wait_send()
            dk_sent.clear()

        def first_step(part):
            push(
                dk_sent,
                dk.at[part, 1 - core],
                cin.at[layer, part],
                dcs.at[layer, part],
                dcr.at[layer, part],
                (p.at_core, s),
            )

        def second_step(part):
            p.arrived(cin.at[layer, part], dcr.at[layer, part])
            for q in range(4):
                dk[part, core, q] = (
                    dk[part, core, q].astype(single) + cin[layer, part, q].astype(single)
                ).astype(bfloat)
            for k, d in enumerate((p.at_x, p.at_y, p.diagonal)):
                push(
                    dk_sent,
                    dk.at[part, core, d // 2],
                    rin.at[layer, part, k],
                    drs.at[layer, part, k],
                    drr.at[layer, part, k],
                    (d, s),
                )

        def third_step(part):
            total = dk[part, core, p.quarter].astype(single)
            for k in range(3):
                p.arrived(rin.at[layer, part, k], drr.at[layer, part, k])
                total = total + rin[layer, part, k].astype(single)
            turned = total.T.astype(bfloat)
            grads[:, D + 256 * part : D + 256 * (part + 1)] = turned[:, :256]
            grads[:, 2 * D + 256 * part : 2 * D + 256 * (part + 1)] = turned[:, 256:]

        if layer == 1:
            for copy in own_parts:
                copy.wait()
            gathers[0].first()
            gathers[1].first()

        for part in range(3):

            def one_pair(local_pair):
                pair = 2 * part + local_pair
                lanes = lane_block(pair, 128)
                lane = lax.broadcasted_iota(jnp.int32, (T, 128), 1)

                def split(value):
                    zero = jnp.zeros_like(value)
                    return jnp.concatenate(
                        [jnp.where(lane < HD, value, zero), jnp.where(lane >= HD, value, zero)]
                    )

                queries = split(query_ref[layer, :, lanes])
                outputs = split(attended_grad[:, lanes])
                keys = kv[part, :, lane_block(local_pair, 128)]
                values = kv[part, :, pl.ds(pl.multiple_of(256 + local_pair * 128, 128), 128)]
                slopes[...] = dot_rows(outputs, values)
                pair_rows = pl.ds(pl.multiple_of(pair * 2 * T, 2 * T), 2 * T)
                for half in range(2):
                    head = 2 * pair + half
                    gathered = jnp.zeros((8, TOE), single)
                    for rows in range(0, T, 32):
                        at = half * T + rows
                        prob = probs[
                            pl.ds(pl.multiple_of(head * T + rows, 32), 32), :
                        ].astype(single)
                        slope = slopes[at : at + 32, :]
                        inner = jnp.sum(prob * slope, axis=-1, keepdims=True)
                        low = (prob * (slope - inner)).astype(bfloat)
                        score_low[at : at + 32, :] = low
                        fold = jnp.concatenate(
                            [low.astype(single), jnp.zeros((32, TOE - low.shape[1]), single)],
                            axis=1,
                        )
                        fold = pltpu.roll(fold[:16], 16, 1) + fold[16:]
                        fold = pltpu.roll(fold[:8], 8, 1) + fold[8:]
                        if rows < T - 32:
                            fold = pltpu.roll(fold, T - 32 - rows, 1)
                        gathered = gathered + fold
                    fold = pltpu.roll(gathered[:4], 4, 1) + gathered[4:]
                    fold = pltpu.roll(fold[:2], 2, 1) + fold[2:]
                    fold = pltpu.roll(fold[:1], 1, 1) + fold[1:]
                    biases[pl.ds(layer * H + head, 1), :] = fold
                mixed = jnp.dot(score_low[...], keys, preferred_element_type=single) * scale
                grads[:, lanes] = jnp.where(lane < HD, mixed[:T], mixed[T:]).astype(bfloat)
                key_grad = dot_columns(queries, score_low[...]) * scale
                value_grad = dot_columns(outputs, probs[pair_rows, :])
                for d in range(8):
                    columns = slice(128 * d, 128 * (d + 1))
                    dk[
                        part, d % 2, d // 2, pl.ds(pl.multiple_of(local_pair * 128, 128), 128), :
                    ] = key_grad[:, columns].astype(bfloat)
                    dk[
                        part,
                        d % 2,
                        d // 2,
                        pl.ds(pl.multiple_of(256 + local_pair * 128, 128), 128),
                        :,
                    ] = value_grad[:, columns].astype(bfloat)

            loop(2, one_pair)
            first_step(part)
            if part > 0:
                second_step(part - 1)
            work[part]()
        second_step(2)
        third_step(0)
        work[3]()
        third_step(1)
        third_step(2)
        if layer == 0:
            exchange_start(j, gsrc.at[j])
        if layer == 1:
            got_qkv.wait()
        else:
            reloads["qkv"].wait()
        return dot_rows(gsrc[j, :, : 3 * D], w_qkv[...])

    dk_sent = []
    reloads = {}

    def part0():
        for i, k in enumerate(p.to_k):
            reshard.append(
                p.push(
                    up_grad_hbm.at[:, row_block(p.near[i], 192), :],
                    expert_up_out.at[:, :, lane_block(s, 768)],
                    us.at[k],
                    ur.at[k],
                    (e, p.near[i]),
                )
            )
        reshard_own.append(
            load(
                up_grad_hbm.at[:, row_block(s, 192), :],
                expert_up_out.at[:, :, lane_block(s, 768)],
                6,
            )
        )

    def part1():
        gathers[0].second()
        gathers[1].second()
        peaks.middle(peak_m)

    def part2():
        pass

    def part3():
        gathers[0].third()
        gathers[1].third()
        peaks.finish(peak_m, peak_out)

    reshard, reshard_own = [], []
    mid_grad = mid_grad_ref[...]
    normed_grad = attention(1, mid_grad, [part0, part1, part2, part3])
    reloads["kv"] = load(kv_hbm.at[0], kv, 7)
    reloads["probs"] = load(probs_hbm.at[0], probs, 8)
    reloads["out"] = load(proj0_hbm, w_out, 17)
    reloads["qkv"] = load(qkv0_hbm, w_qkv, 10)
    input_grad, gain_grad = norm_pull(one_ref[...], gains_ref[1:2, :], normed_grad)
    early[...] = small_ref[...]
    early[17:18, :] = gain_grad
    layer_grad[...] = mid_grad + input_grad
    branch = layer_grad[...].astype(bfloat)
    xg[5, own_rows, :] = branch
    gathers[5].first()
    got_down.wait()
    got_up.wait()
    gathers[5].second()
    gathers[5].third()
    gathers[5].done()
    reduce = PlaneSum(p, sums, sums_core, sums_chips, sum_s, sum_r)

    def units(c, q):
        rows = row_block(2 * q + c, T)
        act_grad = dot_rows(xg[5, rows, :], w_down[...])
        pre_grad = (act_grad * gelu_slope(pre_ref[rows, :])).astype(bfloat)
        gx[2, rows, :] = pre_grad
        sums[c, q] = dot_rows(pre_grad, w_up[...]).astype(bfloat)

    for q in range(4):
        units(1 - core, q)
    reduce.give()
    for q in range(4):
        units(core, q)
    reduce.pass_on()
    gathers[2].first()
    gathers[3].first()
    input_grad, gain_grad = norm_pull(mid_ref[...], gains_ref[2:3, :], reduce.result())
    early[18:19, :] = gain_grad
    layer_grad[...] = layer_grad[...] + input_grad
    small = SmallReduce(
        p, early, early_z, early_p, jnp.add, (szs.at[1], szr.at[1], sps.at[1], spr.at[1])
    )
    small.start()
    got_dense.wait()
    got_act.wait()

    def part4():
        exchange_start(0, gsrc.at[0])

    def part5():
        gathers[2].second()
        gathers[3].second()
        small.middle(early_m)

    def part6():
        tile_up()

    def part7():
        tile_down()
        gathers[0].done()
        gathers[1].done()
        tile_attention(1)
        gathers[2].third()
        gathers[3].third()

    normed_grad = attention(0, layer_grad[...], [part4, part5, part6, part7])
    input_grad, gain_grad = norm_pull(
        hidden_ref[...].astype(single), gains_ref[0:1, :], normed_grad
    )
    hidden_grad_out[...] = layer_grad[...] + input_grad
    late[...] = jnp.zeros_like(late)
    for i in range(6):
        late[i : i + 1, :] = gain_grad[:, 128 * i : 128 * (i + 1)]
    late[8:32, :NB] = lax.dot_general(
        biases[...],
        jnp.where(lax.broadcasted_iota(jnp.int32, (NB, TOE), 0) == buckets_ref[...], 1.0, 0.0),
        (((1,), (1,)), ((), ())),
        precision=lax.Precision.HIGHEST,
        preferred_element_type=single,
    )
    tail = SmallReduce(
        p, late, late_z, late_p, jnp.add, (szs.at[2], szr.at[2], sps.at[2], spr.at[2])
    )
    tail.start()
    z_finish(2, zb.at[2], zin.at[2], 192, up_out)
    gather_up.first()
    z_finish(3, zb_down, zin_down, 96, down_out)
    gather_down.first()
    z_finish(0, zb.at[0], zin.at[0], 192, att_out.at[1])
    gather_att1.first()
    gathers[2].done()
    gathers[3].done()
    tile_attention(0)
    tail.middle(late_m)
    small.finish(early_m, small_out)
    gather_att1.second()
    gather_up.second()
    gather_down.second()
    gather_att1.third()
    gather_up.third()
    gather_down.third()
    z_finish(1, zb.at[1], zin.at[1], 192, att_out.at[0])
    gather_att0.first()
    gather_att1.done()
    gather_up.done()
    gather_down.done()
    gather_att0.second()
    gather_att0.third()
    tail.finish(late_m, late_out)
    for copy in reshard:
        copy.wait_recv()
    reshard_own[0].wait()
    gather_att0.done()
    for copy in p.sent + dk_sent:
        copy.wait_send()


def backward(
    mid_grad, layer_one, hidden, mid, gains, normed, queries, attended, dense_rows, act, pre_act,
    buckets, small, peak_rows, weights, kv, probs, up_grad,
):
    length = T * lax.axis_size("expert")
    vmem = pl.BlockSpec(memory_space=VMEM)
    anywhere = pl.BlockSpec(memory_space=ANY)
    shape = jax.ShapeDtypeStruct
    ff = up_grad.shape[2] * 4
    sem = pltpu.SemaphoreType.DMA
    peak_shape, early_shape, late_shape = (2 * H, 128), small.shape, (32, 128)
    return pl.pallas_call(
        backward_kernel,
        name="backward_layers",
        out_shape=(
            shape((T, D), single),
            shape((2, 8, 192, 384), bfloat),
            shape((8, 192, 384), bfloat),
            shape((8, 96, D), bfloat),
            shape(early_shape, single),
            shape(late_shape, single),
            shape(peak_shape, single),
            shape((EXP_DEV, 192, ff), bfloat),
        ),
        in_specs=[vmem] * 10 + [anywhere] * 13,
        out_specs=(vmem,) * 7 + (anywhere,),
        scratch_shapes=[
            VMEM((D, 4 * D), bfloat),
            VMEM((D, 384), bfloat),
            VMEM((384, D), bfloat),
            VMEM((2, 4, T, D), bfloat),
            VMEM((4, T, D), bfloat),
            VMEM((3, T, D), bfloat),
            VMEM((3, length, 512), bfloat),
            VMEM((H * T, length), bfloat),
            VMEM((6, length, D), bfloat),
            VMEM((4, length, 384), bfloat),
            VMEM((2, T, 4 * D), bfloat),
            VMEM((3, D, 384), bfloat),
            VMEM((3, 3, 192, 384), bfloat),
            VMEM((384, D), bfloat),
            VMEM((3, 96, D), bfloat),
            VMEM((2 * T, length), single),
            VMEM((2 * T, length), bfloat),
            VMEM((3, 2, 4, 512, 128), bfloat),
            VMEM((2, 3, 4, 512, 128), bfloat),
            VMEM((2, 3, 3, 512, 128), bfloat),
            VMEM((T, D), bfloat),
            VMEM((T, D), single),
            VMEM((2 * H, TOE), single),
            VMEM(early_shape, single),
            VMEM((3,) + early_shape, single),
            VMEM((7,) + early_shape, single),
            VMEM(early_shape, single),
            VMEM(late_shape, single),
            VMEM((3,) + late_shape, single),
            VMEM((7,) + late_shape, single),
            VMEM(late_shape, single),
            VMEM((3,) + peak_shape, single),
            VMEM((7,) + peak_shape, single),
            VMEM(peak_shape, single),
            sem((10, 7)), sem((10, 7)),
            sem((4, 7)), sem((4, 7)),
            sem((4, 3)), sem((4, 3)),
            sem((2, 3)), sem((2, 3)),
            sem((2, 3, 3)), sem((2, 3, 3)),
            sem((3, 3)), sem((3, 3)),
            sem((3, 7)), sem((3, 7)),
            sem((3,)), sem((3,)),
            sem((18,)),
            sem((4,)), sem((4,)),
        ],
        compiler_params=pltpu.CompilerParams(
            collective_id=3, has_side_effects=True, vmem_limit_bytes=60 * 2**20
        ),
    )(
        mid_grad, layer_one, hidden, mid, gains, queries, pre_act, buckets, small, peak_rows,
        normed, attended, dense_rows.reshape(length, D), act, *weights, kv, probs, up_grad,
    )


def experts_kernel(
    normed_ref,
    mid_ref,
    gains_ref,
    router_turned_ref,
    slots_ref,
    own_cot_ref,
    cot_hbm,
    up_hbm,
    down_hbm,
    hidden_out,
    mid_grad_out,
    small_out,
    up_grad_hbm,
    down_grad_hbm,
    up_grad_out,
    down_grad_out,
    normed_all,
    cots,
    w_up,
    w_down,
    rows,
    gated,
    gates,
    acts,
    pre_grads,
    raw,
    row_send,
    out_send,
    row_back,
    out_back,
    out_ahead_in,
    slot_grads,
    slot_z,
    slot_sum,
    slot_plane,
    row_part,
    out_part,
    row_z,
    out_z,
    ns,
    nr,
    gs,
    gr,
    rs,
    rr,
    os,
    orr,
    ss,
    sr,
    ps,
    pr,
    rzs,
    rzr,
    ozs,
    ozr,
    loads,
    oas,
    oar,
):
    p = Plane()
    e, s = p.e, p.s
    groups = [s] + [lax.rem(s + 4 - k, 4) for k in range(1, 4)]

    def load(source, target, i):
        copy = pltpu.make_async_copy(source, target, loads.at[i])
        copy.start()
        return copy

    got_cots = [load(cot_hbm.at[groups[k]], cots.at[k], k) for k in range(2)]
    got_up = load(up_hbm, w_up, 4)
    got_down = load(down_hbm, w_down, 5)
    normed_all[s, e] = normed_ref[...]
    greet([(d, s) for d in p.around] + [(e, other) for other in p.others])
    mine = normed_all.at[s, e]
    for i, k in enumerate(p.to_k):
        p.push(mine, mine, ns.at[k], nr.at[k], (e, p.near[i]))

    def gather(k):
        g = groups[k]
        return PlaneGather(p, lambda who: normed_all.at[g, who], gs.at[k], gr.at[k])

    gathers = [gather(k) for k in range(4)]
    gathers[0].first()

    ids = 2 * e * CAP + lax.broadcasted_iota(jnp.int32, (2 * CAP, T), 0)
    expert_low = CAP * lax.broadcasted_iota(jnp.int32, (16, T), 0)

    def route_masks(g, who):
        both = slots_ref[g, who]
        first, second = both[:1], both[1:2]
        return first, second, ids == first, ids == second

    def select_cots(k):
        g = groups[k]
        got_cots[k].wait()

        def one(who):
            _, _, mark0, mark1 = route_masks(g, who)
            mark = jnp.where(mark0 | mark1, 1.0, 0.0).astype(bfloat)
            picked = jnp.dot(mark, cots[k % 2, who], preferred_element_type=single).astype(bfloat)
            for j in range(2):
                raw[j, g, row_block(who, CAP), :] = picked[j * CAP : (j + 1) * CAP]

        for who in range(8):
            one(who)
        if k < 2:
            got_cots.append(load(cot_hbm.at[groups[k + 2]], cots.at[k], k + 2))

    def select_rows(k):
        g = groups[k]

        def one(who):
            slot0, slot1, mark0, mark1 = route_masks(g, who)
            block = normed_all[g, who]
            mark = jnp.where(mark0 | mark1, 1.0, 0.0).astype(bfloat)
            picked = jnp.dot(mark, block, preferred_element_type=single).astype(bfloat)
            logits = dot_rows(router_turned_ref[...], block)
            chosen = [
                jnp.sum(
                    jnp.where((slot >= expert_low) & (slot < expert_low + CAP), logits, 0.0),
                    axis=0,
                    keepdims=True,
                )
                for slot in (slot0, slot1)
            ]
            top = jnp.maximum(chosen[0], chosen[1])
            weight = [jnp.exp(value - top) for value in chosen]
            total = weight[0] + weight[1]
            gate = jnp.sum(
                jnp.where(mark0, weight[0] / total, 0.0) + jnp.where(mark1, weight[1] / total, 0.0),
                axis=1,
                keepdims=True,
            )
            for j in range(2):
                part = slice(j * CAP, (j + 1) * CAP)
                rows[j, g, row_block(who, CAP), :] = picked[part]
                gates[j, g, row_block(who, CAP), :] = jnp.broadcast_to(gate[part], (CAP, 128))

        for who in range(8):
            one(who)

    def compute(k):
        g = groups[k]

        def one(j):
            before = jnp.dot(rows[j, g], w_up[j], preferred_element_type=single)
            act, slope = gelu_both(before)
            act = act.astype(bfloat)
            acts[j, g] = act
            gate = gates[j, g][:, :1]
            cot = raw[j, g].astype(single)
            weighted = (gate * cot).astype(bfloat)
            gated[j, g] = weighted
            act_grad = dot_rows(weighted, w_down[j])
            pre_grad = (act_grad * slope).astype(bfloat)
            pre_grads[j, g] = pre_grad
            row_grad = dot_rows(pre_grad, w_up[j])
            row_send[g, j] = row_grad.astype(bfloat).reshape(8, CAP, D)
            out = jnp.dot(act, w_down[j], preferred_element_type=single)
            out_send[g, j] = (gate * out).astype(bfloat).reshape(8, CAP, D)
            product = out * cot
            folded = product[:, :128]
            for i in range(1, D // 128):
                folded = folded + product[:, 128 * i : 128 * (i + 1)]
            slot_grads[g, j : j + 1, :] = jnp.sum(folded.T, axis=0, keepdims=True)

        for j in range(2):
            one(j)

    def give_back(k, source, target, send_sems, recv_sems):
        g = groups[k]
        slot = k if source is row_send else k // 2
        target[slot, e] = source[g, :, e]
        for i, d in enumerate(p.around):
            p.push(
                source.at[g, :, d], target.at[slot, e], send_sems.at[k, i], recv_sems.at[k, i],
                (d, s),
            )

    def out_ahead(k):
        g = groups[k]
        i = k // 2
        p.push(out_send.at[g], out_ahead_in.at[i], oas.at[i], oar.at[i], (e, g))

    def step(k):
        select_rows(k)
        compute(k)

    def arrive(k):
        p.arrived(mine, nr.at[k - 1])
        gathers[k].first()

    slot_grads[...] = jnp.zeros_like(slot_grads)
    select_cots(0)
    gathers[0].second()
    arrive(1)
    gathers[0].third()
    arrive(2)
    arrive(3)
    gathers[0].done()
    gathers[1].second()
    got_up.wait()
    got_down.wait()
    step(0)
    gathers[1].third()
    gathers[2].second()
    gathers[3].second()
    give_back(0, row_send, row_back, rs, rr)
    select_cots(1)
    gathers[1].done()
    step(1)
    give_back(1, row_send, row_back, rs, rr)
    out_ahead(1)
    gathers[2].third()
    gathers[3].third()
    select_cots(2)
    gathers[2].done()
    step(2)
    give_back(2, row_send, row_back, rs, rr)
    select_cots(3)
    gathers[3].done()
    step(3)
    give_back(3, row_send, row_back, rs, rr)
    give_back(2, out_send, out_back, os, orr)
    for k in range(3):
        p.push(
            slot_grads.at[p.others[k]], slot_z.at[k], ss.at[k], sr.at[k], (e, p.others[k])
        )

    out_ahead(3)

    def weight_grads(i):
        j = i // 3
        lanes = lane_block(lax.rem(i, 3), 256)
        inputs = rows[j].reshape(4 * 8 * CAP, D)
        up_grad_out[j, :, lanes] = dot_columns(
            inputs, pre_grads[j, :, :, lanes].reshape(4 * 8 * CAP, 256)
        ).astype(bfloat)
        inputs = acts[j].reshape(4 * 8 * CAP, -1)
        down_grad_out[j, :, lanes] = dot_columns(
            inputs, gated[j, :, :, lanes].reshape(4 * 8 * CAP, 256)
        ).astype(bfloat)

    loop(3, weight_grads)
    total = slot_grads[s]
    for k in range(3):
        p.arrived(slot_z.at[k], sr.at[k])
        total = total + slot_z[k]
    slot_sum[...] = total
    slot_plane[e] = total
    for i, d in enumerate(p.around):
        p.push(slot_sum, slot_plane.at[e], ps.at[i], pr.at[i], (d, s))

    slot_lanes = lax.broadcasted_iota(jnp.int32, (T, 16 * CAP), 1)

    def slot_columns(g):
        return slots_ref[g, e].astype(single).T.astype(jnp.int32)

    def collect(k, back, recv_sems, part, z_in, z_send, z_recv):
        g = groups[k]
        slot = k if back is row_back else k // 2
        for i in range(7):
            p.arrived(back.at[slot, e], recv_sems.at[k, i])
        columns = slot_columns(g)
        marks = jnp.where(
            (columns[:, :1] == slot_lanes) | (columns[:, 1:2] == slot_lanes), 1.0, 0.0
        ).astype(bfloat)
        combined = jnp.dot(
            marks, back[slot].reshape(16 * CAP, D), preferred_element_type=single
        )
        part[slot] = combined.astype(bfloat)
        if k:
            i = k - 1 if back is row_back else 0
            p.push(part.at[slot], z_in.at[i], z_send.at[i], z_recv.at[i], (e, g))

    for k in (1, 2, 3):
        collect(k, row_back, rr, row_part, row_z, rzs, rzr)

    for i in range(2):
        p.arrived(out_ahead_in.at[i], oar.at[i])
    for j in range(2):
        out_send[s, j] = (
            out_send[s, j].astype(single)
            + out_ahead_in[0, j].astype(single)
            + out_ahead_in[1, j].astype(single)
        ).astype(bfloat)
    give_back(0, out_send, out_back, os, orr)

    def weight_later(i):
        weight_grads(i + 3)

    loop(3, weight_later)
    leaving = [load(up_grad_out, up_grad_hbm, 6), load(down_grad_out, down_grad_hbm, 7)]

    for i in range(7):
        p.arrived(slot_sum, pr.at[i])
    turned = pltpu.roll(
        slot_plane[...].reshape(64, 8 * CAP), lax.rem(8 * CAP - CAP * e, 8 * CAP), 1
    )
    logits = dot_rows(normed_ref[...], router_turned_ref[...])
    columns = slot_columns(s)
    expert_lanes = CAP * lax.broadcasted_iota(jnp.int32, (T, 16), 1)
    picks, chosen, grads = [], [], []
    small_lanes = lax.broadcasted_iota(jnp.int32, (T, CAP), 1)
    for r in range(2):
        slot = columns[:, r : r + 1]
        picks.append((slot >= expert_lanes) & (slot < expert_lanes + CAP))
        chosen.append(jnp.sum(jnp.where(picks[r], logits, 0.0), axis=1, keepdims=True))
        found = jnp.zeros((T, CAP), single)
        for who in range(8):
            for j in range(2):
                values = turned[8 * who + j : 8 * who + j + 1, :CAP]
                found = found + jnp.where(slot - (2 * who + j) * CAP == small_lanes, values, 0.0)
        grads.append(jnp.sum(found, axis=1, keepdims=True))
    top = jnp.maximum(chosen[0], chosen[1])
    weight = [jnp.exp(value - top) for value in chosen]
    total = weight[0] + weight[1]
    weight = [value / total for value in weight]
    mean = weight[0] * grads[0] + weight[1] * grads[1]
    logit_grad = jnp.zeros((T, 16), single)
    for r in range(2):
        logit_grad = logit_grad + jnp.where(picks[r], weight[r] * (grads[r] - mean), 0.0)
    logit_grad = logit_grad.astype(bfloat)
    small_out[...] = jnp.zeros_like(small_out)
    small_out[:16, :] = dot_columns(logit_grad, normed_ref[...])
    normed_grad = jnp.dot(logit_grad, router_turned_ref[...], preferred_element_type=single)
    collect(2, out_back, orr, out_part, out_z, ozs, ozr)
    collect(0, row_back, rr, row_part, row_z, rzs, rzr)
    normed_grad = normed_grad + row_part[0].astype(single)
    for k in range(3):
        p.arrived(row_z.at[k], rzr.at[k])
        normed_grad = normed_grad + row_z[k].astype(single)
    input_grad, gain_grad = norm_pull(mid_ref[...], gains_ref[3:4, :], normed_grad)
    small_out[16:17, :] = gain_grad
    mid_grad_out[...] = own_cot_ref[...].astype(single) + input_grad

    collect(0, out_back, orr, out_part, out_z, ozs, ozr)
    p.arrived(out_z.at[0], ozr.at[0])
    result = mid_ref[...] + out_part[0].astype(single) + out_z[0].astype(single)
    hidden_out[...] = result.astype(bfloat)
    for copy in leaving:
        copy.wait()
    for copy in p.sent:
        copy.wait_send()


def run_experts(
    moe_normed, mid, gains, router, slots, own_cot, cots, up_own, expert_down
):
    vmem = pl.BlockSpec(memory_space=VMEM)
    anywhere = pl.BlockSpec(memory_space=ANY)
    shape = jax.ShapeDtypeStruct
    width = expert_down.shape[1]
    sem = pltpu.SemaphoreType.DMA
    per_expert = (EXP_DEV, 4, 8 * CAP)
    sends = (4, EXP_DEV, 8, CAP, D)
    backs = (4, 8, EXP_DEV, CAP, D)
    return pl.pallas_call(
        experts_kernel,
        name="experts",
        out_shape=(
            shape((T, D), bfloat),
            shape((T, D), single),
            shape((24, D), single),
            shape((EXP_DEV, D, width), bfloat),
            shape((EXP_DEV, width, D), bfloat),
        ),
        in_specs=[vmem] * 6 + [anywhere] * 3,
        out_specs=(vmem,) * 3 + (anywhere,) * 2,
        scratch_shapes=[
            VMEM((EXP_DEV, D, width), bfloat),
            VMEM((EXP_DEV, width, D), bfloat),
            VMEM((4, 8, T, D), bfloat),
            VMEM((2, 8, T, D), bfloat),
            VMEM((EXP_DEV, D, width), bfloat),
            VMEM((EXP_DEV, width, D), bfloat),
            VMEM(per_expert + (D,), bfloat),
            VMEM(per_expert + (D,), bfloat),
            VMEM(per_expert + (128,), single),
            VMEM(per_expert + (width,), bfloat),
            VMEM(per_expert + (width,), bfloat),
            VMEM(per_expert + (D,), bfloat),
            VMEM(sends, bfloat),
            VMEM(sends, bfloat),
            VMEM(backs, bfloat),
            VMEM((2,) + backs[1:], bfloat),
            VMEM((2,) + sends[1:], bfloat),
            VMEM((4, 8, 8 * CAP), single),
            VMEM((3, 8, 8 * CAP), single),
            VMEM((8, 8 * CAP), single),
            VMEM((8, 8, 8 * CAP), single),
            VMEM((4, T, D), bfloat),
            VMEM((2, T, D), bfloat),
            VMEM((3, T, D), bfloat),
            VMEM((1, T, D), bfloat),
            sem((3,)), sem((3,)),
            sem((4, 7)), sem((4, 7)),
            sem((4, 7)), sem((4, 7)),
            sem((4, 7)), sem((4, 7)),
            sem((3,)), sem((3,)),
            sem((7,)), sem((7,)),
            sem((3,)), sem((3,)),
            sem((3,)), sem((3,)),
            sem((8,)),
            sem((2,)), sem((2,)),
        ],
        compiler_params=pltpu.CompilerParams(
            collective_id=4, has_side_effects=True, vmem_limit_bytes=60 * 2**20
        ),
    )(
        moe_normed, mid, gains, router, slots, own_cot, cots, up_own, expert_down
    )


def finish_kernel(
    att_hbm,
    up_hbm,
    down_hbm,
    expert_up_hbm,
    expert_down_hbm,
    small_hbm,
    late_hbm,
    peak_hbm,
    grad_hbm,
    result_hbm,
    qkv_out,
    out_out,
    up_out,
    down_out,
    expert_up_out,
    expert_down_out,
    attn_gain_out,
    mlp_gain_out,
    bias_out,
    router_out,
    clip_out,
    grad_out,
    result_out,
    att,
    up,
    down,
    expert_up,
    expert_down,
    small_ref,
    late_ref,
    peak_ref,
    grad,
    qkv_wide,
    out_wide,
    up_wide,
    down_wide,
    expert_up_wide,
    expert_down_wide,
    turned,
    in_sems,
    out_sems,
):
    s = lax.axis_index("shard")

    def start(source, target, sem):
        copy = pltpu.make_async_copy(source, target, sem)
        copy.start()
        return copy

    got = [
        start(source, target, in_sems.at[i])
        for i, (source, target) in enumerate(
            (
                (expert_down_hbm, expert_down),
                (expert_up_hbm, expert_up),
                (att_hbm, att),
                (up_hbm, up),
                (down_hbm, down),
                (grad_hbm, grad),
                (small_hbm, small_ref),
                (late_hbm, late_ref),
                (peak_hbm, peak_ref),
                (result_hbm, result_out),
            )
        )
    ]
    put = []

    def widen(i):
        rows = row_block(i, 128)
        for j in range(EXP_DEV):
            expert_down_wide[j, rows, :] = expert_down[j, rows, :].astype(single)

    def widen_up(i):
        lanes = lane_block(i, 384)
        for j in range(EXP_DEV):
            expert_up_wide[j, :, lanes] = expert_up[j, :, lanes].astype(single)

    def widen_down(i):
        down_wide[row_block(i, 96), :] = down[i].astype(single)

    got[0].wait()
    loop(expert_down.shape[1] // 128, widen)
    put.append(start(expert_down_wide, expert_down_out, out_sems.at[0]))
    got[1].wait()
    loop(expert_up.shape[2] // 384, widen_up)
    put.append(start(expert_up_wide, expert_up_out, out_sems.at[1]))
    got[2].wait()
    for layer in range(2):
        for b in range(6):
            qkv_wide[layer, :, 384 * b : 384 * (b + 1)] = att[layer, b].astype(single)
        for b in range(2):
            out_wide[layer, :, 384 * b : 384 * (b + 1)] = att[layer, 6 + b].astype(single)
    put.append(start(qkv_wide, qkv_out, out_sems.at[2]))
    put.append(start(out_wide, out_out, out_sems.at[3]))
    got[3].wait()
    for b in range(8):
        for z in range(4):
            up_wide[:, 768 * z + 96 * b : 768 * z + 96 * (b + 1)] = up[
                b, :, 96 * z : 96 * (z + 1)
            ].astype(single)
    put.append(start(up_wide, up_out, out_sems.at[4]))
    got[4].wait()
    loop(8, widen_down)
    put.append(start(down_wide, down_out, out_sems.at[5]))

    for copy in got[5:]:
        copy.wait()
    grad_out[...] = grad[...][:, None, :]
    part = D // 4
    back = lax.rem(D - part * s, D)
    first_gain = jnp.concatenate([late_ref[i : i + 1, :] for i in range(6)], axis=1)
    gains = jnp.concatenate([first_gain, small_ref[16:19, :], jnp.zeros((4, D), single)])
    gains = pltpu.roll(gains, back, 1)[:, :part]
    attn_gain_out[0:1, :] = gains[0:1]
    attn_gain_out[1:2, :] = gains[2:3]
    mlp_gain_out[0:1, :] = gains[3:4]
    mlp_gain_out[1:2, :] = gains[1:2]
    turned[:, :16] = small_ref[:16, :].T
    router_out[...] = turned[row_block(s, part), :16].T
    turned[:128, : 2 * H] = late_ref[8:32, :].T
    biases = turned[row_block(s, 8), : 2 * H]
    peaks = peak_ref[...].T[:1, :]
    clips = jnp.sqrt(clip_limit / jnp.maximum(peaks, clip_limit))
    for layer in range(2):
        bias_out[layer] = biases[:, layer * H : (layer + 1) * H]
        clip_out[layer : layer + 1, :] = clips[:, layer * H : (layer + 1) * H]
    for copy in put:
        copy.wait()


def finish(att, up, down, expert_up, expert_down, small, late, peaks, grad, result):
    vmem = pl.BlockSpec(memory_space=VMEM)
    anywhere = pl.BlockSpec(memory_space=ANY)
    loaded = (att, up, down, expert_up, expert_down, small, late, peaks, grad)
    sem = pltpu.SemaphoreType.DMA
    wide = (
        (2, 192, 3 * D), (2, 192, D), (192, 8 * 384), (8 * 96, D), expert_up.shape,
        expert_down.shape,
    )
    return pl.pallas_call(
        finish_kernel,
        name="finish",
        out_shape=tuple(
            jax.ShapeDtypeStruct(dims, single)
            for dims in wide + ((2, 192), (2, 192), (2, 8, H), (16, 192), (2, H), (T, 1, D))
        )
        + (jax.ShapeDtypeStruct(result.shape, bfloat),),
        in_specs=[anywhere] * 10,
        out_specs=(anywhere,) * 6 + (vmem,) * 7,
        scratch_shapes=[VMEM(item.shape, item.dtype) for item in loaded]
        + [VMEM(dims, single) for dims in wide]
        + [VMEM((D, 128), single), sem((10,)), sem((6,))],
        compiler_params=pltpu.CompilerParams(vmem_limit_bytes=60 * 2**20),
    )(*loaded, result)


def shards(
    hidden_in,
    attn_gain,
    qkv_weight,
    out_weight,
    rel_bias,
    bucket_table,
    mlp_gain,
    mlp_up,
    mlp_down,
    router_weight,
    expert_up,
    expert_down,
    routes,
    out_grad,
):
    block_rows = hidden_in.shape[1]
    length = bucket_table.shape[0]
    groups = lax.axis_size("shard")

    backward_table = jnp.pad(bucket_table[::-1], (0, TOE))
    buckets = lax.dynamic_slice_in_dim(
        backward_table, length - block_rows * (lax.axis_index("expert") + 1), TOE
    )[None]
    cotangent = out_grad.reshape(block_rows, D)
    (
        normed, queries, attended, mid_first, mid_second, dense_normed, layer_one, peak_rows,
        moe_normed, gains, router, slots, qkv0, qkv1, projection0, projection1, dense_up,
        dense_down, kv, probs, up_own, cotangents, dense_rows, pre_act, activation,
    ) = forward(
        hidden_in.reshape(block_rows, D), attn_gain, mlp_gain, rel_bias, router_weight.T, buckets,
        routes.reshape(block_rows, 2).T,
        qkv_weight, out_weight, mlp_up, mlp_down, expert_up, cotangent,
    )
    hidden_out, mid_grad, small_in, up_grad, expert_down_low = run_experts(
        moe_normed, mid_second, gains, router, slots, cotangent, cotangents, up_own, expert_down,
    )
    hidden_grad, attention_sum, up_sum, down_sum, small_sum, late_sum, peaks, expert_up_low = (
        backward(
            mid_grad, layer_one, hidden_in.reshape(block_rows, D), mid_first, gains, normed, queries,
            attended, dense_rows, activation, pre_act, buckets, small_in, peak_rows,
            (qkv0, qkv1, projection0, projection1, dense_up, dense_down), kv, probs,
            up_grad,
        )
    )
    (
        qkv_grad, out_weight_grad, mlp_up_grad, mlp_down_grad, expert_up_grad, expert_down_grad,
        attn_gain_grad, mlp_gain_grad, rel_bias_grad, router_grad, clip_scales, hidden_grad, hidden_out,
    ) = finish(
        attention_sum, up_sum, down_sum, expert_up_low, expert_down_low, small_sum, late_sum, peaks,
        hidden_grad, hidden_out,
    )
    return (
        hidden_out.reshape(hidden_in.shape),
        hidden_grad.reshape(hidden_in.shape),
        attn_gain_grad,
        qkv_grad,
        out_weight_grad,
        rel_bias_grad,
        mlp_gain_grad,
        mlp_up_grad,
        mlp_down_grad,
        router_grad.T,
        expert_up_grad,
        expert_down_grad,
        clip_scales,
    )


def solution(mesh):
    tokens = P("shard", "expert", None, None)
    columns = P(None, "shard")
    layers = P(None, "shard", None)
    rows = P("shard", None)
    owned = P("expert", "shard", None)
    in_specs = (
        tokens, columns, layers, layers, layers, P(), columns, rows, rows, rows, owned, owned,
        tokens, tokens,
    )
    out_specs = (
        tokens, tokens, columns, layers, layers, layers, columns, rows, rows, rows, owned, owned,
        P(),
    )
    sized = mesh.shape["expert"] == 8 and mesh.shape["shard"] == 4
    part = shards if sized else plain_shards
    return jax.shard_map(part, mesh=mesh, in_specs=in_specs, out_specs=out_specs, check_vma=False)
```
